32 devices in a mesh: role: 4 (over x, core), batch: 8 (over z, y).
Axes of the slice: x: 2, y: 2, z: 4, core: 2. Of those that a mesh axis runs over, the one named last changes fastest.
Arguments:
- hidden: bfloat16 [4, 4, 4096, 768], P(None, 'role', 'batch'), may hold values from -6 to 6
- query_weight: bfloat16 [768, 768], replicated, may hold values from -0.21875 to 0.21875
- query_bias: bfloat16 [768], replicated, may hold values from -3 to 3
- key_weight: bfloat16 [768, 768], replicated, may hold values from -0.21875 to 0.21875
- value_weight: bfloat16 [768, 768], replicated, may hold values from -0.21875 to 0.21875
- value_bias: bfloat16 [768], replicated, may hold values from -3 to 3
- output_weight: bfloat16 [768, 768], replicated, may hold values from -0.625 to 0.625
- output_bias: bfloat16 [768], replicated, may hold values from -3 to 3
- first_gain: bfloat16 [768], replicated, may hold values from 0.099609375 to 1.8984375
- first_shift: bfloat16 [768], replicated, may hold values from -3 to 3
- inner_weight: bfloat16 [768, 3072], replicated, may hold values from -0.21875 to 0.21875
- inner_bias: bfloat16 [3072], replicated, may hold values from -3 to 3
- outer_weight: bfloat16 [3072, 768], replicated, may hold values from -0.109375 to 0.109375
- outer_bias: bfloat16 [768], replicated, may hold values from -3 to 3
- second_gain: bfloat16 [768], replicated, may hold values from 0.099609375 to 1.8984375
- second_shift: bfloat16 [768], replicated, may hold values from -3 to 3
- segment: int32 [4, 4, 4096], P(None, 'role', 'batch'), may hold values from -1 to 15, as said below
- positive: int32 [4, 128], replicated, may hold values from 0 to 47, as said below
- negative: int32 [4, 128], replicated, may hold values from 0 to 47
- bins: int32 [4, 128, 1], replicated, may hold values from 0 to 9
- margins: float32 [4, 128], replicated, may hold values from -6 to 6
- clusters: int32 [4, 48], replicated, may hold values from 0 to 15
Outputs:
- layer_out: bfloat16 [4, 4, 4096, 768], P(None, 'role', 'batch')
- loss: float32 [], replicated
- in_grad: float32 [4, 4, 4096, 768], P(None, 'role', 'batch')
- query_weight_grad: float32 [768, 768], P('batch')
- query_bias_grad: float32 [768], P('batch')
- key_weight_grad: float32 [768, 768], P('batch')
- value_weight_grad: float32 [768, 768], P('batch')
- value_bias_grad: float32 [768], P('batch')
- output_weight_grad: float32 [768, 768], P('batch')
- output_bias_grad: float32 [768], P('batch')
- first_gain_grad: float32 [768], P('batch')
- first_shift_grad: float32 [768], P('batch')
- inner_weight_grad: float32 [768, 3072], P('batch')
- inner_bias_grad: float32 [3072], P('batch')
- outer_weight_grad: float32 [3072, 768], P('batch')
- outer_bias_grad: float32 [768], P('batch')
- second_gain_grad: float32 [768], P('batch')
- second_shift_grad: float32 [768], P('batch')
The draws below stay inside these ranges and needn't reach their ends.
Inputs may be any that keep to these rules, and one draw needn't show every extreme that they name: `segment`: on role index 0 each device's 512 rows of a micro-batch are 16 slots of 32 rows; slot k holds k on its first rows (one or more; one slot of every device is full) and -1 on the rest. On the other role indices they are 2 slots of 256 rows; slot j holds j on its first rows (at most 200; one slot of every device holds exactly 200) and -1 on the rest. `bins`: every bin holds some query of some micro-batch. The query in slot k of batch index b (number b * 16 + k) has its positive among the passages of batch index (b - 1) mod 8: of role index 3 if k = 0, of a random role index 1 to 3 otherwise; the slot is random.
All inputs are finite; a program needn't handle non-finite values.
Results may differ from the reference program's by a relative error of at most 0.025.
Values may be sent and summed in bfloat16 or wider, within the bound.
A program may use at most 256 MiB of HBM per device.

```python
import math
import jax
import jax.numpy as jnp
import numpy as np
from jax import lax

D = 768
HEADS = 12
HEAD_DIM = 64
FF = 3072
QLEN = 32
PLEN = 200
PSLOT = 256
PASS_DEV = 2
MICRO = 4
NBINS = 10
NCLUST = 16
ROWS_DEV = 512
QUERY_DEV = 16
ATT = 512
NQ = 128
NP = 48
N_ROLE = 4
N_BATCH = 8


def draw_segment(key, part):
    key_query, key_fill, key_passage, key_longest = jax.random.split(key, 4)
    query_len = jax.random.randint(key_query, (MICRO, N_BATCH, QUERY_DEV), max(QLEN // 4, 1), QLEN + 1)
    query_full = jax.random.randint(key_fill, (MICRO, N_BATCH, 1), 0, QUERY_DEV)
    query_len = jnp.where(jnp.arange(QUERY_DEV)[None, None, :] == query_full, QLEN, query_len)
    passage_len = jax.random.randint(key_passage, (MICRO, N_ROLE - 1, N_BATCH, PASS_DEV), max(PLEN // 3, 1), PLEN + 1)
    passage_full = jax.random.randint(key_longest, (MICRO, N_ROLE - 1, N_BATCH, 1), 0, PASS_DEV)
    passage_len = jnp.where(jnp.arange(PASS_DEV)[None, None, None, :] == passage_full, PLEN, passage_len)
    row_ids = jnp.arange(ROWS_DEV)
    query_slot = row_ids // QLEN
    query_ids = jnp.where(row_ids % QLEN < query_len[..., query_slot], query_slot, -1)
    passage_slot = row_ids // PSLOT
    passage_ids = jnp.where(row_ids % PSLOT < passage_len[..., passage_slot], passage_slot, -1)
    seg_ids = jnp.concatenate([query_ids[:, None], passage_ids], axis=1)
    return seg_ids.reshape(MICRO, N_ROLE, N_BATCH * ROWS_DEV).astype(jnp.int32)


def draw_positive(key, part):
    key_role, key_slot = jax.random.split(jax.random.fold_in(key, 7), 2)
    query_ids = jnp.arange(NQ, dtype=jnp.int32)
    batch_of = query_ids // QUERY_DEV
    slot_of = query_ids % QUERY_DEV
    random_role = jax.random.randint(key_role, (MICRO, NQ), 1, N_ROLE)
    role_pick = jnp.where(slot_of[None, :] == 0, N_ROLE - 1, random_role)
    batch_pick = (batch_of + N_BATCH - 1) % N_BATCH
    slot_pick = jax.random.randint(key_slot, (MICRO, NQ), 0, PASS_DEV)
    index = ((role_pick - 1) * N_BATCH + batch_pick[None, :]) * PASS_DEV + slot_pick
    return index.astype(jnp.int32)


def touch_ends(array, key, least, largest):
    longest = array.shape.index(max(array.shape))
    spots = []
    for shift in (0, 1):
        where = [jax.random.randint(jax.random.fold_in(key, axis), (), 0, length) for axis, length in enumerate(array.shape)]
        where[longest] = (where[longest] + shift) % array.shape[longest]
        spots.append(tuple(where))
    return array.at[spots[0]].set(least).at[spots[1]].set(largest)


def block_levels(own_key, dims, pieces, low, largest):
    gain = 1.0
    for axis_at, parts in pieces:
        steps = jax.random.uniform(jax.random.fold_in(jax.random.fold_in(own_key, 6), axis_at), (parts,), jnp.float32, low / len(pieces), largest / len(pieces))
        gain = gain * jnp.repeat(jnp.exp(steps), dims[axis_at] // parts).reshape((-1,) + (1,) * (len(dims) - 1 - axis_at))
    return gain


def rank_table(amount, skew):
    portions = [(1 << 20) // math.isqrt(standing ** skew) + 1 for standing in range(1, amount + 1)]
    scale = 1 + sum(portions) // (1 << 30)
    return np.cumsum(np.array([max(1, weight // scale) for weight in portions]))


def ranked_ids(rng, extent, count, skew):
    grid = rank_table(count, skew)
    ticket = jax.random.randint(jax.random.fold_in(rng, 1), extent, 0, int(grid[count - 1]))
    rank = jnp.searchsorted(jnp.asarray(grid, jnp.int32), ticket, side="right")
    return jax.random.permutation(jax.random.fold_in(rng, 2), count)[rank].astype(jnp.int32)


def choose_distinct(rng, rows, count, top, lift):
    sequence = jax.random.permutation(jax.random.fold_in(rng, 1), count)
    boost = sequence
    for power in range(3):
        boost = boost * boost // count
    boost = boost * lift // count
    chance = jax.random.randint(jax.random.fold_in(rng, 2), (rows, count), 0, 4096) + boost
    holders = jax.random.permutation(jax.random.fold_in(rng, 3), rows)[jnp.arange(count) % rows]
    chance = jnp.where(jnp.arange(rows)[:, None] == holders[None, :], 1 << 14, chance)
    score = chance * count + jnp.arange(count)
    return lax.top_k(score.astype(jnp.int32), top)[1].astype(jnp.int32)


def scatter_about(rng, dims, spread, most, pieces=(), kind=jnp.bfloat16):
    factor_of = block_levels(rng, dims, pieces, -0.22, 0.18) if pieces else 1.0
    entries = jax.random.normal(rng, dims, jnp.float32) * spread * factor_of
    return jnp.minimum(jnp.maximum(entries, -most), most).astype(kind)


def setup_inputs(seed: int = 0) -> dict:
    streams_of = jax.random.split(jax.random.key(seed), 23)
    hidden = scatter_about(streams_of[0], (MICRO, N_ROLE, N_BATCH * ROWS_DEV, D), 1.0, 6.0, ((1, 4), (2, 8)))
    query_weight = scatter_about(streams_of[1], (D, D), D ** -0.5, 0.21875)
    query_bias = scatter_about(streams_of[2], (D,), 0.5, 3.0)
    key_weight = scatter_about(streams_of[3], (D, D), D ** -0.5, 0.21875)
    value_weight = scatter_about(streams_of[4], (D, D), D ** -0.5, 0.21875)
    value_bias = scatter_about(streams_of[5], (D,), 0.5, 3.0)
    output_weight = scatter_about(streams_of[6], (D, D), (D // 8) ** -0.5, 0.625)
    output_bias = scatter_about(streams_of[7], (D,), 0.5, 3.0)
    first_gain = jnp.clip(1.0 + 0.18 * jax.random.normal(streams_of[8], (D,), jnp.float32), 0.099609375, 1.8984375).astype(jnp.bfloat16)
    first_shift = scatter_about(streams_of[9], (D,), 0.5, 3.0)
    inner_weight = scatter_about(streams_of[10], (D, FF), D ** -0.5, 0.21875)
    inner_bias = scatter_about(streams_of[11], (FF,), 0.5, 3.0)
    outer_weight = scatter_about(streams_of[12], (FF, D), FF ** -0.5, 0.109375)
    outer_bias = scatter_about(streams_of[13], (D,), 0.5, 3.0)
    second_gain = jnp.clip(1.0 + 0.18 * jax.random.normal(streams_of[14], (D,), jnp.float32), 0.099609375, 1.8984375).astype(jnp.bfloat16)
    second_shift = scatter_about(streams_of[15], (D,), 0.5, 3.0)
    segment = draw_segment(jax.random.fold_in(streams_of[22], 71), 0)
    positive = draw_positive(jax.random.fold_in(streams_of[22], 71), 0)
    negative = touch_ends(jax.random.randint(streams_of[18], (MICRO, NQ), 0, NP), jax.random.fold_in(streams_of[18], 1), 0, NP - 1).astype(jnp.int32)
    bins = choose_distinct(streams_of[19], MICRO * NQ, NBINS, 1, 819).reshape((MICRO, NQ, 1))
    margins = scatter_about(streams_of[20], (MICRO, NQ), 1.5, 6.0, (), jnp.float32)
    clusters = touch_ends(ranked_ids(streams_of[21], (MICRO, NP), NCLUST, 2), jax.random.fold_in(streams_of[21], 3), 0, NCLUST - 1).astype(jnp.int32)
    return {"hidden": hidden, "query_weight": query_weight, "query_bias": query_bias, "key_weight": key_weight, "value_weight": value_weight, "value_bias": value_bias, "output_weight": output_weight, "output_bias": output_bias, "first_gain": first_gain, "first_shift": first_shift, "inner_weight": inner_weight, "inner_bias": inner_bias, "outer_weight": outer_weight, "outer_bias": outer_bias, "second_gain": second_gain, "second_shift": second_shift, "segment": segment, "positive": positive, "negative": negative, "bins": bins, "margins": margins, "clusters": clusters}


@jax.custom_vjp
def low(v):
    return lax.optimization_barrier(v.astype(jnp.bfloat16)).astype(jnp.float32)

@jax.custom_vjp
def low_back(v):
    return v

def low_keep(v):
    return (low(v), None)

def low_pass(kept, grad):
    return (grad,)

def back_keep(v):
    return (v, None)

def back_low(kept, grad):
    return (low(grad),)
low.defvjp(low_keep, low_pass)
low_back.defvjp(back_keep, back_low)
highest = lax.Precision.HIGHEST
very_low = -1e+30
epsilon = 1e-12

def product(left, right):
    return jnp.dot(left, right, precision=highest, preferred_element_type=jnp.float32)

def normalize(incoming, gain_vec, shift_vec):
    center = incoming - lax.optimization_barrier(jnp.mean(incoming, axis=-1, keepdims=True))
    inv_std = lax.rsqrt(lax.optimization_barrier(jnp.mean(center * center, axis=-1, keepdims=True)) + epsilon)
    return center * inv_std * gain_vec + shift_vec

def block_forward(params, hidden_rows, seg_rows):
    query_weight, query_bias, key_weight, value_weight, value_bias, output_weight, output_bias, first_gain, first_shift, inner_weight, inner_bias, outer_weight, outer_bias, second_gain, second_shift = params
    row_count = hidden_rows.shape[0]
    query_rows = low_back(low(product(hidden_rows, query_weight) + query_bias)).reshape(row_count, HEADS, HEAD_DIM)
    key_rows = low_back(low(product(hidden_rows, key_weight))).reshape(row_count, HEADS, HEAD_DIM)
    value_rows = low_back(low(product(hidden_rows, value_weight) + value_bias)).reshape(row_count, HEADS, HEAD_DIM)
    scores = jnp.einsum('ihd,jhd->hij', query_rows, key_rows, precision=highest) * HEAD_DIM ** (-0.5)
    scores = low_back(scores)
    same_seg = (seg_rows[:, None] == seg_rows[None, :])[None]
    scores = jnp.where(same_seg, scores, very_low)
    row_max = lax.optimization_barrier(jnp.max(scores, axis=-1, keepdims=True))
    raised = jnp.exp(scores - row_max)
    attn_probs = low(raised / lax.optimization_barrier(jnp.sum(raised, axis=-1, keepdims=True)))
    context = jnp.einsum('hij,jhd->ihd', attn_probs, value_rows, precision=highest).reshape(row_count, D)
    context = low_back(low(context))
    attended = low_back(product(context, output_weight) + output_bias)
    first_norm = normalize(hidden_rows + attended, first_gain, first_shift)
    inner_pre = low_back(product(low(first_norm), inner_weight) + inner_bias)
    outer_out = low_back(product(low(jax.nn.gelu(inner_pre, approximate=False)), outer_weight) + outer_bias)
    return normalize(first_norm + outer_out, second_gain, second_shift)

def forward(hidden_f, params, segment, positive, negative, bin_ids, margins, clusters):
    blocks = hidden_f.reshape(-1, ATT, D)
    seg_blocks = segment.reshape(-1, ATT)
    block_step = jax.checkpoint(lambda pair_in: block_forward(params, pair_in[0], pair_in[1]))
    block_out = lax.map(block_step, (blocks, seg_blocks)).reshape(MICRO, N_ROLE, N_BATCH * ROWS_DEV, D)
    query_cls = low(block_out[:, 0].reshape(MICRO, NQ, QLEN, D)[:, :, 0])
    passage_cls = low(block_out[:, 1:].reshape(MICRO, NP, PSLOT, D)[:, :, 0])
    scores = jnp.einsum('mqd,mpd->mqp', query_cls, passage_cls, precision=highest) * D ** (-0.5)
    columns = jnp.arange(NP, dtype=jnp.int32)
    pos_hit = positive[:, :, None] == columns
    neg_hit = negative[:, :, None] == columns
    pos_cluster = lax.optimization_barrier(jnp.sum(jnp.where(pos_hit, clusters[:, None, :], 0), axis=-1))
    allowed = clusters[:, None, :] == pos_cluster[:, :, None]
    masked = jnp.where(allowed, scores, very_low)
    row_max = lax.optimization_barrier(jnp.max(masked, axis=-1))
    log_total = row_max + jnp.log(lax.optimization_barrier(jnp.sum(jnp.exp(masked - row_max[..., None]), axis=-1)))
    pos_score = lax.optimization_barrier(jnp.sum(jnp.where(pos_hit, scores, 0.0), axis=-1))
    neg_score = lax.optimization_barrier(jnp.sum(jnp.where(neg_hit, scores, 0.0), axis=-1))
    bin_hit = bin_ids[..., None] == jnp.arange(NBINS, dtype=jnp.int32)
    bin_counts = lax.optimization_barrier(jnp.sum(bin_hit.astype(jnp.float32), axis=(0, 1)))
    weight = lax.optimization_barrier(jnp.sum(jnp.where(bin_hit, MICRO * NQ / (NBINS * bin_counts), 0.0), axis=-1))
    margin_gap = pos_score - neg_score - margins
    objective = jnp.sum(log_total - pos_score + weight * margin_gap * margin_gap)
    return (block_out, objective)

def reference(hidden, query_weight, query_bias, key_weight, value_weight, value_bias, output_weight, output_bias, first_gain, first_shift, inner_weight, inner_bias, outer_weight, outer_bias, second_gain, second_shift, segment, positive, negative, bins, margins, clusters):
    params = tuple((weight.astype(jnp.float32) for weight in (query_weight, query_bias, key_weight, value_weight, value_bias, output_weight, output_bias, first_gain, first_shift, inner_weight, inner_bias, outer_weight, outer_bias, second_gain, second_shift)))
    hidden_f = hidden.astype(jnp.float32)
    bin_ids = bins[..., 0]

    def whole(hidden_in, params_in):
        return forward(hidden_in, params_in, segment, positive, negative, bin_ids, margins.astype(jnp.float32), clusters)
    (block_out, objective), pull_back = jax.vjp(whole, hidden_f, params)
    in_grad, gradients = pull_back((jnp.zeros_like(block_out), jnp.ones_like(objective)))
    return (block_out.astype(jnp.bfloat16), objective / (MICRO * NQ), in_grad, gradients[0], gradients[1], gradients[2], gradients[3], gradients[4], gradients[5], gradients[6], gradients[7], gradients[8], gradients[9], gradients[10], gradients[11], gradients[12], gradients[13], gradients[14])
```

```python
import functools

import jax
import jax.numpy as jnp
from jax import lax
from jax.experimental import pallas as pl
from jax.experimental.pallas import tpu as pltpu
from jax.sharding import PartitionSpec as P

D = 768
HEADS = 12
HEAD_DIM = 64
QLEN = 32
PSLOT = 256
NBINS = 10

very_low = -1e30
epsilon = 1e-12
bf16 = jnp.bfloat16
f32 = jnp.float32
MESH = pl.DeviceIdType.MESH
VMEM_BYTES = 60 * 1024 * 1024


def dot(left, right):
    return jnp.dot(left, right, preferred_element_type=f32)


def dot_right(left, right):
    return lax.dot_general(left, right, (((1,), (1,)), ((), ())), preferred_element_type=f32)


def dot_left(left, right):
    return lax.dot_general(left, right, (((0,), (0,)), ((), ())), preferred_element_type=f32)


def three_parts(wide):
    high = wide.astype(bf16)
    rest = wide - high.astype(f32)
    middle = rest.astype(bf16)
    return high, middle, (rest - middle.astype(f32)).astype(bf16)


def norm_parts(incoming):
    center = incoming - jnp.mean(incoming, axis=-1, keepdims=True)
    inv_std = lax.rsqrt(jnp.mean(center * center, axis=-1, keepdims=True) + epsilon)
    return center * inv_std, inv_std


def norm_back(scaled, normed, inv_std):
    return inv_std * (
        scaled
        - jnp.mean(scaled, axis=-1, keepdims=True)
        - normed * jnp.mean(scaled * normed, axis=-1, keepdims=True)
    )


def gelu(u):
    return 0.5 * u * (1.0 + lax.erf(u * 0.7071067811865476))


def gelu_slope(u):
    return 0.5 * (1.0 + lax.erf(u * 0.7071067811865476)) + u * (
        0.3989422804014327 * jnp.exp(-0.5 * u * u)
    )


def head_mask(cands):
    rows = lax.broadcasted_iota(jnp.int32, (HEADS * cands, D), 0)
    cols = lax.broadcasted_iota(jnp.int32, (HEADS * cands, D), 1)
    return rows // cands == cols // HEAD_DIM


def per_head(rows, mask):
    return jnp.where(mask, jnp.concatenate([rows] * HEADS, axis=0), jnp.zeros((), rows.dtype))


def from_heads(wide, mask, cands):
    kept = jnp.where(mask, wide, 0.0)
    total = kept[:cands]
    for head in range(1, HEADS):
        total = total + kept[head * cands : (head + 1) * cands]
    return total


def first_kernel(
    micros, rows, hid, seg, wq, wk, wv, vec, keys, values, probs, query_c, query_msg, pass_msg
):
    cands = rows // QLEN
    mask = head_mask(cands)
    pick = (
        lax.broadcasted_iota(jnp.int32, (cands, rows), 1)
        == lax.broadcasted_iota(jnp.int32, (cands, rows), 0) * QLEN
    )
    pick_low = pick.astype(f32).astype(bf16)
    picked = []
    for m in range(micros):
        picked.append(dot(pick_low, hid[m * rows : (m + 1) * rows, :]).astype(bf16))
    x_cand = jnp.concatenate(picked, axis=0)
    q_cand = ((dot(x_cand, wq[...]) + vec[0:1, :]).astype(bf16).astype(f32) * HEAD_DIM**-0.5).astype(bf16)
    query_c[...] = q_cand
    query_msg[0 : micros * cands, :] = x_cand
    for m in range(micros):
        block = slice(m * rows, (m + 1) * rows)
        x = hid[block, :]
        k = dot(x, wk[...]).astype(bf16)
        v = (dot(x, wv[...]) + vec[1:2, :]).astype(bf16)
        keys[block, :] = k
        values[block, :] = v
        seg_row = seg[m : m + 1, :].astype(f32)
        seg_col = jnp.sum(jnp.where(pick, seg_row, 0.0), axis=-1, keepdims=True)
        bias = jnp.where(seg_col == seg_row, 0.0, very_low)
        q_wide = per_head(q_cand[m * cands : (m + 1) * cands], mask)
        scores = dot_right(q_wide, k) + jnp.concatenate([bias] * HEADS, axis=0)
        raised = jnp.exp(scores - jnp.max(scores, axis=-1, keepdims=True))
        prob = raised * (1.0 / jnp.sum(raised, axis=-1, keepdims=True))
        probs[m * HEADS * cands : (m + 1) * HEADS * cands, :] = prob
        context = from_heads(dot(prob.astype(bf16), v), mask, cands)
        query_msg[(micros + m) * cands : (micros + m + 1) * cands, :] = context.astype(bf16)
    wide = query_msg[...].astype(f32)
    per_slot = PSLOT // QLEN
    chosen = []
    for part in range(2):
        for m in range(micros):
            for slot in range(cands // per_slot):
                at = (part * micros + m) * cands + slot * per_slot
                chosen.append(wide[at : at + 1])
    pass_msg[...] = jnp.concatenate(chosen, axis=0).astype(bf16)


def first_stage(hid, seg, wq, wk, wv, vec, micros):
    rows = hid.shape[0] // micros
    cands = rows // QLEN
    total = micros * cands
    passes = micros * (rows // PSLOT)
    return pl.pallas_call(
        functools.partial(first_kernel, micros, rows),
        out_shape=(
            jax.ShapeDtypeStruct(hid.shape, bf16),
            jax.ShapeDtypeStruct(hid.shape, bf16),
            jax.ShapeDtypeStruct((micros * HEADS * cands, rows), f32),
            jax.ShapeDtypeStruct((total, D), bf16),
            jax.ShapeDtypeStruct((2 * total, D), bf16),
            jax.ShapeDtypeStruct((2 * passes, D), bf16),
        ),
        compiler_params=pltpu.CompilerParams(vmem_limit_bytes=VMEM_BYTES),
        name="first",
    )(hid, seg, wq, wk, wv, vec)


def bulk_kernel(
    hid, seg, keys, values, wq, wo, wi, wu, vec, out, queries, context, bias
):
    x = hid[...]
    queries[...] = (
        (dot(x, wq[...]) + vec[0:1, :]).astype(bf16).astype(f32) * HEAD_DIM**-0.5
    ).astype(bf16)
    seg_row = seg[0].astype(f32)
    rows = seg_row.shape[1]
    seg_col = jnp.broadcast_to(seg_row, (128, rows)).T[:, 0:1]
    bias[...] = jnp.where(seg_col == seg_row, 0.0, very_low)
    for head in range(HEADS):
        part = slice(head * HEAD_DIM, (head + 1) * HEAD_DIM)
        scores = dot_right(queries[:, part], keys[:, part]) + bias[...]
        raised = jnp.exp(scores - jnp.max(scores, axis=-1, keepdims=True))
        summed = jnp.sum(raised, axis=-1, keepdims=True)
        context[:, part] = (dot(raised.astype(bf16), values[:, part]) * (1.0 / summed)).astype(bf16)
    attended = dot(context[...], wo[...]) + vec[2:3, :]
    normed, _ = norm_parts(x.astype(f32) + attended)
    first_norm = normed * vec[3:4, :] + vec[4:5, :]
    first_low = first_norm.astype(bf16)
    total = first_norm + vec[5:6, :]
    for j in range(wi.shape[1] // D):
        part = slice(j * D, (j + 1) * D)
        u = dot(first_low, wi[:, part]) + vec[8 + j : 9 + j, :]
        total = total + dot(gelu(u).astype(bf16), wu[part, :])
    normed, _ = norm_parts(total)
    out[...] = (normed * vec[6:7, :] + vec[7:8, :]).astype(bf16)


def bulk_stage(hid, seg, keys, values, wq, wo, wi, wu, vec, micros):
    rows = hid.shape[0] // micros

    def whole(array):
        return pl.BlockSpec(array.shape, lambda m: (0, 0), pipeline_mode=pl.Buffered(1))

    row_block = pl.BlockSpec((rows, D), lambda m: (m, 0))
    return pl.pallas_call(
        bulk_kernel,
        grid=(micros,),
        in_specs=[
            row_block,
            pl.BlockSpec((1, 1, rows), lambda m: (m, 0, 0)),
            row_block,
            row_block,
            whole(wq),
            whole(wo),
            whole(wi),
            whole(wu),
            whole(vec),
        ],
        out_specs=row_block,
        out_shape=jax.ShapeDtypeStruct(hid.shape, bf16),
        scratch_shapes=[
            pltpu.VMEM((rows, D), bf16),
            pltpu.VMEM((rows, D), bf16),
            pltpu.VMEM((rows, rows), f32),
        ],
        compiler_params=pltpu.CompilerParams(vmem_limit_bytes=VMEM_BYTES),
        name="bulk",
    )(hid, seg[:, None, :], keys, values, wq, wo, wi, wu, vec)


def peer_of(step, roles, batches):
    role, batch = lax.axis_index("role"), lax.axis_index("batch")
    place = (role // 2) * batches + batch
    other = lax.rem(place + step, (roles // 2) * batches)
    return other, (other // batches) * 2 + role % 2, other % batches


def greet(roles, batches):
    role, batch = lax.axis_index("role"), lax.axis_index("batch")
    mate = role + 1 - 2 * (role % 2)
    count = (roles // 2) * batches
    barrier = pltpu.get_barrier_semaphore()
    pl.semaphore_signal(barrier, inc=1, device_id=(mate, batch), device_id_type=MESH)

    def signal(step, carry):
        _, role_to, batch_to = peer_of(step, roles, batches)
        pl.semaphore_signal(barrier, inc=1, device_id=(role_to, batch_to), device_id_type=MESH)
        return carry

    lax.fori_loop(1, count, signal, 0)
    pl.semaphore_wait(barrier, count)


def spread_rows(roles, batches, query_ref, pass_ref, query_all, pass_all, sems):
    send, forward, query_in, pass_in, own = sems
    role, batch = lax.axis_index("role"), lax.axis_index("batch")
    core = role % 2
    mate = role + 1 - 2 * core
    count = (roles // 2) * batches

    def remote(src, dst, out_sem, in_sem, role_to, batch_to):
        return pltpu.make_async_remote_copy(
            src_ref=src,
            dst_ref=dst,
            send_sem=out_sem,
            recv_sem=in_sem,
            device_id=(role_to, batch_to),
            device_id_type=MESH,
        )

    def query_to(out_sem, src, slot, role_to, batch_to):
        return remote(src, query_all.at[slot], out_sem, query_in.at[slot], role_to, batch_to)

    def pass_to(out_sem, src, slot, role_to, batch_to):
        return remote(src, pass_all.at[slot], out_sem, pass_in.at[slot], role_to, batch_to)

    my_pass = (role - 1) * batches + batch

    def begin():
        @pl.when(role == 0)
        def _():
            def go(step, carry):
                _, role_to, batch_to = peer_of(step, roles, batches)
                query_to(send.at[step], query_ref, batch, role_to, batch_to).start()
                return carry

            lax.fori_loop(1, count, go, 0)
            query_to(send.at[0], query_ref, batch, mate, batch).start()
            keep = pltpu.make_async_copy(query_ref, query_all.at[batch], own)
            keep.start()
            keep.wait()

        @pl.when(role > 0)
        def _():
            def go(step, carry):
                _, role_to, batch_to = peer_of(step, roles, batches)
                pass_to(send.at[step], pass_ref, my_pass, role_to, batch_to).start()
                return carry

            lax.fori_loop(1, count, go, 0)
            pass_to(send.at[0], pass_ref, my_pass, mate, batch).start()
            keep = pltpu.make_async_copy(pass_ref, pass_all.at[my_pass], own)
            keep.start()
            keep.wait()

    def relay():
        def hand_query(step, carry):
            other, role_of, batch_of = peer_of(step, roles, batches)
            pl.when(role_of == 0)(
                lambda: query_to(send.at[0], query_ref, batch_of, mate, batch).wait_recv()
            )
            pl.when(role_of == 0)(
                lambda: query_to(
                    forward.at[step], query_all.at[batch_of], batch_of, mate, batch
                ).start()
            )
            return carry

        def hand_pass(step, carry):
            other, role_of, batch_of = peer_of(step, roles, batches)
            slot = (role_of - 1) * batches + batch_of
            pl.when(role_of > 0)(
                lambda: pass_to(send.at[0], pass_ref, slot, mate, batch).wait_recv()
            )
            pl.when(role_of > 0)(
                lambda: pass_to(forward.at[step], pass_all.at[slot], slot, mate, batch).start()
            )
            return carry

        def both(step, carry):
            hand_query(step, 0)
            hand_pass(step, 0)
            return carry

        lax.fori_loop(1, count, both, 0)

    def end():
        def take(step, carry):
            other = lax.rem((role // 2) * batches + batch + step, count)
            role_of, batch_of = (other // batches) * 2 + 1 - core, other % batches
            slot = (role_of - 1) * batches + batch_of
            pl.when(role_of == 0)(
                lambda: query_to(send.at[0], query_ref, batch_of, mate, batch).wait_recv()
            )
            pl.when(role_of > 0)(
                lambda: pass_to(send.at[0], pass_ref, slot, mate, batch).wait_recv()
            )
            return carry

        lax.fori_loop(0, count, take, 0)

        def sent(step, carry):
            pl.when(role == 0)(
                lambda: query_to(send.at[step], query_ref, batch, mate, batch).wait_send()
            )
            pl.when(role > 0)(
                lambda: pass_to(send.at[step], pass_ref, my_pass, mate, batch).wait_send()
            )
            return carry

        lax.fori_loop(0, count, sent, 0)

        def relayed(step, carry):
            other, role_of, batch_of = peer_of(step, roles, batches)
            slot = (role_of - 1) * batches + batch_of
            pl.when(role_of == 0)(
                lambda: query_to(
                    forward.at[step], query_all.at[batch_of], batch_of, mate, batch
                ).wait_send()
            )
            pl.when(role_of > 0)(
                lambda: pass_to(forward.at[step], pass_all.at[slot], slot, mate, batch).wait_send()
            )
            return carry

        lax.fori_loop(1, count, relayed, 0)

    return begin, relay, end


def spread_sems(roles, batches):
    count = (roles // 2) * batches
    return [
        pltpu.SemaphoreType.DMA((count,)),
        pltpu.SemaphoreType.DMA((count,)),
        pltpu.SemaphoreType.DMA((batches,)),
        pltpu.SemaphoreType.DMA(((roles - 1) * batches,)),
        pltpu.SemaphoreType.DMA,
    ]


def gather_kernel(roles, batches, query_ref, pass_ref, query_out, pass_out, query_all, pass_all, *sems):
    greet(roles, batches)
    begin, relay, end = spread_rows(
        roles, batches, query_ref, pass_ref, query_all, pass_all, sems
    )
    begin()
    relay()
    end()
    query_out[...] = query_all[...]
    pass_out[...] = pass_all[...]


def gather_stage(query_msg, pass_msg, roles, batches):
    vmem = pl.BlockSpec(memory_space=pltpu.VMEM)
    shapes = [
        ((batches,) + query_msg.shape, query_msg.dtype),
        (((roles - 1) * batches,) + pass_msg.shape, pass_msg.dtype),
    ]
    return pl.pallas_call(
        functools.partial(gather_kernel, roles, batches),
        in_specs=[vmem, vmem],
        out_specs=(vmem, vmem),
        out_shape=tuple(jax.ShapeDtypeStruct(*s) for s in shapes),
        scratch_shapes=[pltpu.VMEM(*s) for s in shapes] + spread_sems(roles, batches),
        compiler_params=pltpu.CompilerParams(
            collective_id=1, has_side_effects=True, vmem_limit_bytes=VMEM_BYTES
        ),
        name="gather",
    )(query_msg, pass_msg)


def middle_kernel(
    micros,
    cands,
    columns,
    query_all,
    pass_all,
    wo,
    wi,
    wu,
    vec,
    positive,
    negative,
    bins,
    margins,
    clusters,
    loss_out,
    inner_grad,
    outer_grad,
    output_grad,
    vectors,
    x_slice,
    d_own,
    x_all,
    c_all,
    u_all,
    g_all,
    n_one,
    d_rows,
):
    role, batch = lax.axis_index("role"), lax.axis_index("batch")
    batches = query_all.shape[0]
    own_rows = micros * cands
    n_query = batches * own_rows
    n_dev = pass_all.shape[0]
    per_dev = pass_all.shape[1] // 2
    per_micro = per_dev // micros
    n_pass = n_dev * per_dev
    n_rows = n_query + n_pass
    inner = wi.shape[1]
    chunks = [slice(j * D, (j + 1) * D) for j in range(inner // D)]

    for b in range(batches):
        x_all[b * own_rows : (b + 1) * own_rows, :] = query_all[b, 0:own_rows, :]
        c_all[b * own_rows : (b + 1) * own_rows, :] = query_all[b, own_rows : 2 * own_rows, :]
    wide = pass_all[...].astype(f32)
    x_all[n_query:n_rows, :] = wide[:, 0:per_dev, :].reshape(n_pass, D).astype(bf16)
    c_all[n_query:n_rows, :] = wide[:, per_dev:, :].reshape(n_pass, D).astype(bf16)

    attended = dot(c_all[...], wo[...]) + vec[2:3, :]
    normed, inv_one = norm_parts(x_all[...].astype(f32) + attended)
    n_one[...] = normed
    first_norm = normed * vec[3:4, :] + vec[4:5, :]
    first_low = first_norm.astype(bf16)
    total = first_norm + vec[5:6, :]
    for j, part in enumerate(chunks):
        u = dot(first_low, wi[:, part]) + vec[8 + j : 9 + j, :]
        u_all[:, part] = u
        g = gelu(u).astype(bf16)
        g_all[:, part] = g
        total = total + dot(g, wu[part, :])
    n_two, inv_two = norm_parts(total)
    low = (n_two * vec[6:7, :] + vec[7:8, :]).astype(bf16)
    q_low, p_low = low[:n_query], low[n_query:]

    bin_ids = bins[...]
    queries_total = bin_ids.shape[0] * bin_ids.shape[1]
    weight = jnp.zeros(bin_ids.shape, f32)
    for k in range(NBINS):
        hit = (bin_ids == k).astype(f32)
        amount = jnp.sum(jnp.sum(hit, axis=1, keepdims=True), axis=0, keepdims=True)
        weight = weight + hit * (queries_total / (NBINS * jnp.maximum(amount, 1.0)))

    lane = lax.broadcasted_iota(jnp.int32, (n_query, bin_ids.shape[1]), 1)
    row = lax.broadcasted_iota(jnp.int32, (n_query, bin_ids.shape[1]), 0)
    here = lane == (row // own_rows) * cands + row % cands

    def by_micro(table):
        parts = [
            jnp.broadcast_to(table[m : m + 1, :], (cands, table.shape[1])) for m in range(micros)
        ]
        return jnp.concatenate(parts * batches, axis=0)

    def per_query(table):
        return jnp.sum(jnp.where(here, by_micro(table), 0.0), axis=-1, keepdims=True)

    pos = per_query(positive[...].astype(f32))
    neg = per_query(negative[...].astype(f32))
    margin = per_query(margins[...])
    weight = per_query(weight)

    col = lax.broadcasted_iota(jnp.int32, (n_query, n_pass), 1)
    row = lax.broadcasted_iota(jnp.int32, (n_query, n_pass), 0)
    same = (col % per_dev) // per_micro == (row % own_rows) // cands
    ident = ((col // per_dev) * per_micro + col % per_micro).astype(f32)
    n_ids = n_dev * per_micro
    tab_row = lax.broadcasted_iota(jnp.int32, (n_ids, n_pass), 0)
    tab_col = lax.broadcasted_iota(jnp.int32, (n_ids, n_pass), 1)
    table = tab_row == (tab_col // per_dev) * per_micro + tab_col % per_micro
    cluster = by_micro(dot(clusters[...].astype(f32).astype(bf16), table.astype(f32).astype(bf16)))
    pos_hit = jnp.logical_and(same, ident == pos)
    neg_hit = jnp.logical_and(same, ident == neg)
    pos_cluster = jnp.sum(jnp.where(pos_hit, cluster, 0.0), axis=-1, keepdims=True)
    allowed = jnp.logical_and(same, cluster == pos_cluster)
    scores = dot_right(q_low, p_low) * D**-0.5
    masked = jnp.where(allowed, scores, very_low)
    row_max = jnp.max(masked, axis=-1, keepdims=True)
    raised = jnp.exp(masked - row_max)
    summed = jnp.sum(raised, axis=-1, keepdims=True)
    pos_score = jnp.sum(jnp.where(pos_hit, scores, 0.0), axis=-1, keepdims=True)
    neg_score = jnp.sum(jnp.where(neg_hit, scores, 0.0), axis=-1, keepdims=True)
    gap = pos_score - neg_score - margin
    terms = row_max + jnp.log(summed) - pos_score + weight * gap * gap
    loss_out[...] = jnp.broadcast_to(
        jnp.sum(terms, axis=0, keepdims=True) / queries_total, loss_out.shape
    )
    pull = 2.0 * weight * gap
    pos_one, neg_one = pos_hit.astype(f32), neg_hit.astype(f32)
    d_scores = (raised * (1.0 / summed) - pos_one + pull * (pos_one - neg_one)) * D**-0.5
    parts = three_parts(d_scores)
    d_query = sum(dot(part, p_low) for part in parts)
    d_pass = sum(dot_left(part, q_low) for part in parts)
    grad = jnp.concatenate([d_query, d_pass], axis=0)

    def total_of(array):
        return jnp.sum(array, axis=0, keepdims=True)

    vectors[6:7, :] = total_of(grad * n_two)
    vectors[7:8, :] = total_of(grad)
    d_two = norm_back(grad * vec[6:7, :], n_two, inv_two)
    d_outer = d_two.astype(bf16)
    vectors[5:6, :] = total_of(d_outer.astype(f32))
    select = (
        lax.broadcasted_iota(jnp.int32, (D, 128), 0)
        == lax.broadcasted_iota(jnp.int32, (D, 128), 1) + batch * columns
    )
    select = jnp.logical_and(select, lax.broadcasted_iota(jnp.int32, (D, 128), 1) < columns)
    select = select.astype(f32).astype(bf16)
    first_low = (n_one[...] * vec[3:4, :] + vec[4:5, :]).astype(bf16)
    y_slice = dot(first_low, select).astype(bf16)
    d_first = d_two
    for j, part in enumerate(chunks):
        d_inner = (dot_right(d_outer, wu[part, :]) * gelu_slope(u_all[:, part])).astype(bf16)
        vectors[8 + j : 9 + j, :] = total_of(d_inner.astype(f32))
        inner_grad[:, part] = dot_left(y_slice, d_inner)[:columns]
        d_first = d_first + dot_right(d_inner, wi[:, part])
    span = inner // batches
    outer_grad[...] = dot_left(g_all[:, pl.ds(pl.multiple_of(batch * span, 128), span)], d_outer)
    vectors[3:4, :] = total_of(d_first * n_one[...])
    vectors[4:5, :] = total_of(d_first)
    d_one = norm_back(d_first * vec[3:4, :], n_one[...], inv_one)
    d_rows[...] = d_one
    d_low = d_one.astype(bf16)
    bias_row = total_of(d_low.astype(f32))
    vectors[2:3, :] = bias_row
    vectors[1:2, :] = sum(dot_right(part, wo[...]) for part in three_parts(bias_row))
    vectors[0:1, :] = jnp.zeros_like(bias_row)
    c_slice = dot(c_all[...], select).astype(bf16)
    output_grad[...] = dot_left(c_slice, d_low)[:columns]
    x_slice[...] = dot(x_all[...], select).astype(bf16)

    @pl.when(role == 0)
    def _():
        d_own[...] = d_rows[pl.ds(pl.multiple_of(batch * own_rows, 8), own_rows), :]

    @pl.when(role > 0)
    def _():
        d_own[...] = jnp.zeros_like(d_own)
        begin = pl.multiple_of(n_query + ((role - 1) * batches + batch) * per_dev, 8)
        mine = d_rows[pl.ds(begin, per_dev), :]
        for m in range(micros):
            for slot in range(per_micro):
                at = m * cands + slot * (PSLOT // QLEN)
                d_own[at : at + 1, :] = mine[m * per_micro + slot : m * per_micro + slot + 1, :]


def middle_stage(query_all, pass_all, wo, wi, wu, vec, positive, negative, bins, margins, clusters):
    batches = query_all.shape[0]
    micros = positive.shape[0]
    own_rows = query_all.shape[1] // 2
    n_pass = pass_all.shape[0] * pass_all.shape[1] // 2
    n_rows = batches * own_rows + n_pass
    columns = D // batches
    inner = wi.shape[1]
    return pl.pallas_call(
        functools.partial(middle_kernel, micros, own_rows // micros, columns),
        out_shape=(
            jax.ShapeDtypeStruct((1, 128), f32),
            jax.ShapeDtypeStruct((columns, inner), f32),
            jax.ShapeDtypeStruct((inner // batches, D), f32),
            jax.ShapeDtypeStruct((columns, D), f32),
            jax.ShapeDtypeStruct((8 + inner // D, D), f32),
            jax.ShapeDtypeStruct((n_rows, 128), bf16),
            jax.ShapeDtypeStruct((own_rows, D), f32),
        ),
        scratch_shapes=[
            pltpu.VMEM((n_rows, D), bf16),
            pltpu.VMEM((n_rows, D), bf16),
            pltpu.VMEM((n_rows, inner), f32),
            pltpu.VMEM((n_rows, inner), bf16),
            pltpu.VMEM((n_rows, D), f32),
            pltpu.VMEM((n_rows, D), f32),
        ],
        compiler_params=pltpu.CompilerParams(vmem_limit_bytes=VMEM_BYTES),
        name="middle",
    )(query_all, pass_all, wo, wi, wu, vec, positive, negative, bins, margins, clusters)


def attention_back_kernel(
    hid, keys, values, probs, query_c, d_own, wq, wk, wv, wo, in_grad, dq_out, dq_pass, key_part, value_part,
    z_key, z_value, q_keep, c_keep,
):
    m = pl.program_id(0)
    cands = query_c.shape[0]
    mask = head_mask(cands)
    wide_rows = HEADS * cands
    d_low = d_own[...].astype(bf16)
    d_context = dot_right(d_low, wo[...]).astype(bf16)
    q_wide = per_head(query_c[...], mask)
    c_wide = per_head(d_context, mask)
    prob = probs[...]
    d_prob = dot_right(c_wide, values[...])
    pulled = prob * d_prob
    d_scores = (pulled - prob * jnp.sum(pulled, axis=-1, keepdims=True)).astype(bf16)
    both = jnp.concatenate([d_scores, prob.astype(bf16)], axis=0)
    d_query = (from_heads(dot(d_scores, keys[...]), mask, cands) * HEAD_DIM**-0.5).astype(bf16)
    dq_out[...] = d_query
    d_query_wide = d_query.astype(f32)
    slots = dq_pass.shape[0] // pl.num_programs(0)
    for slot in range(slots):
        at = slot * (PSLOT // QLEN)
        dq_pass[pl.ds(m * slots + slot, 1), :] = d_query_wide[at : at + 1, :]
    sums = dot(both, hid[...])
    here = pl.ds(pl.multiple_of(m * wide_rows, 16), wide_rows)
    z_key[here, :] = sums[:wide_rows].astype(bf16)
    z_value[here, :] = sums[wide_rows:].astype(bf16)
    q_keep[here, :] = q_wide
    c_keep[here, :] = c_wide
    back = jnp.concatenate(
        [dot_right(q_wide, wk[...]).astype(bf16), dot_right(c_wide, wv[...]).astype(bf16)], axis=0
    )
    in_grad[...] = dot_left(both, back)
    extra = dot_right(d_query, wq[...]) + d_own[...]
    for cand in range(cands):
        at = slice(cand * QLEN, cand * QLEN + 1)
        in_grad[at, :] = in_grad[at, :] + extra[cand : cand + 1, :]

    @pl.when(m == pl.num_programs(0) - 1)
    def _():
        key_part[...] = dot_left(z_key[...], q_keep[...]).astype(bf16)
        value_part[...] = dot_left(z_value[...], c_keep[...]).astype(bf16)


def attention_back_stage(hid, keys, values, probs, query_c, d_own, wq, wk, wv, wo, micros):
    rows = hid.shape[0] // micros
    cands = rows // QLEN
    wide_rows = HEADS * cands
    passes = micros * (rows // PSLOT)

    def whole(array):
        return pl.BlockSpec(array.shape, lambda m: (0, 0), pipeline_mode=pl.Buffered(1))

    def block(count, width):
        return pl.BlockSpec((count, width), lambda m: (m, 0))

    fixed = pl.BlockSpec((D, D), lambda m: (0, 0))
    return pl.pallas_call(
        attention_back_kernel,
        grid=(micros,),
        in_specs=[
            block(rows, D),
            block(rows, D),
            block(rows, D),
            block(wide_rows, rows),
            block(cands, D),
            block(cands, D),
            whole(wq),
            whole(wk),
            whole(wv),
            whole(wo),
        ],
        out_specs=(
            block(rows, D),
            block(cands, D),
            pl.BlockSpec((passes, D), lambda m: (0, 0)),
            fixed,
            fixed,
        ),
        out_shape=(
            jax.ShapeDtypeStruct(hid.shape, f32),
            jax.ShapeDtypeStruct(query_c.shape, bf16),
            jax.ShapeDtypeStruct((passes, D), f32),
            jax.ShapeDtypeStruct((D, D), bf16),
            jax.ShapeDtypeStruct((D, D), bf16),
        ),
        scratch_shapes=[pltpu.VMEM((micros * wide_rows, D), bf16)] * 4,
        compiler_params=pltpu.CompilerParams(vmem_limit_bytes=VMEM_BYTES),
        name="attention_back",
    )(hid, keys, values, probs, query_c, d_own, wq, wk, wv, wo)


def reduce_kernel(
    roles, batches, dq_ref, dq_pass, key_part, value_part, x_slice, query_grad, query_bias, key_grad, value_grad,
    query_all, pass_all, from_mate, summed, received, partial, across, final, other_final,
    send, forward, query_in, pass_in, own, mate_out, mate_in, part_out, part_in, x_out, x_in, last_out, last_in,
):
    role, batch = lax.axis_index("role"), lax.axis_index("batch")
    core = role % 2
    mate = role + 1 - 2 * core
    across_role = lax.rem(role + 2, roles)
    columns = key_grad.shape[0]

    def remote(src, dst, out_sem, in_sem, role_to, batch_to):
        return pltpu.make_async_remote_copy(
            src_ref=src,
            dst_ref=dst,
            send_sem=out_sem,
            recv_sem=in_sem,
            device_id=(role_to, batch_to),
            device_id_type=MESH,
        )

    greet(roles, batches)
    begin, relay, end = spread_rows(
        roles, batches, dq_ref, dq_pass, query_all, pass_all, (send, forward, query_in, pass_in, own)
    )

    @pl.when(core == 0)
    def _():
        remote(value_part, from_mate, mate_out, mate_in, mate, batch).start()

    @pl.when(core == 1)
    def _():
        remote(key_part, from_mate, mate_out, mate_in, mate, batch).start()

    begin()
    remote(key_part, from_mate, mate_out, mate_in, mate, batch).wait()

    @pl.when(core == 0)
    def _():
        summed[...] = (key_part[...].astype(f32) + from_mate[...].astype(f32)).astype(bf16)

    @pl.when(core == 1)
    def _():
        summed[...] = (value_part[...].astype(f32) + from_mate[...].astype(f32)).astype(bf16)

    def to_batch(step):
        other = lax.rem(batch + step, batches)
        return remote(
            summed.at[other], received.at[batch], part_out.at[other], part_in.at[batch], role, other
        )

    def from_batch(step):
        other = lax.rem(batch + step, batches)
        return remote(
            summed.at[other], received.at[other], part_out.at[other], part_in.at[other], role, other
        )

    def start_part(step, carry):
        to_batch(step).start()
        return carry

    lax.fori_loop(1, batches, start_part, 0)
    relay()
    partial[...] = summed[batch].astype(f32)

    def add_part(step, carry):
        from_batch(step).wait_recv()
        other = lax.rem(batch + step, batches)
        partial[...] += received[other].astype(f32)
        return carry

    lax.fori_loop(1, batches, add_part, 0)
    swap = remote(partial, across, x_out, x_in, across_role, batch)
    swap.start()
    end()
    count = query_all.shape[0] * query_all.shape[1]
    d_query = query_all[...].reshape(count, D)
    d_pass = pass_all[...].reshape(-1, D)
    query_grad[...] = (
        dot_left(x_slice[0:count, :], d_query) + dot_left(x_slice[count:, :], d_pass.astype(bf16))
    )[:columns]
    query_bias[...] = jnp.sum(d_query.astype(f32), axis=0, keepdims=True) + jnp.sum(
        d_pass, axis=0, keepdims=True
    )
    swap.wait()
    final[...] = partial[...] + across[...]
    last = remote(final, other_final, last_out, last_in, mate, batch)
    last.start()

    def sent_part(step, carry):
        to_batch(step).wait_send()
        return carry

    lax.fori_loop(1, batches, sent_part, 0)
    last.wait()

    @pl.when(core == 0)
    def _():
        key_grad[...] = final[...]
        value_grad[...] = other_final[...]

    @pl.when(core == 1)
    def _():
        key_grad[...] = other_final[...]
        value_grad[...] = final[...]


def reduce_stage(dq, dq_pass, key_part, value_part, x_slice, roles, batches):
    columns = D // batches
    count = (roles // 2) * batches
    vmem = pl.BlockSpec(memory_space=pltpu.VMEM)
    block = (columns, D)
    dma = pltpu.SemaphoreType.DMA
    return pl.pallas_call(
        functools.partial(reduce_kernel, roles, batches),
        in_specs=[vmem] * 5,
        out_specs=(vmem,) * 4,
        out_shape=(
            jax.ShapeDtypeStruct(block, f32),
            jax.ShapeDtypeStruct((1, D), f32),
            jax.ShapeDtypeStruct(block, f32),
            jax.ShapeDtypeStruct(block, f32),
        ),
        scratch_shapes=[
            pltpu.VMEM((batches,) + dq.shape, bf16),
            pltpu.VMEM(((roles - 1) * batches,) + dq_pass.shape, f32),
            pltpu.VMEM((batches,) + block, bf16),
            pltpu.VMEM((batches,) + block, bf16),
            pltpu.VMEM((batches,) + block, bf16),
            pltpu.VMEM(block, f32),
            pltpu.VMEM(block, f32),
            pltpu.VMEM(block, f32),
            pltpu.VMEM(block, f32),
        ]
        + spread_sems(roles, batches)
        + [dma, dma, dma((batches,)), dma((batches,)), dma, dma, dma, dma],
        compiler_params=pltpu.CompilerParams(
            collective_id=2, has_side_effects=True, vmem_limit_bytes=VMEM_BYTES
        ),
        name="reduce",
    )(
        dq,
        dq_pass,
        key_part.reshape(batches, columns, D),
        value_part.reshape(batches, columns, D),
        x_slice,
    )


def body(
    roles,
    batches,
    hidden,
    query_weight,
    query_bias,
    key_weight,
    value_weight,
    value_bias,
    output_weight,
    output_bias,
    first_gain,
    first_shift,
    inner_weight,
    inner_bias,
    outer_weight,
    outer_bias,
    second_gain,
    second_shift,
    segment,
    positive,
    negative,
    bins,
    margins,
    clusters,
):
    micros, rows = hidden.shape[0], hidden.shape[2]
    hid = hidden.reshape(micros * rows, D)
    seg = segment.reshape(micros, rows)
    vec = jnp.concatenate(
        [
            query_bias,
            value_bias,
            output_bias,
            first_gain,
            first_shift,
            outer_bias,
            second_gain,
            second_shift,
            inner_bias,
        ]
    )
    vec = vec.astype(f32).reshape(-1, D)
    keys, values, probs, query_c, query_msg, pass_msg = first_stage(
        hid, seg, query_weight, key_weight, value_weight, vec, micros
    )
    query_all, pass_all = gather_stage(query_msg, pass_msg, roles, batches)
    layer_out = bulk_stage(
        hid, seg, keys, values, query_weight, output_weight, inner_weight, outer_weight, vec, micros
    )
    loss, inner_grad, outer_grad, output_grad, vectors, x_slice, d_own = middle_stage(
        query_all,
        pass_all,
        output_weight,
        inner_weight,
        outer_weight,
        vec,
        positive,
        negative,
        bins[..., 0],
        margins,
        clusters,
    )
    in_grad, dq, dq_pass, key_part, value_part = attention_back_stage(
        hid,
        keys,
        values,
        probs,
        query_c,
        d_own,
        query_weight,
        key_weight,
        value_weight,
        output_weight,
        micros,
    )
    query_grad, query_bias_row, key_grad, value_grad = reduce_stage(
        dq, dq_pass, key_part, value_part, x_slice, roles, batches
    )
    batch = lax.axis_index("batch")
    columns = D // batches
    span = inner_weight.shape[1] // batches
    mine = lax.dynamic_slice_in_dim(vectors[:8], batch * columns, columns, axis=1)
    mine_inner = lax.dynamic_slice_in_dim(vectors[8:].reshape(-1), batch * span, span)
    mine_query = lax.dynamic_slice_in_dim(query_bias_row[0], batch * columns, columns)
    return (
        layer_out.reshape(hidden.shape),
        loss[0, 0],
        in_grad.reshape(hidden.shape),
        query_grad,
        mine_query,
        key_grad,
        value_grad,
        mine[1],
        output_grad,
        mine[2],
        mine[3],
        mine[4],
        inner_grad,
        mine_inner,
        outer_grad,
        mine[5],
        mine[6],
        mine[7],
    )


highest = lax.Precision.HIGHEST


def multiply(left, right):
    return jnp.dot(left, right, preferred_element_type=jnp.float32)


def left_product(left, right):
    return jnp.einsum("rd,re->de", left, right, preferred_element_type=jnp.float32)


def right_product(left, right):
    return jnp.einsum("rd,ed->re", left, right, preferred_element_type=jnp.float32)


def select_rows(array, stride):
    return array.reshape((array.shape[0] // stride, stride) + array.shape[1:])[:, 0]


def normalize(incoming, gain_vec, shift_vec):
    center = incoming - jnp.mean(incoming, axis=-1, keepdims=True)
    inv_std = lax.rsqrt(jnp.mean(center * center, axis=-1, keepdims=True) + epsilon)
    normed = center * inv_std
    return (normed * gain_vec + shift_vec, normed, inv_std)


def normalize_back(grad_in, normed, inv_std, gain_vec):
    scaled = grad_in * gain_vec
    return inv_std * (
        scaled
        - jnp.mean(scaled, axis=-1, keepdims=True)
        - normed * jnp.mean(scaled * normed, axis=-1, keepdims=True)
    )


def encode(hidden_rows, seg_rows, weights, att_rows):
    (
        query_weight,
        query_bias,
        key_weight,
        value_weight,
        value_bias,
        output_weight,
        output_bias,
        first_gain,
        first_shift,
        inner_weight,
        inner_bias,
        outer_weight,
        outer_bias,
        second_gain,
        second_shift,
    ) = weights
    row_count = hidden_rows.shape[0]
    blocks = row_count // att_rows
    head_scale = HEAD_DIM ** (-0.5)
    block_shape = (blocks, att_rows, HEADS, HEAD_DIM)
    query_rows = (multiply(hidden_rows, query_weight) + query_bias).astype(jnp.bfloat16)
    key_rows = multiply(hidden_rows, key_weight).astype(jnp.bfloat16)
    value_rows = (multiply(hidden_rows, value_weight) + value_bias).astype(jnp.bfloat16)
    scores = (
        jnp.einsum(
            "bihd,bjhd->bhij",
            query_rows.reshape(block_shape),
            key_rows.reshape(block_shape),
            preferred_element_type=jnp.float32,
        )
        * head_scale
    )
    seg_blocks = seg_rows.reshape(blocks, att_rows)
    same_seg = (seg_blocks[:, :, None] == seg_blocks[:, None, :])[:, None]
    scores = jnp.where(same_seg, scores, very_low)
    row_max = jnp.max(scores, axis=-1, keepdims=True)
    raised = jnp.exp(scores - row_max)
    summed = jnp.sum(raised, axis=-1, keepdims=True)
    attn_probs = (raised / summed).astype(jnp.bfloat16)
    log_total = (row_max + jnp.log(summed))[..., 0]
    context = (
        jnp.einsum(
            "bhij,bjhd->bihd",
            attn_probs,
            value_rows.reshape(block_shape),
            preferred_element_type=jnp.float32,
        )
        .reshape(row_count, D)
        .astype(jnp.bfloat16)
    )
    attended = multiply(context, output_weight) + output_bias
    first_norm, normed_one, inv_one = normalize(
        hidden_rows.astype(jnp.float32) + attended, first_gain, first_shift
    )
    first_low = first_norm.astype(jnp.bfloat16)
    inner_pre = multiply(first_low, inner_weight) + inner_bias
    activated = jax.nn.gelu(inner_pre, approximate=False).astype(jnp.bfloat16)
    outer_out = multiply(activated, outer_weight) + outer_bias
    block_out, normed_two, inv_two = normalize(first_norm + outer_out, second_gain, second_shift)
    log_cand = log_total.reshape(blocks, HEADS, att_rows // QLEN, QLEN)[..., 0]
    kept = (
        key_rows,
        value_rows,
        select_rows(query_rows, QLEN),
        log_cand,
        select_rows(context, QLEN),
        select_rows(normed_one, QLEN),
        select_rows(inv_one, QLEN),
        select_rows(first_low, QLEN),
        select_rows(inner_pre, QLEN),
        select_rows(activated, QLEN),
        select_rows(normed_two, QLEN),
        select_rows(inv_two, QLEN),
    )
    return (block_out, kept)


def encode_back(grad_out, hidden_rows, seg_rows, weights, kept, att_rows):
    (
        query_weight,
        query_bias,
        key_weight,
        value_weight,
        value_bias,
        output_weight,
        output_bias,
        first_gain,
        first_shift,
        inner_weight,
        inner_bias,
        outer_weight,
        outer_bias,
        second_gain,
        second_shift,
    ) = weights
    (
        key_rows,
        value_rows,
        query_cand,
        log_cand,
        context_cand,
        normed_one,
        inv_one,
        first_cand,
        inner_cand,
        active_cand,
        normed_two,
        inv_two,
    ) = kept
    row_count = hidden_rows.shape[0]
    blocks = row_count // att_rows
    cand_rows = row_count // QLEN
    per_block = att_rows // QLEN
    head_scale = HEAD_DIM ** (-0.5)
    hidden_cand = select_rows(hidden_rows, QLEN)
    second_gain_grad = jnp.sum(grad_out * normed_two, axis=0)
    second_shift_grad = jnp.sum(grad_out, axis=0)
    d_second = normalize_back(grad_out, normed_two, inv_two, second_gain)
    d_outer = d_second.astype(jnp.bfloat16)
    outer_weight_grad = left_product(active_cand, d_outer)
    outer_bias_grad = jnp.sum(d_outer.astype(jnp.float32), axis=0)
    d_active = right_product(d_outer, outer_weight)
    gelu_pull = jax.vjp(functools.partial(jax.nn.gelu, approximate=False), inner_cand)[1]
    d_inner = gelu_pull(d_active)[0].astype(jnp.bfloat16)
    inner_weight_grad = left_product(first_cand, d_inner)
    inner_bias_grad = jnp.sum(d_inner.astype(jnp.float32), axis=0)
    d_first = d_second + right_product(d_inner, inner_weight)
    first_gain_grad = jnp.sum(d_first * normed_one, axis=0)
    first_shift_grad = jnp.sum(d_first, axis=0)
    d_attend = normalize_back(d_first, normed_one, inv_one, first_gain)
    d_attend_low = d_attend.astype(jnp.bfloat16)
    output_weight_grad = left_product(context_cand, d_attend_low)
    output_bias_grad = jnp.sum(d_attend_low.astype(jnp.float32), axis=0)
    cand_shape = (blocks, per_block, HEADS, HEAD_DIM)
    block_shape = (blocks, att_rows, HEADS, HEAD_DIM)
    d_context = right_product(d_attend_low, output_weight).astype(jnp.bfloat16).reshape(cand_shape)
    query_heads = query_cand.reshape(cand_shape)
    key_heads = key_rows.reshape(block_shape)
    value_heads = value_rows.reshape(block_shape)
    scores = (
        jnp.einsum("bihd,bjhd->bhij", query_heads, key_heads, preferred_element_type=jnp.float32)
        * head_scale
    )
    seg_blocks = seg_rows.reshape(blocks, att_rows)
    seg_cand = seg_blocks.reshape(blocks, per_block, QLEN)[..., 0]
    same_seg = (seg_cand[:, :, None] == seg_blocks[:, None, :])[:, None]
    attn_probs = jnp.where(same_seg, jnp.exp(scores - log_cand[..., None]), 0.0)
    d_probs = jnp.einsum(
        "bihd,bjhd->bhij", d_context, value_heads, preferred_element_type=jnp.float32
    )
    d_scores = (
        attn_probs * (d_probs - jnp.sum(attn_probs * d_probs, axis=-1, keepdims=True))
    ).astype(jnp.bfloat16)
    d_query = (
        (
            jnp.einsum("bhij,bjhd->bihd", d_scores, key_heads, preferred_element_type=jnp.float32)
            * head_scale
        )
        .reshape(cand_rows, D)
        .astype(jnp.bfloat16)
    )
    d_keys = (
        (
            jnp.einsum("bhij,bihd->bjhd", d_scores, query_heads, preferred_element_type=jnp.float32)
            * head_scale
        )
        .reshape(row_count, D)
        .astype(jnp.bfloat16)
    )
    d_values = (
        jnp.einsum(
            "bhij,bihd->bjhd",
            attn_probs.astype(jnp.bfloat16),
            d_context,
            preferred_element_type=jnp.float32,
        )
        .reshape(row_count, D)
        .astype(jnp.bfloat16)
    )
    query_weight_grad = left_product(hidden_cand, d_query)
    query_bias_grad = jnp.sum(d_query.astype(jnp.float32), axis=0)
    key_weight_grad = left_product(hidden_rows, d_keys)
    value_weight_grad = left_product(hidden_rows, d_values)
    value_bias_grad = jnp.sum(d_values.astype(jnp.float32), axis=0)
    d_hidden = right_product(d_keys, key_weight) + right_product(d_values, value_weight)
    d_cand = right_product(d_query, query_weight) + d_attend
    d_hidden = d_hidden.reshape(cand_rows, QLEN, D)
    d_hidden = jnp.concatenate(
        [d_hidden[:, :1] + d_cand[:, None], d_hidden[:, 1:]], axis=1
    ).reshape(row_count, D)
    gradients = (
        query_weight_grad,
        query_bias_grad,
        key_weight_grad,
        value_weight_grad,
        value_bias_grad,
        output_weight_grad,
        output_bias_grad,
        first_gain_grad,
        first_shift_grad,
        inner_weight_grad,
        inner_bias_grad,
        outer_weight_grad,
        outer_bias_grad,
        second_gain_grad,
        second_shift_grad,
    )
    return (d_hidden, gradients)


def general_body(
    hidden,
    query_weight,
    query_bias,
    key_weight,
    value_weight,
    value_bias,
    output_weight,
    output_bias,
    first_gain,
    first_shift,
    inner_weight,
    inner_bias,
    outer_weight,
    outer_bias,
    second_gain,
    second_shift,
    segment,
    positive,
    negative,
    bins,
    margins,
    clusters,
):
    weights = (
        query_weight,
        query_bias,
        key_weight,
        value_weight,
        value_bias,
        output_weight,
        output_bias,
        first_gain,
        first_shift,
        inner_weight,
        inner_bias,
        outer_weight,
        outer_bias,
        second_gain,
        second_shift,
    )
    micro_count = hidden.shape[0]
    row_count = hidden.shape[2]
    att_rows = min(512, row_count)
    cand_rows = row_count // QLEN
    slot_stride = PSLOT // QLEN
    emb_scale = D ** (-0.5)
    query_flag = jnp.where(lax.axis_index("role") == 0, 1.0, 0.0).astype(jnp.float32)
    first_query = lax.axis_index("batch") * cand_rows
    bin_ids = bins[..., 0]
    query_total = bin_ids.shape[0] * bin_ids.shape[1]
    bin_slots = jnp.arange(NBINS, dtype=jnp.int32)
    bin_counts = jnp.sum((bin_ids[..., None] == bin_slots).astype(jnp.float32), axis=(0, 1))
    bin_table = query_total / (NBINS * bin_counts)
    loss_accum = jnp.zeros((), jnp.float32)
    accum = None
    layer_list = []
    grad_list = []
    for micro_idx in range(micro_count):
        hidden_rows = hidden[micro_idx, 0]
        seg_rows = segment[micro_idx, 0]
        block_out, kept = encode(hidden_rows, seg_rows, weights, att_rows)
        layer_list.append(block_out.astype(jnp.bfloat16))
        cls_rows = select_rows(block_out, QLEN).astype(jnp.bfloat16)
        passage_cls = cls_rows.reshape(-1, slot_stride, D)[:, 0]
        gathered = lax.all_gather(passage_cls, ("role", "batch"), axis=0, tiled=True)
        offset = lax.axis_size("batch") * passage_cls.shape[0]
        passages = gathered[offset:]
        scores = right_product(cls_rows, passages) * emb_scale
        columns = jnp.arange(passages.shape[0], dtype=jnp.int32)
        pos_ids = lax.dynamic_slice_in_dim(positive[micro_idx], first_query, cand_rows)
        neg_ids = lax.dynamic_slice_in_dim(negative[micro_idx], first_query, cand_rows)
        bin_mine = lax.dynamic_slice_in_dim(bin_ids[micro_idx], first_query, cand_rows)
        margin_mine = lax.dynamic_slice_in_dim(margins[micro_idx], first_query, cand_rows)
        pos_hit = pos_ids[:, None] == columns
        neg_hit = neg_ids[:, None] == columns
        cluster_row = clusters[micro_idx]
        pos_cluster = jnp.sum(jnp.where(pos_hit, cluster_row[None, :], 0), axis=-1)
        allowed = cluster_row[None, :] == pos_cluster[:, None]
        masked = jnp.where(allowed, scores, very_low)
        row_max = jnp.max(masked, axis=-1, keepdims=True)
        raised = jnp.exp(masked - row_max)
        summed = jnp.sum(raised, axis=-1, keepdims=True)
        softened = raised / summed
        log_total = (row_max + jnp.log(summed))[:, 0]
        pos_score = jnp.sum(jnp.where(pos_hit, scores, 0.0), axis=-1)
        neg_score = jnp.sum(jnp.where(neg_hit, scores, 0.0), axis=-1)
        weight_query = jnp.sum(jnp.where(bin_mine[:, None] == bin_slots, bin_table, 0.0), axis=-1)
        margin_gap = pos_score - neg_score - margin_mine
        loss_accum = loss_accum + query_flag * jnp.sum(
            log_total - pos_score + weight_query * margin_gap * margin_gap
        )
        pos_float = pos_hit.astype(jnp.float32)
        neg_float = neg_hit.astype(jnp.float32)
        d_scores = query_flag * (
            softened
            - pos_float
            + (2.0 * weight_query * margin_gap)[:, None] * (pos_float - neg_float)
        )
        passages_wide = passages.astype(jnp.float32)
        cls_wide = cls_rows.astype(jnp.float32)
        d_cls = (
            jnp.dot(d_scores, passages_wide, precision=highest, preferred_element_type=jnp.float32)
            * emb_scale
        )
        padded = jnp.concatenate([jnp.zeros((cand_rows, offset), jnp.float32), d_scores], axis=1)
        received = lax.psum_scatter(
            jnp.einsum(
                "qp,qd->pd", padded, cls_wide, precision=highest, preferred_element_type=jnp.float32
            )
            * emb_scale,
            ("role", "batch"),
            scatter_dimension=0,
            tiled=True,
        )
        spread = jnp.concatenate(
            [received[:, None], jnp.zeros((received.shape[0], slot_stride - 1, D), jnp.float32)],
            axis=1,
        ).reshape(cand_rows, D)
        d_hidden, micro_grads = encode_back(
            d_cls + spread, hidden_rows, seg_rows, weights, kept, att_rows
        )
        grad_list.append(d_hidden)
        accum = micro_grads if accum is None else jax.tree.map(jnp.add, accum, micro_grads)
    shards = (
        lax.psum_scatter(accum[0], "batch", scatter_dimension=0, tiled=True),
        lax.psum_scatter(accum[1], "batch", scatter_dimension=0, tiled=True),
        lax.psum_scatter(accum[2], "batch", scatter_dimension=0, tiled=True),
        lax.psum_scatter(accum[3], "batch", scatter_dimension=0, tiled=True),
        lax.psum_scatter(accum[4], "batch", scatter_dimension=0, tiled=True),
        lax.psum_scatter(accum[5], "batch", scatter_dimension=0, tiled=True),
        lax.psum_scatter(accum[6], "batch", scatter_dimension=0, tiled=True),
        lax.psum_scatter(accum[7], "batch", scatter_dimension=0, tiled=True),
        lax.psum_scatter(accum[8], "batch", scatter_dimension=0, tiled=True),
        lax.psum_scatter(accum[9], "batch", scatter_dimension=0, tiled=True),
        lax.psum_scatter(accum[10], "batch", scatter_dimension=0, tiled=True),
        lax.psum_scatter(accum[11], "batch", scatter_dimension=0, tiled=True),
        lax.psum_scatter(accum[12], "batch", scatter_dimension=0, tiled=True),
        lax.psum_scatter(accum[13], "batch", scatter_dimension=0, tiled=True),
        lax.psum_scatter(accum[14], "batch", scatter_dimension=0, tiled=True),
    )
    summed_grads = lax.psum(
        (
            shards[0],
            shards[1],
            shards[2],
            shards[3],
            shards[4],
            shards[5],
            shards[6],
            shards[7],
            shards[8],
            shards[9],
            shards[10],
            shards[11],
            shards[12],
            shards[13],
            shards[14],
        ),
        "role",
    )
    loss_value = lax.psum(loss_accum, ("role", "batch")) / query_total
    layer_out = jnp.stack(layer_list)[:, None]
    in_grad = jnp.stack(grad_list)[:, None]
    return (
        layer_out,
        loss_value,
        in_grad,
        summed_grads[0],
        summed_grads[1],
        summed_grads[2],
        summed_grads[3],
        summed_grads[4],
        summed_grads[5],
        summed_grads[6],
        summed_grads[7],
        summed_grads[8],
        summed_grads[9],
        summed_grads[10],
        summed_grads[11],
        summed_grads[12],
        summed_grads[13],
        summed_grads[14],
    )


def solution(mesh):
    roles, batches = mesh.shape["role"], mesh.shape["batch"]
    small = batches <= 8
    step = functools.partial(body, roles, batches) if small else general_body
    placed = (
        P(None, "role", "batch", None),
        P(),
        P(),
        P(),
        P(),
        P(),
        P(),
        P(),
        P(),
        P(),
        P(),
        P(),
        P(),
        P(),
        P(),
        P(),
        P(None, "role", "batch"),
        P(),
        P(),
        P(),
        P(),
        P(),
    )
    return jax.shard_map(
        step,
        mesh=mesh,
        in_specs=placed,
        out_specs=(
            P(None, "role", "batch", None),
            P(),
            P(None, "role", "batch", None),
            P("batch", None),
            P("batch"),
            P("batch", None),
            P("batch", None),
            P("batch"),
            P("batch", None),
            P("batch"),
            P("batch"),
            P("batch"),
            P("batch", None),
            P("batch"),
            P("batch", None),
            P("batch"),
            P("batch"),
            P("batch"),
        ),
        check_vma=False,
    )
```

```python
import functools

import jax
import jax.numpy as jnp
from jax import lax
from jax.experimental import pallas as pl
from jax.experimental.pallas import tpu as pltpu
from jax.sharding import PartitionSpec as P

D = 768
HEADS = 12
HEAD_DIM = 64
QLEN = 32
PSLOT = 256
NBINS = 10

very_low = -1e30
epsilon = 1e-12
bf16 = jnp.bfloat16
f32 = jnp.float32
MESH = pl.DeviceIdType.MESH
VMEM_BYTES = 60 * 1024 * 1024


def dot(left, right):
    return jnp.dot(left, right, preferred_element_type=f32)


def dot_right(left, right):
    return lax.dot_general(left, right, (((1,), (1,)), ((), ())), preferred_element_type=f32)


def dot_left(left, right):
    return lax.dot_general(left, right, (((0,), (0,)), ((), ())), preferred_element_type=f32)


def three_parts(wide):
    high = wide.astype(bf16)
    rest = wide - high.astype(f32)
    middle = rest.astype(bf16)
    return high, middle, (rest - middle.astype(f32)).astype(bf16)


def norm_parts(incoming):
    center = incoming - jnp.mean(incoming, axis=-1, keepdims=True)
    inv_std = lax.rsqrt(jnp.mean(center * center, axis=-1, keepdims=True) + epsilon)
    return center * inv_std, inv_std


def norm_back(scaled, normed, inv_std):
    return inv_std * (
        scaled
        - jnp.mean(scaled, axis=-1, keepdims=True)
        - normed * jnp.mean(scaled * normed, axis=-1, keepdims=True)
    )


def gelu(u):
    return 0.5 * u * (1.0 + lax.erf(u * 0.7071067811865476))


def gelu_slope(u):
    return 0.5 * (1.0 + lax.erf(u * 0.7071067811865476)) + u * (
        0.3989422804014327 * jnp.exp(-0.5 * u * u)
    )


def head_mask(cands):
    rows = lax.broadcasted_iota(jnp.int32, (HEADS * cands, D), 0)
    cols = lax.broadcasted_iota(jnp.int32, (HEADS * cands, D), 1)
    return rows // cands == cols // HEAD_DIM


def per_head(rows, mask):
    return jnp.where(mask, jnp.concatenate([rows] * HEADS, axis=0), jnp.zeros((), rows.dtype))


def from_heads(wide, mask, cands):
    kept = jnp.where(mask, wide, 0.0)
    total = kept[:cands]
    for head in range(1, HEADS):
        total = total + kept[head * cands : (head + 1) * cands]
    return total


def first_kernel(
    micros, rows, hid, seg, wq, wk, wv, *refs
):
    lines, (keys, values, probs, query_c, query_msg, pass_msg, vec) = refs[:-7], refs[-7:]
    at = 0
    for line in lines:
        wide = line[...].astype(f32).reshape(1, -1)
        for j in range(wide.shape[1] // D):
            vec[at : at + 1, :] = wide[:, j * D : (j + 1) * D]
            at += 1
    cands = rows // QLEN
    mask = head_mask(cands)
    pick = (
        lax.broadcasted_iota(jnp.int32, (cands, rows), 1)
        == lax.broadcasted_iota(jnp.int32, (cands, rows), 0) * QLEN
    )
    pick_low = pick.astype(f32).astype(bf16)
    picked = []
    for m in range(micros):
        picked.append(dot(pick_low, hid[m * rows : (m + 1) * rows, :]).astype(bf16))
    x_cand = jnp.concatenate(picked, axis=0)
    q_cand = ((dot(x_cand, wq[...]) + vec[0:1, :]).astype(bf16).astype(f32) * HEAD_DIM**-0.5).astype(bf16)
    query_c[...] = q_cand
    query_msg[0 : micros * cands, :] = x_cand
    for m in range(micros):
        block = slice(m * rows, (m + 1) * rows)
        x = hid[block, :]
        k = dot(x, wk[...]).astype(bf16)
        v = (dot(x, wv[...]) + vec[1:2, :]).astype(bf16)
        keys[block, :] = k
        values[block, :] = v
        seg_row = seg[m : m + 1, :].astype(f32)
        seg_col = jnp.sum(jnp.where(pick, seg_row, 0.0), axis=-1, keepdims=True)
        bias = jnp.where(seg_col == seg_row, 0.0, very_low)
        q_wide = per_head(q_cand[m * cands : (m + 1) * cands], mask)
        scores = dot_right(q_wide, k) + jnp.concatenate([bias] * HEADS, axis=0)
        raised = jnp.exp(scores - jnp.max(scores, axis=-1, keepdims=True))
        prob = raised * (1.0 / jnp.sum(raised, axis=-1, keepdims=True))
        probs[m * HEADS * cands : (m + 1) * HEADS * cands, :] = prob
        context = from_heads(dot(prob.astype(bf16), v), mask, cands)
        query_msg[(micros + m) * cands : (micros + m + 1) * cands, :] = context.astype(bf16)
    wide = query_msg[...].astype(f32)
    per_slot = PSLOT // QLEN
    chosen = []
    for part in range(2):
        for m in range(micros):
            for slot in range(cands // per_slot):
                at = (part * micros + m) * cands + slot * per_slot
                chosen.append(wide[at : at + 1])
    pass_msg[...] = jnp.concatenate(chosen, axis=0).astype(bf16)


def first_stage(hid, seg, wq, wk, wv, lines, micros):
    rows = hid.shape[0] // micros
    cands = rows // QLEN
    total = micros * cands
    passes = micros * (rows // PSLOT)
    return pl.pallas_call(
        functools.partial(first_kernel, micros, rows),
        out_shape=(
            jax.ShapeDtypeStruct(hid.shape, bf16),
            jax.ShapeDtypeStruct(hid.shape, bf16),
            jax.ShapeDtypeStruct((micros * HEADS * cands, rows), f32),
            jax.ShapeDtypeStruct((total, D), bf16),
            jax.ShapeDtypeStruct((2 * total, D), bf16),
            jax.ShapeDtypeStruct((2 * passes, D), bf16),
            jax.ShapeDtypeStruct((sum(line.size for line in lines) // D, D), f32),
        ),
        compiler_params=pltpu.CompilerParams(vmem_limit_bytes=VMEM_BYTES),
        name="first",
    )(hid, seg, wq, wk, wv, *lines)


def layer_steps(x_ref, seg_row, keys, values, wq, wo, wi, wu, vec, out, queries, context, bias):
    queries[...] = (
        (dot(x_ref[...], wq[...]) + vec[0:1, :]).astype(bf16).astype(f32) * HEAD_DIM**-0.5
    ).astype(bf16)
    rows = seg_row.shape[1]
    seg_row = seg_row.astype(f32)
    seg_col = jnp.broadcast_to(seg_row, (128, rows)).T[:, 0:1]
    bias[...] = jnp.where(seg_col == seg_row, 0.0, very_low)
    yield
    for head in range(HEADS):
        part = slice(head * HEAD_DIM, (head + 1) * HEAD_DIM)
        scores = dot_right(queries[:, part], keys[:, part]) + bias[...]
        raised = jnp.exp(scores - jnp.max(scores, axis=-1, keepdims=True))
        summed = jnp.sum(raised, axis=-1, keepdims=True)
        context[:, part] = (dot(raised.astype(bf16), values[:, part]) * (1.0 / summed)).astype(bf16)
        if head % 3 == 2:
            yield
    attended = dot(context[...], wo[...]) + vec[2:3, :]
    normed, _ = norm_parts(x_ref[...].astype(f32) + attended)
    first_norm = normed * vec[3:4, :] + vec[4:5, :]
    first_low = first_norm.astype(bf16)
    total = first_norm + vec[5:6, :]
    yield
    for j in range(wi.shape[1] // D):
        part = slice(j * D, (j + 1) * D)
        u = dot(first_low, wi[:, part]) + vec[8 + j : 9 + j, :]
        total = total + dot(gelu(u).astype(bf16), wu[part, :])
        if j % 2 == 1:
            yield
    normed, _ = norm_parts(total)
    out[...] = (normed * vec[6:7, :] + vec[7:8, :]).astype(bf16)


class Layer:
    def __init__(self, first, count, rows, hbm, vec, seg, out_hbm, scratch):
        self.first, self.count, self.rows, self.seg, self.vec, self.out_hbm = (
            first, count, rows, seg, vec, out_hbm,
        )
        held, self.out, self.queries, self.context, self.bias, self.in_sem, self.out_sem = scratch
        self.held = held
        span = pl.ds(first * rows, count * rows)
        views = [ref.at[span] for ref in hbm[:3]] + list(hbm[3:])
        self.loads = [
            pltpu.make_async_copy(src, dst, self.in_sem.at[i])
            for i, (src, dst) in enumerate(zip(views, held))
        ]

    @staticmethod
    def scratch(count, rows, weights):
        row_block = pltpu.VMEM((rows, D), bf16)
        return (
            [pltpu.VMEM((count * rows, D), bf16)] * 3
            + [pltpu.VMEM(w.shape, bf16) for w in weights]
            + [
                pltpu.VMEM((count * rows, D), bf16),
                row_block,
                row_block,
                pltpu.VMEM((rows, rows), f32),
                pltpu.SemaphoreType.DMA((3 + len(weights),)),
                pltpu.SemaphoreType.DMA((count,)),
            ]
        )

    def store(self, m):
        block = pl.ds(m * self.rows, self.rows)
        return pltpu.make_async_copy(self.out.at[block], self.out_hbm.at[block], self.out_sem.at[m])

    def load(self):
        for copy in self.loads:
            copy.start()

    def steps(self):
        for copy in self.loads:
            copy.wait()
        hid, keys, values, wq, wo, wi, wu = self.held
        for m in range(self.count):
            block = pl.ds(m * self.rows, self.rows)
            seg_row = self.seg[self.first + m : self.first + m + 1, :]
            yield from layer_steps(
                hid.at[block], seg_row, keys.at[block], values.at[block], wq, wo, wi, wu, self.vec,
                self.out.at[block], self.queries, self.context, self.bias,
            )
            self.store(m).start()
            yield

    def finish(self):
        for m in range(self.count):
            self.store(m).wait()


def run_beside(layer, actions):
    for at, _ in enumerate(layer.steps()):
        for action in actions.pop(at, ()):
            action()
    for at in sorted(actions):
        for action in actions[at]:
            action()
    layer.finish()


def peer_of(step, roles, batches):
    role, batch = lax.axis_index("role"), lax.axis_index("batch")
    other = lax.rem((role // 2) * batches + batch + step, (roles // 2) * batches)
    return (other // batches) * 2 + role % 2, other % batches


def greet(roles, batches):
    role, batch = lax.axis_index("role"), lax.axis_index("batch")
    mate = role + 1 - 2 * (role % 2)
    count = (roles // 2) * batches
    barrier = pltpu.get_barrier_semaphore()
    for other in range(roles):
        if other % 2 == 0:
            there = other + 1 - role % 2
            pl.semaphore_signal(barrier, inc=1, device_id=(there, batch), device_id_type=MESH)

    def signal(step, carry):
        role_to, batch_to = peer_of(step, roles, batches)
        pl.semaphore_signal(barrier, inc=1, device_id=(role_to, batch_to), device_id_type=MESH)
        return carry

    lax.fori_loop(1, count, signal, 0)
    pl.semaphore_wait(barrier, count - 1 + roles // 2)


def remote(src, dst, out_sem, in_sem, role_to, batch_to):
    return pltpu.make_async_remote_copy(
        src_ref=src,
        dst_ref=dst,
        send_sem=out_sem,
        recv_sem=in_sem,
        device_id=(role_to, batch_to),
        device_id_type=MESH,
    )


class Spread:
    def __init__(self, roles, batches, query_ref, pass_ref, query_all, pass_all, sems):
        self.roles, self.batches = roles, batches
        self.query_ref, self.pass_ref = query_ref, pass_ref
        self.query_all, self.pass_all = query_all, pass_all
        self.first_out, self.q_out, self.p_out, self.q_on, self.p_on, self.q_in, self.p_in, self.own = sems
        self.role, self.batch = lax.axis_index("role"), lax.axis_index("batch")
        self.core = self.role % 2
        self.mate = self.role + 1 - 2 * self.core
        self.count = (roles // 2) * batches
        self.mine = (self.role - 1) * batches + self.batch

    @staticmethod
    def sems(roles, batches):
        count = (roles // 2) * batches
        dma = pltpu.SemaphoreType.DMA
        return [
            dma((3,)),
            dma((count,)),
            dma((count,)),
            dma((batches, 2)),
            dma((count,)),
            dma((batches, 2)),
            dma(((roles - 1) * batches,)),
            dma((2,)),
        ]

    def query_to(self, src, slot, half, sem, role_to, batch_to):
        return remote(
            src, self.query_all.at[slot, half], sem, self.q_in.at[slot, half], role_to, batch_to
        )

    def pass_to(self, src, slot, sem, role_to, batch_to):
        return remote(src, self.pass_all.at[slot], sem, self.p_in.at[slot], role_to, batch_to)

    def each(self, begin, end, do):
        def go(step, carry):
            do(step)
            return carry

        lax.fori_loop(begin, end, go, 0)

    def firsts(self):
        ref, batch = self.query_ref, self.batch
        return (
            self.query_to(ref.at[1], batch, 1, self.first_out.at[0], self.role + 2, batch),
            self.query_to(ref.at[0], batch, 0, self.first_out.at[1], self.mate, batch),
            self.query_to(ref.at[1], batch, 1, self.first_out.at[2], self.mate, batch),
        )

    def half_zero(self, step):
        role_to, batch_to = peer_of(step, self.roles, self.batches)
        return self.query_to(self.query_ref.at[0], self.batch, 0, self.q_out.at[step], role_to, batch_to)

    def half_one(self, step):
        role_to, batch_to = peer_of(step, self.roles, self.batches)
        src = self.query_all.at[self.batch, 1]
        return self.query_to(src, self.batch, 1, self.q_out.at[step], role_to, batch_to)

    def pass_block(self, step):
        role_to, batch_to = peer_of(step, self.roles, self.batches)
        return self.pass_to(self.pass_ref, self.mine, self.p_out.at[step], role_to, batch_to)

    def pass_mate(self):
        return self.pass_to(self.pass_ref, self.mine, self.p_out.at[0], self.mate, self.batch)

    def begin(self):
        role, batch, count = self.role, self.batch, self.count

        @pl.when(role == 0)
        def _():
            for copy in self.firsts():
                copy.start()
            self.each(1, count, lambda step: self.half_zero(step).start())
            for half in range(2):
                keep = pltpu.make_async_copy(
                    self.query_ref.at[half], self.query_all.at[batch, half], self.own.at[half]
                )
                keep.start()
                keep.wait()

        @pl.when(role > 0)
        def _():
            self.each(1, count, lambda step: self.pass_block(step).start())
            self.pass_mate().start()
            keep = pltpu.make_async_copy(
                self.pass_ref, self.pass_all.at[self.mine], self.own.at[0]
            )
            keep.start()
            keep.wait()

    def second(self):
        @pl.when(self.role == 2)
        def _():
            self.query_to(
                self.query_ref.at[1], self.batch, 1, self.q_out.at[0], self.mate, self.batch
            ).wait_recv()

            def go(step):
                pl.when(step != self.batches)(lambda: self.half_one(step).start())

            self.each(1, self.count, go)

    def on(self, slot, half):
        src = self.query_all.at[slot, half]
        return self.query_to(src, slot, half, self.q_on.at[slot, half], self.mate, self.batch)

    def pass_on(self, step, slot):
        return self.pass_to(self.pass_all.at[slot], slot, self.p_on.at[step], self.mate, self.batch)

    def relay_query(self):
        @pl.when(self.core == 0)
        def _():
            def go(step):
                slot = lax.rem(self.batch + step, self.batches)
                away = jnp.logical_or(self.role != 0, step > 0)
                for half in range(2):
                    came = jnp.logical_or(half == 0, jnp.logical_or(self.role != 2, step > 0))
                    pl.when(jnp.logical_and(away, came))(
                        lambda: self.on(slot, half).wait_recv()
                    )
                    pl.when(away)(lambda: self.on(slot, half).start())

            self.each(0, self.batches, go)

    def relay_pass(self):
        def go(step):
            role_of, batch_of = peer_of(step, self.roles, self.batches)
            slot = (role_of - 1) * self.batches + batch_of

            @pl.when(role_of > 0)
            def _():
                self.pass_on(step, slot).wait_recv()
                self.pass_on(step, slot).start()

        self.each(1, self.count, go)

    def relay(self):
        self.relay_query()
        self.relay_pass()

    def end(self):
        role, batch, batches, count = self.role, self.batch, self.batches, self.count

        @pl.when(self.core == 1)
        def _():
            def go(step):
                for half in range(2):
                    self.on(step, half).wait_recv()

            self.each(0, batches, go)

        def take(step):
            other = lax.rem((role // 2) * batches + batch + step, count)
            role_of = (other // batches) * 2 + 1 - self.core
            slot = (role_of - 1) * batches + other % batches
            pl.when(role_of > 0)(lambda: self.pass_on(step, slot).wait_recv())

        self.each(0, count, take)

        @pl.when(role == 0)
        def _():
            for copy in self.firsts():
                copy.wait_send()
            self.each(1, count, lambda step: self.half_zero(step).wait_send())

        @pl.when(role > 0)
        def _():
            self.each(1, count, lambda step: self.pass_block(step).wait_send())
            self.pass_mate().wait_send()

        @pl.when(role == 2)
        def _():
            self.each(
                1,
                count,
                lambda step: pl.when(step != batches)(lambda: self.half_one(step).wait_send()),
            )

        @pl.when(self.core == 0)
        def _():
            def go(step):
                slot = lax.rem(batch + step, batches)
                away = jnp.logical_or(role != 0, step > 0)
                for half in range(2):
                    pl.when(away)(lambda: self.on(slot, half).wait_send())

            self.each(0, batches, go)

        def passed(step):
            role_of, batch_of = peer_of(step, self.roles, batches)
            slot = (role_of - 1) * batches + batch_of
            pl.when(role_of > 0)(lambda: self.pass_on(step, slot).wait_send())

        self.each(1, count, passed)


def gather_kernel(
    roles, batches, first, amount, rows,
    query_ref, pass_ref, seg, vec, hid, keys, values, wq, wo, wi, wu, query_out, pass_out, layer_out,
    query_all, pass_all, *scratch,
):
    sems, scratch = scratch[:8], scratch[8:]
    layer = Layer(
        first, amount, rows, (hid, keys, values, wq, wo, wi, wu), vec, seg, layer_out,
        (scratch[:7],) + tuple(scratch[7:]),
    )
    greet(roles, batches)
    spread = Spread(roles, batches, query_ref, pass_ref, query_all, pass_all, sems)
    spread.begin()
    layer.load()
    spread.second()
    run_beside(layer, {8: [spread.relay_pass], 10: [spread.relay_query]})
    spread.end()
    query_out[...] = query_all[...]
    pass_out[...] = pass_all[...]


def gather_stage(query_msg, pass_msg, seg, vec, hid, keys, values, weights, first, amount, roles, batches):
    vmem = pl.BlockSpec(memory_space=pltpu.VMEM)
    far = pl.BlockSpec(memory_space=pl.ANY)
    rows = seg.shape[1]
    shapes = [
        ((batches,) + query_msg.shape, query_msg.dtype),
        (((roles - 1) * batches,) + pass_msg.shape, pass_msg.dtype),
    ]
    return pl.pallas_call(
        functools.partial(gather_kernel, roles, batches, first, amount, rows),
        in_specs=[vmem] * 4 + [far] * 7,
        out_specs=(vmem, vmem, far),
        out_shape=tuple(jax.ShapeDtypeStruct(*s) for s in shapes)
        + (jax.ShapeDtypeStruct((amount * rows, D), bf16),),
        scratch_shapes=[pltpu.VMEM(*s) for s in shapes]
        + Spread.sems(roles, batches)
        + Layer.scratch(amount, rows, weights),
        compiler_params=pltpu.CompilerParams(
            collective_id=1, has_side_effects=True, vmem_limit_bytes=VMEM_BYTES
        ),
        name="gather",
    )(query_msg, pass_msg, seg, vec, hid, keys, values, *weights)


def middle_kernel(
    micros,
    cands,
    columns,
    query_all,
    pass_all,
    wo,
    wi,
    wu,
    vec,
    positive,
    negative,
    bins,
    margins,
    clusters,
    loss_out,
    inner_grad,
    outer_grad,
    output_grad,
    vectors,
    x_slice,
    d_own,
    x_all,
    c_all,
    u_all,
    g_all,
    n_one,
    d_rows,
):
    role, batch = lax.axis_index("role"), lax.axis_index("batch")
    batches = query_all.shape[0]
    own_rows = micros * cands
    n_query = batches * own_rows
    n_dev = pass_all.shape[0]
    per_dev = pass_all.shape[1] // 2
    per_micro = per_dev // micros
    n_pass = n_dev * per_dev
    n_rows = n_query + n_pass
    inner = wi.shape[1]
    chunks = [slice(j * D, (j + 1) * D) for j in range(inner // D)]

    for b in range(batches):
        x_all[b * own_rows : (b + 1) * own_rows, :] = query_all[b, 0:own_rows, :]
        c_all[b * own_rows : (b + 1) * own_rows, :] = query_all[b, own_rows : 2 * own_rows, :]
    wide = pass_all[...].astype(f32)
    x_all[n_query:n_rows, :] = wide[:, 0:per_dev, :].reshape(n_pass, D).astype(bf16)
    c_all[n_query:n_rows, :] = wide[:, per_dev:, :].reshape(n_pass, D).astype(bf16)

    attended = dot(c_all[...], wo[...]) + vec[2:3, :]
    normed, inv_one = norm_parts(x_all[...].astype(f32) + attended)
    n_one[...] = normed
    first_norm = normed * vec[3:4, :] + vec[4:5, :]
    first_low = first_norm.astype(bf16)
    total = first_norm + vec[5:6, :]
    for j, part in enumerate(chunks):
        u = dot(first_low, wi[:, part]) + vec[8 + j : 9 + j, :]
        u_all[:, part] = u
        g = gelu(u).astype(bf16)
        g_all[:, part] = g
        total = total + dot(g, wu[part, :])
    n_two, inv_two = norm_parts(total)
    low = (n_two * vec[6:7, :] + vec[7:8, :]).astype(bf16)
    q_low, p_low = low[:n_query], low[n_query:]

    bin_ids = bins[...]
    queries_total = bin_ids.shape[0] * bin_ids.shape[1]
    weight = jnp.zeros(bin_ids.shape, f32)
    for k in range(NBINS):
        hit = (bin_ids == k).astype(f32)
        amount = jnp.sum(jnp.sum(hit, axis=1, keepdims=True), axis=0, keepdims=True)
        weight = weight + hit * (queries_total / (NBINS * jnp.maximum(amount, 1.0)))

    lane = lax.broadcasted_iota(jnp.int32, (n_query, bin_ids.shape[1]), 1)
    row = lax.broadcasted_iota(jnp.int32, (n_query, bin_ids.shape[1]), 0)
    here = lane == (row // own_rows) * cands + row % cands

    def by_micro(table):
        parts = [
            jnp.broadcast_to(table[m : m + 1, :], (cands, table.shape[1])) for m in range(micros)
        ]
        return jnp.concatenate(parts * batches, axis=0)

    def per_query(table):
        return jnp.sum(jnp.where(here, by_micro(table), 0.0), axis=-1, keepdims=True)

    pos = per_query(positive[...].astype(f32))
    neg = per_query(negative[...].astype(f32))
    margin = per_query(margins[...])
    weight = per_query(weight)

    col = lax.broadcasted_iota(jnp.int32, (n_query, n_pass), 1)
    row = lax.broadcasted_iota(jnp.int32, (n_query, n_pass), 0)
    same = (col % per_dev) // per_micro == (row % own_rows) // cands
    ident = ((col // per_dev) * per_micro + col % per_micro).astype(f32)
    n_ids = n_dev * per_micro
    tab_row = lax.broadcasted_iota(jnp.int32, (n_ids, n_pass), 0)
    tab_col = lax.broadcasted_iota(jnp.int32, (n_ids, n_pass), 1)
    table = tab_row == (tab_col // per_dev) * per_micro + tab_col % per_micro
    cluster = by_micro(dot(clusters[...].astype(f32).astype(bf16), table.astype(f32).astype(bf16)))
    pos_hit = jnp.logical_and(same, ident == pos)
    neg_hit = jnp.logical_and(same, ident == neg)
    pos_cluster = jnp.sum(jnp.where(pos_hit, cluster, 0.0), axis=-1, keepdims=True)
    allowed = jnp.logical_and(same, cluster == pos_cluster)
    scores = dot_right(q_low, p_low) * D**-0.5
    masked = jnp.where(allowed, scores, very_low)
    row_max = jnp.max(masked, axis=-1, keepdims=True)
    raised = jnp.exp(masked - row_max)
    summed = jnp.sum(raised, axis=-1, keepdims=True)
    pos_score = jnp.sum(jnp.where(pos_hit, scores, 0.0), axis=-1, keepdims=True)
    neg_score = jnp.sum(jnp.where(neg_hit, scores, 0.0), axis=-1, keepdims=True)
    gap = pos_score - neg_score - margin
    terms = row_max + jnp.log(summed) - pos_score + weight * gap * gap
    loss_out[...] = jnp.broadcast_to(
        jnp.sum(terms, axis=0, keepdims=True) / queries_total, loss_out.shape
    )
    pull = 2.0 * weight * gap
    pos_one, neg_one = pos_hit.astype(f32), neg_hit.astype(f32)
    d_scores = (raised * (1.0 / summed) - pos_one + pull * (pos_one - neg_one)) * D**-0.5
    parts = three_parts(d_scores)
    d_query = sum(dot(part, p_low) for part in parts)
    d_pass = sum(dot_left(part, q_low) for part in parts)
    grad = jnp.concatenate([d_query, d_pass], axis=0)

    def total_of(array):
        return jnp.sum(array, axis=0, keepdims=True)

    vectors[6:7, :] = total_of(grad * n_two)
    vectors[7:8, :] = total_of(grad)
    d_two = norm_back(grad * vec[6:7, :], n_two, inv_two)
    d_outer = d_two.astype(bf16)
    vectors[5:6, :] = total_of(d_outer.astype(f32))
    select = (
        lax.broadcasted_iota(jnp.int32, (D, 128), 0)
        == lax.broadcasted_iota(jnp.int32, (D, 128), 1) + batch * columns
    )
    select = jnp.logical_and(select, lax.broadcasted_iota(jnp.int32, (D, 128), 1) < columns)
    select = select.astype(f32).astype(bf16)
    first_low = (n_one[...] * vec[3:4, :] + vec[4:5, :]).astype(bf16)
    y_slice = dot(first_low, select).astype(bf16)
    d_first = d_two
    for j, part in enumerate(chunks):
        d_inner = (dot_right(d_outer, wu[part, :]) * gelu_slope(u_all[:, part])).astype(bf16)
        vectors[8 + j : 9 + j, :] = total_of(d_inner.astype(f32))
        inner_grad[:, part] = dot_left(y_slice, d_inner)[:columns]
        d_first = d_first + dot_right(d_inner, wi[:, part])
    span = inner // batches
    outer_grad[...] = dot_left(g_all[:, pl.ds(pl.multiple_of(batch * span, 128), span)], d_outer)
    vectors[3:4, :] = total_of(d_first * n_one[...])
    vectors[4:5, :] = total_of(d_first)
    d_one = norm_back(d_first * vec[3:4, :], n_one[...], inv_one)
    d_rows[...] = d_one
    d_low = d_one.astype(bf16)
    bias_row = total_of(d_low.astype(f32))
    vectors[2:3, :] = bias_row
    vectors[1:2, :] = sum(dot_right(part, wo[...]) for part in three_parts(bias_row))
    vectors[0:1, :] = jnp.zeros_like(bias_row)
    c_slice = dot(c_all[...], select).astype(bf16)
    output_grad[...] = dot_left(c_slice, d_low)[:columns]
    x_slice[...] = dot(x_all[...], select).astype(bf16)

    @pl.when(role == 0)
    def _():
        d_own[...] = d_rows[pl.ds(pl.multiple_of(batch * own_rows, 8), own_rows), :]

    @pl.when(role > 0)
    def _():
        d_own[...] = jnp.zeros_like(d_own)
        begin = pl.multiple_of(n_query + ((role - 1) * batches + batch) * per_dev, 8)
        mine = d_rows[pl.ds(begin, per_dev), :]
        for m in range(micros):
            for slot in range(per_micro):
                at = m * cands + slot * (PSLOT // QLEN)
                d_own[at : at + 1, :] = mine[m * per_micro + slot : m * per_micro + slot + 1, :]


def middle_stage(query_all, pass_all, wo, wi, wu, vec, positive, negative, bins, margins, clusters):
    batches = query_all.shape[0]
    micros = positive.shape[0]
    own_rows = query_all.shape[1] // 2
    n_pass = pass_all.shape[0] * pass_all.shape[1] // 2
    n_rows = batches * own_rows + n_pass
    columns = D // batches
    inner = wi.shape[1]
    return pl.pallas_call(
        functools.partial(middle_kernel, micros, own_rows // micros, columns),
        out_shape=(
            jax.ShapeDtypeStruct((1, 128), f32),
            jax.ShapeDtypeStruct((columns, inner), f32),
            jax.ShapeDtypeStruct((inner // batches, D), f32),
            jax.ShapeDtypeStruct((columns, D), f32),
            jax.ShapeDtypeStruct((8 + inner // D, D), f32),
            jax.ShapeDtypeStruct((n_rows, 128), bf16),
            jax.ShapeDtypeStruct((own_rows, D), f32),
        ),
        scratch_shapes=[
            pltpu.VMEM((n_rows, D), bf16),
            pltpu.VMEM((n_rows, D), bf16),
            pltpu.VMEM((n_rows, inner), f32),
            pltpu.VMEM((n_rows, inner), bf16),
            pltpu.VMEM((n_rows, D), f32),
            pltpu.VMEM((n_rows, D), f32),
        ],
        compiler_params=pltpu.CompilerParams(vmem_limit_bytes=VMEM_BYTES),
        name="middle",
    )(query_all, pass_all, wo, wi, wu, vec, positive, negative, bins, margins, clusters)


def attention_back_kernel(
    hid, keys, values, probs, query_c, d_own, wq, wk, wv, wo, in_grad, dq_out, dq_pass, key_part, value_part,
    z_key, z_value, q_keep, c_keep,
):
    m = pl.program_id(0)
    cands = query_c.shape[0]
    mask = head_mask(cands)
    wide_rows = HEADS * cands
    d_low = d_own[...].astype(bf16)
    d_context = dot_right(d_low, wo[...]).astype(bf16)
    q_wide = per_head(query_c[...], mask)
    c_wide = per_head(d_context, mask)
    prob = probs[...]
    d_prob = dot_right(c_wide, values[...])
    pulled = prob * d_prob
    d_scores = (pulled - prob * jnp.sum(pulled, axis=-1, keepdims=True)).astype(bf16)
    both = jnp.concatenate([d_scores, prob.astype(bf16)], axis=0)
    d_query = (from_heads(dot(d_scores, keys[...]), mask, cands) * HEAD_DIM**-0.5).astype(bf16)
    dq_out[...] = d_query
    d_query_wide = d_query.astype(f32)
    slots = dq_pass.shape[0] // pl.num_programs(0)
    for slot in range(slots):
        at = slot * (PSLOT // QLEN)
        dq_pass[pl.ds(m * slots + slot, 1), :] = d_query_wide[at : at + 1, :]
    sums = dot(both, hid[...])
    here = pl.ds(pl.multiple_of(m * wide_rows, 16), wide_rows)
    z_key[here, :] = sums[:wide_rows].astype(bf16)
    z_value[here, :] = sums[wide_rows:].astype(bf16)
    q_keep[here, :] = q_wide
    c_keep[here, :] = c_wide
    back = jnp.concatenate(
        [dot_right(q_wide, wk[...]).astype(bf16), dot_right(c_wide, wv[...]).astype(bf16)], axis=0
    )
    in_grad[...] = dot_left(both, back)
    extra = dot_right(d_query, wq[...]) + d_own[...]
    for cand in range(cands):
        at = slice(cand * QLEN, cand * QLEN + 1)
        in_grad[at, :] = in_grad[at, :] + extra[cand : cand + 1, :]

    @pl.when(m == pl.num_programs(0) - 1)
    def _():
        key_part[...] = dot_left(z_key[...], q_keep[...]).astype(bf16)
        value_part[...] = dot_left(z_value[...], c_keep[...]).astype(bf16)


def attention_back_stage(hid, keys, values, probs, query_c, d_own, wq, wk, wv, wo, micros):
    rows = hid.shape[0] // micros
    cands = rows // QLEN
    wide_rows = HEADS * cands
    passes = micros * (rows // PSLOT)

    def whole(array):
        return pl.BlockSpec(array.shape, lambda m: (0, 0), pipeline_mode=pl.Buffered(1))

    def block(count, width):
        return pl.BlockSpec((count, width), lambda m: (m, 0))

    fixed = pl.BlockSpec((D, D), lambda m: (0, 0))
    return pl.pallas_call(
        attention_back_kernel,
        grid=(micros,),
        in_specs=[
            block(rows, D),
            block(rows, D),
            block(rows, D),
            block(wide_rows, rows),
            block(cands, D),
            block(cands, D),
            whole(wq),
            whole(wk),
            whole(wv),
            whole(wo),
        ],
        out_specs=(
            block(rows, D),
            block(cands, D),
            pl.BlockSpec((passes, D), lambda m: (0, 0)),
            fixed,
            fixed,
        ),
        out_shape=(
            jax.ShapeDtypeStruct(hid.shape, f32),
            jax.ShapeDtypeStruct(query_c.shape, bf16),
            jax.ShapeDtypeStruct((passes, D), f32),
            jax.ShapeDtypeStruct((D, D), bf16),
            jax.ShapeDtypeStruct((D, D), bf16),
        ),
        scratch_shapes=[pltpu.VMEM((micros * wide_rows, D), bf16)] * 4,
        compiler_params=pltpu.CompilerParams(vmem_limit_bytes=VMEM_BYTES),
        name="attention_back",
    )(hid, keys, values, probs, query_c, d_own, wq, wk, wv, wo)


def reduce_kernel(
    roles, batches, first, amount, rows,
    dq_ref, dq_pass, key_part, value_part, x_slice, seg, vec, hid, keys, values, wq, wo, wi, wu,
    query_grad, query_bias, key_grad, value_grad, layer_out,
    query_all, pass_all, from_mate, summed, from_x, halves, received, finals,
    mate_out, mate_in, x_out, x_in, part_out, part_in, last_out, last_in, *scratch,
):
    sems, scratch = scratch[:8], scratch[8:]
    role, batch = lax.axis_index("role"), lax.axis_index("batch")
    core, side = role % 2, role // 2
    mate = role + 1 - 2 * core
    across = lax.rem(role + 2, roles)
    pieces = key_part.shape[2]
    layer = Layer(
        first, amount, rows, (hid, keys, values, wq, wo, wi, wu), vec, seg, layer_out,
        (scratch[:7],) + tuple(scratch[7:]),
    )
    greet(roles, batches)
    spread = Spread(roles, batches, dq_ref, dq_pass, query_all, pass_all, sems)

    @pl.when(core == 0)
    def _():
        remote(value_part, from_mate, mate_out, mate_in, mate, batch).start()

    @pl.when(core == 1)
    def _():
        remote(key_part, from_mate, mate_out, mate_in, mate, batch).start()

    spread.begin()
    layer.load()

    def to_x(piece):
        return remote(
            summed.at[:, 1 - side, piece], from_x.at[:, piece], x_out.at[piece], x_in.at[piece], across, batch
        )

    def begin_x():
        remote(key_part, from_mate, mate_out, mate_in, mate, batch).wait()

        @pl.when(core == 0)
        def _():
            summed[...] = (key_part[...].astype(f32) + from_mate[...].astype(f32)).astype(bf16)

        @pl.when(core == 1)
        def _():
            summed[...] = (value_part[...].astype(f32) + from_mate[...].astype(f32)).astype(bf16)

        for piece in range(pieces):
            to_x(piece).start()

    def to_batch(piece, step):
        other = lax.rem(batch + step, batches)
        return remote(
            halves.at[other, piece], received.at[batch, piece], part_out.at[other, piece],
            part_in.at[batch, piece], role, other,
        )

    def from_batch(piece, step):
        other = lax.rem(batch + step, batches)
        return remote(
            halves.at[other, piece], received.at[other, piece], part_out.at[other, piece],
            part_in.at[other, piece], role, other,
        )

    def begin_part(piece):
        to_x(piece).wait()
        halves[:, piece] = (
            summed[:, side, piece].astype(f32) + from_x[:, piece].astype(f32)
        ).astype(bf16)
        spread.each(1, batches, lambda step: to_batch(piece, step).start())

    def to_role(step):
        other = lax.rem(role + step, roles)
        return remote(
            finals.at[role], finals.at[role], last_out.at[step], last_in.at[role], other, batch
        )

    def from_role(step):
        other = lax.rem(role + step, roles)
        return remote(
            finals.at[other], finals.at[other], last_out.at[step], last_in.at[other], other, batch
        )

    def begin_last():
        for piece in range(pieces):
            spread.each(1, batches, lambda step: from_batch(piece, step).wait_recv())
            total = halves[batch, piece].astype(f32)

            def add(step, total):
                return total + received[lax.rem(batch + step, batches), piece].astype(f32)

            total = lax.fori_loop(1, batches, add, total)
            finals[role, piece] = total.astype(bf16)
        for step in range(1, roles):
            to_role(step).start()

    def finish():
        count = query_all.shape[0] * query_all.shape[1] * query_all.shape[2]
        columns = query_grad.shape[0]
        d_query = query_all[...].reshape(count, D)
        d_pass = pass_all[...].reshape(-1, D)
        query_grad[...] = (
            dot_left(x_slice[0:count, :], d_query) + dot_left(x_slice[count:, :], d_pass.astype(bf16))
        )[:columns]
        query_bias[...] = jnp.sum(d_query.astype(f32), axis=0, keepdims=True) + jnp.sum(
            d_pass, axis=0, keepdims=True
        )

    actions = reduce_plan(
        begin_x, spread, [functools.partial(begin_part, piece) for piece in range(pieces)], begin_last
    )
    run_beside(layer, actions)
    spread.end()
    finish()
    for piece in range(pieces):
        spread.each(1, batches, lambda step: to_batch(piece, step).wait_send())
    for step in range(1, roles):
        from_role(step).wait_recv()
        to_role(step).wait_send()
    half = pieces * finals.shape[2]
    for x in range(roles // 2):
        here = slice(x * half, (x + 1) * half)
        key_grad[here, :] = finals[2 * x].astype(f32).reshape(half, D)
        value_grad[here, :] = finals[2 * x + 1].astype(f32).reshape(half, D)


def reduce_plan(begin_x, spread, parts, begin_last):
    return {
        0: [spread.second, begin_x],
        4: [parts[0]],
        6: [parts[1]],
        8: [parts[2], spread.relay_pass],
        10: [spread.relay_query],
        14: [begin_last],
    }


def reduce_stage(
    dq, dq_pass, key_part, value_part, x_slice, seg, vec, hid, keys, values, weights, first, amount, roles, batches
):
    columns = D // batches
    rows = seg.shape[1]
    vmem = pl.BlockSpec(memory_space=pltpu.VMEM)
    far = pl.BlockSpec(memory_space=pl.ANY)
    block = (columns, D)
    sides, tile = roles // 2, 16
    pieces = columns // sides // tile
    split = (batches, sides, pieces, tile, D)
    half = (batches, pieces, tile, D)
    dma = pltpu.SemaphoreType.DMA
    return pl.pallas_call(
        functools.partial(reduce_kernel, roles, batches, first, amount, rows),
        in_specs=[vmem] * 7 + [far] * 7,
        out_specs=(vmem,) * 4 + (far,),
        out_shape=(
            jax.ShapeDtypeStruct(block, f32),
            jax.ShapeDtypeStruct((1, D), f32),
            jax.ShapeDtypeStruct(block, f32),
            jax.ShapeDtypeStruct(block, f32),
            jax.ShapeDtypeStruct((amount * rows, D), bf16),
        ),
        scratch_shapes=[
            pltpu.VMEM((batches, 2, dq.shape[0] // 2, D), bf16),
            pltpu.VMEM(((roles - 1) * batches,) + dq_pass.shape, f32),
            pltpu.VMEM(split, bf16),
            pltpu.VMEM(split, bf16),
            pltpu.VMEM(half, bf16),
            pltpu.VMEM(half, bf16),
            pltpu.VMEM(half, bf16),
            pltpu.VMEM((roles, pieces, tile, D), bf16),
            dma,
            dma,
            dma((pieces,)),
            dma((pieces,)),
            dma((batches, pieces)),
            dma((batches, pieces)),
            dma((roles,)),
            dma((roles,)),
        ]
        + Spread.sems(roles, batches)
        + Layer.scratch(amount, rows, weights),
        compiler_params=pltpu.CompilerParams(
            collective_id=2, has_side_effects=True, vmem_limit_bytes=VMEM_BYTES
        ),
        name="reduce",
    )(
        dq.reshape(2, -1, D),
        dq_pass,
        key_part.reshape(split),
        value_part.reshape(split),
        x_slice,
        seg,
        vec,
        hid,
        keys,
        values,
        *weights,
    )


def body(
    roles,
    batches,
    hidden,
    query_weight,
    query_bias,
    key_weight,
    value_weight,
    value_bias,
    output_weight,
    output_bias,
    first_gain,
    first_shift,
    inner_weight,
    inner_bias,
    outer_weight,
    outer_bias,
    second_gain,
    second_shift,
    segment,
    positive,
    negative,
    bins,
    margins,
    clusters,
):
    micros, rows = hidden.shape[0], hidden.shape[2]
    hid = hidden.reshape(micros * rows, D)
    seg = segment.reshape(micros, rows)
    lines = [
        query_bias,
        value_bias,
        output_bias,
        first_gain,
        first_shift,
        outer_bias,
        second_gain,
        second_shift,
        inner_bias,
    ]
    keys, values, probs, query_c, query_msg, pass_msg, vec = first_stage(
        hid, seg, query_weight, key_weight, value_weight, lines, micros
    )
    layer_weights = (query_weight, output_weight, inner_weight, outer_weight)
    early = micros // 2
    query_all, pass_all, layer_early = gather_stage(
        query_msg.reshape(2, -1, D), pass_msg, seg, vec, hid, keys, values, layer_weights, 0, early, roles, batches
    )
    query_all = query_all.reshape(batches, -1, D)
    loss, inner_grad, outer_grad, output_grad, vectors, x_slice, d_own = middle_stage(
        query_all,
        pass_all,
        output_weight,
        inner_weight,
        outer_weight,
        vec,
        positive,
        negative,
        bins[..., 0],
        margins,
        clusters,
    )
    in_grad, dq, dq_pass, key_part, value_part = attention_back_stage(
        hid,
        keys,
        values,
        probs,
        query_c,
        d_own,
        query_weight,
        key_weight,
        value_weight,
        output_weight,
        micros,
    )
    query_grad, query_bias_row, key_grad, value_grad, layer_late = reduce_stage(
        dq, dq_pass, key_part, value_part, x_slice, seg, vec, hid, keys, values, layer_weights,
        early, micros - early, roles, batches,
    )
    layer_out = jnp.concatenate([layer_early, layer_late], axis=0)
    batch = lax.axis_index("batch")
    columns = D // batches
    span = inner_weight.shape[1] // batches
    mine = lax.dynamic_slice_in_dim(vectors[:8], batch * columns, columns, axis=1)
    mine_inner = lax.dynamic_slice_in_dim(vectors[8:].reshape(-1), batch * span, span)
    mine_query = lax.dynamic_slice_in_dim(query_bias_row[0], batch * columns, columns)
    return (
        layer_out.reshape(hidden.shape),
        loss[0, 0],
        in_grad.reshape(hidden.shape),
        query_grad,
        mine_query,
        key_grad,
        value_grad,
        mine[1],
        output_grad,
        mine[2],
        mine[3],
        mine[4],
        inner_grad,
        mine_inner,
        outer_grad,
        mine[5],
        mine[6],
        mine[7],
    )


highest = lax.Precision.HIGHEST


def multiply(left, right):
    return jnp.dot(left, right, preferred_element_type=jnp.float32)


def left_product(left, right):
    return jnp.einsum("rd,re->de", left, right, preferred_element_type=jnp.float32)


def right_product(left, right):
    return jnp.einsum("rd,ed->re", left, right, preferred_element_type=jnp.float32)


def select_rows(array, stride):
    return array.reshape((array.shape[0] // stride, stride) + array.shape[1:])[:, 0]


def normalize(incoming, gain_vec, shift_vec):
    center = incoming - jnp.mean(incoming, axis=-1, keepdims=True)
    inv_std = lax.rsqrt(jnp.mean(center * center, axis=-1, keepdims=True) + epsilon)
    normed = center * inv_std
    return (normed * gain_vec + shift_vec, normed, inv_std)


def normalize_back(grad_in, normed, inv_std, gain_vec):
    scaled = grad_in * gain_vec
    return inv_std * (
        scaled
        - jnp.mean(scaled, axis=-1, keepdims=True)
        - normed * jnp.mean(scaled * normed, axis=-1, keepdims=True)
    )


def encode(hidden_rows, seg_rows, weights, att_rows):
    (
        query_weight,
        query_bias,
        key_weight,
        value_weight,
        value_bias,
        output_weight,
        output_bias,
        first_gain,
        first_shift,
        inner_weight,
        inner_bias,
        outer_weight,
        outer_bias,
        second_gain,
        second_shift,
    ) = weights
    row_count = hidden_rows.shape[0]
    blocks = row_count // att_rows
    head_scale = HEAD_DIM ** (-0.5)
    block_shape = (blocks, att_rows, HEADS, HEAD_DIM)
    query_rows = (multiply(hidden_rows, query_weight) + query_bias).astype(jnp.bfloat16)
    key_rows = multiply(hidden_rows, key_weight).astype(jnp.bfloat16)
    value_rows = (multiply(hidden_rows, value_weight) + value_bias).astype(jnp.bfloat16)
    scores = (
        jnp.einsum(
            "bihd,bjhd->bhij",
            query_rows.reshape(block_shape),
            key_rows.reshape(block_shape),
            preferred_element_type=jnp.float32,
        )
        * head_scale
    )
    seg_blocks = seg_rows.reshape(blocks, att_rows)
    same_seg = (seg_blocks[:, :, None] == seg_blocks[:, None, :])[:, None]
    scores = jnp.where(same_seg, scores, very_low)
    row_max = jnp.max(scores, axis=-1, keepdims=True)
    raised = jnp.exp(scores - row_max)
    summed = jnp.sum(raised, axis=-1, keepdims=True)
    attn_probs = (raised / summed).astype(jnp.bfloat16)
    log_total = (row_max + jnp.log(summed))[..., 0]
    context = (
        jnp.einsum(
            "bhij,bjhd->bihd",
            attn_probs,
            value_rows.reshape(block_shape),
            preferred_element_type=jnp.float32,
        )
        .reshape(row_count, D)
        .astype(jnp.bfloat16)
    )
    attended = multiply(context, output_weight) + output_bias
    first_norm, normed_one, inv_one = normalize(
        hidden_rows.astype(jnp.float32) + attended, first_gain, first_shift
    )
    first_low = first_norm.astype(jnp.bfloat16)
    inner_pre = multiply(first_low, inner_weight) + inner_bias
    activated = jax.nn.gelu(inner_pre, approximate=False).astype(jnp.bfloat16)
    outer_out = multiply(activated, outer_weight) + outer_bias
    block_out, normed_two, inv_two = normalize(first_norm + outer_out, second_gain, second_shift)
    log_cand = log_total.reshape(blocks, HEADS, att_rows // QLEN, QLEN)[..., 0]
    kept = (
        key_rows,
        value_rows,
        select_rows(query_rows, QLEN),
        log_cand,
        select_rows(context, QLEN),
        select_rows(normed_one, QLEN),
        select_rows(inv_one, QLEN),
        select_rows(first_low, QLEN),
        select_rows(inner_pre, QLEN),
        select_rows(activated, QLEN),
        select_rows(normed_two, QLEN),
        select_rows(inv_two, QLEN),
    )
    return (block_out, kept)


def encode_back(grad_out, hidden_rows, seg_rows, weights, kept, att_rows):
    (
        query_weight,
        query_bias,
        key_weight,
        value_weight,
        value_bias,
        output_weight,
        output_bias,
        first_gain,
        first_shift,
        inner_weight,
        inner_bias,
        outer_weight,
        outer_bias,
        second_gain,
        second_shift,
    ) = weights
    (
        key_rows,
        value_rows,
        query_cand,
        log_cand,
        context_cand,
        normed_one,
        inv_one,
        first_cand,
        inner_cand,
        active_cand,
        normed_two,
        inv_two,
    ) = kept
    row_count = hidden_rows.shape[0]
    blocks = row_count // att_rows
    cand_rows = row_count // QLEN
    per_block = att_rows // QLEN
    head_scale = HEAD_DIM ** (-0.5)
    hidden_cand = select_rows(hidden_rows, QLEN)
    second_gain_grad = jnp.sum(grad_out * normed_two, axis=0)
    second_shift_grad = jnp.sum(grad_out, axis=0)
    d_second = normalize_back(grad_out, normed_two, inv_two, second_gain)
    d_outer = d_second.astype(jnp.bfloat16)
    outer_weight_grad = left_product(active_cand, d_outer)
    outer_bias_grad = jnp.sum(d_outer.astype(jnp.float32), axis=0)
    d_active = right_product(d_outer, outer_weight)
    gelu_pull = jax.vjp(functools.partial(jax.nn.gelu, approximate=False), inner_cand)[1]
    d_inner = gelu_pull(d_active)[0].astype(jnp.bfloat16)
    inner_weight_grad = left_product(first_cand, d_inner)
    inner_bias_grad = jnp.sum(d_inner.astype(jnp.float32), axis=0)
    d_first = d_second + right_product(d_inner, inner_weight)
    first_gain_grad = jnp.sum(d_first * normed_one, axis=0)
    first_shift_grad = jnp.sum(d_first, axis=0)
    d_attend = normalize_back(d_first, normed_one, inv_one, first_gain)
    d_attend_low = d_attend.astype(jnp.bfloat16)
    output_weight_grad = left_product(context_cand, d_attend_low)
    output_bias_grad = jnp.sum(d_attend_low.astype(jnp.float32), axis=0)
    cand_shape = (blocks, per_block, HEADS, HEAD_DIM)
    block_shape = (blocks, att_rows, HEADS, HEAD_DIM)
    d_context = right_product(d_attend_low, output_weight).astype(jnp.bfloat16).reshape(cand_shape)
    query_heads = query_cand.reshape(cand_shape)
    key_heads = key_rows.reshape(block_shape)
    value_heads = value_rows.reshape(block_shape)
    scores = (
        jnp.einsum("bihd,bjhd->bhij", query_heads, key_heads, preferred_element_type=jnp.float32)
        * head_scale
    )
    seg_blocks = seg_rows.reshape(blocks, att_rows)
    seg_cand = seg_blocks.reshape(blocks, per_block, QLEN)[..., 0]
    same_seg = (seg_cand[:, :, None] == seg_blocks[:, None, :])[:, None]
    attn_probs = jnp.where(same_seg, jnp.exp(scores - log_cand[..., None]), 0.0)
    d_probs = jnp.einsum(
        "bihd,bjhd->bhij", d_context, value_heads, preferred_element_type=jnp.float32
    )
    d_scores = (
        attn_probs * (d_probs - jnp.sum(attn_probs * d_probs, axis=-1, keepdims=True))
    ).astype(jnp.bfloat16)
    d_query = (
        (
            jnp.einsum("bhij,bjhd->bihd", d_scores, key_heads, preferred_element_type=jnp.float32)
            * head_scale
        )
        .reshape(cand_rows, D)
        .astype(jnp.bfloat16)
    )
    d_keys = (
        (
            jnp.einsum("bhij,bihd->bjhd", d_scores, query_heads, preferred_element_type=jnp.float32)
            * head_scale
        )
        .reshape(row_count, D)
        .astype(jnp.bfloat16)
    )
    d_values = (
        jnp.einsum(
            "bhij,bihd->bjhd",
            attn_probs.astype(jnp.bfloat16),
            d_context,
            preferred_element_type=jnp.float32,
        )
        .reshape(row_count, D)
        .astype(jnp.bfloat16)
    )
    query_weight_grad = left_product(hidden_cand, d_query)
    query_bias_grad = jnp.sum(d_query.astype(jnp.float32), axis=0)
    key_weight_grad = left_product(hidden_rows, d_keys)
    value_weight_grad = left_product(hidden_rows, d_values)
    value_bias_grad = jnp.sum(d_values.astype(jnp.float32), axis=0)
    d_hidden = right_product(d_keys, key_weight) + right_product(d_values, value_weight)
    d_cand = right_product(d_query, query_weight) + d_attend
    d_hidden = d_hidden.reshape(cand_rows, QLEN, D)
    d_hidden = jnp.concatenate(
        [d_hidden[:, :1] + d_cand[:, None], d_hidden[:, 1:]], axis=1
    ).reshape(row_count, D)
    gradients = (
        query_weight_grad,
        query_bias_grad,
        key_weight_grad,
        value_weight_grad,
        value_bias_grad,
        output_weight_grad,
        output_bias_grad,
        first_gain_grad,
        first_shift_grad,
        inner_weight_grad,
        inner_bias_grad,
        outer_weight_grad,
        outer_bias_grad,
        second_gain_grad,
        second_shift_grad,
    )
    return (d_hidden, gradients)


def general_body(
    hidden,
    query_weight,
    query_bias,
    key_weight,
    value_weight,
    value_bias,
    output_weight,
    output_bias,
    first_gain,
    first_shift,
    inner_weight,
    inner_bias,
    outer_weight,
    outer_bias,
    second_gain,
    second_shift,
    segment,
    positive,
    negative,
    bins,
    margins,
    clusters,
):
    weights = (
        query_weight,
        query_bias,
        key_weight,
        value_weight,
        value_bias,
        output_weight,
        output_bias,
        first_gain,
        first_shift,
        inner_weight,
        inner_bias,
        outer_weight,
        outer_bias,
        second_gain,
        second_shift,
    )
    micro_count = hidden.shape[0]
    row_count = hidden.shape[2]
    att_rows = min(512, row_count)
    cand_rows = row_count // QLEN
    slot_stride = PSLOT // QLEN
    emb_scale = D ** (-0.5)
    query_flag = jnp.where(lax.axis_index("role") == 0, 1.0, 0.0).astype(jnp.float32)
    first_query = lax.axis_index("batch") * cand_rows
    bin_ids = bins[..., 0]
    query_total = bin_ids.shape[0] * bin_ids.shape[1]
    bin_slots = jnp.arange(NBINS, dtype=jnp.int32)
    bin_counts = jnp.sum((bin_ids[..., None] == bin_slots).astype(jnp.float32), axis=(0, 1))
    bin_table = query_total / (NBINS * bin_counts)
    loss_accum = jnp.zeros((), jnp.float32)
    accum = None
    layer_list = []
    grad_list = []
    for micro_idx in range(micro_count):
        hidden_rows = hidden[micro_idx, 0]
        seg_rows = segment[micro_idx, 0]
        block_out, kept = encode(hidden_rows, seg_rows, weights, att_rows)
        layer_list.append(block_out.astype(jnp.bfloat16))
        cls_rows = select_rows(block_out, QLEN).astype(jnp.bfloat16)
        passage_cls = cls_rows.reshape(-1, slot_stride, D)[:, 0]
        gathered = lax.all_gather(passage_cls, ("role", "batch"), axis=0, tiled=True)
        offset = lax.axis_size("batch") * passage_cls.shape[0]
        passages = gathered[offset:]
        scores = right_product(cls_rows, passages) * emb_scale
        columns = jnp.arange(passages.shape[0], dtype=jnp.int32)
        pos_ids = lax.dynamic_slice_in_dim(positive[micro_idx], first_query, cand_rows)
        neg_ids = lax.dynamic_slice_in_dim(negative[micro_idx], first_query, cand_rows)
        bin_mine = lax.dynamic_slice_in_dim(bin_ids[micro_idx], first_query, cand_rows)
        margin_mine = lax.dynamic_slice_in_dim(margins[micro_idx], first_query, cand_rows)
        pos_hit = pos_ids[:, None] == columns
        neg_hit = neg_ids[:, None] == columns
        cluster_row = clusters[micro_idx]
        pos_cluster = jnp.sum(jnp.where(pos_hit, cluster_row[None, :], 0), axis=-1)
        allowed = cluster_row[None, :] == pos_cluster[:, None]
        masked = jnp.where(allowed, scores, very_low)
        row_max = jnp.max(masked, axis=-1, keepdims=True)
        raised = jnp.exp(masked - row_max)
        summed = jnp.sum(raised, axis=-1, keepdims=True)
        softened = raised / summed
        log_total = (row_max + jnp.log(summed))[:, 0]
        pos_score = jnp.sum(jnp.where(pos_hit, scores, 0.0), axis=-1)
        neg_score = jnp.sum(jnp.where(neg_hit, scores, 0.0), axis=-1)
        weight_query = jnp.sum(jnp.where(bin_mine[:, None] == bin_slots, bin_table, 0.0), axis=-1)
        margin_gap = pos_score - neg_score - margin_mine
        loss_accum = loss_accum + query_flag * jnp.sum(
            log_total - pos_score + weight_query * margin_gap * margin_gap
        )
        pos_float = pos_hit.astype(jnp.float32)
        neg_float = neg_hit.astype(jnp.float32)
        d_scores = query_flag * (
            softened
            - pos_float
            + (2.0 * weight_query * margin_gap)[:, None] * (pos_float - neg_float)
        )
        passages_wide = passages.astype(jnp.float32)
        cls_wide = cls_rows.astype(jnp.float32)
        d_cls = (
            jnp.dot(d_scores, passages_wide, precision=highest, preferred_element_type=jnp.float32)
            * emb_scale
        )
        padded = jnp.concatenate([jnp.zeros((cand_rows, offset), jnp.float32), d_scores], axis=1)
        received = lax.psum_scatter(
            jnp.einsum(
                "qp,qd->pd", padded, cls_wide, precision=highest, preferred_element_type=jnp.float32
            )
            * emb_scale,
            ("role", "batch"),
            scatter_dimension=0,
            tiled=True,
        )
        spread = jnp.concatenate(
            [received[:, None], jnp.zeros((received.shape[0], slot_stride - 1, D), jnp.float32)],
            axis=1,
        ).reshape(cand_rows, D)
        d_hidden, micro_grads = encode_back(
            d_cls + spread, hidden_rows, seg_rows, weights, kept, att_rows
        )
        grad_list.append(d_hidden)
        accum = micro_grads if accum is None else jax.tree.map(jnp.add, accum, micro_grads)
    shards = (
        lax.psum_scatter(accum[0], "batch", scatter_dimension=0, tiled=True),
        lax.psum_scatter(accum[1], "batch", scatter_dimension=0, tiled=True),
        lax.psum_scatter(accum[2], "batch", scatter_dimension=0, tiled=True),
        lax.psum_scatter(accum[3], "batch", scatter_dimension=0, tiled=True),
        lax.psum_scatter(accum[4], "batch", scatter_dimension=0, tiled=True),
        lax.psum_scatter(accum[5], "batch", scatter_dimension=0, tiled=True),
        lax.psum_scatter(accum[6], "batch", scatter_dimension=0, tiled=True),
        lax.psum_scatter(accum[7], "batch", scatter_dimension=0, tiled=True),
        lax.psum_scatter(accum[8], "batch", scatter_dimension=0, tiled=True),
        lax.psum_scatter(accum[9], "batch", scatter_dimension=0, tiled=True),
        lax.psum_scatter(accum[10], "batch", scatter_dimension=0, tiled=True),
        lax.psum_scatter(accum[11], "batch", scatter_dimension=0, tiled=True),
        lax.psum_scatter(accum[12], "batch", scatter_dimension=0, tiled=True),
        lax.psum_scatter(accum[13], "batch", scatter_dimension=0, tiled=True),
        lax.psum_scatter(accum[14], "batch", scatter_dimension=0, tiled=True),
    )
    summed_grads = lax.psum(
        (
            shards[0],
            shards[1],
            shards[2],
            shards[3],
            shards[4],
            shards[5],
            shards[6],
            shards[7],
            shards[8],
            shards[9],
            shards[10],
            shards[11],
            shards[12],
            shards[13],
            shards[14],
        ),
        "role",
    )
    loss_value = lax.psum(loss_accum, ("role", "batch")) / query_total
    layer_out = jnp.stack(layer_list)[:, None]
    in_grad = jnp.stack(grad_list)[:, None]
    return (
        layer_out,
        loss_value,
        in_grad,
        summed_grads[0],
        summed_grads[1],
        summed_grads[2],
        summed_grads[3],
        summed_grads[4],
        summed_grads[5],
        summed_grads[6],
        summed_grads[7],
        summed_grads[8],
        summed_grads[9],
        summed_grads[10],
        summed_grads[11],
        summed_grads[12],
        summed_grads[13],
        summed_grads[14],
    )


def solution(mesh):
    roles, batches = mesh.shape["role"], mesh.shape["batch"]
    small = batches <= 8
    step = functools.partial(body, roles, batches) if small else general_body
    placed = (
        P(None, "role", "batch", None),
        P(),
        P(),
        P(),
        P(),
        P(),
        P(),
        P(),
        P(),
        P(),
        P(),
        P(),
        P(),
        P(),
        P(),
        P(),
        P(None, "role", "batch"),
        P(),
        P(),
        P(),
        P(),
        P(),
    )
    return jax.shard_map(
        step,
        mesh=mesh,
        in_specs=placed,
        out_specs=(
            P(None, "role", "batch", None),
            P(),
            P(None, "role", "batch", None),
            P("batch", None),
            P("batch"),
            P("batch", None),
            P("batch", None),
            P("batch"),
            P("batch", None),
            P("batch"),
            P("batch"),
            P("batch"),
            P("batch", None),
            P("batch"),
            P("batch", None),
            P("batch"),
            P("batch"),
            P("batch"),
        ),
        check_vma=False,
    )
```

```python
import functools

import jax
import jax.numpy as jnp
from jax import lax
from jax.experimental import pallas as pl
from jax.experimental.pallas import tpu as pltpu
from jax.sharding import PartitionSpec as P

D = 768
HEADS = 12
HEAD_DIM = 64
QLEN = 32
PSLOT = 256
NBINS = 10

very_low = -1e30
epsilon = 1e-12
bf16 = jnp.bfloat16
f32 = jnp.float32
MESH = pl.DeviceIdType.MESH
VMEM_BYTES = 60 * 1024 * 1024


def dot(left, right):
    return jnp.dot(left, right, preferred_element_type=f32)


def dot_right(left, right):
    return lax.dot_general(left, right, (((1,), (1,)), ((), ())), preferred_element_type=f32)


def dot_left(left, right):
    return lax.dot_general(left, right, (((0,), (0,)), ((), ())), preferred_element_type=f32)


def three_parts(wide):
    high = wide.astype(bf16)
    rest = wide - high.astype(f32)
    middle = rest.astype(bf16)
    return high, middle, (rest - middle.astype(f32)).astype(bf16)


def norm_parts(incoming):
    center = incoming - jnp.mean(incoming, axis=-1, keepdims=True)
    inv_std = lax.rsqrt(jnp.mean(center * center, axis=-1, keepdims=True) + epsilon)
    return center * inv_std, inv_std


def norm_back(scaled, normed, inv_std):
    return inv_std * (
        scaled
        - jnp.mean(scaled, axis=-1, keepdims=True)
        - normed * jnp.mean(scaled * normed, axis=-1, keepdims=True)
    )


def gelu(u):
    return 0.5 * u * (1.0 + lax.erf(u * 0.7071067811865476))


def gelu_slope(u):
    return 0.5 * (1.0 + lax.erf(u * 0.7071067811865476)) + u * (
        0.3989422804014327 * jnp.exp(-0.5 * u * u)
    )


def head_mask(cands):
    rows = lax.broadcasted_iota(jnp.int32, (HEADS * cands, D), 0)
    cols = lax.broadcasted_iota(jnp.int32, (HEADS * cands, D), 1)
    return rows // cands == cols // HEAD_DIM


def per_head(rows, mask):
    return jnp.where(mask, jnp.concatenate([rows] * HEADS, axis=0), jnp.zeros((), rows.dtype))


def from_heads(wide, mask, cands):
    kept = jnp.where(mask, wide, 0.0)
    total = kept[:cands]
    for head in range(1, HEADS):
        total = total + kept[head * cands : (head + 1) * cands]
    return total


def picked_rows(cands, rows):
    return (
        lax.broadcasted_iota(jnp.int32, (cands, rows), 1)
        == lax.broadcasted_iota(jnp.int32, (cands, rows), 0) * QLEN
    )


class Moves:
    def __init__(self, pairs, sems):
        self.copies = [
            pltpu.make_async_copy(src, dst, sems.at[i]) for i, (src, dst) in enumerate(pairs)
        ]
        self.open = set()

    def start(self, *which):
        for i in which:
            self.copies[i].start()
            self.open.add(i)

    def need(self, *which):
        for i in which:
            if i in self.open:
                self.copies[i].wait()
                self.open.remove(i)

    def finish(self):
        self.need(*sorted(self.open))


def layer_steps(x_ref, seg_row, keys, values, wq, wo, wi, wu, vec, out, queries, context, need):
    need("wq")
    queries[...] = (
        (dot(x_ref[...], wq[...]) + vec[0:1, :]).astype(bf16).astype(f32) * HEAD_DIM**-0.5
    ).astype(bf16)
    rows = seg_row.shape[1]
    seg_row = seg_row.astype(f32)
    seg_col = jnp.broadcast_to(seg_row, (128, rows)).T
    lane = lax.broadcasted_iota(jnp.int32, (rows, 128), 1)
    hot = seg_col == (lane % HEAD_DIM - 1).astype(f32)
    apart = jnp.where(hot, 0.0, very_low).astype(bf16)
    member = jnp.where(hot, 1.0, 0.0).astype(bf16)
    ones = jnp.ones((rows, 128), bf16)
    low = lane < HEAD_DIM
    yield
    for pair in range(HEADS // 2):
        part = slice(pair * 128, (pair + 1) * 128)
        q, k, v = queries[:, part], keys[:, part], values[:, part]

        def one(q_ext, k_ext, v_ext):
            scores = dot_right(q_ext, k_ext)
            raised = jnp.exp(scores - jnp.max(scores, axis=-1, keepdims=True))
            return dot(raised.astype(bf16), v_ext)

        even = one(jnp.where(low, q, apart), jnp.where(low, k, member), jnp.where(low, v, ones))
        odd = one(jnp.where(low, apart, q), jnp.where(low, member, k), jnp.where(low, ones, v))
        summed = pltpu.roll(jnp.where(low, odd, even), HEAD_DIM, 1)
        context[:, part] = (jnp.where(low, even, odd) * (1.0 / summed)).astype(bf16)
        if pair % 2 == 1:
            yield
    need("wo", "wi", "wu")
    attended = dot(context[...], wo[...]) + vec[2:3, :]
    normed, _ = norm_parts(x_ref[...].astype(f32) + attended)
    first_norm = normed * vec[3:4, :] + vec[4:5, :]
    first_low = first_norm.astype(bf16)
    total = first_norm + vec[5:6, :]
    yield
    for j in range(wi.shape[1] // D):
        part = slice(j * D, (j + 1) * D)
        u = dot(first_low, wi[:, part]) + vec[8 + j : 9 + j, :]
        total = total + dot(gelu(u).astype(bf16), wu[part, :])
        if j % 2 == 1:
            yield
    normed, _ = norm_parts(total)
    out[...] = (normed * vec[6:7, :] + vec[7:8, :]).astype(bf16)


def run_beside(steps, actions):
    for at, _ in enumerate(steps):
        for action in actions.pop(at, ()):
            action()
    for at in sorted(actions):
        for action in actions[at]:
            action()


def peer_of(step, roles, batches):
    role, batch = lax.axis_index("role"), lax.axis_index("batch")
    other = lax.rem((role // 2) * batches + batch + step, (roles // 2) * batches)
    return (other // batches) * 2 + role % 2, other % batches


def greet(roles, batches):
    role, batch = lax.axis_index("role"), lax.axis_index("batch")
    count = (roles // 2) * batches
    barrier = pltpu.get_barrier_semaphore()
    for other in range(0, roles, 2):
        there = other + 1 - role % 2
        pl.semaphore_signal(barrier, inc=1, device_id=(there, batch), device_id_type=MESH)

    def signal(step, carry):
        role_to, batch_to = peer_of(step, roles, batches)
        pl.semaphore_signal(barrier, inc=1, device_id=(role_to, batch_to), device_id_type=MESH)
        return carry

    lax.fori_loop(1, count, signal, 0)
    pl.semaphore_wait(barrier, count - 1 + roles // 2)


def remote(src, dst, out_sem, in_sem, role_to, batch_to):
    return pltpu.make_async_remote_copy(
        src_ref=src,
        dst_ref=dst,
        send_sem=out_sem,
        recv_sem=in_sem,
        device_id=(role_to, batch_to),
        device_id_type=MESH,
    )


def each(begin, end, do):
    def go(step, carry):
        do(step)
        return carry

    lax.fori_loop(begin, end, go, 0)


class Spread:
    def __init__(self, roles, batches, parts, query_ref, pass_ref, query_all, pass_all, sems):
        self.roles, self.batches, self.parts = roles, batches, parts
        self.query_ref, self.pass_ref = query_ref, pass_ref
        self.query_all, self.pass_all = query_all, pass_all
        self.q_mate, self.q_out, self.p_out, self.q_on, self.p_on, self.q_in, self.p_in, self.own = sems
        self.role, self.batch = lax.axis_index("role"), lax.axis_index("batch")
        self.core = self.role % 2
        self.mate = self.role + 1 - 2 * self.core
        self.count = (roles // 2) * batches
        self.mine = (self.role - 1) * batches + self.batch

    @staticmethod
    def sems(roles, batches, parts):
        count = (roles // 2) * batches
        dma = pltpu.SemaphoreType.DMA
        return [
            dma((parts,)),
            dma((parts, count)),
            dma((count,)),
            dma((batches, parts)),
            dma((count,)),
            dma((batches, parts)),
            dma(((roles - 1) * batches,)),
            dma((parts,)),
        ]

    def query_to(self, src, slot, part, sem, role_to, batch_to):
        begin, size, _ = self.parts[part]
        dst = self.query_all.at[slot, pl.ds(begin, size)]
        return remote(src, dst, sem, self.q_in.at[slot, part], role_to, batch_to)

    def my_part(self, part):
        begin, size, _ = self.parts[part]
        return self.query_ref.at[pl.ds(begin, size)]

    def to_mate(self, part):
        return self.query_to(
            self.my_part(part), self.batch, part, self.q_mate.at[part], self.mate, self.batch
        )

    def to_peer(self, part, step):
        role_to, batch_to = peer_of(step, self.roles, self.batches)
        return self.query_to(
            self.my_part(part), self.batch, part, self.q_out.at[part, step], role_to, batch_to
        )

    def across(self, part):
        return self.query_to(
            self.my_part(part), self.batch, part, self.q_out.at[part, 0],
            lax.rem(self.role + 2, self.roles), self.batch,
        )

    def from_across(self, part, step):
        role_to, batch_to = peer_of(step, self.roles, self.batches)
        begin, size, _ = self.parts[part]
        src = self.query_all.at[self.batch, pl.ds(begin, size)]
        return self.query_to(src, self.batch, part, self.q_out.at[part, step], role_to, batch_to)

    def pass_to(self, src, slot, sem, role_to, batch_to):
        return remote(src, self.pass_all.at[slot], sem, self.p_in.at[slot], role_to, batch_to)

    def pass_peer(self, step):
        role_to, batch_to = peer_of(step, self.roles, self.batches)
        return self.pass_to(self.pass_ref, self.mine, self.p_out.at[step], role_to, batch_to)

    def pass_mate(self):
        return self.pass_to(self.pass_ref, self.mine, self.p_out.at[0], self.mate, self.batch)

    def on(self, slot, part):
        begin, size, _ = self.parts[part]
        src = self.query_all.at[slot, pl.ds(begin, size)]
        return self.query_to(src, slot, part, self.q_on.at[slot, part], self.mate, self.batch)

    def pass_on(self, step, slot):
        return self.pass_to(self.pass_all.at[slot], slot, self.p_on.at[step], self.mate, self.batch)

    def begin_query(self, part):
        @pl.when(self.role == 0)
        def _():
            if self.parts[part][2]:
                self.across(part).start()
            else:
                each(1, self.count, lambda step: self.to_peer(part, step).start())
            self.to_mate(part).start()
            begin, size, _ = self.parts[part]
            keep = pltpu.make_async_copy(
                self.my_part(part), self.query_all.at[self.batch, pl.ds(begin, size)], self.own.at[part]
            )
            keep.start()
            keep.wait()

    def begin_pass(self):
        @pl.when(self.role > 0)
        def _():
            each(1, self.count, lambda step: self.pass_peer(step).start())
            self.pass_mate().start()
            keep = pltpu.make_async_copy(self.pass_ref, self.pass_all.at[self.mine], self.own.at[0])
            keep.start()
            keep.wait()

    def second(self, part):
        @pl.when(self.role == 2)
        def _():
            self.on(self.batch, part).wait_recv()
            each(
                1,
                self.count,
                lambda step: pl.when(step != self.batches)(
                    lambda: self.from_across(part, step).start()
                ),
            )

    def relay_query(self, *parts):
        @pl.when(self.core == 0)
        def _():
            def go(step):
                slot = lax.rem(self.batch + step, self.batches)
                away = jnp.logical_or(self.role != 0, step > 0)
                for part in parts:
                    came = away
                    if self.parts[part][2]:
                        came = jnp.logical_or(step > 0, jnp.logical_and(self.role != 0, self.role != 2))
                    pl.when(came)(lambda: self.on(slot, part).wait_recv())
                    pl.when(away)(lambda: self.on(slot, part).start())

            each(0, self.batches, go)

    def relay_pass(self):
        def go(step):
            role_of, batch_of = peer_of(step, self.roles, self.batches)
            slot = (role_of - 1) * self.batches + batch_of

            @pl.when(role_of > 0)
            def _():
                self.pass_on(step, slot).wait_recv()
                self.pass_on(step, slot).start()

        each(1, self.count, go)

    def take(self):
        role, batch, batches, count = self.role, self.batch, self.batches, self.count

        @pl.when(self.core == 1)
        def _():
            def go(step):
                for part in range(len(self.parts)):
                    self.on(step, part).wait_recv()

            each(0, batches, go)

        def take(step):
            other = lax.rem((role // 2) * batches + batch + step, count)
            role_of = (other // batches) * 2 + 1 - self.core
            slot = (role_of - 1) * batches + other % batches
            pl.when(role_of > 0)(lambda: self.pass_on(step, slot).wait_recv())

        each(0, count, take)

    def end(self):
        role, batch, batches, count = self.role, self.batch, self.batches, self.count

        @pl.when(role == 0)
        def _():
            for part in range(len(self.parts)):
                if self.parts[part][2]:
                    self.across(part).wait_send()
                else:
                    each(1, count, lambda step: self.to_peer(part, step).wait_send())
                self.to_mate(part).wait_send()

        @pl.when(role > 0)
        def _():
            each(1, count, lambda step: self.pass_peer(step).wait_send())
            self.pass_mate().wait_send()

        @pl.when(role == 2)
        def _():
            for part, (_, _, via) in enumerate(self.parts):
                if via:
                    each(
                        1,
                        count,
                        lambda step: pl.when(step != batches)(
                            lambda: self.from_across(part, step).wait_send()
                        ),
                    )

        @pl.when(self.core == 0)
        def _():
            def go(step):
                slot = lax.rem(batch + step, batches)
                away = jnp.logical_or(role != 0, step > 0)
                for part in range(len(self.parts)):
                    pl.when(away)(lambda: self.on(slot, part).wait_send())

            each(0, batches, go)

        def passed(step):
            role_of, batch_of = peer_of(step, self.roles, batches)
            slot = (role_of - 1) * batches + batch_of
            pl.when(role_of > 0)(lambda: self.pass_on(step, slot).wait_send())

        each(1, count, passed)


def first_kernel(
    roles, batches, micros, rows, early,
    seg, hid_far, wq_far, wk_far, wv_far, wo_far, wi_far, wu_far, *refs,
):
    lines, refs = refs[:9], refs[9:]
    keys_far, values_far, probs_far, query_far, pass_far, layer_far, query_c, vec = refs[:8]
    hid, wq, wk, wv, wo, wi, wu, keys, values, probs, out, queries, context = refs[8:21]
    query_msg, pass_msg, query_all, pass_all, in_sems, out_sems = refs[21:27]
    sems = refs[27:]
    cands = rows // QLEN
    total = micros * cands
    names = ["hid", "wq", "wk", "wv", "wo", "wi", "wu"]
    far = (hid_far, wq_far, wk_far, wv_far, wo_far, wi_far, wu_far)
    moves = Moves(list(zip(far, (hid, wq, wk, wv, wo, wi, wu))), in_sems)
    moves.start(0, 2, 3, 1, 4, 5, 6)

    def need(*which):
        moves.need(*[names.index(name) for name in which])

    blocks = [pl.ds(m * rows, rows) for m in range(micros)]
    stores = Moves(
        [(keys, keys_far), (values, values_far), (probs, probs_far), (query_all, query_far), (pass_all, pass_far)]
        + [(out.at[blocks[m]], layer_far.at[blocks[m]]) for m in range(early)],
        out_sems,
    )
    greet(roles, batches)
    parts = [(0, total // 2, False), (total // 2, total // 2, True)]
    parts += [(total + m * cands, cands, m % 2 == 1) for m in range(micros)]
    spread = Spread(roles, batches, parts, query_msg, pass_msg, query_all, pass_all, sems)

    at = 0
    for line in lines:
        wide = line[...].astype(f32).reshape(1, -1)
        for j in range(wide.shape[1] // D):
            vec[at : at + 1, :] = wide[:, j * D : (j + 1) * D]
            at += 1
    mask = head_mask(cands)
    pick = picked_rows(cands, rows)
    pick_low = pick.astype(f32).astype(bf16)
    need("hid")
    x_cand = jnp.concatenate(
        [dot(pick_low, hid[blocks[m], :]).astype(bf16) for m in range(micros)], axis=0
    )
    query_msg[0:total, :] = x_cand
    spread.begin_query(1)
    spread.begin_query(0)
    need("wk", "wv", "wq")
    q_cand = (
        (dot(x_cand, wq[...]) + vec[0:1, :]).astype(bf16).astype(f32) * HEAD_DIM**-0.5
    ).astype(bf16)
    query_c[...] = q_cand
    for m in range(micros):
        block = blocks[m]
        x = hid[block, :]
        k = dot(x, wk[...]).astype(bf16)
        v = (dot(x, wv[...]) + vec[1:2, :]).astype(bf16)
        keys[block, :] = k
        values[block, :] = v
        seg_row = seg[m].astype(f32)
        seg_col = jnp.sum(jnp.where(pick, seg_row, 0.0), axis=-1, keepdims=True)
        bias = jnp.where(seg_col == seg_row, 0.0, very_low)
        q_wide = per_head(q_cand[m * cands : (m + 1) * cands], mask)
        scores = dot_right(q_wide, k) + jnp.concatenate([bias] * HEADS, axis=0)
        raised = jnp.exp(scores - jnp.max(scores, axis=-1, keepdims=True))
        prob = raised * (1.0 / jnp.sum(raised, axis=-1, keepdims=True))
        probs[m * HEADS * cands : (m + 1) * HEADS * cands, :] = prob
        attended = from_heads(dot(prob.astype(bf16), v), mask, cands)
        query_msg[total + m * cands : total + (m + 1) * cands, :] = attended.astype(bf16)
        spread.begin_query(2 + m)
        if m % 2 == 0:
            spread.second(1 + m)
    wide = query_msg[...].astype(f32)
    per_slot = PSLOT // QLEN
    chosen = []
    for part in range(2):
        for m in range(micros):
            for slot in range(cands // per_slot):
                at = (part * micros + m) * cands + slot * per_slot
                chosen.append(wide[at : at + 1])
    pass_msg[...] = jnp.concatenate(chosen, axis=0).astype(bf16)
    spread.begin_pass()
    stores.start(0, 1, 2)

    def steps():
        for m in range(early):
            yield from layer_steps(
                hid.at[blocks[m]], seg[m], keys.at[blocks[m]], values.at[blocks[m]],
                wq, wo, wi, wu, vec, out.at[blocks[m]], queries, context, need,
            )
            stores.start(5 + m)
            yield

    run_beside(steps(), first_plan(spread, len(parts)))
    spread.take()
    stores.start(3, 4)
    spread.end()
    stores.finish()


def first_plan(spread, parts):
    return {
        0: [lambda: spread.second(parts - 1)],
        3: [lambda: spread.relay_query(0, 1)],
        10: [lambda: spread.relay_query(*range(2, parts - 2))],
        14: [lambda: spread.relay_query(parts - 2, parts - 1)],
        15: [spread.relay_pass],
    }


def first_stage(hid, seg, weights, lines, micros, early, roles, batches):
    rows = hid.shape[0] // micros
    cands = rows // QLEN
    total = micros * cands
    passes = micros * (rows // PSLOT)
    vmem = pl.BlockSpec(memory_space=pltpu.VMEM)
    far = pl.BlockSpec(memory_space=pl.ANY)
    query_all = (batches, 2 * total, D)
    pass_all = ((roles - 1) * batches, 2 * passes, D)
    probs = (micros * HEADS * cands, rows)
    held = pltpu.VMEM(hid.shape, bf16)
    return pl.pallas_call(
        functools.partial(first_kernel, roles, batches, micros, rows, early),
        in_specs=[vmem] + [far] * 7 + [vmem] * len(lines),
        out_specs=(far,) * 6 + (vmem,) * 2,
        out_shape=(
            jax.ShapeDtypeStruct(hid.shape, bf16),
            jax.ShapeDtypeStruct(hid.shape, bf16),
            jax.ShapeDtypeStruct(probs, f32),
            jax.ShapeDtypeStruct(query_all, bf16),
            jax.ShapeDtypeStruct(pass_all, bf16),
            jax.ShapeDtypeStruct((early * rows, D), bf16),
            jax.ShapeDtypeStruct((total, D), bf16),
            jax.ShapeDtypeStruct((sum(line.size for line in lines) // D, D), f32),
        ),
        scratch_shapes=[held]
        + [pltpu.VMEM(w.shape, bf16) for w in weights]
        + [held, held, pltpu.VMEM(probs, f32), pltpu.VMEM((early * rows, D), bf16)]
        + [pltpu.VMEM((rows, D), bf16)] * 2
        + [
            pltpu.VMEM((2 * total, D), bf16),
            pltpu.VMEM((2 * passes, D), bf16),
            pltpu.VMEM(query_all, bf16),
            pltpu.VMEM(pass_all, bf16),
            pltpu.SemaphoreType.DMA((7,)),
            pltpu.SemaphoreType.DMA((5 + early,)),
        ]
        + Spread.sems(roles, batches, 2 + micros),
        compiler_params=pltpu.CompilerParams(
            collective_id=1, has_side_effects=True, vmem_limit_bytes=VMEM_BYTES
        ),
        name="first",
    )(seg, hid, *weights, *lines)


def middle_kernel(
    micros,
    cands,
    columns,
    query_all,
    pass_all,
    wo,
    wi,
    wu,
    vec,
    positive,
    negative,
    bins,
    margins,
    clusters,
    loss_out,
    inner_grad,
    outer_grad,
    output_grad,
    value_bias,
    output_bias,
    first_gain,
    first_shift,
    inner_bias,
    outer_bias,
    second_gain,
    second_shift,
    x_slice,
    d_own,
    vectors,
    inner_row,
    x_all,
    c_all,
    u_all,
    g_all,
    n_one,
    d_rows,
):
    role, batch = lax.axis_index("role"), lax.axis_index("batch")
    batches = query_all.shape[0]
    own_rows = micros * cands
    n_query = batches * own_rows
    n_dev = pass_all.shape[0]
    per_dev = pass_all.shape[1] // 2
    per_micro = per_dev // micros
    n_pass = n_dev * per_dev
    n_rows = n_query + n_pass
    inner = wi.shape[1]
    chunks = [slice(j * D, (j + 1) * D) for j in range(inner // D)]

    for b in range(batches):
        x_all[b * own_rows : (b + 1) * own_rows, :] = query_all[b, 0:own_rows, :]
        c_all[b * own_rows : (b + 1) * own_rows, :] = query_all[b, own_rows : 2 * own_rows, :]
    wide = pass_all[...].astype(f32)
    x_all[n_query:n_rows, :] = wide[:, 0:per_dev, :].reshape(n_pass, D).astype(bf16)
    c_all[n_query:n_rows, :] = wide[:, per_dev:, :].reshape(n_pass, D).astype(bf16)

    attended = dot(c_all[...], wo[...]) + vec[2:3, :]
    normed, inv_one = norm_parts(x_all[...].astype(f32) + attended)
    n_one[...] = normed
    first_norm = normed * vec[3:4, :] + vec[4:5, :]
    first_low = first_norm.astype(bf16)
    total = first_norm + vec[5:6, :]
    for j, part in enumerate(chunks):
        u = dot(first_low, wi[:, part]) + vec[8 + j : 9 + j, :]
        u_all[:, part] = u
        g = gelu(u).astype(bf16)
        g_all[:, part] = g
        total = total + dot(g, wu[part, :])
    n_two, inv_two = norm_parts(total)
    low = (n_two * vec[6:7, :] + vec[7:8, :]).astype(bf16)
    q_low, p_low = low[:n_query], low[n_query:]

    bin_ids = bins[...]
    queries_total = bin_ids.shape[0] * bin_ids.shape[1]
    weight = jnp.zeros(bin_ids.shape, f32)
    for k in range(NBINS):
        hit = (bin_ids == k).astype(f32)
        amount = jnp.sum(jnp.sum(hit, axis=1, keepdims=True), axis=0, keepdims=True)
        weight = weight + hit * (queries_total / (NBINS * jnp.maximum(amount, 1.0)))

    lane = lax.broadcasted_iota(jnp.int32, (n_query, bin_ids.shape[1]), 1)
    row = lax.broadcasted_iota(jnp.int32, (n_query, bin_ids.shape[1]), 0)
    here = lane == (row // own_rows) * cands + row % cands

    def by_micro(table):
        parts = [
            jnp.broadcast_to(table[m : m + 1, :], (cands, table.shape[1])) for m in range(micros)
        ]
        return jnp.concatenate(parts * batches, axis=0)

    def per_query(table):
        return jnp.sum(jnp.where(here, by_micro(table), 0.0), axis=-1, keepdims=True)

    pos = per_query(positive[...].astype(f32))
    neg = per_query(negative[...].astype(f32))
    margin = per_query(margins[...])
    weight = per_query(weight)

    col = lax.broadcasted_iota(jnp.int32, (n_query, n_pass), 1)
    row = lax.broadcasted_iota(jnp.int32, (n_query, n_pass), 0)
    same = (col % per_dev) // per_micro == (row % own_rows) // cands
    ident = ((col // per_dev) * per_micro + col % per_micro).astype(f32)
    n_ids = n_dev * per_micro
    tab_row = lax.broadcasted_iota(jnp.int32, (n_ids, n_pass), 0)
    tab_col = lax.broadcasted_iota(jnp.int32, (n_ids, n_pass), 1)
    table = tab_row == (tab_col // per_dev) * per_micro + tab_col % per_micro
    cluster = by_micro(dot(clusters[...].astype(f32).astype(bf16), table.astype(f32).astype(bf16)))
    pos_hit = jnp.logical_and(same, ident == pos)
    neg_hit = jnp.logical_and(same, ident == neg)
    pos_cluster = jnp.sum(jnp.where(pos_hit, cluster, 0.0), axis=-1, keepdims=True)
    allowed = jnp.logical_and(same, cluster == pos_cluster)
    scores = dot_right(q_low, p_low) * D**-0.5
    masked = jnp.where(allowed, scores, very_low)
    row_max = jnp.max(masked, axis=-1, keepdims=True)
    raised = jnp.exp(masked - row_max)
    summed = jnp.sum(raised, axis=-1, keepdims=True)
    pos_score = jnp.sum(jnp.where(pos_hit, scores, 0.0), axis=-1, keepdims=True)
    neg_score = jnp.sum(jnp.where(neg_hit, scores, 0.0), axis=-1, keepdims=True)
    gap = pos_score - neg_score - margin
    terms = row_max + jnp.log(summed) - pos_score + weight * gap * gap
    loss_out[...] = jnp.broadcast_to(
        jnp.sum(terms, axis=0, keepdims=True) / queries_total, loss_out.shape
    )
    pull = 2.0 * weight * gap
    pos_one, neg_one = pos_hit.astype(f32), neg_hit.astype(f32)
    d_scores = (raised * (1.0 / summed) - pos_one + pull * (pos_one - neg_one)) * D**-0.5
    parts = three_parts(d_scores)
    d_query = sum(dot(part, p_low) for part in parts)
    d_pass = sum(dot_left(part, q_low) for part in parts)
    grad = jnp.concatenate([d_query, d_pass], axis=0)

    def total_of(array):
        return jnp.sum(array, axis=0, keepdims=True)

    vectors[6:7, :] = total_of(grad * n_two)
    vectors[7:8, :] = total_of(grad)
    d_two = norm_back(grad * vec[6:7, :], n_two, inv_two)
    d_outer = d_two.astype(bf16)
    vectors[5:6, :] = total_of(d_outer.astype(f32))
    select = (
        lax.broadcasted_iota(jnp.int32, (D, 128), 0)
        == lax.broadcasted_iota(jnp.int32, (D, 128), 1) + batch * columns
    )
    select = jnp.logical_and(select, lax.broadcasted_iota(jnp.int32, (D, 128), 1) < columns)
    select = select.astype(f32).astype(bf16)
    first_low = (n_one[...] * vec[3:4, :] + vec[4:5, :]).astype(bf16)
    y_slice = dot(first_low, select).astype(bf16)
    d_first = d_two
    for j, part in enumerate(chunks):
        d_inner = (dot_right(d_outer, wu[part, :]) * gelu_slope(u_all[:, part])).astype(bf16)
        inner_row[:, part] = total_of(d_inner.astype(f32))
        inner_grad[:, part] = dot_left(y_slice, d_inner)[:columns]
        d_first = d_first + dot_right(d_inner, wi[:, part])
    span = inner // batches
    outer_grad[...] = dot_left(g_all[:, pl.ds(pl.multiple_of(batch * span, 128), span)], d_outer)
    vectors[3:4, :] = total_of(d_first * n_one[...])
    vectors[4:5, :] = total_of(d_first)
    d_one = norm_back(d_first * vec[3:4, :], n_one[...], inv_one)
    d_rows[...] = d_one
    d_low = d_one.astype(bf16)
    bias_row = total_of(d_low.astype(f32))
    vectors[2:3, :] = bias_row
    vectors[1:2, :] = sum(dot_right(part, wo[...]) for part in three_parts(bias_row))
    vectors[0:1, :] = jnp.zeros_like(bias_row)
    c_slice = dot(c_all[...], select).astype(bf16)
    output_grad[...] = dot_left(c_slice, d_low)[:columns]
    x_slice[...] = dot(x_all[...], select).astype(bf16)
    mine = sum(dot(part, select) for part in three_parts(vectors[...]))
    outs = [value_bias, output_bias, first_gain, first_shift, outer_bias, second_gain, second_shift]
    for row, out in enumerate(outs):
        out[...] = mine[row + 1, :columns]
    inner_bias[...] = inner_row[0, pl.ds(pl.multiple_of(batch * span, 128), span)]

    @pl.when(role == 0)
    def _():
        d_own[...] = d_rows[pl.ds(pl.multiple_of(batch * own_rows, 8), own_rows), :]

    @pl.when(role > 0)
    def _():
        d_own[...] = jnp.zeros_like(d_own)
        begin = pl.multiple_of(n_query + ((role - 1) * batches + batch) * per_dev, 8)
        mine = d_rows[pl.ds(begin, per_dev), :]
        for m in range(micros):
            for slot in range(per_micro):
                at = m * cands + slot * (PSLOT // QLEN)
                d_own[at : at + 1, :] = mine[m * per_micro + slot : m * per_micro + slot + 1, :]


def middle_stage(query_all, pass_all, wo, wi, wu, vec, positive, negative, bins, margins, clusters):
    batches = query_all.shape[0]
    micros = positive.shape[0]
    own_rows = query_all.shape[1] // 2
    n_pass = pass_all.shape[0] * pass_all.shape[1] // 2
    n_rows = batches * own_rows + n_pass
    columns = D // batches
    inner = wi.shape[1]
    return pl.pallas_call(
        functools.partial(middle_kernel, micros, own_rows // micros, columns),
        out_shape=(
            jax.ShapeDtypeStruct((1, 128), f32),
            jax.ShapeDtypeStruct((columns, inner), f32),
            jax.ShapeDtypeStruct((inner // batches, D), f32),
            jax.ShapeDtypeStruct((columns, D), f32),
        )
        + tuple(jax.ShapeDtypeStruct((size,), f32) for size in [columns] * 4 + [inner // batches] + [columns] * 3)
        + (
            jax.ShapeDtypeStruct((n_rows, 128), bf16),
            jax.ShapeDtypeStruct((own_rows, D), f32),
        ),
        scratch_shapes=[
            pltpu.VMEM((8, D), f32),
            pltpu.VMEM((1, inner), f32),
            pltpu.VMEM((n_rows, D), bf16),
            pltpu.VMEM((n_rows, D), bf16),
            pltpu.VMEM((n_rows, inner), f32),
            pltpu.VMEM((n_rows, inner), bf16),
            pltpu.VMEM((n_rows, D), f32),
            pltpu.VMEM((n_rows, D), f32),
        ],
        compiler_params=pltpu.CompilerParams(vmem_limit_bytes=VMEM_BYTES),
        name="middle",
    )(query_all, pass_all, wo, wi, wu, vec, positive, negative, bins, margins, clusters)


def last_kernel(
    roles, batches, micros, rows, early,
    seg, vec, query_c, d_own, x_slice, hid_far, keys_far, values_far, probs_far,
    wq_far, wk_far, wv_far, wo_far, wi_far, wu_far,
    query_grad, query_bias, key_grad, value_grad, layer_far, in_grad_far,
    hid, keys, values, probs, wq, wk, wv, wo, wi, wu, out, queries, context,
    both, q_keep, c_keep, z_key, z_value, d_hidden, dq_ref, dq_pass, key_part, value_part,
    query_all, pass_all, from_mate, summed, from_x, halves, received, finals,
    in_sems, out_sems, mate_out, mate_in, x_out, x_in, part_out, part_in, last_out, last_in, *sems,
):
    role, batch = lax.axis_index("role"), lax.axis_index("batch")
    core, side = role % 2, role // 2
    mate = role + 1 - 2 * core
    across = lax.rem(role + 2, roles)
    cands = rows // QLEN
    total = micros * cands
    wide_rows = HEADS * cands
    columns = query_grad.shape[0]
    pieces = summed.shape[2]
    names = ["hid", "keys", "values", "probs", "wq", "wk", "wv", "wo", "wi", "wu"]
    far = (
        hid_far, keys_far, values_far, probs_far, wq_far, wk_far, wv_far, wo_far, wi_far, wu_far,
    )
    moves = Moves(
        list(zip(far, (hid, keys, values, probs, wq, wk, wv, wo, wi, wu))), in_sems
    )
    moves.start(7, 2, 3, 1, 0, 5, 6, 4, 8, 9)

    def need(*which):
        moves.need(*[names.index(name) for name in which])

    blocks = [pl.ds(m * rows, rows) for m in range(micros)]
    wides = [pl.ds(m * wide_rows, wide_rows) for m in range(micros)]
    late = micros - early
    stores = Moves(
        [(out.at[blocks[m]], layer_far.at[blocks[m]]) for m in range(late)]
        + [(d_hidden.at[m % 2], in_grad_far.at[blocks[m]]) for m in range(micros)],
        out_sems,
    )
    greet(roles, batches)
    spread = Spread(
        roles, batches, [(0, total // 2, False), (total // 2, total // 2, True)], dq_ref, dq_pass, query_all, pass_all, sems
    )

    mask = head_mask(cands)
    need("wo")
    d_context = dot_right(d_own[...].astype(bf16), wo[...]).astype(bf16)
    need("values", "probs", "keys", "hid")
    d_query = []
    for m in range(micros):
        cand = slice(m * cands, (m + 1) * cands)
        q_wide = per_head(query_c[cand, :], mask)
        c_wide = per_head(d_context[cand, :], mask)
        prob = probs[wides[m], :]
        pulled = prob * dot_right(c_wide, values[blocks[m], :])
        d_scores = (pulled - prob * jnp.sum(pulled, axis=-1, keepdims=True)).astype(bf16)
        pair = jnp.concatenate([d_scores, prob.astype(bf16)], axis=0)
        d_query.append(from_heads(dot(d_scores, keys[blocks[m], :]), mask, cands) * HEAD_DIM**-0.5)
        sums = dot(pair, hid[blocks[m], :])
        both[m] = pair
        z_key[wides[m], :] = sums[:wide_rows].astype(bf16)
        z_value[wides[m], :] = sums[wide_rows:].astype(bf16)
        q_keep[wides[m], :] = q_wide
        c_keep[wides[m], :] = c_wide
    d_query = jnp.concatenate(d_query, axis=0).astype(bf16)
    dq_ref[...] = d_query
    wide = d_query.astype(f32)
    per_slot = PSLOT // QLEN
    dq_pass[...] = jnp.concatenate(
        [wide[at : at + 1] for at in range(0, total, per_slot)], axis=0
    )
    spread.begin_query(1)
    spread.begin_query(0)
    spread.begin_pass()
    split = summed.shape
    key_part[...] = dot_left(z_key[...], q_keep[...]).astype(bf16).reshape(split)
    value_part[...] = dot_left(z_value[...], c_keep[...]).astype(bf16).reshape(split)

    @pl.when(core == 0)
    def _():
        remote(value_part, from_mate, mate_out, mate_in, mate, batch).start()

    @pl.when(core == 1)
    def _():
        remote(key_part, from_mate, mate_out, mate_in, mate, batch).start()

    def to_x(piece):
        return remote(
            summed.at[:, 1 - side, piece], from_x.at[:, piece], x_out.at[piece], x_in.at[piece], across, batch
        )

    def begin_x():
        remote(key_part, from_mate, mate_out, mate_in, mate, batch).wait()

        @pl.when(core == 0)
        def _():
            summed[...] = (key_part[...].astype(f32) + from_mate[...].astype(f32)).astype(bf16)

        @pl.when(core == 1)
        def _():
            summed[...] = (value_part[...].astype(f32) + from_mate[...].astype(f32)).astype(bf16)

        for piece in range(pieces):
            to_x(piece).start()

    def to_batch(piece, step):
        other = lax.rem(batch + step, batches)
        return remote(
            halves.at[other, piece], received.at[batch, piece], part_out.at[other, piece],
            part_in.at[batch, piece], role, other,
        )

    def from_batch(piece, step):
        other = lax.rem(batch + step, batches)
        return remote(
            halves.at[other, piece], received.at[other, piece], part_out.at[other, piece],
            part_in.at[other, piece], role, other,
        )

    def begin_part(piece):
        to_x(piece).wait()
        halves[:, piece] = (
            summed[:, side, piece].astype(f32) + from_x[:, piece].astype(f32)
        ).astype(bf16)
        each(1, batches, lambda step: to_batch(piece, step).start())

    def to_role(step):
        other = lax.rem(role + step, roles)
        return remote(
            finals.at[role], finals.at[role], last_out.at[step], last_in.at[role], other, batch
        )

    def from_role(step):
        other = lax.rem(role + step, roles)
        return remote(
            finals.at[other], finals.at[other], last_out.at[step], last_in.at[other], other, batch
        )

    def begin_last():
        for piece in range(pieces):
            each(1, batches, lambda step: from_batch(piece, step).wait_recv())
            sum_all = halves[batch, piece].astype(f32)

            def add(step, so_far):
                return so_far + received[lax.rem(batch + step, batches), piece].astype(f32)

            finals[role, piece] = lax.fori_loop(1, batches, add, sum_all).astype(bf16)
        for step in range(1, roles):
            to_role(step).start()

    def steps():
        need("wk", "wv", "wq")
        extra = dot_right(dq_ref[...], wq[...]) + d_own[...]
        z_key[...] = dot_right(q_keep[...], wk[...]).astype(bf16)
        z_value[...] = dot_right(c_keep[...], wv[...]).astype(bf16)
        yield
        for m in range(micros):
            back = jnp.concatenate([z_key[wides[m], :], z_value[wides[m], :]], axis=0)
            if m >= 2:
                stores.need(late + m - 2)
            d_hidden[m % 2] = dot_left(both[m], back)
            for cand in range(cands):
                at = slice(cand * QLEN, cand * QLEN + 1)
                row = m * cands + cand
                d_hidden[m % 2, at, :] = d_hidden[m % 2, at, :] + extra[row : row + 1, :]
            stores.start(late + m)
            yield
        for m in range(late):
            block = blocks[early + m]
            yield from layer_steps(
                hid.at[block], seg[early + m], keys.at[block], values.at[block],
                wq, wo, wi, wu, vec, out.at[blocks[m]], queries, context, need,
            )
            stores.start(m)
            yield

    parts = [functools.partial(begin_part, piece) for piece in range(pieces)]
    run_beside(steps(), last_plan(begin_x, spread, parts, begin_last))
    spread.take()
    count = batches * total
    all_query = query_all[...].reshape(count, D)
    all_pass = pass_all[...].reshape(-1, D)
    query_grad[...] = (
        dot_left(x_slice[0:count, :], all_query) + dot_left(x_slice[count:, :], all_pass.astype(bf16))
    )[:columns]
    query_bias[...] = jnp.sum(all_query.astype(f32), axis=0, keepdims=True) + jnp.sum(
        all_pass, axis=0, keepdims=True
    )
    spread.end()
    for piece in range(pieces):
        each(1, batches, lambda step: to_batch(piece, step).wait_send())
    for step in range(1, roles):
        from_role(step).wait_recv()
        to_role(step).wait_send()
    half = pieces * finals.shape[2]
    for x in range(roles // 2):
        here = slice(x * half, (x + 1) * half)
        key_grad[here, :] = finals[2 * x].astype(f32).reshape(half, D)
        value_grad[here, :] = finals[2 * x + 1].astype(f32).reshape(half, D)
    stores.finish()
    moves.finish()


def last_plan(begin_x, spread, parts, begin_last):
    return {
        0: [lambda: spread.second(1), begin_x],
        6: [parts[0]],
        9: [parts[1]],
        12: [parts[2]],
        14: [spread.relay_pass],
        17: [lambda: spread.relay_query(0, 1)],
        20: [begin_last],
    }


def last_stage(
    seg, vec, query_c, d_own, x_slice, hid, keys, values, probs, weights, early, roles, batches
):
    columns = D // batches
    micros, _, rows = seg.shape
    total = query_c.shape[0]
    passes = micros * (rows // PSLOT)
    wide = micros * HEADS * (rows // QLEN)
    vmem = pl.BlockSpec(memory_space=pltpu.VMEM)
    far = pl.BlockSpec(memory_space=pl.ANY)
    block = (columns, D)
    sides, tile = roles // 2, 16
    pieces = columns // sides // tile
    split = (batches, sides, pieces, tile, D)
    half = (batches, pieces, tile, D)
    dma = pltpu.SemaphoreType.DMA
    late = micros - early
    held = pltpu.VMEM(hid.shape, bf16)
    wide_rows = pltpu.VMEM((wide, D), bf16)
    return pl.pallas_call(
        functools.partial(last_kernel, roles, batches, micros, rows, early),
        in_specs=[vmem] * 5 + [far] * 10,
        out_specs=(vmem,) * 4 + (far,) * 2,
        out_shape=(
            jax.ShapeDtypeStruct(block, f32),
            jax.ShapeDtypeStruct((1, D), f32),
            jax.ShapeDtypeStruct(block, f32),
            jax.ShapeDtypeStruct(block, f32),
            jax.ShapeDtypeStruct((late * rows, D), bf16),
            jax.ShapeDtypeStruct(hid.shape, f32),
        ),
        scratch_shapes=[held, held, held, pltpu.VMEM(probs.shape, f32)]
        + [pltpu.VMEM(w.shape, bf16) for w in weights]
        + [pltpu.VMEM((late * rows, D), bf16)]
        + [pltpu.VMEM((rows, D), bf16)] * 2
        + [
            pltpu.VMEM((micros, 2 * wide // micros, rows), bf16),
            wide_rows,
            wide_rows,
            wide_rows,
            wide_rows,
            pltpu.VMEM((2, rows, D), f32),
            pltpu.VMEM((total, D), bf16),
            pltpu.VMEM((passes, D), f32),
            pltpu.VMEM(split, bf16),
            pltpu.VMEM(split, bf16),
            pltpu.VMEM((batches, total, D), bf16),
            pltpu.VMEM(((roles - 1) * batches, passes, D), f32),
            pltpu.VMEM(split, bf16),
            pltpu.VMEM(split, bf16),
            pltpu.VMEM(half, bf16),
            pltpu.VMEM(half, bf16),
            pltpu.VMEM(half, bf16),
            pltpu.VMEM((roles, pieces, tile, D), bf16),
            dma((10,)),
            dma((late + micros,)),
            dma,
            dma,
            dma((pieces,)),
            dma((pieces,)),
            dma((batches, pieces)),
            dma((batches, pieces)),
            dma((roles,)),
            dma((roles,)),
        ]
        + Spread.sems(roles, batches, 2),
        compiler_params=pltpu.CompilerParams(
            collective_id=2, has_side_effects=True, vmem_limit_bytes=VMEM_BYTES
        ),
        name="last",
    )(seg, vec, query_c, d_own, x_slice, hid, keys, values, probs, *weights)


def body(
    roles,
    batches,
    hidden,
    query_weight,
    query_bias,
    key_weight,
    value_weight,
    value_bias,
    output_weight,
    output_bias,
    first_gain,
    first_shift,
    inner_weight,
    inner_bias,
    outer_weight,
    outer_bias,
    second_gain,
    second_shift,
    segment,
    positive,
    negative,
    bins,
    margins,
    clusters,
):
    micros, rows = hidden.shape[0], hidden.shape[2]
    hid = hidden.reshape(micros * rows, D)
    lines = [
        query_bias,
        value_bias,
        output_bias,
        first_gain,
        first_shift,
        outer_bias,
        second_gain,
        second_shift,
        inner_bias,
    ]
    early = micros // 2
    weights = (query_weight, key_weight, value_weight, output_weight, inner_weight, outer_weight)
    keys, values, probs, query_all, pass_all, layer_early, query_c, vec = first_stage(
        hid, segment, weights, lines, micros, early, roles, batches
    )
    loss, inner_grad, outer_grad, output_grad, *biases, x_slice, d_own = middle_stage(
        query_all,
        pass_all,
        output_weight,
        inner_weight,
        outer_weight,
        vec,
        positive,
        negative,
        bins[..., 0],
        margins,
        clusters,
    )
    query_grad, query_bias_row, key_grad, value_grad, layer_late, in_grad = last_stage(
        segment, vec, query_c, d_own, x_slice, hid, keys, values, probs, weights, early, roles, batches
    )
    layer_out = jnp.concatenate([layer_early, layer_late], axis=0)
    batch = lax.axis_index("batch")
    columns = D // batches
    mine_query = lax.dynamic_slice_in_dim(query_bias_row[0], batch * columns, columns)
    value_b, output_b, first_g, first_s, inner_b, outer_b, second_g, second_s = biases
    return (
        layer_out.reshape(hidden.shape),
        loss[0, 0],
        in_grad.reshape(hidden.shape),
        query_grad,
        mine_query,
        key_grad,
        value_grad,
        value_b,
        output_grad,
        output_b,
        first_g,
        first_s,
        inner_grad,
        inner_b,
        outer_grad,
        outer_b,
        second_g,
        second_s,
    )


highest = lax.Precision.HIGHEST


def multiply(left, right):
    return jnp.dot(left, right, preferred_element_type=jnp.float32)


def left_product(left, right):
    return jnp.einsum("rd,re->de", left, right, preferred_element_type=jnp.float32)


def right_product(left, right):
    return jnp.einsum("rd,ed->re", left, right, preferred_element_type=jnp.float32)


def select_rows(array, stride):
    return array.reshape((array.shape[0] // stride, stride) + array.shape[1:])[:, 0]


def normalize(incoming, gain_vec, shift_vec):
    center = incoming - jnp.mean(incoming, axis=-1, keepdims=True)
    inv_std = lax.rsqrt(jnp.mean(center * center, axis=-1, keepdims=True) + epsilon)
    normed = center * inv_std
    return (normed * gain_vec + shift_vec, normed, inv_std)


def normalize_back(grad_in, normed, inv_std, gain_vec):
    scaled = grad_in * gain_vec
    return inv_std * (
        scaled
        - jnp.mean(scaled, axis=-1, keepdims=True)
        - normed * jnp.mean(scaled * normed, axis=-1, keepdims=True)
    )


def encode(hidden_rows, seg_rows, weights, att_rows):
    (
        query_weight,
        query_bias,
        key_weight,
        value_weight,
        value_bias,
        output_weight,
        output_bias,
        first_gain,
        first_shift,
        inner_weight,
        inner_bias,
        outer_weight,
        outer_bias,
        second_gain,
        second_shift,
    ) = weights
    row_count = hidden_rows.shape[0]
    blocks = row_count // att_rows
    head_scale = HEAD_DIM ** (-0.5)
    block_shape = (blocks, att_rows, HEADS, HEAD_DIM)
    query_rows = (multiply(hidden_rows, query_weight) + query_bias).astype(jnp.bfloat16)
    key_rows = multiply(hidden_rows, key_weight).astype(jnp.bfloat16)
    value_rows = (multiply(hidden_rows, value_weight) + value_bias).astype(jnp.bfloat16)
    scores = (
        jnp.einsum(
            "bihd,bjhd->bhij",
            query_rows.reshape(block_shape),
            key_rows.reshape(block_shape),
            preferred_element_type=jnp.float32,
        )
        * head_scale
    )
    seg_blocks = seg_rows.reshape(blocks, att_rows)
    same_seg = (seg_blocks[:, :, None] == seg_blocks[:, None, :])[:, None]
    scores = jnp.where(same_seg, scores, very_low)
    row_max = jnp.max(scores, axis=-1, keepdims=True)
    raised = jnp.exp(scores - row_max)
    summed = jnp.sum(raised, axis=-1, keepdims=True)
    attn_probs = (raised / summed).astype(jnp.bfloat16)
    log_total = (row_max + jnp.log(summed))[..., 0]
    context = (
        jnp.einsum(
            "bhij,bjhd->bihd",
            attn_probs,
            value_rows.reshape(block_shape),
            preferred_element_type=jnp.float32,
        )
        .reshape(row_count, D)
        .astype(jnp.bfloat16)
    )
    attended = multiply(context, output_weight) + output_bias
    first_norm, normed_one, inv_one = normalize(
        hidden_rows.astype(jnp.float32) + attended, first_gain, first_shift
    )
    first_low = first_norm.astype(jnp.bfloat16)
    inner_pre = multiply(first_low, inner_weight) + inner_bias
    activated = jax.nn.gelu(inner_pre, approximate=False).astype(jnp.bfloat16)
    outer_out = multiply(activated, outer_weight) + outer_bias
    block_out, normed_two, inv_two = normalize(first_norm + outer_out, second_gain, second_shift)
    log_cand = log_total.reshape(blocks, HEADS, att_rows // QLEN, QLEN)[..., 0]
    kept = (
        key_rows,
        value_rows,
        select_rows(query_rows, QLEN),
        log_cand,
        select_rows(context, QLEN),
        select_rows(normed_one, QLEN),
        select_rows(inv_one, QLEN),
        select_rows(first_low, QLEN),
        select_rows(inner_pre, QLEN),
        select_rows(activated, QLEN),
        select_rows(normed_two, QLEN),
        select_rows(inv_two, QLEN),
    )
    return (block_out, kept)


def encode_back(grad_out, hidden_rows, seg_rows, weights, kept, att_rows):
    (
        query_weight,
        query_bias,
        key_weight,
        value_weight,
        value_bias,
        output_weight,
        output_bias,
        first_gain,
        first_shift,
        inner_weight,
        inner_bias,
        outer_weight,
        outer_bias,
        second_gain,
        second_shift,
    ) = weights
    (
        key_rows,
        value_rows,
        query_cand,
        log_cand,
        context_cand,
        normed_one,
        inv_one,
        first_cand,
        inner_cand,
        active_cand,
        normed_two,
        inv_two,
    ) = kept
    row_count = hidden_rows.shape[0]
    blocks = row_count // att_rows
    cand_rows = row_count // QLEN
    per_block = att_rows // QLEN
    head_scale = HEAD_DIM ** (-0.5)
    hidden_cand = select_rows(hidden_rows, QLEN)
    second_gain_grad = jnp.sum(grad_out * normed_two, axis=0)
    second_shift_grad = jnp.sum(grad_out, axis=0)
    d_second = normalize_back(grad_out, normed_two, inv_two, second_gain)
    d_outer = d_second.astype(jnp.bfloat16)
    outer_weight_grad = left_product(active_cand, d_outer)
    outer_bias_grad = jnp.sum(d_outer.astype(jnp.float32), axis=0)
    d_active = right_product(d_outer, outer_weight)
    gelu_pull = jax.vjp(functools.partial(jax.nn.gelu, approximate=False), inner_cand)[1]
    d_inner = gelu_pull(d_active)[0].astype(jnp.bfloat16)
    inner_weight_grad = left_product(first_cand, d_inner)
    inner_bias_grad = jnp.sum(d_inner.astype(jnp.float32), axis=0)
    d_first = d_second + right_product(d_inner, inner_weight)
    first_gain_grad = jnp.sum(d_first * normed_one, axis=0)
    first_shift_grad = jnp.sum(d_first, axis=0)
    d_attend = normalize_back(d_first, normed_one, inv_one, first_gain)
    d_attend_low = d_attend.astype(jnp.bfloat16)
    output_weight_grad = left_product(context_cand, d_attend_low)
    output_bias_grad = jnp.sum(d_attend_low.astype(jnp.float32), axis=0)
    cand_shape = (blocks, per_block, HEADS, HEAD_DIM)
    block_shape = (blocks, att_rows, HEADS, HEAD_DIM)
    d_context = right_product(d_attend_low, output_weight).astype(jnp.bfloat16).reshape(cand_shape)
    query_heads = query_cand.reshape(cand_shape)
    key_heads = key_rows.reshape(block_shape)
    value_heads = value_rows.reshape(block_shape)
    scores = (
        jnp.einsum("bihd,bjhd->bhij", query_heads, key_heads, preferred_element_type=jnp.float32)
        * head_scale
    )
    seg_blocks = seg_rows.reshape(blocks, att_rows)
    seg_cand = seg_blocks.reshape(blocks, per_block, QLEN)[..., 0]
    same_seg = (seg_cand[:, :, None] == seg_blocks[:, None, :])[:, None]
    attn_probs = jnp.where(same_seg, jnp.exp(scores - log_cand[..., None]), 0.0)
    d_probs = jnp.einsum(
        "bihd,bjhd->bhij", d_context, value_heads, preferred_element_type=jnp.float32
    )
    d_scores = (
        attn_probs * (d_probs - jnp.sum(attn_probs * d_probs, axis=-1, keepdims=True))
    ).astype(jnp.bfloat16)
    d_query = (
        (
            jnp.einsum("bhij,bjhd->bihd", d_scores, key_heads, preferred_element_type=jnp.float32)
            * head_scale
        )
        .reshape(cand_rows, D)
        .astype(jnp.bfloat16)
    )
    d_keys = (
        (
            jnp.einsum("bhij,bihd->bjhd", d_scores, query_heads, preferred_element_type=jnp.float32)
            * head_scale
        )
        .reshape(row_count, D)
        .astype(jnp.bfloat16)
    )
    d_values = (
        jnp.einsum(
            "bhij,bihd->bjhd",
            attn_probs.astype(jnp.bfloat16),
            d_context,
            preferred_element_type=jnp.float32,
        )
        .reshape(row_count, D)
        .astype(jnp.bfloat16)
    )
    query_weight_grad = left_product(hidden_cand, d_query)
    query_bias_grad = jnp.sum(d_query.astype(jnp.float32), axis=0)
    key_weight_grad = left_product(hidden_rows, d_keys)
    value_weight_grad = left_product(hidden_rows, d_values)
    value_bias_grad = jnp.sum(d_values.astype(jnp.float32), axis=0)
    d_hidden = right_product(d_keys, key_weight) + right_product(d_values, value_weight)
    d_cand = right_product(d_query, query_weight) + d_attend
    d_hidden = d_hidden.reshape(cand_rows, QLEN, D)
    d_hidden = jnp.concatenate(
        [d_hidden[:, :1] + d_cand[:, None], d_hidden[:, 1:]], axis=1
    ).reshape(row_count, D)
    gradients = (
        query_weight_grad,
        query_bias_grad,
        key_weight_grad,
        value_weight_grad,
        value_bias_grad,
        output_weight_grad,
        output_bias_grad,
        first_gain_grad,
        first_shift_grad,
        inner_weight_grad,
        inner_bias_grad,
        outer_weight_grad,
        outer_bias_grad,
        second_gain_grad,
        second_shift_grad,
    )
    return (d_hidden, gradients)


def general_body(
    hidden,
    query_weight,
    query_bias,
    key_weight,
    value_weight,
    value_bias,
    output_weight,
    output_bias,
    first_gain,
    first_shift,
    inner_weight,
    inner_bias,
    outer_weight,
    outer_bias,
    second_gain,
    second_shift,
    segment,
    positive,
    negative,
    bins,
    margins,
    clusters,
):
    weights = (
        query_weight,
        query_bias,
        key_weight,
        value_weight,
        value_bias,
        output_weight,
        output_bias,
        first_gain,
        first_shift,
        inner_weight,
        inner_bias,
        outer_weight,
        outer_bias,
        second_gain,
        second_shift,
    )
    micro_count = hidden.shape[0]
    row_count = hidden.shape[2]
    att_rows = min(512, row_count)
    cand_rows = row_count // QLEN
    slot_stride = PSLOT // QLEN
    emb_scale = D ** (-0.5)
    query_flag = jnp.where(lax.axis_index("role") == 0, 1.0, 0.0).astype(jnp.float32)
    first_query = lax.axis_index("batch") * cand_rows
    bin_ids = bins[..., 0]
    query_total = bin_ids.shape[0] * bin_ids.shape[1]
    bin_slots = jnp.arange(NBINS, dtype=jnp.int32)
    bin_counts = jnp.sum((bin_ids[..., None] == bin_slots).astype(jnp.float32), axis=(0, 1))
    bin_table = query_total / (NBINS * bin_counts)
    loss_accum = jnp.zeros((), jnp.float32)
    accum = None
    layer_list = []
    grad_list = []
    for micro_idx in range(micro_count):
        hidden_rows = hidden[micro_idx, 0]
        seg_rows = segment[micro_idx, 0]
        block_out, kept = encode(hidden_rows, seg_rows, weights, att_rows)
        layer_list.append(block_out.astype(jnp.bfloat16))
        cls_rows = select_rows(block_out, QLEN).astype(jnp.bfloat16)
        passage_cls = cls_rows.reshape(-1, slot_stride, D)[:, 0]
        gathered = lax.all_gather(passage_cls, ("role", "batch"), axis=0, tiled=True)
        offset = lax.axis_size("batch") * passage_cls.shape[0]
        passages = gathered[offset:]
        scores = right_product(cls_rows, passages) * emb_scale
        columns = jnp.arange(passages.shape[0], dtype=jnp.int32)
        pos_ids = lax.dynamic_slice_in_dim(positive[micro_idx], first_query, cand_rows)
        neg_ids = lax.dynamic_slice_in_dim(negative[micro_idx], first_query, cand_rows)
        bin_mine = lax.dynamic_slice_in_dim(bin_ids[micro_idx], first_query, cand_rows)
        margin_mine = lax.dynamic_slice_in_dim(margins[micro_idx], first_query, cand_rows)
        pos_hit = pos_ids[:, None] == columns
        neg_hit = neg_ids[:, None] == columns
        cluster_row = clusters[micro_idx]
        pos_cluster = jnp.sum(jnp.where(pos_hit, cluster_row[None, :], 0), axis=-1)
        allowed = cluster_row[None, :] == pos_cluster[:, None]
        masked = jnp.where(allowed, scores, very_low)
        row_max = jnp.max(masked, axis=-1, keepdims=True)
        raised = jnp.exp(masked - row_max)
        summed = jnp.sum(raised, axis=-1, keepdims=True)
        softened = raised / summed
        log_total = (row_max + jnp.log(summed))[:, 0]
        pos_score = jnp.sum(jnp.where(pos_hit, scores, 0.0), axis=-1)
        neg_score = jnp.sum(jnp.where(neg_hit, scores, 0.0), axis=-1)
        weight_query = jnp.sum(jnp.where(bin_mine[:, None] == bin_slots, bin_table, 0.0), axis=-1)
        margin_gap = pos_score - neg_score - margin_mine
        loss_accum = loss_accum + query_flag * jnp.sum(
            log_total - pos_score + weight_query * margin_gap * margin_gap
        )
        pos_float = pos_hit.astype(jnp.float32)
        neg_float = neg_hit.astype(jnp.float32)
        d_scores = query_flag * (
            softened
            - pos_float
            + (2.0 * weight_query * margin_gap)[:, None] * (pos_float - neg_float)
        )
        passages_wide = passages.astype(jnp.float32)
        cls_wide = cls_rows.astype(jnp.float32)
        d_cls = (
            jnp.dot(d_scores, passages_wide, precision=highest, preferred_element_type=jnp.float32)
            * emb_scale
        )
        padded = jnp.concatenate([jnp.zeros((cand_rows, offset), jnp.float32), d_scores], axis=1)
        received = lax.psum_scatter(
            jnp.einsum(
                "qp,qd->pd", padded, cls_wide, precision=highest, preferred_element_type=jnp.float32
            )
            * emb_scale,
            ("role", "batch"),
            scatter_dimension=0,
            tiled=True,
        )
        spread = jnp.concatenate(
            [received[:, None], jnp.zeros((received.shape[0], slot_stride - 1, D), jnp.float32)],
            axis=1,
        ).reshape(cand_rows, D)
        d_hidden, micro_grads = encode_back(
            d_cls + spread, hidden_rows, seg_rows, weights, kept, att_rows
        )
        grad_list.append(d_hidden)
        accum = micro_grads if accum is None else jax.tree.map(jnp.add, accum, micro_grads)
    shards = (
        lax.psum_scatter(accum[0], "batch", scatter_dimension=0, tiled=True),
        lax.psum_scatter(accum[1], "batch", scatter_dimension=0, tiled=True),
        lax.psum_scatter(accum[2], "batch", scatter_dimension=0, tiled=True),
        lax.psum_scatter(accum[3], "batch", scatter_dimension=0, tiled=True),
        lax.psum_scatter(accum[4], "batch", scatter_dimension=0, tiled=True),
        lax.psum_scatter(accum[5], "batch", scatter_dimension=0, tiled=True),
        lax.psum_scatter(accum[6], "batch", scatter_dimension=0, tiled=True),
        lax.psum_scatter(accum[7], "batch", scatter_dimension=0, tiled=True),
        lax.psum_scatter(accum[8], "batch", scatter_dimension=0, tiled=True),
        lax.psum_scatter(accum[9], "batch", scatter_dimension=0, tiled=True),
        lax.psum_scatter(accum[10], "batch", scatter_dimension=0, tiled=True),
        lax.psum_scatter(accum[11], "batch", scatter_dimension=0, tiled=True),
        lax.psum_scatter(accum[12], "batch", scatter_dimension=0, tiled=True),
        lax.psum_scatter(accum[13], "batch", scatter_dimension=0, tiled=True),
        lax.psum_scatter(accum[14], "batch", scatter_dimension=0, tiled=True),
    )
    summed_grads = lax.psum(
        (
            shards[0],
            shards[1],
            shards[2],
            shards[3],
            shards[4],
            shards[5],
            shards[6],
            shards[7],
            shards[8],
            shards[9],
            shards[10],
            shards[11],
            shards[12],
            shards[13],
            shards[14],
        ),
        "role",
    )
    loss_value = lax.psum(loss_accum, ("role", "batch")) / query_total
    layer_out = jnp.stack(layer_list)[:, None]
    in_grad = jnp.stack(grad_list)[:, None]
    return (
        layer_out,
        loss_value,
        in_grad,
        summed_grads[0],
        summed_grads[1],
        summed_grads[2],
        summed_grads[3],
        summed_grads[4],
        summed_grads[5],
        summed_grads[6],
        summed_grads[7],
        summed_grads[8],
        summed_grads[9],
        summed_grads[10],
        summed_grads[11],
        summed_grads[12],
        summed_grads[13],
        summed_grads[14],
    )


def solution(mesh):
    roles, batches = mesh.shape["role"], mesh.shape["batch"]
    small = batches <= 8
    step = functools.partial(body, roles, batches) if small else general_body
    placed = (
        P(None, "role", "batch", None),
        P(),
        P(),
        P(),
        P(),
        P(),
        P(),
        P(),
        P(),
        P(),
        P(),
        P(),
        P(),
        P(),
        P(),
        P(),
        P(None, "role", "batch"),
        P(),
        P(),
        P(),
        P(),
        P(),
    )
    return jax.shard_map(
        step,
        mesh=mesh,
        in_specs=placed,
        out_specs=(
            P(None, "role", "batch", None),
            P(),
            P(None, "role", "batch", None),
            P("batch", None),
            P("batch"),
            P("batch", None),
            P("batch", None),
            P("batch"),
            P("batch", None),
            P("batch"),
            P("batch"),
            P("batch"),
            P("batch", None),
            P("batch"),
            P("batch", None),
            P("batch"),
            P("batch"),
            P("batch"),
        ),
        check_vma=False,
    )
```

```python
import functools

import jax
import jax.numpy as jnp
from jax import lax
from jax.experimental import pallas as pl
from jax.experimental.pallas import tpu as pltpu
from jax.sharding import PartitionSpec as P

D = 768
HEADS = 12
HEAD_DIM = 64
QLEN = 32
PSLOT = 256
NBINS = 10

very_low = -1e30
epsilon = 1e-12
bf16 = jnp.bfloat16
f32 = jnp.float32
MESH = pl.DeviceIdType.MESH
VMEM_BYTES = 60 * 1024 * 1024


def dot(left, right):
    return jnp.dot(left, right, preferred_element_type=f32)


def dot_right(left, right):
    return lax.dot_general(left, right, (((1,), (1,)), ((), ())), preferred_element_type=f32)


def dot_left(left, right):
    return lax.dot_general(left, right, (((0,), (0,)), ((), ())), preferred_element_type=f32)


def three_parts(wide):
    high = wide.astype(bf16)
    rest = wide - high.astype(f32)
    middle = rest.astype(bf16)
    return high, middle, (rest - middle.astype(f32)).astype(bf16)


def norm_parts(incoming):
    center = incoming - jnp.mean(incoming, axis=-1, keepdims=True)
    inv_std = lax.rsqrt(jnp.mean(center * center, axis=-1, keepdims=True) + epsilon)
    return center * inv_std, inv_std


def norm_back(scaled, normed, inv_std):
    return inv_std * (
        scaled
        - jnp.mean(scaled, axis=-1, keepdims=True)
        - normed * jnp.mean(scaled * normed, axis=-1, keepdims=True)
    )


def gelu(u):
    return 0.5 * u * (1.0 + lax.erf(u * 0.7071067811865476))


def gelu_slope(u):
    return 0.5 * (1.0 + lax.erf(u * 0.7071067811865476)) + u * (
        0.3989422804014327 * jnp.exp(-0.5 * u * u)
    )


def head_mask(cands):
    rows = lax.broadcasted_iota(jnp.int32, (HEADS * cands, D), 0)
    cols = lax.broadcasted_iota(jnp.int32, (HEADS * cands, D), 1)
    return rows // cands == cols // HEAD_DIM


def per_head(rows, mask):
    return jnp.where(mask, jnp.concatenate([rows] * HEADS, axis=0), jnp.zeros((), rows.dtype))


def from_heads(wide, mask, cands):
    kept = jnp.where(mask, wide, 0.0)
    total = kept[:cands]
    for head in range(1, HEADS):
        total = total + kept[head * cands : (head + 1) * cands]
    return total


def picked_rows(cands, rows):
    return (
        lax.broadcasted_iota(jnp.int32, (cands, rows), 1)
        == lax.broadcasted_iota(jnp.int32, (cands, rows), 0) * QLEN
    )


class Moves:
    def __init__(self, pairs, sems):
        self.copies = [
            pltpu.make_async_copy(src, dst, sems.at[i]) for i, (src, dst) in enumerate(pairs)
        ]
        self.open = set()

    def start(self, *which):
        for i in which:
            self.copies[i].start()
            self.open.add(i)

    def need(self, *which):
        for i in which:
            if i in self.open:
                self.copies[i].wait()
                self.open.remove(i)

    def finish(self):
        self.need(*sorted(self.open))


def layer_steps(x_ref, seg_row, keys, values, wq, wo, wi, wu, vec, out, queries, context, need):
    need("wq")
    queries[...] = (
        (dot(x_ref[...], wq[...]) + vec[0:1, :]).astype(bf16).astype(f32) * HEAD_DIM**-0.5
    ).astype(bf16)
    rows = seg_row.shape[1]
    seg_row = seg_row.astype(f32)
    seg_col = jnp.broadcast_to(seg_row, (128, rows)).T
    lane = lax.broadcasted_iota(jnp.int32, (rows, 128), 1)
    hot = seg_col == (lane % HEAD_DIM - 1).astype(f32)
    apart = jnp.where(hot, 0.0, very_low).astype(bf16)
    member = jnp.where(hot, 1.0, 0.0).astype(bf16)
    ones = jnp.ones((rows, 128), bf16)
    low = lane < HEAD_DIM
    yield
    for pair in range(HEADS // 2):
        part = slice(pair * 128, (pair + 1) * 128)
        q, k, v = queries[:, part], keys[:, part], values[:, part]

        def one(q_ext, k_ext, v_ext):
            scores = dot_right(q_ext, k_ext)
            raised = jnp.exp(scores - jnp.max(scores, axis=-1, keepdims=True))
            return dot(raised.astype(bf16), v_ext)

        even = one(jnp.where(low, q, apart), jnp.where(low, k, member), jnp.where(low, v, ones))
        odd = one(jnp.where(low, apart, q), jnp.where(low, member, k), jnp.where(low, ones, v))
        summed = pltpu.roll(jnp.where(low, odd, even), HEAD_DIM, 1)
        context[:, part] = (jnp.where(low, even, odd) * (1.0 / summed)).astype(bf16)
        if pair % 2 == 1:
            yield
    need("wo", "wi", "wu")
    attended = dot(context[...], wo[...]) + vec[2:3, :]
    normed, _ = norm_parts(x_ref[...].astype(f32) + attended)
    first_norm = normed * vec[3:4, :] + vec[4:5, :]
    first_low = first_norm.astype(bf16)
    total = first_norm + vec[5:6, :]
    yield
    for j in range(wi.shape[1] // D):
        part = slice(j * D, (j + 1) * D)
        u = dot(first_low, wi[:, part]) + vec[8 + j : 9 + j, :]
        total = total + dot(gelu(u).astype(bf16), wu[part, :])
        if j % 2 == 1:
            yield
    normed, _ = norm_parts(total)
    out[...] = (normed * vec[6:7, :] + vec[7:8, :]).astype(bf16)


def run_beside(steps, actions):
    for at, _ in enumerate(steps):
        for action in actions.pop(at, ()):
            action()
    for at in sorted(actions):
        for action in actions[at]:
            action()


def peer_of(step, roles, batches):
    role, batch = lax.axis_index("role"), lax.axis_index("batch")
    other = lax.rem((role // 2) * batches + batch + step, (roles // 2) * batches)
    return (other // batches) * 2 + role % 2, other % batches


def greet(roles, batches):
    role, batch = lax.axis_index("role"), lax.axis_index("batch")
    count = (roles // 2) * batches
    barrier = pltpu.get_barrier_semaphore()
    for other in range(0, roles, 2):
        there = other + 1 - role % 2
        pl.semaphore_signal(barrier, inc=1, device_id=(there, batch), device_id_type=MESH)

    def signal(step, carry):
        role_to, batch_to = peer_of(step, roles, batches)
        pl.semaphore_signal(barrier, inc=1, device_id=(role_to, batch_to), device_id_type=MESH)
        return carry

    lax.fori_loop(1, count, signal, 0)
    return lambda: pl.semaphore_wait(barrier, count - 1 + roles // 2)


def remote(src, dst, out_sem, in_sem, role_to, batch_to):
    return pltpu.make_async_remote_copy(
        src_ref=src,
        dst_ref=dst,
        send_sem=out_sem,
        recv_sem=in_sem,
        device_id=(role_to, batch_to),
        device_id_type=MESH,
    )


def each(begin, end, do):
    def go(step, carry):
        do(step)
        return carry

    lax.fori_loop(begin, end, go, 0)


class Spread:
    def __init__(self, roles, batches, parts, query_ref, pass_ref, query_all, pass_all, sems):
        self.roles, self.batches, self.parts = roles, batches, parts
        self.wide = 2
        self.deep = batches // self.wide
        self.flat = (roles // 2) * self.wide
        self.query_ref, self.pass_ref = query_ref, pass_ref
        self.query_all, self.pass_all = query_all, pass_all
        (
            self.q_across, self.q_z, self.q_plane, self.q_on, self.q_in,
            self.p_z, self.p_plane, self.p_on, self.p_in, self.own,
        ) = sems
        self.role, self.batch = lax.axis_index("role"), lax.axis_index("batch")
        self.core = self.role % 2
        self.mate = self.role + 1 - 2 * self.core
        self.z, self.y = self.batch // self.wide, self.batch % self.wide

    @staticmethod
    def sems(roles, batches, parts):
        deep, flat = batches // 2, roles
        dma = pltpu.SemaphoreType.DMA
        return [
            dma((parts,)),
            dma((parts, deep)),
            dma((parts, deep, flat)),
            dma((batches, parts)),
            dma((batches, parts)),
            dma((deep,)),
            dma((deep, flat)),
            dma(((roles - 1) * batches,)),
            dma(((roles - 1) * batches,)),
            dma((parts,)),
        ]

    def along_z(self, step):
        return lax.rem(self.z + step, self.deep) * self.wide + self.y

    def in_plane(self, step):
        place = lax.rem((self.role // 2) * self.wide + self.y + step, self.flat)
        return (place // self.wide) * 2 + self.core, place % self.wide

    def query_to(self, slot, part, sem, role_to, batch_to, src=None):
        begin, size, _ = self.parts[part]
        there = self.query_all.at[slot, pl.ds(begin, size)]
        return remote(there if src is None else src, there, sem, self.q_in.at[slot, part], role_to, batch_to)

    def query_z(self, part, step):
        return self.query_to(self.batch, part, self.q_z.at[part, step], self.role, self.along_z(step))

    def query_plane(self, part, depth, step):
        role_to, y_to = self.in_plane(step)
        return self.query_to(
            self.along_z(depth), part, self.q_plane.at[part, depth, step], role_to, self.z * self.wide + y_to
        )

    def query_on(self, slot, part):
        return self.query_to(slot, part, self.q_on.at[slot, part], self.mate, self.batch)

    def across(self, part):
        return self.query_to(
            self.batch, part, self.q_across.at[part], lax.rem(self.role + 2, self.roles), self.batch
        )

    def pass_to(self, slot, sem, role_to, batch_to):
        there = self.pass_all.at[slot]
        return remote(there, there, sem, self.p_in.at[slot], role_to, batch_to)

    def pass_slot(self, role, batch):
        return (role - 1) * self.batches + batch

    def pass_z(self, step):
        mine = self.pass_slot(self.role, self.batch)
        return self.pass_to(mine, self.p_z.at[step], self.role, self.along_z(step))

    def pass_plane(self, depth, step):
        role_to, y_to = self.in_plane(step)
        slot = self.pass_slot(self.role, self.along_z(depth))
        return self.pass_to(slot, self.p_plane.at[depth, step], role_to, self.z * self.wide + y_to)

    def pass_on(self, slot):
        return self.pass_to(slot, self.p_on.at[slot], self.mate, self.batch)

    def planes(self, do):
        each(1, self.flat, do)

    def hand_query(self, part, depth):
        self.planes(lambda step: self.query_plane(part, depth, step).start())
        self.query_on(self.along_z(depth), part).start()

    def not_source(self, step, do):
        pl.when(step != self.wide)(do)

    def begin_query(self, part):
        @pl.when(self.role == 0)
        def _():
            begin, size, via = self.parts[part]
            keep = pltpu.make_async_copy(
                self.query_ref.at[pl.ds(begin, size)],
                self.query_all.at[self.batch, pl.ds(begin, size)],
                self.own.at[part],
            )
            keep.start()
            keep.wait()
            if via:
                self.across(part).start()
                self.query_on(self.batch, part).start()
            else:
                each(1, self.deep, lambda step: self.query_z(part, step).start())
                self.hand_query(part, 0)

    def second(self, part):
        @pl.when(self.role == 2)
        def _():
            self.query_on(self.batch, part).wait_recv()
            each(1, self.deep, lambda step: self.query_z(part, step).start())
            self.planes(
                lambda step: self.not_source(step, lambda: self.query_plane(part, 0, step).start())
            )
            self.query_on(self.batch, part).start()

    def begin_pass(self):
        @pl.when(self.role > 0)
        def _():
            mine = self.pass_slot(self.role, self.batch)
            keep = pltpu.make_async_copy(self.pass_ref, self.pass_all.at[mine], self.own.at[0])
            keep.start()
            keep.wait()
            each(1, self.deep, lambda step: self.pass_z(step).start())
            self.planes(lambda step: self.pass_plane(0, step).start())
            self.pass_on(mine).start()

    def carrier(self, part):
        return 2 if self.parts[part][2] else 0

    def relay_query(self, *parts):
        for part in parts:

            @pl.when(self.role == self.carrier(part))
            def _():
                def go(depth):
                    self.query_on(self.along_z(depth), part).wait_recv()
                    self.hand_query(part, depth)

                each(1, self.deep, go)

    def relay_pass(self):
        @pl.when(self.role > 0)
        def _():
            def go(depth):
                slot = self.pass_slot(self.role, self.along_z(depth))
                self.pass_on(slot).wait_recv()
                self.planes(lambda step: self.pass_plane(depth, step).start())
                self.pass_on(slot).start()

            each(1, self.deep, go)

    def from_plane(self, part, do):
        via = self.parts[part][2]

        @pl.when(self.core == 0)
        def _():
            def go(slot):
                mine = jnp.logical_and(self.role == self.carrier(part), slot % self.wide == self.y)
                if via:
                    mine = jnp.logical_or(
                        mine, jnp.logical_and(self.role == 0, slot == self.batch)
                    )
                pl.when(jnp.logical_not(mine))(lambda: do(slot))

            each(0, self.batches, go)

    def pass_from_plane(self, do):
        def plane(step):
            role_of, y_of = self.in_plane(step)

            def go(depth):
                do(self.pass_slot(role_of, depth * self.wide + y_of))

            pl.when(role_of > 0)(lambda: each(0, self.deep, go))

        self.planes(plane)

    def share_query(self, *parts):
        for part in parts:

            def go(slot):
                self.query_on(slot, part).wait_recv()
                self.query_on(slot, part).start()

            self.from_plane(part, go)

    def share_pass(self):
        def go(slot):
            self.pass_on(slot).wait_recv()
            self.pass_on(slot).start()

        self.pass_from_plane(go)

    def take(self):
        @pl.when(self.core == 1)
        def _():
            def go(slot):
                for part in range(len(self.parts)):
                    self.query_on(slot, part).wait_recv()

            each(0, self.batches, go)

        for other in range(0, self.roles, 2):
            role_of = other + 1 - self.core

            def go(batch):
                self.pass_on(self.pass_slot(role_of, batch)).wait_recv()

            pl.when(role_of > 0)(lambda: each(0, self.batches, go))

    def end(self):
        def query_sent(part):
            via = self.parts[part][2]

            @pl.when(self.role == self.carrier(part))
            def _():
                each(1, self.deep, lambda step: self.query_z(part, step).wait_send())

                def go(depth):
                    def plane(step):
                        done = self.query_plane(part, depth, step).wait_send
                        if via:
                            pl.when(jnp.logical_or(depth > 0, step != self.wide))(lambda: done())
                        else:
                            done()

                    self.planes(plane)

                each(0, self.deep, go)

            if via:
                pl.when(self.role == 0)(lambda: self.across(part).wait_send())

            @pl.when(self.core == 0)
            def _():
                each(0, self.batches, lambda slot: self.query_on(slot, part).wait_send())

        for part in range(len(self.parts)):
            query_sent(part)

        @pl.when(self.role > 0)
        def _():
            each(1, self.deep, lambda step: self.pass_z(step).wait_send())

            def go(depth):
                self.planes(lambda step: self.pass_plane(depth, step).wait_send())
                self.pass_on(self.pass_slot(self.role, self.along_z(depth))).wait_send()

            each(0, self.deep, go)

        self.pass_from_plane(lambda slot: self.pass_on(slot).wait_send())


def first_kernel(
    roles, batches, micros, rows, early,
    seg, hid_far, wq_far, wk_far, wv_far, wo_far, wi_far, wu_far, *refs,
):
    lines, refs = refs[:9], refs[9:]
    keys_far, values_far, probs_far, query_far, pass_far, layer_far, query_c, vec = refs[:8]
    hid, wq, wk, wv, wo, wi, wu, keys, values, probs, out, queries, context = refs[8:21]
    query_msg, pass_msg, query_all, pass_all, in_sems, out_sems = refs[21:27]
    sems = refs[27:]
    cands = rows // QLEN
    total = micros * cands
    names = ["hid", "wq", "wk", "wv", "wo", "wi", "wu"]
    far = (hid_far, wq_far, wk_far, wv_far, wo_far, wi_far, wu_far)
    moves = Moves(list(zip(far, (hid, wq, wk, wv, wo, wi, wu))), in_sems)
    moves.start(0, 2, 3, 1, 4, 5, 6)

    def need(*which):
        moves.need(*[names.index(name) for name in which])

    blocks = [pl.ds(m * rows, rows) for m in range(micros)]
    stores = Moves(
        [(keys, keys_far), (values, values_far), (probs, probs_far), (query_all, query_far), (pass_all, pass_far)]
        + [(out.at[blocks[m]], layer_far.at[blocks[m]]) for m in range(early)],
        out_sems,
    )
    greeted = greet(roles, batches)
    parts = [(0, total // 2, False), (total // 2, total // 2, True)]
    parts += [(total + m * cands, cands, m % 2 == 1) for m in range(micros)]
    spread = Spread(roles, batches, parts, query_msg, pass_msg, query_all, pass_all, sems)

    at = 0
    for line in lines:
        wide = line[...].astype(f32).reshape(1, -1)
        for j in range(wide.shape[1] // D):
            vec[at : at + 1, :] = wide[:, j * D : (j + 1) * D]
            at += 1
    mask = head_mask(cands)
    pick = picked_rows(cands, rows)
    pick_low = pick.astype(f32).astype(bf16)
    need("hid")
    x_cand = jnp.concatenate(
        [dot(pick_low, hid[blocks[m], :]).astype(bf16) for m in range(micros)], axis=0
    )
    query_msg[0:total, :] = x_cand
    need("wk", "wv", "wq")
    q_cand = (
        (dot(x_cand, wq[...]) + vec[0:1, :]).astype(bf16).astype(f32) * HEAD_DIM**-0.5
    ).astype(bf16)
    query_c[...] = q_cand
    for m in range(micros):
        block = blocks[m]
        x = hid[block, :]
        k = dot(x, wk[...]).astype(bf16)
        v = (dot(x, wv[...]) + vec[1:2, :]).astype(bf16)
        keys[block, :] = k
        values[block, :] = v
        seg_row = seg[m].astype(f32)
        seg_col = jnp.sum(jnp.where(pick, seg_row, 0.0), axis=-1, keepdims=True)
        bias = jnp.where(seg_col == seg_row, 0.0, very_low)
        q_wide = per_head(q_cand[m * cands : (m + 1) * cands], mask)
        scores = dot_right(q_wide, k) + jnp.concatenate([bias] * HEADS, axis=0)
        raised = jnp.exp(scores - jnp.max(scores, axis=-1, keepdims=True))
        prob = raised * (1.0 / jnp.sum(raised, axis=-1, keepdims=True))
        probs[m * HEADS * cands : (m + 1) * HEADS * cands, :] = prob
        attended = from_heads(dot(prob.astype(bf16), v), mask, cands)
        query_msg[total + m * cands : total + (m + 1) * cands, :] = attended.astype(bf16)
        if m == 0:
            greeted()
            spread.begin_query(1)
            spread.begin_query(0)
        spread.begin_query(2 + m)
        if m % 2 == 0:
            spread.second(1 + m)
    wide = query_msg[...].astype(f32)
    per_slot = PSLOT // QLEN
    chosen = []
    for part in range(2):
        for m in range(micros):
            for slot in range(cands // per_slot):
                at = (part * micros + m) * cands + slot * per_slot
                chosen.append(wide[at : at + 1])
    pass_msg[...] = jnp.concatenate(chosen, axis=0).astype(bf16)
    spread.begin_pass()
    stores.start(0, 1, 2)

    def steps():
        for m in range(early):
            yield from layer_steps(
                hid.at[blocks[m]], seg[m], keys.at[blocks[m]], values.at[blocks[m]],
                wq, wo, wi, wu, vec, out.at[blocks[m]], queries, context, need,
            )
            stores.start(5 + m)
            yield

    run_beside(steps(), first_plan(spread, len(parts)))
    spread.take()
    stores.start(3, 4)
    spread.end()
    stores.finish()


def first_plan(spread, parts):
    every = range(parts)
    return {
        0: [
            lambda: spread.second(parts - 1),
            lambda: spread.relay_query(*every[:-1]),
            spread.relay_pass,
        ],
        2: [lambda: spread.relay_query(parts - 1)],
        6: [lambda: spread.share_query(*every[:-1])],
        10: [lambda: spread.share_query(parts - 1), spread.share_pass],
    }


def first_stage(hid, seg, weights, lines, micros, early, roles, batches):
    rows = hid.shape[0] // micros
    cands = rows // QLEN
    total = micros * cands
    passes = micros * (rows // PSLOT)
    vmem = pl.BlockSpec(memory_space=pltpu.VMEM)
    far = pl.BlockSpec(memory_space=pl.ANY)
    query_all = (batches, 2 * total, D)
    pass_all = ((roles - 1) * batches, 2 * passes, D)
    probs = (micros * HEADS * cands, rows)
    held = pltpu.VMEM(hid.shape, bf16)
    return pl.pallas_call(
        functools.partial(first_kernel, roles, batches, micros, rows, early),
        in_specs=[vmem] + [far] * 7 + [vmem] * len(lines),
        out_specs=(far,) * 6 + (vmem,) * 2,
        out_shape=(
            jax.ShapeDtypeStruct(hid.shape, bf16),
            jax.ShapeDtypeStruct(hid.shape, bf16),
            jax.ShapeDtypeStruct(probs, f32),
            jax.ShapeDtypeStruct(query_all, bf16),
            jax.ShapeDtypeStruct(pass_all, bf16),
            jax.ShapeDtypeStruct((early * rows, D), bf16),
            jax.ShapeDtypeStruct((total, D), bf16),
            jax.ShapeDtypeStruct((sum(line.size for line in lines) // D, D), f32),
        ),
        scratch_shapes=[held]
        + [pltpu.VMEM(w.shape, bf16) for w in weights]
        + [held, held, pltpu.VMEM(probs, f32), pltpu.VMEM((early * rows, D), bf16)]
        + [pltpu.VMEM((rows, D), bf16)] * 2
        + [
            pltpu.VMEM((2 * total, D), bf16),
            pltpu.VMEM((2 * passes, D), bf16),
            pltpu.VMEM(query_all, bf16),
            pltpu.VMEM(pass_all, bf16),
            pltpu.SemaphoreType.DMA((7,)),
            pltpu.SemaphoreType.DMA((5 + early,)),
        ]
        + Spread.sems(roles, batches, 2 + micros),
        compiler_params=pltpu.CompilerParams(
            collective_id=1, has_side_effects=True, vmem_limit_bytes=VMEM_BYTES
        ),
        name="first",
    )(seg, hid, *weights, *lines)


def middle_kernel(
    micros,
    cands,
    columns,
    query_all,
    pass_all,
    wo_far,
    wi_far,
    wu_far,
    layer_early,
    vec,
    positive,
    negative,
    bins,
    margins,
    clusters,
    loss_out,
    inner_grad,
    outer_grad,
    output_grad,
    value_bias,
    output_bias,
    first_gain,
    first_shift,
    inner_bias,
    outer_bias,
    second_gain,
    second_shift,
    x_slice,
    d_own,
    layer_far,
    wo,
    wi,
    wu,
    early,
    sems,
    vectors,
    inner_row,
    x_all,
    c_all,
    u_all,
    g_all,
    n_one,
    d_rows,
):
    role, batch = lax.axis_index("role"), lax.axis_index("batch")
    batches = query_all.shape[0]
    own_rows = micros * cands
    n_query = batches * own_rows
    n_dev = pass_all.shape[0]
    per_dev = pass_all.shape[1] // 2
    per_micro = per_dev // micros
    n_pass = n_dev * per_dev
    n_rows = n_query + n_pass
    inner = wi.shape[1]
    chunks = [slice(j * D, (j + 1) * D) for j in range(inner // D)]

    moves = Moves(
        [
            (wo_far, wo),
            (wi_far, wi),
            (wu_far, wu),
            (layer_early, early),
            (early, layer_far.at[pl.ds(0, early.shape[0])]),
        ],
        sems,
    )
    moves.start(0, 1, 2, 3)
    for b in range(batches):
        x_all[b * own_rows : (b + 1) * own_rows, :] = query_all[b, 0:own_rows, :]
        c_all[b * own_rows : (b + 1) * own_rows, :] = query_all[b, own_rows : 2 * own_rows, :]
    wide = pass_all[...].astype(f32)
    x_all[n_query:n_rows, :] = wide[:, 0:per_dev, :].reshape(n_pass, D).astype(bf16)
    c_all[n_query:n_rows, :] = wide[:, per_dev:, :].reshape(n_pass, D).astype(bf16)

    moves.need(0)
    attended = dot(c_all[...], wo[...]) + vec[2:3, :]
    normed, inv_one = norm_parts(x_all[...].astype(f32) + attended)
    n_one[...] = normed
    first_norm = normed * vec[3:4, :] + vec[4:5, :]
    first_low = first_norm.astype(bf16)
    total = first_norm + vec[5:6, :]
    moves.need(1, 2, 3)
    moves.start(4)
    for j, part in enumerate(chunks):
        u = dot(first_low, wi[:, part]) + vec[8 + j : 9 + j, :]
        u_all[:, part] = u
        g = gelu(u).astype(bf16)
        g_all[:, part] = g
        total = total + dot(g, wu[part, :])
    n_two, inv_two = norm_parts(total)
    low = (n_two * vec[6:7, :] + vec[7:8, :]).astype(bf16)
    q_low, p_low = low[:n_query], low[n_query:]

    bin_ids = bins[...]
    queries_total = bin_ids.shape[0] * bin_ids.shape[1]
    weight = jnp.zeros(bin_ids.shape, f32)
    for k in range(NBINS):
        hit = (bin_ids == k).astype(f32)
        amount = jnp.sum(jnp.sum(hit, axis=1, keepdims=True), axis=0, keepdims=True)
        weight = weight + hit * (queries_total / (NBINS * jnp.maximum(amount, 1.0)))

    lane = lax.broadcasted_iota(jnp.int32, (n_query, bin_ids.shape[1]), 1)
    row = lax.broadcasted_iota(jnp.int32, (n_query, bin_ids.shape[1]), 0)
    here = lane == (row // own_rows) * cands + row % cands

    def by_micro(table):
        parts = [
            jnp.broadcast_to(table[m : m + 1, :], (cands, table.shape[1])) for m in range(micros)
        ]
        return jnp.concatenate(parts * batches, axis=0)

    def per_query(table):
        return jnp.sum(jnp.where(here, by_micro(table), 0.0), axis=-1, keepdims=True)

    pos = per_query(positive[...].astype(f32))
    neg = per_query(negative[...].astype(f32))
    margin = per_query(margins[...])
    weight = per_query(weight)

    col = lax.broadcasted_iota(jnp.int32, (n_query, n_pass), 1)
    row = lax.broadcasted_iota(jnp.int32, (n_query, n_pass), 0)
    same = (col % per_dev) // per_micro == (row % own_rows) // cands
    ident = ((col // per_dev) * per_micro + col % per_micro).astype(f32)
    n_ids = n_dev * per_micro
    tab_row = lax.broadcasted_iota(jnp.int32, (n_ids, n_pass), 0)
    tab_col = lax.broadcasted_iota(jnp.int32, (n_ids, n_pass), 1)
    table = tab_row == (tab_col // per_dev) * per_micro + tab_col % per_micro
    cluster = by_micro(dot(clusters[...].astype(f32).astype(bf16), table.astype(f32).astype(bf16)))
    pos_hit = jnp.logical_and(same, ident == pos)
    neg_hit = jnp.logical_and(same, ident == neg)
    pos_cluster = jnp.sum(jnp.where(pos_hit, cluster, 0.0), axis=-1, keepdims=True)
    allowed = jnp.logical_and(same, cluster == pos_cluster)
    scores = dot_right(q_low, p_low) * D**-0.5
    masked = jnp.where(allowed, scores, very_low)
    row_max = jnp.max(masked, axis=-1, keepdims=True)
    raised = jnp.exp(masked - row_max)
    summed = jnp.sum(raised, axis=-1, keepdims=True)
    pos_score = jnp.sum(jnp.where(pos_hit, scores, 0.0), axis=-1, keepdims=True)
    neg_score = jnp.sum(jnp.where(neg_hit, scores, 0.0), axis=-1, keepdims=True)
    gap = pos_score - neg_score - margin
    terms = row_max + jnp.log(summed) - pos_score + weight * gap * gap
    loss_out[...] = jnp.broadcast_to(
        jnp.sum(terms, axis=0, keepdims=True) / queries_total, loss_out.shape
    )
    pull = 2.0 * weight * gap
    pos_one, neg_one = pos_hit.astype(f32), neg_hit.astype(f32)
    d_scores = (raised * (1.0 / summed) - pos_one + pull * (pos_one - neg_one)) * D**-0.5
    parts = three_parts(d_scores)
    d_query = sum(dot(part, p_low) for part in parts)
    d_pass = sum(dot_left(part, q_low) for part in parts)
    grad = jnp.concatenate([d_query, d_pass], axis=0)

    def total_of(array):
        return jnp.sum(array, axis=0, keepdims=True)

    vectors[6:7, :] = total_of(grad * n_two)
    vectors[7:8, :] = total_of(grad)
    d_two = norm_back(grad * vec[6:7, :], n_two, inv_two)
    d_outer = d_two.astype(bf16)
    vectors[5:6, :] = total_of(d_outer.astype(f32))
    select = (
        lax.broadcasted_iota(jnp.int32, (D, 128), 0)
        == lax.broadcasted_iota(jnp.int32, (D, 128), 1) + batch * columns
    )
    select = jnp.logical_and(select, lax.broadcasted_iota(jnp.int32, (D, 128), 1) < columns)
    select = select.astype(f32).astype(bf16)
    first_low = (n_one[...] * vec[3:4, :] + vec[4:5, :]).astype(bf16)
    y_slice = dot(first_low, select).astype(bf16)
    d_first = d_two
    for j, part in enumerate(chunks):
        d_inner = (dot_right(d_outer, wu[part, :]) * gelu_slope(u_all[:, part])).astype(bf16)
        inner_row[:, part] = total_of(d_inner.astype(f32))
        inner_grad[:, part] = dot_left(y_slice, d_inner)[:columns]
        d_first = d_first + dot_right(d_inner, wi[:, part])
    span = inner // batches
    outer_grad[...] = dot_left(g_all[:, pl.ds(pl.multiple_of(batch * span, 128), span)], d_outer)
    vectors[3:4, :] = total_of(d_first * n_one[...])
    vectors[4:5, :] = total_of(d_first)
    d_one = norm_back(d_first * vec[3:4, :], n_one[...], inv_one)
    d_rows[...] = d_one
    d_low = d_one.astype(bf16)
    bias_row = total_of(d_low.astype(f32))
    vectors[2:3, :] = bias_row
    vectors[1:2, :] = sum(dot_right(part, wo[...]) for part in three_parts(bias_row))
    vectors[0:1, :] = jnp.zeros_like(bias_row)
    c_slice = dot(c_all[...], select).astype(bf16)
    output_grad[...] = dot_left(c_slice, d_low)[:columns]
    x_slice[...] = dot(x_all[...], select).astype(bf16)
    mine = sum(dot(part, select) for part in three_parts(vectors[...]))
    outs = [value_bias, output_bias, first_gain, first_shift, outer_bias, second_gain, second_shift]
    for row, out in enumerate(outs):
        out[...] = mine[row + 1, :columns]
    inner_bias[...] = inner_row[0, pl.ds(pl.multiple_of(batch * span, 128), span)]

    moves.finish()

    @pl.when(role == 0)
    def _():
        d_own[...] = d_rows[pl.ds(pl.multiple_of(batch * own_rows, 8), own_rows), :]

    @pl.when(role > 0)
    def _():
        d_own[...] = jnp.zeros_like(d_own)
        begin = pl.multiple_of(n_query + ((role - 1) * batches + batch) * per_dev, 8)
        mine = d_rows[pl.ds(begin, per_dev), :]
        for m in range(micros):
            for slot in range(per_micro):
                at = m * cands + slot * (PSLOT // QLEN)
                d_own[at : at + 1, :] = mine[m * per_micro + slot : m * per_micro + slot + 1, :]


def middle_stage(
    query_all, pass_all, wo, wi, wu, layer_early, layer_rows, vec, positive, negative, bins, margins, clusters
):
    batches = query_all.shape[0]
    micros = positive.shape[0]
    own_rows = query_all.shape[1] // 2
    n_pass = pass_all.shape[0] * pass_all.shape[1] // 2
    n_rows = batches * own_rows + n_pass
    columns = D // batches
    inner = wi.shape[1]
    vmem = pl.BlockSpec(memory_space=pltpu.VMEM)
    far = pl.BlockSpec(memory_space=pl.ANY)
    return pl.pallas_call(
        functools.partial(middle_kernel, micros, own_rows // micros, columns),
        in_specs=[vmem] * 2 + [far] * 4 + [vmem] * 6,
        out_specs=(vmem,) * 14 + (far,),
        out_shape=(
            jax.ShapeDtypeStruct((1, 128), f32),
            jax.ShapeDtypeStruct((columns, inner), f32),
            jax.ShapeDtypeStruct((inner // batches, D), f32),
            jax.ShapeDtypeStruct((columns, D), f32),
        )
        + tuple(jax.ShapeDtypeStruct((size,), f32) for size in [columns] * 4 + [inner // batches] + [columns] * 3)
        + (
            jax.ShapeDtypeStruct((n_rows, 128), bf16),
            jax.ShapeDtypeStruct((own_rows, D), f32),
            jax.ShapeDtypeStruct((layer_rows, D), bf16),
        ),
        scratch_shapes=[pltpu.VMEM(w.shape, bf16) for w in (wo, wi, wu, layer_early)]
        + [
            pltpu.SemaphoreType.DMA((5,)),
            pltpu.VMEM((8, D), f32),
            pltpu.VMEM((1, inner), f32),
            pltpu.VMEM((n_rows, D), bf16),
            pltpu.VMEM((n_rows, D), bf16),
            pltpu.VMEM((n_rows, inner), f32),
            pltpu.VMEM((n_rows, inner), bf16),
            pltpu.VMEM((n_rows, D), f32),
            pltpu.VMEM((n_rows, D), f32),
        ],
        compiler_params=pltpu.CompilerParams(vmem_limit_bytes=VMEM_BYTES),
        name="middle",
    )(query_all, pass_all, wo, wi, wu, layer_early, vec, positive, negative, bins, margins, clusters)


def last_kernel(
    roles, batches, micros, rows, early,
    seg, vec, query_c, d_own, x_slice, hid_far, keys_far, values_far, probs_far,
    wq_far, wk_far, wv_far, wo_far, wi_far, wu_far,
    grads, query_bias, extra, both_far, back_far, layer_far,
    hid, keys, values, probs, wq, wk, wv, wo, wi, wu, out, queries, context,
    both, q_keep, c_keep, z_key, z_value, back, dq_ref, dq_pass, key_part, value_part,
    query_all, pass_all, from_mate, summed, from_x, halves, received, finals,
    in_sems, out_sems, mate_out, mate_in, x_out, x_in, part_out, part_in, last_out, last_in, *sems,
):
    role, batch = lax.axis_index("role"), lax.axis_index("batch")
    core, side = role % 2, role // 2
    mate = role + 1 - 2 * core
    across = lax.rem(role + 2, roles)
    cands = rows // QLEN
    total = micros * cands
    wide_rows = HEADS * cands
    columns = grads.shape[1]
    pieces = summed.shape[2]
    blocks = [pl.ds(m * rows, rows) for m in range(micros)]
    wides = [pl.ds(m * wide_rows, wide_rows) for m in range(micros)]
    names = ["wo", "wk", "wv", "wq", "wi", "wu"]
    pairs = [(wo_far, wo), (wk_far, wk), (wv_far, wv), (wq_far, wq), (wi_far, wi), (wu_far, wu)]
    for m in range(micros):
        names += [(m, "values"), (m, "probs"), (m, "keys"), (m, "hid")]
        pairs += [
            (values_far.at[blocks[m]], values.at[blocks[m]]),
            (probs_far.at[wides[m]], probs.at[wides[m]]),
            (keys_far.at[blocks[m]], keys.at[blocks[m]]),
            (hid_far.at[blocks[m]], hid.at[blocks[m]]),
        ]
    moves = Moves(pairs, in_sems)
    moves.start(0, *range(6, len(pairs)), 1, 2, 3, 4, 5)

    def need(*which):
        moves.need(*[names.index(name) for name in which])

    late = micros - early
    stores = Moves(
        [(out.at[blocks[m]], layer_far.at[blocks[m]]) for m in range(late)]
        + [(both, both_far), (back, back_far)],
        out_sems,
    )
    greeted = greet(roles, batches)
    spread = Spread(
        roles, batches, [(0, total // 2, False), (total // 2, total // 2, True)], dq_ref, dq_pass, query_all, pass_all, sems
    )

    mask = head_mask(cands)
    need("wo")
    d_context = dot_right(d_own[...].astype(bf16), wo[...]).astype(bf16)
    d_query = []
    for m in range(micros):
        need((m, "values"), (m, "probs"), (m, "keys"), (m, "hid"))
        cand = slice(m * cands, (m + 1) * cands)
        q_wide = per_head(query_c[cand, :], mask)
        c_wide = per_head(d_context[cand, :], mask)
        prob = probs[wides[m], :]
        pulled = prob * dot_right(c_wide, values[blocks[m], :])
        d_scores = (pulled - prob * jnp.sum(pulled, axis=-1, keepdims=True)).astype(bf16)
        pair = jnp.concatenate([d_scores, prob.astype(bf16)], axis=0)
        d_query.append(from_heads(dot(d_scores, keys[blocks[m], :]), mask, cands) * HEAD_DIM**-0.5)
        sums = dot(pair, hid[blocks[m], :])
        both[m] = pair
        z_key[wides[m], :] = sums[:wide_rows].astype(bf16)
        z_value[wides[m], :] = sums[wide_rows:].astype(bf16)
        q_keep[wides[m], :] = q_wide
        c_keep[wides[m], :] = c_wide
    d_query = jnp.concatenate(d_query, axis=0).astype(bf16)
    dq_ref[...] = d_query
    wide = d_query.astype(f32)
    per_slot = PSLOT // QLEN
    dq_pass[...] = jnp.concatenate(
        [wide[at : at + 1] for at in range(0, total, per_slot)], axis=0
    )
    split = summed.shape
    key_part[...] = dot_left(z_key[...], q_keep[...]).astype(bf16).reshape(split)
    value_part[...] = dot_left(z_value[...], c_keep[...]).astype(bf16).reshape(split)

    greeted()

    @pl.when(core == 0)
    def _():
        remote(value_part, from_mate, mate_out, mate_in, mate, batch).start()

    @pl.when(core == 1)
    def _():
        remote(key_part, from_mate, mate_out, mate_in, mate, batch).start()

    spread.begin_query(1)

    def to_x(piece):
        return remote(
            summed.at[:, 1 - side, piece], from_x.at[:, piece], x_out.at[piece], x_in.at[piece], across, batch
        )

    def begin_x():
        remote(key_part, from_mate, mate_out, mate_in, mate, batch).wait()

        @pl.when(core == 0)
        def _():
            summed[...] = (key_part[...].astype(f32) + from_mate[...].astype(f32)).astype(bf16)

        @pl.when(core == 1)
        def _():
            summed[...] = (value_part[...].astype(f32) + from_mate[...].astype(f32)).astype(bf16)

        for piece in range(pieces):
            to_x(piece).start()

    def to_batch(piece, step):
        other = lax.rem(batch + step, batches)
        return remote(
            halves.at[other, piece], received.at[batch, piece], part_out.at[other, piece],
            part_in.at[batch, piece], role, other,
        )

    def from_batch(piece, step):
        other = lax.rem(batch + step, batches)
        return remote(
            halves.at[other, piece], received.at[other, piece], part_out.at[other, piece],
            part_in.at[other, piece], role, other,
        )

    def begin_part(piece):
        to_x(piece).wait()
        halves[:, piece] = (
            summed[:, side, piece].astype(f32) + from_x[:, piece].astype(f32)
        ).astype(bf16)
        each(1, batches, lambda step: to_batch(piece, step).start())

    def to_role(step):
        other = lax.rem(role + step, roles)
        return remote(
            finals.at[role], finals.at[role], last_out.at[step], last_in.at[role], other, batch
        )

    def from_role(step):
        other = lax.rem(role + step, roles)
        return remote(
            finals.at[other], finals.at[other], last_out.at[step], last_in.at[other], other, batch
        )

    def begin_last():
        for piece in range(pieces):
            each(1, batches, lambda step: from_batch(piece, step).wait_recv())
            sum_all = halves[batch, piece].astype(f32)

            def add(step, so_far):
                return so_far + received[lax.rem(batch + step, batches), piece].astype(f32)

            finals[role, piece] = lax.fori_loop(1, batches, add, sum_all).astype(bf16)
        for step in range(1, roles):
            to_role(step).start()

    def steps():
        need("wk", "wv", "wq")
        extra[...] = dot_right(dq_ref[...], wq[...]) + d_own[...]
        q_back = dot_right(q_keep[...], wk[...]).astype(bf16)
        c_back = dot_right(c_keep[...], wv[...]).astype(bf16)
        for m in range(micros):
            at = slice(m * wide_rows, (m + 1) * wide_rows)
            back[m, :wide_rows, :] = q_back[at]
            back[m, wide_rows:, :] = c_back[at]
        stores.start(late, late + 1)
        yield
        for m in range(late):
            block = blocks[early + m]
            yield from layer_steps(
                hid.at[block], seg[early + m], keys.at[block], values.at[block],
                wq, wo, wi, wu, vec, out.at[blocks[m]], queries, context, need,
            )
            stores.start(m)
            yield

    parts = [functools.partial(begin_part, piece) for piece in range(pieces)]
    run_beside(steps(), last_plan(begin_x, spread, parts, begin_last))
    spread.take()
    count = batches * total
    all_query = query_all[...].reshape(count, D)
    all_pass = pass_all[...].reshape(-1, D)
    grads[0] = (
        dot_left(x_slice[0:count, :], all_query) + dot_left(x_slice[count:, :], all_pass.astype(bf16))
    )[:columns]
    query_bias[...] = jnp.sum(all_query.astype(f32), axis=0, keepdims=True) + jnp.sum(
        all_pass, axis=0, keepdims=True
    )
    spread.end()
    for piece in range(pieces):
        each(1, batches, lambda step: to_batch(piece, step).wait_send())
    for step in range(1, roles):
        from_role(step).wait_recv()
        to_role(step).wait_send()
    half = pieces * finals.shape[2]
    for x in range(roles // 2):
        here = slice(x * half, (x + 1) * half)
        grads[1, here, :] = finals[2 * x].astype(f32).reshape(half, D)
        grads[2, here, :] = finals[2 * x + 1].astype(f32).reshape(half, D)
    stores.finish()
    moves.finish()


def last_plan(begin_x, spread, parts, begin_last):
    return {
        0: [begin_x, lambda: spread.second(1), lambda: spread.begin_query(0), spread.begin_pass],
        3: [lambda: spread.relay_query(0, 1), spread.relay_pass],
        6: [parts[0]],
        8: [parts[1]],
        11: [parts[2]],
        12: [lambda: spread.share_query(0, 1), spread.share_pass],
        15: [begin_last],
    }


def last_stage(
    seg, vec, query_c, d_own, x_slice, hid, keys, values, probs, weights, early, roles, batches
):
    columns = D // batches
    micros, _, rows = seg.shape
    total = query_c.shape[0]
    passes = micros * (rows // PSLOT)
    wide = micros * HEADS * (rows // QLEN)
    vmem = pl.BlockSpec(memory_space=pltpu.VMEM)
    far = pl.BlockSpec(memory_space=pl.ANY)
    block = (columns, D)
    sides, tile = roles // 2, 16
    pieces = columns // sides // tile
    split = (batches, sides, pieces, tile, D)
    half = (batches, pieces, tile, D)
    dma = pltpu.SemaphoreType.DMA
    late = micros - early
    held = pltpu.VMEM(hid.shape, bf16)
    wide_rows = pltpu.VMEM((wide, D), bf16)
    both = (micros, 2 * wide // micros, rows)
    back = (micros, 2 * wide // micros, D)
    return pl.pallas_call(
        functools.partial(last_kernel, roles, batches, micros, rows, early),
        in_specs=[vmem] * 5 + [far] * 10,
        out_specs=(vmem,) * 3 + (far,) * 3,
        out_shape=(
            jax.ShapeDtypeStruct((3,) + block, f32),
            jax.ShapeDtypeStruct((1, D), f32),
            jax.ShapeDtypeStruct((total, D), f32),
            jax.ShapeDtypeStruct(both, bf16),
            jax.ShapeDtypeStruct(back, bf16),
            jax.ShapeDtypeStruct((late * rows, D), bf16),
        ),
        scratch_shapes=[held, held, held, pltpu.VMEM(probs.shape, f32)]
        + [pltpu.VMEM(w.shape, bf16) for w in weights]
        + [pltpu.VMEM((late * rows, D), bf16)]
        + [pltpu.VMEM((rows, D), bf16)] * 2
        + [
            pltpu.VMEM(both, bf16),
            wide_rows,
            wide_rows,
            wide_rows,
            wide_rows,
            pltpu.VMEM(back, bf16),
            pltpu.VMEM((total, D), bf16),
            pltpu.VMEM((passes, D), f32),
            pltpu.VMEM(split, bf16),
            pltpu.VMEM(split, bf16),
            pltpu.VMEM((batches, total, D), bf16),
            pltpu.VMEM(((roles - 1) * batches, passes, D), f32),
            pltpu.VMEM(split, bf16),
            pltpu.VMEM(split, bf16),
            pltpu.VMEM(half, bf16),
            pltpu.VMEM(half, bf16),
            pltpu.VMEM(half, bf16),
            pltpu.VMEM((roles, pieces, tile, D), bf16),
            dma((6 + 4 * micros,)),
            dma((late + 2,)),
            dma,
            dma,
            dma((pieces,)),
            dma((pieces,)),
            dma((batches, pieces)),
            dma((batches, pieces)),
            dma((roles,)),
            dma((roles,)),
        ]
        + Spread.sems(roles, batches, 2),
        compiler_params=pltpu.CompilerParams(
            collective_id=2, has_side_effects=True, vmem_limit_bytes=VMEM_BYTES
        ),
        name="last",
    )(seg, vec, query_c, d_own, x_slice, hid, keys, values, probs, *weights)


def finish_kernel(
    columns, layer_in, late, both, back, extra, grads, query_bias,
    layer_out, in_grad, query_grad, key_grad, value_grad, bias_out,
):
    del layer_in
    m = pl.program_id(0)
    layer_out[...] = late[...]

    @pl.when(m == 0)
    def _():
        query_grad[...] = grads[0]
        key_grad[...] = grads[1]
        value_grad[...] = grads[2]
        select = (
            lax.broadcasted_iota(jnp.int32, (D, 128), 0)
            == lax.broadcasted_iota(jnp.int32, (D, 128), 1) + lax.axis_index("batch") * columns
        )
        select = select.astype(f32).astype(bf16)
        mine = sum(dot(part, select) for part in three_parts(jnp.broadcast_to(query_bias[...], (8, D))))
        bias_out[...] = mine[0, :columns]

    in_grad[...] = dot_left(both[0], back[0])
    for cand in range(extra.shape[0]):
        at = slice(cand * QLEN, cand * QLEN + 1)
        in_grad[at, :] = in_grad[at, :] + extra[cand : cand + 1, :]


def finish_stage(layer, layer_late, both, back, extra, grads, query_bias):
    micros, wide, rows = both.shape
    columns = grads.shape[1]
    far = pl.BlockSpec(memory_space=pl.ANY)
    cands = rows // QLEN

    def fixed(shape):
        return pl.BlockSpec(shape, lambda m: (0,) * len(shape))

    block = (columns, D)
    piece = layer_late.shape[0] // micros
    skip = (layer.shape[0] - layer_late.shape[0]) // piece
    return pl.pallas_call(
        functools.partial(finish_kernel, columns),
        grid=(micros,),
        in_specs=[
            far,
            pl.BlockSpec((piece, D), lambda m: (m, 0)),
            pl.BlockSpec((1, wide, rows), lambda m: (m, 0, 0)),
            pl.BlockSpec((1, wide, D), lambda m: (m, 0, 0)),
            pl.BlockSpec((cands, D), lambda m: (m, 0)),
            fixed((3,) + block),
            fixed((1, D)),
        ],
        out_specs=(
            pl.BlockSpec((piece, D), lambda m: (m + skip, 0)),
            pl.BlockSpec((rows, D), lambda m: (m, 0)),
            fixed(block),
            fixed(block),
            fixed(block),
            fixed((columns,)),
        ),
        out_shape=(
            jax.ShapeDtypeStruct(layer.shape, layer.dtype),
            jax.ShapeDtypeStruct((micros * rows, D), f32),
            jax.ShapeDtypeStruct(block, f32),
            jax.ShapeDtypeStruct(block, f32),
            jax.ShapeDtypeStruct(block, f32),
            jax.ShapeDtypeStruct((columns,), f32),
        ),
        input_output_aliases={0: 0},
        compiler_params=pltpu.CompilerParams(vmem_limit_bytes=VMEM_BYTES),
        name="finish",
    )(layer, layer_late, both, back, extra, grads, query_bias)


def body(
    roles,
    batches,
    hidden,
    query_weight,
    query_bias,
    key_weight,
    value_weight,
    value_bias,
    output_weight,
    output_bias,
    first_gain,
    first_shift,
    inner_weight,
    inner_bias,
    outer_weight,
    outer_bias,
    second_gain,
    second_shift,
    segment,
    positive,
    negative,
    bins,
    margins,
    clusters,
):
    micros, rows = hidden.shape[0], hidden.shape[2]
    hid = hidden.reshape(micros * rows, D)
    lines = [
        query_bias,
        value_bias,
        output_bias,
        first_gain,
        first_shift,
        outer_bias,
        second_gain,
        second_shift,
        inner_bias,
    ]
    early = micros // 2
    weights = (query_weight, key_weight, value_weight, output_weight, inner_weight, outer_weight)
    keys, values, probs, query_all, pass_all, layer_early, query_c, vec = first_stage(
        hid, segment, weights, lines, micros, early, roles, batches
    )
    loss, inner_grad, outer_grad, output_grad, *biases, x_slice, d_own, layer = middle_stage(
        query_all,
        pass_all,
        output_weight,
        inner_weight,
        outer_weight,
        layer_early,
        micros * rows,
        vec,
        positive,
        negative,
        bins[..., 0],
        margins,
        clusters,
    )
    grads, query_bias_row, extra, both, back, layer_late = last_stage(
        segment, vec, query_c, d_own, x_slice, hid, keys, values, probs, weights, early, roles, batches
    )
    layer_out, in_grad, query_grad, key_grad, value_grad, mine_query = finish_stage(
        layer, layer_late, both, back, extra, grads, query_bias_row
    )
    value_b, output_b, first_g, first_s, inner_b, outer_b, second_g, second_s = biases
    return (
        layer_out.reshape(hidden.shape),
        loss[0, 0],
        in_grad.reshape(hidden.shape),
        query_grad,
        mine_query,
        key_grad,
        value_grad,
        value_b,
        output_grad,
        output_b,
        first_g,
        first_s,
        inner_grad,
        inner_b,
        outer_grad,
        outer_b,
        second_g,
        second_s,
    )


highest = lax.Precision.HIGHEST


def multiply(left, right):
    return jnp.dot(left, right, preferred_element_type=jnp.float32)


def left_product(left, right):
    return jnp.einsum("rd,re->de", left, right, preferred_element_type=jnp.float32)


def right_product(left, right):
    return jnp.einsum("rd,ed->re", left, right, preferred_element_type=jnp.float32)


def select_rows(array, stride):
    return array.reshape((array.shape[0] // stride, stride) + array.shape[1:])[:, 0]


def normalize(incoming, gain_vec, shift_vec):
    center = incoming - jnp.mean(incoming, axis=-1, keepdims=True)
    inv_std = lax.rsqrt(jnp.mean(center * center, axis=-1, keepdims=True) + epsilon)
    normed = center * inv_std
    return (normed * gain_vec + shift_vec, normed, inv_std)


def normalize_back(grad_in, normed, inv_std, gain_vec):
    scaled = grad_in * gain_vec
    return inv_std * (
        scaled
        - jnp.mean(scaled, axis=-1, keepdims=True)
        - normed * jnp.mean(scaled * normed, axis=-1, keepdims=True)
    )


def encode(hidden_rows, seg_rows, weights, att_rows):
    (
        query_weight,
        query_bias,
        key_weight,
        value_weight,
        value_bias,
        output_weight,
        output_bias,
        first_gain,
        first_shift,
        inner_weight,
        inner_bias,
        outer_weight,
        outer_bias,
        second_gain,
        second_shift,
    ) = weights
    row_count = hidden_rows.shape[0]
    blocks = row_count // att_rows
    head_scale = HEAD_DIM ** (-0.5)
    block_shape = (blocks, att_rows, HEADS, HEAD_DIM)
    query_rows = (multiply(hidden_rows, query_weight) + query_bias).astype(jnp.bfloat16)
    key_rows = multiply(hidden_rows, key_weight).astype(jnp.bfloat16)
    value_rows = (multiply(hidden_rows, value_weight) + value_bias).astype(jnp.bfloat16)
    scores = (
        jnp.einsum(
            "bihd,bjhd->bhij",
            query_rows.reshape(block_shape),
            key_rows.reshape(block_shape),
            preferred_element_type=jnp.float32,
        )
        * head_scale
    )
    seg_blocks = seg_rows.reshape(blocks, att_rows)
    same_seg = (seg_blocks[:, :, None] == seg_blocks[:, None, :])[:, None]
    scores = jnp.where(same_seg, scores, very_low)
    row_max = jnp.max(scores, axis=-1, keepdims=True)
    raised = jnp.exp(scores - row_max)
    summed = jnp.sum(raised, axis=-1, keepdims=True)
    attn_probs = (raised / summed).astype(jnp.bfloat16)
    log_total = (row_max + jnp.log(summed))[..., 0]
    context = (
        jnp.einsum(
            "bhij,bjhd->bihd",
            attn_probs,
            value_rows.reshape(block_shape),
            preferred_element_type=jnp.float32,
        )
        .reshape(row_count, D)
        .astype(jnp.bfloat16)
    )
    attended = multiply(context, output_weight) + output_bias
    first_norm, normed_one, inv_one = normalize(
        hidden_rows.astype(jnp.float32) + attended, first_gain, first_shift
    )
    first_low = first_norm.astype(jnp.bfloat16)
    inner_pre = multiply(first_low, inner_weight) + inner_bias
    activated = jax.nn.gelu(inner_pre, approximate=False).astype(jnp.bfloat16)
    outer_out = multiply(activated, outer_weight) + outer_bias
    block_out, normed_two, inv_two = normalize(first_norm + outer_out, second_gain, second_shift)
    log_cand = log_total.reshape(blocks, HEADS, att_rows // QLEN, QLEN)[..., 0]
    kept = (
        key_rows,
        value_rows,
        select_rows(query_rows, QLEN),
        log_cand,
        select_rows(context, QLEN),
        select_rows(normed_one, QLEN),
        select_rows(inv_one, QLEN),
        select_rows(first_low, QLEN),
        select_rows(inner_pre, QLEN),
        select_rows(activated, QLEN),
        select_rows(normed_two, QLEN),
        select_rows(inv_two, QLEN),
    )
    return (block_out, kept)


def encode_back(grad_out, hidden_rows, seg_rows, weights, kept, att_rows):
    (
        query_weight,
        query_bias,
        key_weight,
        value_weight,
        value_bias,
        output_weight,
        output_bias,
        first_gain,
        first_shift,
        inner_weight,
        inner_bias,
        outer_weight,
        outer_bias,
        second_gain,
        second_shift,
    ) = weights
    (
        key_rows,
        value_rows,
        query_cand,
        log_cand,
        context_cand,
        normed_one,
        inv_one,
        first_cand,
        inner_cand,
        active_cand,
        normed_two,
        inv_two,
    ) = kept
    row_count = hidden_rows.shape[0]
    blocks = row_count // att_rows
    cand_rows = row_count // QLEN
    per_block = att_rows // QLEN
    head_scale = HEAD_DIM ** (-0.5)
    hidden_cand = select_rows(hidden_rows, QLEN)
    second_gain_grad = jnp.sum(grad_out * normed_two, axis=0)
    second_shift_grad = jnp.sum(grad_out, axis=0)
    d_second = normalize_back(grad_out, normed_two, inv_two, second_gain)
    d_outer = d_second.astype(jnp.bfloat16)
    outer_weight_grad = left_product(active_cand, d_outer)
    outer_bias_grad = jnp.sum(d_outer.astype(jnp.float32), axis=0)
    d_active = right_product(d_outer, outer_weight)
    gelu_pull = jax.vjp(functools.partial(jax.nn.gelu, approximate=False), inner_cand)[1]
    d_inner = gelu_pull(d_active)[0].astype(jnp.bfloat16)
    inner_weight_grad = left_product(first_cand, d_inner)
    inner_bias_grad = jnp.sum(d_inner.astype(jnp.float32), axis=0)
    d_first = d_second + right_product(d_inner, inner_weight)
    first_gain_grad = jnp.sum(d_first * normed_one, axis=0)
    first_shift_grad = jnp.sum(d_first, axis=0)
    d_attend = normalize_back(d_first, normed_one, inv_one, first_gain)
    d_attend_low = d_attend.astype(jnp.bfloat16)
    output_weight_grad = left_product(context_cand, d_attend_low)
    output_bias_grad = jnp.sum(d_attend_low.astype(jnp.float32), axis=0)
    cand_shape = (blocks, per_block, HEADS, HEAD_DIM)
    block_shape = (blocks, att_rows, HEADS, HEAD_DIM)
    d_context = right_product(d_attend_low, output_weight).astype(jnp.bfloat16).reshape(cand_shape)
    query_heads = query_cand.reshape(cand_shape)
    key_heads = key_rows.reshape(block_shape)
    value_heads = value_rows.reshape(block_shape)
    scores = (
        jnp.einsum("bihd,bjhd->bhij", query_heads, key_heads, preferred_element_type=jnp.float32)
        * head_scale
    )
    seg_blocks = seg_rows.reshape(blocks, att_rows)
    seg_cand = seg_blocks.reshape(blocks, per_block, QLEN)[..., 0]
    same_seg = (seg_cand[:, :, None] == seg_blocks[:, None, :])[:, None]
    attn_probs = jnp.where(same_seg, jnp.exp(scores - log_cand[..., None]), 0.0)
    d_probs = jnp.einsum(
        "bihd,bjhd->bhij", d_context, value_heads, preferred_element_type=jnp.float32
    )
    d_scores = (
        attn_probs * (d_probs - jnp.sum(attn_probs * d_probs, axis=-1, keepdims=True))
    ).astype(jnp.bfloat16)
    d_query = (
        (
            jnp.einsum("bhij,bjhd->bihd", d_scores, key_heads, preferred_element_type=jnp.float32)
            * head_scale
        )
        .reshape(cand_rows, D)
        .astype(jnp.bfloat16)
    )
    d_keys = (
        (
            jnp.einsum("bhij,bihd->bjhd", d_scores, query_heads, preferred_element_type=jnp.float32)
            * head_scale
        )
        .reshape(row_count, D)
        .astype(jnp.bfloat16)
    )
    d_values = (
        jnp.einsum(
            "bhij,bihd->bjhd",
            attn_probs.astype(jnp.bfloat16),
            d_context,
            preferred_element_type=jnp.float32,
        )
        .reshape(row_count, D)
        .astype(jnp.bfloat16)
    )
    query_weight_grad = left_product(hidden_cand, d_query)
    query_bias_grad = jnp.sum(d_query.astype(jnp.float32), axis=0)
    key_weight_grad = left_product(hidden_rows, d_keys)
    value_weight_grad = left_product(hidden_rows, d_values)
    value_bias_grad = jnp.sum(d_values.astype(jnp.float32), axis=0)
    d_hidden = right_product(d_keys, key_weight) + right_product(d_values, value_weight)
    d_cand = right_product(d_query, query_weight) + d_attend
    d_hidden = d_hidden.reshape(cand_rows, QLEN, D)
    d_hidden = jnp.concatenate(
        [d_hidden[:, :1] + d_cand[:, None], d_hidden[:, 1:]], axis=1
    ).reshape(row_count, D)
    gradients = (
        query_weight_grad,
        query_bias_grad,
        key_weight_grad,
        value_weight_grad,
        value_bias_grad,
        output_weight_grad,
        output_bias_grad,
        first_gain_grad,
        first_shift_grad,
        inner_weight_grad,
        inner_bias_grad,
        outer_weight_grad,
        outer_bias_grad,
        second_gain_grad,
        second_shift_grad,
    )
    return (d_hidden, gradients)


def general_body(
    hidden,
    query_weight,
    query_bias,
    key_weight,
    value_weight,
    value_bias,
    output_weight,
    output_bias,
    first_gain,
    first_shift,
    inner_weight,
    inner_bias,
    outer_weight,
    outer_bias,
    second_gain,
    second_shift,
    segment,
    positive,
    negative,
    bins,
    margins,
    clusters,
):
    weights = (
        query_weight,
        query_bias,
        key_weight,
        value_weight,
        value_bias,
        output_weight,
        output_bias,
        first_gain,
        first_shift,
        inner_weight,
        inner_bias,
        outer_weight,
        outer_bias,
        second_gain,
        second_shift,
    )
    micro_count = hidden.shape[0]
    row_count = hidden.shape[2]
    att_rows = min(512, row_count)
    cand_rows = row_count // QLEN
    slot_stride = PSLOT // QLEN
    emb_scale = D ** (-0.5)
    query_flag = jnp.where(lax.axis_index("role") == 0, 1.0, 0.0).astype(jnp.float32)
    first_query = lax.axis_index("batch") * cand_rows
    bin_ids = bins[..., 0]
    query_total = bin_ids.shape[0] * bin_ids.shape[1]
    bin_slots = jnp.arange(NBINS, dtype=jnp.int32)
    bin_counts = jnp.sum((bin_ids[..., None] == bin_slots).astype(jnp.float32), axis=(0, 1))
    bin_table = query_total / (NBINS * bin_counts)
    loss_accum = jnp.zeros((), jnp.float32)
    accum = None
    layer_list = []
    grad_list = []
    for micro_idx in range(micro_count):
        hidden_rows = hidden[micro_idx, 0]
        seg_rows = segment[micro_idx, 0]
        block_out, kept = encode(hidden_rows, seg_rows, weights, att_rows)
        layer_list.append(block_out.astype(jnp.bfloat16))
        cls_rows = select_rows(block_out, QLEN).astype(jnp.bfloat16)
        passage_cls = cls_rows.reshape(-1, slot_stride, D)[:, 0]
        gathered = lax.all_gather(passage_cls, ("role", "batch"), axis=0, tiled=True)
        offset = lax.axis_size("batch") * passage_cls.shape[0]
        passages = gathered[offset:]
        scores = right_product(cls_rows, passages) * emb_scale
        columns = jnp.arange(passages.shape[0], dtype=jnp.int32)
        pos_ids = lax.dynamic_slice_in_dim(positive[micro_idx], first_query, cand_rows)
        neg_ids = lax.dynamic_slice_in_dim(negative[micro_idx], first_query, cand_rows)
        bin_mine = lax.dynamic_slice_in_dim(bin_ids[micro_idx], first_query, cand_rows)
        margin_mine = lax.dynamic_slice_in_dim(margins[micro_idx], first_query, cand_rows)
        pos_hit = pos_ids[:, None] == columns
        neg_hit = neg_ids[:, None] == columns
        cluster_row = clusters[micro_idx]
        pos_cluster = jnp.sum(jnp.where(pos_hit, cluster_row[None, :], 0), axis=-1)
        allowed = cluster_row[None, :] == pos_cluster[:, None]
        masked = jnp.where(allowed, scores, very_low)
        row_max = jnp.max(masked, axis=-1, keepdims=True)
        raised = jnp.exp(masked - row_max)
        summed = jnp.sum(raised, axis=-1, keepdims=True)
        softened = raised / summed
        log_total = (row_max + jnp.log(summed))[:, 0]
        pos_score = jnp.sum(jnp.where(pos_hit, scores, 0.0), axis=-1)
        neg_score = jnp.sum(jnp.where(neg_hit, scores, 0.0), axis=-1)
        weight_query = jnp.sum(jnp.where(bin_mine[:, None] == bin_slots, bin_table, 0.0), axis=-1)
        margin_gap = pos_score - neg_score - margin_mine
        loss_accum = loss_accum + query_flag * jnp.sum(
            log_total - pos_score + weight_query * margin_gap * margin_gap
        )
        pos_float = pos_hit.astype(jnp.float32)
        neg_float = neg_hit.astype(jnp.float32)
        d_scores = query_flag * (
            softened
            - pos_float
            + (2.0 * weight_query * margin_gap)[:, None] * (pos_float - neg_float)
        )
        passages_wide = passages.astype(jnp.float32)
        cls_wide = cls_rows.astype(jnp.float32)
        d_cls = (
            jnp.dot(d_scores, passages_wide, precision=highest, preferred_element_type=jnp.float32)
            * emb_scale
        )
        padded = jnp.concatenate([jnp.zeros((cand_rows, offset), jnp.float32), d_scores], axis=1)
        received = lax.psum_scatter(
            jnp.einsum(
                "qp,qd->pd", padded, cls_wide, precision=highest, preferred_element_type=jnp.float32
            )
            * emb_scale,
            ("role", "batch"),
            scatter_dimension=0,
            tiled=True,
        )
        spread = jnp.concatenate(
            [received[:, None], jnp.zeros((received.shape[0], slot_stride - 1, D), jnp.float32)],
            axis=1,
        ).reshape(cand_rows, D)
        d_hidden, micro_grads = encode_back(
            d_cls + spread, hidden_rows, seg_rows, weights, kept, att_rows
        )
        grad_list.append(d_hidden)
        accum = micro_grads if accum is None else jax.tree.map(jnp.add, accum, micro_grads)
    shards = (
        lax.psum_scatter(accum[0], "batch", scatter_dimension=0, tiled=True),
        lax.psum_scatter(accum[1], "batch", scatter_dimension=0, tiled=True),
        lax.psum_scatter(accum[2], "batch", scatter_dimension=0, tiled=True),
        lax.psum_scatter(accum[3], "batch", scatter_dimension=0, tiled=True),
        lax.psum_scatter(accum[4], "batch", scatter_dimension=0, tiled=True),
        lax.psum_scatter(accum[5], "batch", scatter_dimension=0, tiled=True),
        lax.psum_scatter(accum[6], "batch", scatter_dimension=0, tiled=True),
        lax.psum_scatter(accum[7], "batch", scatter_dimension=0, tiled=True),
        lax.psum_scatter(accum[8], "batch", scatter_dimension=0, tiled=True),
        lax.psum_scatter(accum[9], "batch", scatter_dimension=0, tiled=True),
        lax.psum_scatter(accum[10], "batch", scatter_dimension=0, tiled=True),
        lax.psum_scatter(accum[11], "batch", scatter_dimension=0, tiled=True),
        lax.psum_scatter(accum[12], "batch", scatter_dimension=0, tiled=True),
        lax.psum_scatter(accum[13], "batch", scatter_dimension=0, tiled=True),
        lax.psum_scatter(accum[14], "batch", scatter_dimension=0, tiled=True),
    )
    summed_grads = lax.psum(
        (
            shards[0],
            shards[1],
            shards[2],
            shards[3],
            shards[4],
            shards[5],
            shards[6],
            shards[7],
            shards[8],
            shards[9],
            shards[10],
            shards[11],
            shards[12],
            shards[13],
            shards[14],
        ),
        "role",
    )
    loss_value = lax.psum(loss_accum, ("role", "batch")) / query_total
    layer_out = jnp.stack(layer_list)[:, None]
    in_grad = jnp.stack(grad_list)[:, None]
    return (
        layer_out,
        loss_value,
        in_grad,
        summed_grads[0],
        summed_grads[1],
        summed_grads[2],
        summed_grads[3],
        summed_grads[4],
        summed_grads[5],
        summed_grads[6],
        summed_grads[7],
        summed_grads[8],
        summed_grads[9],
        summed_grads[10],
        summed_grads[11],
        summed_grads[12],
        summed_grads[13],
        summed_grads[14],
    )


def solution(mesh):
    roles, batches = mesh.shape["role"], mesh.shape["batch"]
    small = batches <= 8
    step = functools.partial(body, roles, batches) if small else general_body
    placed = (
        P(None, "role", "batch", None),
        P(),
        P(),
        P(),
        P(),
        P(),
        P(),
        P(),
        P(),
        P(),
        P(),
        P(),
        P(),
        P(),
        P(),
        P(),
        P(None, "role", "batch"),
        P(),
        P(),
        P(),
        P(),
        P(),
    )
    return jax.shard_map(
        step,
        mesh=mesh,
        in_specs=placed,
        out_specs=(
            P(None, "role", "batch", None),
            P(),
            P(None, "role", "batch", None),
            P("batch", None),
            P("batch"),
            P("batch", None),
            P("batch", None),
            P("batch"),
            P("batch", None),
            P("batch"),
            P("batch"),
            P("batch"),
            P("batch", None),
            P("batch"),
            P("batch", None),
            P("batch"),
            P("batch"),
            P("batch"),
        ),
        check_vma=False,
    )
```

```python
import functools

import jax
import jax.numpy as jnp
from jax import lax
from jax.experimental import pallas as pl
from jax.experimental.pallas import tpu as pltpu
from jax.sharding import PartitionSpec as P

D = 768
HEADS = 12
HEAD_DIM = 64
QLEN = 32
PSLOT = 256
NBINS = 10

very_low = -1e30
epsilon = 1e-12
bf16 = jnp.bfloat16
f32 = jnp.float32
MESH = pl.DeviceIdType.MESH
VMEM_BYTES = 60 * 1024 * 1024


def dot(left, right):
    return jnp.dot(left, right, preferred_element_type=f32)


def dot_right(left, right):
    return lax.dot_general(left, right, (((1,), (1,)), ((), ())), preferred_element_type=f32)


def dot_left(left, right):
    return lax.dot_general(left, right, (((0,), (0,)), ((), ())), preferred_element_type=f32)


def three_parts(wide):
    high = wide.astype(bf16)
    rest = wide - high.astype(f32)
    middle = rest.astype(bf16)
    return high, middle, (rest - middle.astype(f32)).astype(bf16)


def norm_parts(incoming):
    center = incoming - jnp.mean(incoming, axis=-1, keepdims=True)
    inv_std = lax.rsqrt(jnp.mean(center * center, axis=-1, keepdims=True) + epsilon)
    return center * inv_std, inv_std


def norm_back(scaled, normed, inv_std):
    return inv_std * (
        scaled
        - jnp.mean(scaled, axis=-1, keepdims=True)
        - normed * jnp.mean(scaled * normed, axis=-1, keepdims=True)
    )


def gelu(u):
    return 0.5 * u * (1.0 + lax.erf(u * 0.7071067811865476))


def gelu_slope(u):
    return 0.5 * (1.0 + lax.erf(u * 0.7071067811865476)) + u * (
        0.3989422804014327 * jnp.exp(-0.5 * u * u)
    )


def head_mask(cands):
    rows = lax.broadcasted_iota(jnp.int32, (HEADS * cands, D), 0)
    cols = lax.broadcasted_iota(jnp.int32, (HEADS * cands, D), 1)
    return rows // cands == cols // HEAD_DIM


def per_head(rows, mask):
    return jnp.where(mask, jnp.concatenate([rows] * HEADS, axis=0), jnp.zeros((), rows.dtype))


def from_heads(wide, mask, cands):
    kept = jnp.where(mask, wide, 0.0)
    total = kept[:cands]
    for head in range(1, HEADS):
        total = total + kept[head * cands : (head + 1) * cands]
    return total


def picked_rows(cands, rows):
    return (
        lax.broadcasted_iota(jnp.int32, (cands, rows), 1)
        == lax.broadcasted_iota(jnp.int32, (cands, rows), 0) * QLEN
    )


class Moves:
    def __init__(self, pairs, sems):
        self.copies = [
            pltpu.make_async_copy(src, dst, sems.at[i]) for i, (src, dst) in enumerate(pairs)
        ]
        self.open = set()

    def start(self, *which):
        for i in which:
            self.copies[i].start()
            self.open.add(i)

    def need(self, *which):
        for i in which:
            if i in self.open:
                self.copies[i].wait()
                self.open.remove(i)

    def finish(self):
        self.need(*sorted(self.open))


def layer_steps(x_ref, seg_row, keys, values, wq, wo, wi, wu, vec, out, queries, context, need):
    need("wq")
    queries[...] = (
        (dot(x_ref[...], wq[...]) + vec[0:1, :]).astype(bf16).astype(f32) * HEAD_DIM**-0.5
    ).astype(bf16)
    rows = seg_row.shape[1]
    seg_row = seg_row.astype(f32)
    seg_col = jnp.broadcast_to(seg_row, (128, rows)).T
    lane = lax.broadcasted_iota(jnp.int32, (rows, 128), 1)
    hot = seg_col == (lane % HEAD_DIM - 1).astype(f32)
    apart = jnp.where(hot, 0.0, very_low).astype(bf16)
    member = jnp.where(hot, 1.0, 0.0).astype(bf16)
    ones = jnp.ones((rows, 128), bf16)
    low = lane < HEAD_DIM
    yield
    for pair in range(HEADS // 2):
        part = slice(pair * 128, (pair + 1) * 128)
        q, k, v = queries[:, part], keys[:, part], values[:, part]

        def one(q_ext, k_ext, v_ext):
            scores = dot_right(q_ext, k_ext)
            raised = jnp.exp(scores - jnp.max(scores, axis=-1, keepdims=True))
            return dot(raised.astype(bf16), v_ext)

        even = one(jnp.where(low, q, apart), jnp.where(low, k, member), jnp.where(low, v, ones))
        odd = one(jnp.where(low, apart, q), jnp.where(low, member, k), jnp.where(low, ones, v))
        summed = pltpu.roll(jnp.where(low, odd, even), HEAD_DIM, 1)
        context[:, part] = (jnp.where(low, even, odd) * (1.0 / summed)).astype(bf16)
        if pair % 2 == 1:
            yield
    need("wo", "wi", "wu")
    attended = dot(context[...], wo[...]) + vec[2:3, :]
    normed, _ = norm_parts(x_ref[...].astype(f32) + attended)
    first_norm = normed * vec[3:4, :] + vec[4:5, :]
    first_low = first_norm.astype(bf16)
    total = first_norm + vec[5:6, :]
    yield
    for j in range(wi.shape[1] // D):
        part = slice(j * D, (j + 1) * D)
        u = dot(first_low, wi[:, part]) + vec[8 + j : 9 + j, :]
        total = total + dot(gelu(u).astype(bf16), wu[part, :])
        if j % 2 == 1:
            yield
    normed, _ = norm_parts(total)
    out[...] = (normed * vec[6:7, :] + vec[7:8, :]).astype(bf16)


def run_beside(steps, actions):
    for at, _ in enumerate(steps):
        for action in actions.pop(at, ()):
            action()
    for at in sorted(actions):
        for action in actions[at]:
            action()


def peer_of(step, roles, batches):
    role, batch = lax.axis_index("role"), lax.axis_index("batch")
    other = lax.rem((role // 2) * batches + batch + step, (roles // 2) * batches)
    return (other // batches) * 2 + role % 2, other % batches


def greet(roles, batches):
    role, batch = lax.axis_index("role"), lax.axis_index("batch")
    count = (roles // 2) * batches
    barrier = pltpu.get_barrier_semaphore()
    for other in range(0, roles, 2):
        there = other + 1 - role % 2
        pl.semaphore_signal(barrier, inc=1, device_id=(there, batch), device_id_type=MESH)

    def signal(step, carry):
        role_to, batch_to = peer_of(step, roles, batches)
        pl.semaphore_signal(barrier, inc=1, device_id=(role_to, batch_to), device_id_type=MESH)
        return carry

    lax.fori_loop(1, count, signal, 0)
    return lambda: pl.semaphore_wait(barrier, count - 1 + roles // 2)


def remote(src, dst, out_sem, in_sem, role_to, batch_to):
    return pltpu.make_async_remote_copy(
        src_ref=src,
        dst_ref=dst,
        send_sem=out_sem,
        recv_sem=in_sem,
        device_id=(role_to, batch_to),
        device_id_type=MESH,
    )


def each(begin, end, do):
    def go(step, carry):
        do(step)
        return carry

    lax.fori_loop(begin, end, go, 0)


class Spread:
    def __init__(self, roles, batches, parts, query_ref, pass_ref, query_all, pass_all, sems):
        self.roles, self.batches, self.parts = roles, batches, parts
        self.wide = 2
        self.deep = batches // self.wide
        self.flat = (roles // 2) * self.wide
        self.query_ref, self.pass_ref = query_ref, pass_ref
        self.query_all, self.pass_all = query_all, pass_all
        (
            self.q_across, self.q_z, self.q_plane, self.q_on, self.q_in,
            self.p_z, self.p_plane, self.p_on, self.p_in, self.own,
        ) = sems
        self.role, self.batch = lax.axis_index("role"), lax.axis_index("batch")
        self.core = self.role % 2
        self.mate = self.role + 1 - 2 * self.core
        self.z, self.y = self.batch // self.wide, self.batch % self.wide

    @staticmethod
    def sems(roles, batches, parts):
        deep, flat = batches // 2, roles
        dma = pltpu.SemaphoreType.DMA
        return [
            dma((parts,)),
            dma((parts, deep)),
            dma((parts, deep, flat)),
            dma((batches, parts)),
            dma((batches, parts)),
            dma((deep,)),
            dma((deep, flat)),
            dma(((roles - 1) * batches,)),
            dma(((roles - 1) * batches,)),
            dma((parts,)),
        ]

    def along_z(self, step):
        return lax.rem(self.z + step, self.deep) * self.wide + self.y

    def in_plane(self, step):
        place = lax.rem((self.role // 2) * self.wide + self.y + step, self.flat)
        return (place // self.wide) * 2 + self.core, place % self.wide

    def query_to(self, slot, part, sem, role_to, batch_to, src=None):
        begin, size, _ = self.parts[part]
        there = self.query_all.at[slot, pl.ds(begin, size)]
        return remote(there if src is None else src, there, sem, self.q_in.at[slot, part], role_to, batch_to)

    def query_z(self, part, step):
        return self.query_to(self.batch, part, self.q_z.at[part, step], self.role, self.along_z(step))

    def query_plane(self, part, depth, step):
        role_to, y_to = self.in_plane(step)
        return self.query_to(
            self.along_z(depth), part, self.q_plane.at[part, depth, step], role_to, self.z * self.wide + y_to
        )

    def query_on(self, slot, part):
        return self.query_to(slot, part, self.q_on.at[slot, part], self.mate, self.batch)

    def across(self, part):
        return self.query_to(
            self.batch, part, self.q_across.at[part], lax.rem(self.role + 2, self.roles), self.batch
        )

    def pass_to(self, slot, sem, role_to, batch_to):
        there = self.pass_all.at[slot]
        return remote(there, there, sem, self.p_in.at[slot], role_to, batch_to)

    def pass_slot(self, role, batch):
        return (role - 1) * self.batches + batch

    def pass_z(self, step):
        mine = self.pass_slot(self.role, self.batch)
        return self.pass_to(mine, self.p_z.at[step], self.role, self.along_z(step))

    def pass_plane(self, depth, step):
        role_to, y_to = self.in_plane(step)
        slot = self.pass_slot(self.role, self.along_z(depth))
        return self.pass_to(slot, self.p_plane.at[depth, step], role_to, self.z * self.wide + y_to)

    def pass_on(self, slot):
        return self.pass_to(slot, self.p_on.at[slot], self.mate, self.batch)

    def planes(self, do):
        each(1, self.flat, do)

    def hand_query(self, part, depth):
        self.planes(lambda step: self.query_plane(part, depth, step).start())
        self.query_on(self.along_z(depth), part).start()

    def not_source(self, step, do):
        pl.when(step != self.wide)(do)

    def begin_query(self, part):
        @pl.when(self.role == 0)
        def _():
            begin, size, via = self.parts[part]
            keep = pltpu.make_async_copy(
                self.query_ref.at[pl.ds(begin, size)],
                self.query_all.at[self.batch, pl.ds(begin, size)],
                self.own.at[part],
            )
            keep.start()
            keep.wait()
            if via:
                self.across(part).start()
                self.query_on(self.batch, part).start()
            else:
                each(1, self.deep, lambda step: self.query_z(part, step).start())
                self.hand_query(part, 0)

    def second(self, part):
        @pl.when(self.role == 2)
        def _():
            self.query_on(self.batch, part).wait_recv()
            each(1, self.deep, lambda step: self.query_z(part, step).start())
            self.planes(
                lambda step: self.not_source(step, lambda: self.query_plane(part, 0, step).start())
            )
            self.query_on(self.batch, part).start()

    def begin_pass(self):
        @pl.when(self.role > 0)
        def _():
            mine = self.pass_slot(self.role, self.batch)
            keep = pltpu.make_async_copy(self.pass_ref, self.pass_all.at[mine], self.own.at[0])
            keep.start()
            keep.wait()
            each(1, self.deep, lambda step: self.pass_z(step).start())
            self.planes(lambda step: self.pass_plane(0, step).start())
            self.pass_on(mine).start()

    def carrier(self, part):
        return 2 if self.parts[part][2] else 0

    def relay_query(self, *parts):
        for part in parts:

            @pl.when(self.role == self.carrier(part))
            def _():
                def go(depth):
                    self.query_on(self.along_z(depth), part).wait_recv()
                    self.hand_query(part, depth)

                each(1, self.deep, go)

    def relay_pass(self):
        @pl.when(self.role > 0)
        def _():
            def go(depth):
                slot = self.pass_slot(self.role, self.along_z(depth))
                self.pass_on(slot).wait_recv()
                self.planes(lambda step: self.pass_plane(depth, step).start())
                self.pass_on(slot).start()

            each(1, self.deep, go)

    def from_plane(self, part, do):
        via = self.parts[part][2]

        @pl.when(self.core == 0)
        def _():
            def go(slot):
                mine = jnp.logical_and(self.role == self.carrier(part), slot % self.wide == self.y)
                if via:
                    mine = jnp.logical_or(
                        mine, jnp.logical_and(self.role == 0, slot == self.batch)
                    )
                pl.when(jnp.logical_not(mine))(lambda: do(slot))

            each(0, self.batches, go)

    def pass_from_plane(self, do):
        def plane(step):
            role_of, y_of = self.in_plane(step)

            def go(depth):
                do(self.pass_slot(role_of, depth * self.wide + y_of))

            pl.when(role_of > 0)(lambda: each(0, self.deep, go))

        self.planes(plane)

    def share_query(self, *parts):
        for part in parts:

            def go(slot):
                self.query_on(slot, part).wait_recv()
                self.query_on(slot, part).start()

            self.from_plane(part, go)

    def share_pass(self):
        def go(slot):
            self.pass_on(slot).wait_recv()
            self.pass_on(slot).start()

        self.pass_from_plane(go)

    def take(self):
        @pl.when(self.core == 1)
        def _():
            def go(slot):
                for part in range(len(self.parts)):
                    self.query_on(slot, part).wait_recv()

            each(0, self.batches, go)

        for other in range(0, self.roles, 2):
            role_of = other + 1 - self.core

            def go(batch):
                self.pass_on(self.pass_slot(role_of, batch)).wait_recv()

            pl.when(role_of > 0)(lambda: each(0, self.batches, go))

    def end(self):
        def query_sent(part):
            via = self.parts[part][2]

            @pl.when(self.role == self.carrier(part))
            def _():
                each(1, self.deep, lambda step: self.query_z(part, step).wait_send())

                def go(depth):
                    def plane(step):
                        done = self.query_plane(part, depth, step).wait_send
                        if via:
                            pl.when(jnp.logical_or(depth > 0, step != self.wide))(lambda: done())
                        else:
                            done()

                    self.planes(plane)

                each(0, self.deep, go)

            if via:
                pl.when(self.role == 0)(lambda: self.across(part).wait_send())

            @pl.when(self.core == 0)
            def _():
                each(0, self.batches, lambda slot: self.query_on(slot, part).wait_send())

        for part in range(len(self.parts)):
            query_sent(part)

        @pl.when(self.role > 0)
        def _():
            each(1, self.deep, lambda step: self.pass_z(step).wait_send())

            def go(depth):
                self.planes(lambda step: self.pass_plane(depth, step).wait_send())
                self.pass_on(self.pass_slot(self.role, self.along_z(depth))).wait_send()

            each(0, self.deep, go)

        self.pass_from_plane(lambda slot: self.pass_on(slot).wait_send())


def first_kernel(
    roles, batches, micros, rows, early,
    seg, hid_far, wq_far, wk_far, wv_far, wo_far, wi_far, wu_far, *refs,
):
    lines, refs = refs[:9], refs[9:]
    keys_far, values_far, probs_far, query_far, pass_far, layer_far, query_c, vec = refs[:8]
    hid, wq, wk, wv, wo, wi, wu, keys, values, probs, out, queries, context = refs[8:21]
    query_msg, pass_msg, query_all, pass_all, in_sems, out_sems = refs[21:27]
    sems = refs[27:]
    cands = rows // QLEN
    total = micros * cands
    names = ["hid", "wq", "wk", "wv", "wo", "wi", "wu"]
    far = (hid_far, wq_far, wk_far, wv_far, wo_far, wi_far, wu_far)
    moves = Moves(list(zip(far, (hid, wq, wk, wv, wo, wi, wu))), in_sems)
    moves.start(0, 2, 3, 1, 4, 5, 6)

    def need(*which):
        moves.need(*[names.index(name) for name in which])

    blocks = [pl.ds(m * rows, rows) for m in range(micros)]
    stores = Moves(
        [(keys, keys_far), (values, values_far), (probs, probs_far), (query_all, query_far), (pass_all, pass_far)]
        + [(out.at[blocks[m]], layer_far.at[blocks[m]]) for m in range(early)],
        out_sems,
    )
    greeted = greet(roles, batches)
    parts = [(0, total // 2, False), (total // 2, total // 2, True)]
    parts += [(total + m * cands, cands, m % 2 == 1) for m in range(micros)]
    spread = Spread(roles, batches, parts, query_msg, pass_msg, query_all, pass_all, sems)

    at = 0
    for line in lines:
        wide = line[...].astype(f32).reshape(1, -1)
        for j in range(wide.shape[1] // D):
            vec[at : at + 1, :] = wide[:, j * D : (j + 1) * D]
            at += 1
    mask = head_mask(cands)
    pick = picked_rows(cands, rows)
    pick_low = pick.astype(f32).astype(bf16)
    need("hid")
    x_cand = jnp.concatenate(
        [dot(pick_low, hid[blocks[m], :]).astype(bf16) for m in range(micros)], axis=0
    )
    query_msg[0:total, :] = x_cand
    need("wk", "wv", "wq")
    q_cand = (
        (dot(x_cand, wq[...]) + vec[0:1, :]).astype(bf16).astype(f32) * HEAD_DIM**-0.5
    ).astype(bf16)
    query_c[...] = q_cand

    def project(m):
        x = hid[blocks[m], :]
        keys[blocks[m], :] = dot(x, wk[...]).astype(bf16)
        values[blocks[m], :] = (dot(x, wv[...]) + vec[1:2, :]).astype(bf16)

    project(0)
    for m in range(micros):
        seg_row = seg[m].astype(f32)
        seg_col = jnp.sum(jnp.where(pick, seg_row, 0.0), axis=-1, keepdims=True)
        bias = jnp.where(seg_col == seg_row, 0.0, very_low)
        q_wide = per_head(q_cand[m * cands : (m + 1) * cands], mask)
        scores = dot_right(q_wide, keys[blocks[m], :]) + jnp.concatenate([bias] * HEADS, axis=0)
        if m + 1 < micros:
            project(m + 1)
        raised = jnp.exp(scores - jnp.max(scores, axis=-1, keepdims=True))
        prob = raised * (1.0 / jnp.sum(raised, axis=-1, keepdims=True))
        probs[m * HEADS * cands : (m + 1) * HEADS * cands, :] = prob
        attended = from_heads(dot(prob.astype(bf16), values[blocks[m], :]), mask, cands)
        query_msg[total + m * cands : total + (m + 1) * cands, :] = attended.astype(bf16)
        if m == 0:
            greeted()
            spread.begin_query(1)
            spread.begin_query(0)
        spread.begin_query(2 + m)
        if m == 1:
            spread.second(1)
        elif m > 1 and m % 2 == 0:
            spread.second(1 + m)
    wide = query_msg[...].astype(f32)
    per_slot = PSLOT // QLEN
    chosen = []
    for part in range(2):
        for m in range(micros):
            for slot in range(cands // per_slot):
                at = (part * micros + m) * cands + slot * per_slot
                chosen.append(wide[at : at + 1])
    pass_msg[...] = jnp.concatenate(chosen, axis=0).astype(bf16)
    spread.begin_pass()
    stores.start(0, 1, 2)

    def steps():
        for m in range(early):
            yield from layer_steps(
                hid.at[blocks[m]], seg[m], keys.at[blocks[m]], values.at[blocks[m]],
                wq, wo, wi, wu, vec, out.at[blocks[m]], queries, context, need,
            )
            stores.start(5 + m)
            yield

    run_beside(steps(), first_plan(spread, len(parts)))
    spread.take()
    stores.start(3, 4)
    spread.end()
    stores.finish()


def first_plan(spread, parts):
    every = range(parts)
    return {
        1: [lambda: spread.second(parts - 1)],
        2: [lambda: spread.relay_query(*every[:-1]), spread.relay_pass],
        4: [lambda: spread.relay_query(parts - 1)],
        8: [lambda: spread.share_query(*every[:-1])],
        12: [lambda: spread.share_query(parts - 1), spread.share_pass],
    }


def first_stage(hid, seg, weights, lines, micros, early, roles, batches):
    rows = hid.shape[0] // micros
    cands = rows // QLEN
    total = micros * cands
    passes = micros * (rows // PSLOT)
    vmem = pl.BlockSpec(memory_space=pltpu.VMEM)
    far = pl.BlockSpec(memory_space=pl.ANY)
    query_all = (batches, 2 * total, D)
    pass_all = ((roles - 1) * batches, 2 * passes, D)
    probs = (micros * HEADS * cands, rows)
    held = pltpu.VMEM(hid.shape, bf16)
    return pl.pallas_call(
        functools.partial(first_kernel, roles, batches, micros, rows, early),
        in_specs=[vmem] + [far] * 7 + [vmem] * len(lines),
        out_specs=(far,) * 6 + (vmem,) * 2,
        out_shape=(
            jax.ShapeDtypeStruct(hid.shape, bf16),
            jax.ShapeDtypeStruct(hid.shape, bf16),
            jax.ShapeDtypeStruct(probs, f32),
            jax.ShapeDtypeStruct(query_all, bf16),
            jax.ShapeDtypeStruct(pass_all, bf16),
            jax.ShapeDtypeStruct((early * rows, D), bf16),
            jax.ShapeDtypeStruct((total, D), bf16),
            jax.ShapeDtypeStruct((sum(line.size for line in lines) // D, D), f32),
        ),
        scratch_shapes=[held]
        + [pltpu.VMEM(w.shape, bf16) for w in weights]
        + [held, held, pltpu.VMEM(probs, f32), pltpu.VMEM((early * rows, D), bf16)]
        + [pltpu.VMEM((rows, D), bf16)] * 2
        + [
            pltpu.VMEM((2 * total, D), bf16),
            pltpu.VMEM((2 * passes, D), bf16),
            pltpu.VMEM(query_all, bf16),
            pltpu.VMEM(pass_all, bf16),
            pltpu.SemaphoreType.DMA((7,)),
            pltpu.SemaphoreType.DMA((5 + early,)),
        ]
        + Spread.sems(roles, batches, 2 + micros),
        compiler_params=pltpu.CompilerParams(
            collective_id=1, has_side_effects=True, vmem_limit_bytes=VMEM_BYTES
        ),
        name="first",
    )(seg, hid, *weights, *lines)


def middle_kernel(
    micros,
    cands,
    columns,
    query_all,
    pass_all,
    wo_far,
    wi_far,
    wu_far,
    layer_early,
    vec,
    positive,
    negative,
    bins,
    margins,
    clusters,
    loss_out,
    inner_grad,
    outer_grad,
    output_grad,
    value_bias,
    output_bias,
    first_gain,
    first_shift,
    inner_bias,
    outer_bias,
    second_gain,
    second_shift,
    x_slice,
    d_own,
    layer_far,
    wo,
    wi,
    wu,
    early,
    sems,
    vectors,
    inner_row,
    x_all,
    c_all,
    u_all,
    g_all,
    n_one,
    d_rows,
):
    role, batch = lax.axis_index("role"), lax.axis_index("batch")
    batches = query_all.shape[0]
    own_rows = micros * cands
    n_query = batches * own_rows
    n_dev = pass_all.shape[0]
    per_dev = pass_all.shape[1] // 2
    per_micro = per_dev // micros
    n_pass = n_dev * per_dev
    n_rows = n_query + n_pass
    inner = wi.shape[1]
    chunks = [slice(j * D, (j + 1) * D) for j in range(inner // D)]

    moves = Moves(
        [
            (wo_far, wo),
            (wi_far, wi),
            (wu_far, wu),
            (layer_early, early),
            (early, layer_far.at[pl.ds(0, early.shape[0])]),
        ],
        sems,
    )
    moves.start(0, 1, 2, 3)
    for b in range(batches):
        x_all[b * own_rows : (b + 1) * own_rows, :] = query_all[b, 0:own_rows, :]
        c_all[b * own_rows : (b + 1) * own_rows, :] = query_all[b, own_rows : 2 * own_rows, :]
    wide = pass_all[...].astype(f32)
    x_all[n_query:n_rows, :] = wide[:, 0:per_dev, :].reshape(n_pass, D).astype(bf16)
    c_all[n_query:n_rows, :] = wide[:, per_dev:, :].reshape(n_pass, D).astype(bf16)

    moves.need(0)
    attended = dot(c_all[...], wo[...]) + vec[2:3, :]
    normed, inv_one = norm_parts(x_all[...].astype(f32) + attended)
    n_one[...] = normed
    first_norm = normed * vec[3:4, :] + vec[4:5, :]
    first_low = first_norm.astype(bf16)
    total = first_norm + vec[5:6, :]
    moves.need(1, 2, 3)
    moves.start(4)
    for j, part in enumerate(chunks):
        u = dot(first_low, wi[:, part]) + vec[8 + j : 9 + j, :]
        u_all[:, part] = u
        g = gelu(u).astype(bf16)
        g_all[:, part] = g
        total = total + dot(g, wu[part, :])
    n_two, inv_two = norm_parts(total)
    low = (n_two * vec[6:7, :] + vec[7:8, :]).astype(bf16)
    q_low, p_low = low[:n_query], low[n_query:]

    bin_ids = bins[...]
    queries_total = bin_ids.shape[0] * bin_ids.shape[1]
    weight = jnp.zeros(bin_ids.shape, f32)
    for k in range(NBINS):
        hit = (bin_ids == k).astype(f32)
        amount = jnp.sum(jnp.sum(hit, axis=1, keepdims=True), axis=0, keepdims=True)
        weight = weight + hit * (queries_total / (NBINS * jnp.maximum(amount, 1.0)))

    lane = lax.broadcasted_iota(jnp.int32, (n_query, bin_ids.shape[1]), 1)
    row = lax.broadcasted_iota(jnp.int32, (n_query, bin_ids.shape[1]), 0)
    here = lane == (row // own_rows) * cands + row % cands

    def by_micro(table):
        parts = [
            jnp.broadcast_to(table[m : m + 1, :], (cands, table.shape[1])) for m in range(micros)
        ]
        return jnp.concatenate(parts * batches, axis=0)

    def per_query(table):
        return jnp.sum(jnp.where(here, by_micro(table), 0.0), axis=-1, keepdims=True)

    pos = per_query(positive[...].astype(f32))
    neg = per_query(negative[...].astype(f32))
    margin = per_query(margins[...])
    weight = per_query(weight)

    col = lax.broadcasted_iota(jnp.int32, (n_query, n_pass), 1)
    row = lax.broadcasted_iota(jnp.int32, (n_query, n_pass), 0)
    same = (col % per_dev) // per_micro == (row % own_rows) // cands
    ident = ((col // per_dev) * per_micro + col % per_micro).astype(f32)
    n_ids = n_dev * per_micro
    tab_row = lax.broadcasted_iota(jnp.int32, (n_ids, n_pass), 0)
    tab_col = lax.broadcasted_iota(jnp.int32, (n_ids, n_pass), 1)
    table = tab_row == (tab_col // per_dev) * per_micro + tab_col % per_micro
    cluster = by_micro(dot(clusters[...].astype(f32).astype(bf16), table.astype(f32).astype(bf16)))
    pos_hit = jnp.logical_and(same, ident == pos)
    neg_hit = jnp.logical_and(same, ident == neg)
    pos_cluster = jnp.sum(jnp.where(pos_hit, cluster, 0.0), axis=-1, keepdims=True)
    allowed = jnp.logical_and(same, cluster == pos_cluster)
    scores = dot_right(q_low, p_low) * D**-0.5
    masked = jnp.where(allowed, scores, very_low)
    row_max = jnp.max(masked, axis=-1, keepdims=True)
    raised = jnp.exp(masked - row_max)
    summed = jnp.sum(raised, axis=-1, keepdims=True)
    pos_score = jnp.sum(jnp.where(pos_hit, scores, 0.0), axis=-1, keepdims=True)
    neg_score = jnp.sum(jnp.where(neg_hit, scores, 0.0), axis=-1, keepdims=True)
    gap = pos_score - neg_score - margin
    terms = row_max + jnp.log(summed) - pos_score + weight * gap * gap
    loss_out[...] = jnp.broadcast_to(
        jnp.sum(terms, axis=0, keepdims=True) / queries_total, loss_out.shape
    )
    pull = 2.0 * weight * gap
    pos_one, neg_one = pos_hit.astype(f32), neg_hit.astype(f32)
    d_scores = (raised * (1.0 / summed) - pos_one + pull * (pos_one - neg_one)) * D**-0.5
    parts = three_parts(d_scores)
    d_query = sum(dot(part, p_low) for part in parts)
    d_pass = sum(dot_left(part, q_low) for part in parts)
    grad = jnp.concatenate([d_query, d_pass], axis=0)

    def total_of(array):
        return jnp.sum(array, axis=0, keepdims=True)

    vectors[6:7, :] = total_of(grad * n_two)
    vectors[7:8, :] = total_of(grad)
    d_two = norm_back(grad * vec[6:7, :], n_two, inv_two)
    d_outer = d_two.astype(bf16)
    vectors[5:6, :] = total_of(d_outer.astype(f32))
    select = (
        lax.broadcasted_iota(jnp.int32, (D, 128), 0)
        == lax.broadcasted_iota(jnp.int32, (D, 128), 1) + batch * columns
    )
    select = jnp.logical_and(select, lax.broadcasted_iota(jnp.int32, (D, 128), 1) < columns)
    select = select.astype(f32).astype(bf16)
    first_low = (n_one[...] * vec[3:4, :] + vec[4:5, :]).astype(bf16)
    y_slice = dot(first_low, select).astype(bf16)
    d_first = d_two
    for j, part in enumerate(chunks):
        d_inner = (dot_right(d_outer, wu[part, :]) * gelu_slope(u_all[:, part])).astype(bf16)
        inner_row[:, part] = total_of(d_inner.astype(f32))
        inner_grad[:, part] = dot_left(y_slice, d_inner)[:columns]
        d_first = d_first + dot_right(d_inner, wi[:, part])
    span = inner // batches
    outer_grad[...] = dot_left(g_all[:, pl.ds(pl.multiple_of(batch * span, 128), span)], d_outer)
    vectors[3:4, :] = total_of(d_first * n_one[...])
    vectors[4:5, :] = total_of(d_first)
    d_one = norm_back(d_first * vec[3:4, :], n_one[...], inv_one)
    d_rows[...] = d_one
    d_low = d_one.astype(bf16)
    bias_row = total_of(d_low.astype(f32))
    vectors[2:3, :] = bias_row
    vectors[1:2, :] = sum(dot_right(part, wo[...]) for part in three_parts(bias_row))
    vectors[0:1, :] = jnp.zeros_like(bias_row)
    c_slice = dot(c_all[...], select).astype(bf16)
    output_grad[...] = dot_left(c_slice, d_low)[:columns]
    x_slice[...] = dot(x_all[...], select).astype(bf16)
    mine = sum(dot(part, select) for part in three_parts(vectors[...]))
    outs = [value_bias, output_bias, first_gain, first_shift, outer_bias, second_gain, second_shift]
    for row, out in enumerate(outs):
        out[...] = mine[row + 1, :columns]
    inner_bias[...] = inner_row[0, pl.ds(pl.multiple_of(batch * span, 128), span)]

    moves.finish()

    @pl.when(role == 0)
    def _():
        d_own[...] = d_rows[pl.ds(pl.multiple_of(batch * own_rows, 8), own_rows), :]

    @pl.when(role > 0)
    def _():
        d_own[...] = jnp.zeros_like(d_own)
        begin = pl.multiple_of(n_query + ((role - 1) * batches + batch) * per_dev, 8)
        mine = d_rows[pl.ds(begin, per_dev), :]
        for m in range(micros):
            for slot in range(per_micro):
                at = m * cands + slot * (PSLOT // QLEN)
                d_own[at : at + 1, :] = mine[m * per_micro + slot : m * per_micro + slot + 1, :]


def middle_stage(
    query_all, pass_all, wo, wi, wu, layer_early, layer_rows, vec, positive, negative, bins, margins, clusters
):
    batches = query_all.shape[0]
    micros = positive.shape[0]
    own_rows = query_all.shape[1] // 2
    n_pass = pass_all.shape[0] * pass_all.shape[1] // 2
    n_rows = batches * own_rows + n_pass
    columns = D // batches
    inner = wi.shape[1]
    vmem = pl.BlockSpec(memory_space=pltpu.VMEM)
    far = pl.BlockSpec(memory_space=pl.ANY)
    return pl.pallas_call(
        functools.partial(middle_kernel, micros, own_rows // micros, columns),
        in_specs=[vmem] * 2 + [far] * 4 + [vmem] * 6,
        out_specs=(vmem,) * 14 + (far,),
        out_shape=(
            jax.ShapeDtypeStruct((1, 128), f32),
            jax.ShapeDtypeStruct((columns, inner), f32),
            jax.ShapeDtypeStruct((inner // batches, D), f32),
            jax.ShapeDtypeStruct((columns, D), f32),
        )
        + tuple(jax.ShapeDtypeStruct((size,), f32) for size in [columns] * 4 + [inner // batches] + [columns] * 3)
        + (
            jax.ShapeDtypeStruct((n_rows, 128), bf16),
            jax.ShapeDtypeStruct((own_rows, D), f32),
            jax.ShapeDtypeStruct((layer_rows, D), bf16),
        ),
        scratch_shapes=[pltpu.VMEM(w.shape, bf16) for w in (wo, wi, wu, layer_early)]
        + [
            pltpu.SemaphoreType.DMA((5,)),
            pltpu.VMEM((8, D), f32),
            pltpu.VMEM((1, inner), f32),
            pltpu.VMEM((n_rows, D), bf16),
            pltpu.VMEM((n_rows, D), bf16),
            pltpu.VMEM((n_rows, inner), f32),
            pltpu.VMEM((n_rows, inner), bf16),
            pltpu.VMEM((n_rows, D), f32),
            pltpu.VMEM((n_rows, D), f32),
        ],
        compiler_params=pltpu.CompilerParams(vmem_limit_bytes=VMEM_BYTES),
        name="middle",
    )(query_all, pass_all, wo, wi, wu, layer_early, vec, positive, negative, bins, margins, clusters)


def last_kernel(
    roles, batches, micros, rows, early,
    seg, vec, query_c, d_own, x_slice, hid_far, keys_far, values_far, probs_far,
    wq_far, wk_far, wv_far, wo_far, wi_far, wu_far,
    grads, query_bias, extra, both_far, back_far, layer_far,
    hid, keys, values, probs, wq, wk, wv, wo, wi, wu, out, queries, context,
    both, q_keep, c_keep, z_key, z_value, back, dq_ref, dq_pass, key_part, value_part,
    query_all, pass_all, from_mate, summed, from_x, halves, received, finals,
    in_sems, out_sems, mate_out, mate_in, x_out, x_in, part_out, part_in, last_out, last_in, *sems,
):
    role, batch = lax.axis_index("role"), lax.axis_index("batch")
    core, side = role % 2, role // 2
    mate = role + 1 - 2 * core
    across = lax.rem(role + 2, roles)
    cands = rows // QLEN
    total = micros * cands
    wide_rows = HEADS * cands
    columns = grads.shape[1]
    pieces = summed.shape[2]
    blocks = [pl.ds(m * rows, rows) for m in range(micros)]
    wides = [pl.ds(m * wide_rows, wide_rows) for m in range(micros)]
    names = ["wo", "wk", "wv", "wq", "wi", "wu"]
    pairs = [(wo_far, wo), (wk_far, wk), (wv_far, wv), (wq_far, wq), (wi_far, wi), (wu_far, wu)]
    for m in range(micros):
        names += [(m, "values"), (m, "probs"), (m, "keys"), (m, "hid")]
        pairs += [
            (values_far.at[blocks[m]], values.at[blocks[m]]),
            (probs_far.at[wides[m]], probs.at[wides[m]]),
            (keys_far.at[blocks[m]], keys.at[blocks[m]]),
            (hid_far.at[blocks[m]], hid.at[blocks[m]]),
        ]
    moves = Moves(pairs, in_sems)
    moves.start(0, *range(6, len(pairs)), 1, 2, 3, 4, 5)

    def need(*which):
        moves.need(*[names.index(name) for name in which])

    late = micros - early
    stores = Moves(
        [(out.at[blocks[m]], layer_far.at[blocks[m]]) for m in range(late)]
        + [(both, both_far), (back, back_far)],
        out_sems,
    )
    greeted = greet(roles, batches)
    spread = Spread(
        roles, batches, [(0, total // 2, False), (total // 2, total // 2, True)], dq_ref, dq_pass, query_all, pass_all, sems
    )

    mask = head_mask(cands)
    need("wo")
    d_context = dot_right(d_own[...].astype(bf16), wo[...]).astype(bf16)
    d_query = []
    for m in range(micros):
        need((m, "values"), (m, "probs"), (m, "keys"), (m, "hid"))
        cand = slice(m * cands, (m + 1) * cands)
        q_wide = per_head(query_c[cand, :], mask)
        c_wide = per_head(d_context[cand, :], mask)
        prob = probs[wides[m], :]
        pulled = prob * dot_right(c_wide, values[blocks[m], :])
        d_scores = (pulled - prob * jnp.sum(pulled, axis=-1, keepdims=True)).astype(bf16)
        pair = jnp.concatenate([d_scores, prob.astype(bf16)], axis=0)
        d_query.append(from_heads(dot(d_scores, keys[blocks[m], :]), mask, cands) * HEAD_DIM**-0.5)
        sums = dot(pair, hid[blocks[m], :])
        both[m] = pair
        z_key[wides[m], :] = sums[:wide_rows].astype(bf16)
        z_value[wides[m], :] = sums[wide_rows:].astype(bf16)
        q_keep[wides[m], :] = q_wide
        c_keep[wides[m], :] = c_wide
    d_query = jnp.concatenate(d_query, axis=0).astype(bf16)
    dq_ref[...] = d_query
    wide = d_query.astype(f32)
    per_slot = PSLOT // QLEN
    dq_pass[...] = jnp.concatenate(
        [wide[at : at + 1] for at in range(0, total, per_slot)], axis=0
    )
    split = summed.shape
    key_part[...] = dot_left(z_key[...], q_keep[...]).astype(bf16).reshape(split)
    value_part[...] = dot_left(z_value[...], c_keep[...]).astype(bf16).reshape(split)

    greeted()

    @pl.when(core == 0)
    def _():
        remote(value_part, from_mate, mate_out, mate_in, mate, batch).start()

    @pl.when(core == 1)
    def _():
        remote(key_part, from_mate, mate_out, mate_in, mate, batch).start()

    spread.begin_query(1)

    def to_x(piece):
        return remote(
            summed.at[:, 1 - side, piece], from_x.at[:, piece], x_out.at[piece], x_in.at[piece], across, batch
        )

    def begin_x():
        remote(key_part, from_mate, mate_out, mate_in, mate, batch).wait()

        @pl.when(core == 0)
        def _():
            summed[...] = (key_part[...].astype(f32) + from_mate[...].astype(f32)).astype(bf16)

        @pl.when(core == 1)
        def _():
            summed[...] = (value_part[...].astype(f32) + from_mate[...].astype(f32)).astype(bf16)

        for piece in range(pieces):
            to_x(piece).start()

    def to_batch(piece, step):
        other = lax.rem(batch + step, batches)
        return remote(
            halves.at[other, piece], received.at[batch, piece], part_out.at[other, piece],
            part_in.at[batch, piece], role, other,
        )

    def from_batch(piece, step):
        other = lax.rem(batch + step, batches)
        return remote(
            halves.at[other, piece], received.at[other, piece], part_out.at[other, piece],
            part_in.at[other, piece], role, other,
        )

    def begin_part(piece):
        to_x(piece).wait()
        halves[:, piece] = (
            summed[:, side, piece].astype(f32) + from_x[:, piece].astype(f32)
        ).astype(bf16)
        each(1, batches, lambda step: to_batch(piece, step).start())

    def to_role(step):
        other = lax.rem(role + step, roles)
        return remote(
            finals.at[role], finals.at[role], last_out.at[step], last_in.at[role], other, batch
        )

    def from_role(step):
        other = lax.rem(role + step, roles)
        return remote(
            finals.at[other], finals.at[other], last_out.at[step], last_in.at[other], other, batch
        )

    def begin_last():
        for piece in range(pieces):
            each(1, batches, lambda step: from_batch(piece, step).wait_recv())
            sum_all = halves[batch, piece].astype(f32)

            def add(step, so_far):
                return so_far + received[lax.rem(batch + step, batches), piece].astype(f32)

            finals[role, piece] = lax.fori_loop(1, batches, add, sum_all).astype(bf16)
        for step in range(1, roles):
            to_role(step).start()

    def steps():
        need("wk", "wv", "wq")
        extra[...] = dot_right(dq_ref[...], wq[...]) + d_own[...]
        q_back = dot_right(q_keep[...], wk[...]).astype(bf16)
        c_back = dot_right(c_keep[...], wv[...]).astype(bf16)
        for m in range(micros):
            at = slice(m * wide_rows, (m + 1) * wide_rows)
            back[m, :wide_rows, :] = q_back[at]
            back[m, wide_rows:, :] = c_back[at]
        stores.start(late, late + 1)
        yield
        for m in range(late):
            block = blocks[early + m]
            yield from layer_steps(
                hid.at[block], seg[early + m], keys.at[block], values.at[block],
                wq, wo, wi, wu, vec, out.at[blocks[m]], queries, context, need,
            )
            stores.start(m)
            yield

    parts = [functools.partial(begin_part, piece) for piece in range(pieces)]
    run_beside(steps(), last_plan(begin_x, spread, parts, begin_last))
    spread.take()
    count = batches * total
    all_query = query_all[...].reshape(count, D)
    all_pass = pass_all[...].reshape(-1, D)
    grads[0] = (
        dot_left(x_slice[0:count, :], all_query) + dot_left(x_slice[count:, :], all_pass.astype(bf16))
    )[:columns]
    query_bias[...] = jnp.sum(all_query.astype(f32), axis=0, keepdims=True) + jnp.sum(
        all_pass, axis=0, keepdims=True
    )
    spread.end()
    for piece in range(pieces):
        each(1, batches, lambda step: to_batch(piece, step).wait_send())
    for step in range(1, roles):
        from_role(step).wait_recv()
        to_role(step).wait_send()
    half = pieces * finals.shape[2]
    for x in range(roles // 2):
        here = slice(x * half, (x + 1) * half)
        grads[1, here, :] = finals[2 * x].astype(f32).reshape(half, D)
        grads[2, here, :] = finals[2 * x + 1].astype(f32).reshape(half, D)
    stores.finish()
    moves.finish()


def last_plan(begin_x, spread, parts, begin_last):
    return {
        0: [begin_x, lambda: spread.second(1), lambda: spread.begin_query(0), spread.begin_pass],
        3: [lambda: spread.relay_query(0, 1), spread.relay_pass],
        7: [parts[0]],
        10: [parts[1]],
        13: [parts[2]],
        14: [lambda: spread.share_query(0, 1), spread.share_pass],
        99: [begin_last],
    }


def last_stage(
    seg, vec, query_c, d_own, x_slice, hid, keys, values, probs, weights, early, roles, batches
):
    columns = D // batches
    micros, _, rows = seg.shape
    total = query_c.shape[0]
    passes = micros * (rows // PSLOT)
    wide = micros * HEADS * (rows // QLEN)
    vmem = pl.BlockSpec(memory_space=pltpu.VMEM)
    far = pl.BlockSpec(memory_space=pl.ANY)
    block = (columns, D)
    sides, tile = roles // 2, 16
    pieces = columns // sides // tile
    split = (batches, sides, pieces, tile, D)
    half = (batches, pieces, tile, D)
    dma = pltpu.SemaphoreType.DMA
    late = micros - early
    held = pltpu.VMEM(hid.shape, bf16)
    wide_rows = pltpu.VMEM((wide, D), bf16)
    both = (micros, 2 * wide // micros, rows)
    back = (micros, 2 * wide // micros, D)
    return pl.pallas_call(
        functools.partial(last_kernel, roles, batches, micros, rows, early),
        in_specs=[vmem] * 5 + [far] * 10,
        out_specs=(vmem,) * 3 + (far,) * 3,
        out_shape=(
            jax.ShapeDtypeStruct((3,) + block, f32),
            jax.ShapeDtypeStruct((1, D), f32),
            jax.ShapeDtypeStruct((total, D), f32),
            jax.ShapeDtypeStruct(both, bf16),
            jax.ShapeDtypeStruct(back, bf16),
            jax.ShapeDtypeStruct((late * rows, D), bf16),
        ),
        scratch_shapes=[held, held, held, pltpu.VMEM(probs.shape, f32)]
        + [pltpu.VMEM(w.shape, bf16) for w in weights]
        + [pltpu.VMEM((late * rows, D), bf16)]
        + [pltpu.VMEM((rows, D), bf16)] * 2
        + [
            pltpu.VMEM(both, bf16),
            wide_rows,
            wide_rows,
            wide_rows,
            wide_rows,
            pltpu.VMEM(back, bf16),
            pltpu.VMEM((total, D), bf16),
            pltpu.VMEM((passes, D), f32),
            pltpu.VMEM(split, bf16),
            pltpu.VMEM(split, bf16),
            pltpu.VMEM((batches, total, D), bf16),
            pltpu.VMEM(((roles - 1) * batches, passes, D), f32),
            pltpu.VMEM(split, bf16),
            pltpu.VMEM(split, bf16),
            pltpu.VMEM(half, bf16),
            pltpu.VMEM(half, bf16),
            pltpu.VMEM(half, bf16),
            pltpu.VMEM((roles, pieces, tile, D), bf16),
            dma((6 + 4 * micros,)),
            dma((late + 2,)),
            dma,
            dma,
            dma((pieces,)),
            dma((pieces,)),
            dma((batches, pieces)),
            dma((batches, pieces)),
            dma((roles,)),
            dma((roles,)),
        ]
        + Spread.sems(roles, batches, 2),
        compiler_params=pltpu.CompilerParams(
            collective_id=2, has_side_effects=True, vmem_limit_bytes=VMEM_BYTES
        ),
        name="last",
    )(seg, vec, query_c, d_own, x_slice, hid, keys, values, probs, *weights)


def finish_kernel(
    columns, layer_in, late, both, back, extra, grads, query_bias,
    layer_out, in_grad, query_grad, key_grad, value_grad, bias_out,
):
    del layer_in
    m = pl.program_id(0)
    layer_out[...] = late[...]

    @pl.when(m == 0)
    def _():
        query_grad[...] = grads[0]
        key_grad[...] = grads[1]
        value_grad[...] = grads[2]
        select = (
            lax.broadcasted_iota(jnp.int32, (D, 128), 0)
            == lax.broadcasted_iota(jnp.int32, (D, 128), 1) + lax.axis_index("batch") * columns
        )
        select = select.astype(f32).astype(bf16)
        mine = sum(dot(part, select) for part in three_parts(jnp.broadcast_to(query_bias[...], (8, D))))
        bias_out[...] = mine[0, :columns]

    in_grad[...] = dot_left(both[0], back[0])
    for cand in range(extra.shape[0]):
        at = slice(cand * QLEN, cand * QLEN + 1)
        in_grad[at, :] = in_grad[at, :] + extra[cand : cand + 1, :]


def finish_stage(layer, layer_late, both, back, extra, grads, query_bias):
    micros, wide, rows = both.shape
    columns = grads.shape[1]
    far = pl.BlockSpec(memory_space=pl.ANY)
    cands = rows // QLEN

    def fixed(shape):
        return pl.BlockSpec(shape, lambda m: (0,) * len(shape))

    block = (columns, D)
    piece = layer_late.shape[0] // micros
    skip = (layer.shape[0] - layer_late.shape[0]) // piece
    return pl.pallas_call(
        functools.partial(finish_kernel, columns),
        grid=(micros,),
        in_specs=[
            far,
            pl.BlockSpec((piece, D), lambda m: (m, 0)),
            pl.BlockSpec((1, wide, rows), lambda m: (m, 0, 0)),
            pl.BlockSpec((1, wide, D), lambda m: (m, 0, 0)),
            pl.BlockSpec((cands, D), lambda m: (m, 0)),
            fixed((3,) + block),
            fixed((1, D)),
        ],
        out_specs=(
            pl.BlockSpec((piece, D), lambda m: (m + skip, 0)),
            pl.BlockSpec((rows, D), lambda m: (m, 0)),
            fixed(block),
            fixed(block),
            fixed(block),
            fixed((columns,)),
        ),
        out_shape=(
            jax.ShapeDtypeStruct(layer.shape, layer.dtype),
            jax.ShapeDtypeStruct((micros * rows, D), f32),
            jax.ShapeDtypeStruct(block, f32),
            jax.ShapeDtypeStruct(block, f32),
            jax.ShapeDtypeStruct(block, f32),
            jax.ShapeDtypeStruct((columns,), f32),
        ),
        input_output_aliases={0: 0},
        compiler_params=pltpu.CompilerParams(vmem_limit_bytes=VMEM_BYTES),
        name="finish",
    )(layer, layer_late, both, back, extra, grads, query_bias)


def body(
    roles,
    batches,
    hidden,
    query_weight,
    query_bias,
    key_weight,
    value_weight,
    value_bias,
    output_weight,
    output_bias,
    first_gain,
    first_shift,
    inner_weight,
    inner_bias,
    outer_weight,
    outer_bias,
    second_gain,
    second_shift,
    segment,
    positive,
    negative,
    bins,
    margins,
    clusters,
):
    micros, rows = hidden.shape[0], hidden.shape[2]
    hid = hidden.reshape(micros * rows, D)
    lines = [
        query_bias,
        value_bias,
        output_bias,
        first_gain,
        first_shift,
        outer_bias,
        second_gain,
        second_shift,
        inner_bias,
    ]
    early = micros // 2
    weights = (query_weight, key_weight, value_weight, output_weight, inner_weight, outer_weight)
    keys, values, probs, query_all, pass_all, layer_early, query_c, vec = first_stage(
        hid, segment, weights, lines, micros, early, roles, batches
    )
    loss, inner_grad, outer_grad, output_grad, *biases, x_slice, d_own, layer = middle_stage(
        query_all,
        pass_all,
        output_weight,
        inner_weight,
        outer_weight,
        layer_early,
        micros * rows,
        vec,
        positive,
        negative,
        bins[..., 0],
        margins,
        clusters,
    )
    grads, query_bias_row, extra, both, back, layer_late = last_stage(
        segment, vec, query_c, d_own, x_slice, hid, keys, values, probs, weights, early, roles, batches
    )
    layer_out, in_grad, query_grad, key_grad, value_grad, mine_query = finish_stage(
        layer, layer_late, both, back, extra, grads, query_bias_row
    )
    value_b, output_b, first_g, first_s, inner_b, outer_b, second_g, second_s = biases
    return (
        layer_out.reshape(hidden.shape),
        loss[0, 0],
        in_grad.reshape(hidden.shape),
        query_grad,
        mine_query,
        key_grad,
        value_grad,
        value_b,
        output_grad,
        output_b,
        first_g,
        first_s,
        inner_grad,
        inner_b,
        outer_grad,
        outer_b,
        second_g,
        second_s,
    )


highest = lax.Precision.HIGHEST


def multiply(left, right):
    return jnp.dot(left, right, preferred_element_type=jnp.float32)


def left_product(left, right):
    return jnp.einsum("rd,re->de", left, right, preferred_element_type=jnp.float32)


def right_product(left, right):
    return jnp.einsum("rd,ed->re", left, right, preferred_element_type=jnp.float32)


def select_rows(array, stride):
    return array.reshape((array.shape[0] // stride, stride) + array.shape[1:])[:, 0]


def normalize(incoming, gain_vec, shift_vec):
    center = incoming - jnp.mean(incoming, axis=-1, keepdims=True)
    inv_std = lax.rsqrt(jnp.mean(center * center, axis=-1, keepdims=True) + epsilon)
    normed = center * inv_std
    return (normed * gain_vec + shift_vec, normed, inv_std)


def normalize_back(grad_in, normed, inv_std, gain_vec):
    scaled = grad_in * gain_vec
    return inv_std * (
        scaled
        - jnp.mean(scaled, axis=-1, keepdims=True)
        - normed * jnp.mean(scaled * normed, axis=-1, keepdims=True)
    )


def encode(hidden_rows, seg_rows, weights, att_rows):
    (
        query_weight,
        query_bias,
        key_weight,
        value_weight,
        value_bias,
        output_weight,
        output_bias,
        first_gain,
        first_shift,
        inner_weight,
        inner_bias,
        outer_weight,
        outer_bias,
        second_gain,
        second_shift,
    ) = weights
    row_count = hidden_rows.shape[0]
    blocks = row_count // att_rows
    head_scale = HEAD_DIM ** (-0.5)
    block_shape = (blocks, att_rows, HEADS, HEAD_DIM)
    query_rows = (multiply(hidden_rows, query_weight) + query_bias).astype(jnp.bfloat16)
    key_rows = multiply(hidden_rows, key_weight).astype(jnp.bfloat16)
    value_rows = (multiply(hidden_rows, value_weight) + value_bias).astype(jnp.bfloat16)
    scores = (
        jnp.einsum(
            "bihd,bjhd->bhij",
            query_rows.reshape(block_shape),
            key_rows.reshape(block_shape),
            preferred_element_type=jnp.float32,
        )
        * head_scale
    )
    seg_blocks = seg_rows.reshape(blocks, att_rows)
    same_seg = (seg_blocks[:, :, None] == seg_blocks[:, None, :])[:, None]
    scores = jnp.where(same_seg, scores, very_low)
    row_max = jnp.max(scores, axis=-1, keepdims=True)
    raised = jnp.exp(scores - row_max)
    summed = jnp.sum(raised, axis=-1, keepdims=True)
    attn_probs = (raised / summed).astype(jnp.bfloat16)
    log_total = (row_max + jnp.log(summed))[..., 0]
    context = (
        jnp.einsum(
            "bhij,bjhd->bihd",
            attn_probs,
            value_rows.reshape(block_shape),
            preferred_element_type=jnp.float32,
        )
        .reshape(row_count, D)
        .astype(jnp.bfloat16)
    )
    attended = multiply(context, output_weight) + output_bias
    first_norm, normed_one, inv_one = normalize(
        hidden_rows.astype(jnp.float32) + attended, first_gain, first_shift
    )
    first_low = first_norm.astype(jnp.bfloat16)
    inner_pre = multiply(first_low, inner_weight) + inner_bias
    activated = jax.nn.gelu(inner_pre, approximate=False).astype(jnp.bfloat16)
    outer_out = multiply(activated, outer_weight) + outer_bias
    block_out, normed_two, inv_two = normalize(first_norm + outer_out, second_gain, second_shift)
    log_cand = log_total.reshape(blocks, HEADS, att_rows // QLEN, QLEN)[..., 0]
    kept = (
        key_rows,
        value_rows,
        select_rows(query_rows, QLEN),
        log_cand,
        select_rows(context, QLEN),
        select_rows(normed_one, QLEN),
        select_rows(inv_one, QLEN),
        select_rows(first_low, QLEN),
        select_rows(inner_pre, QLEN),
        select_rows(activated, QLEN),
        select_rows(normed_two, QLEN),
        select_rows(inv_two, QLEN),
    )
    return (block_out, kept)


def encode_back(grad_out, hidden_rows, seg_rows, weights, kept, att_rows):
    (
        query_weight,
        query_bias,
        key_weight,
        value_weight,
        value_bias,
        output_weight,
        output_bias,
        first_gain,
        first_shift,
        inner_weight,
        inner_bias,
        outer_weight,
        outer_bias,
        second_gain,
        second_shift,
    ) = weights
    (
        key_rows,
        value_rows,
        query_cand,
        log_cand,
        context_cand,
        normed_one,
        inv_one,
        first_cand,
        inner_cand,
        active_cand,
        normed_two,
        inv_two,
    ) = kept
    row_count = hidden_rows.shape[0]
    blocks = row_count // att_rows
    cand_rows = row_count // QLEN
    per_block = att_rows // QLEN
    head_scale = HEAD_DIM ** (-0.5)
    hidden_cand = select_rows(hidden_rows, QLEN)
    second_gain_grad = jnp.sum(grad_out * normed_two, axis=0)
    second_shift_grad = jnp.sum(grad_out, axis=0)
    d_second = normalize_back(grad_out, normed_two, inv_two, second_gain)
    d_outer = d_second.astype(jnp.bfloat16)
    outer_weight_grad = left_product(active_cand, d_outer)
    outer_bias_grad = jnp.sum(d_outer.astype(jnp.float32), axis=0)
    d_active = right_product(d_outer, outer_weight)
    gelu_pull = jax.vjp(functools.partial(jax.nn.gelu, approximate=False), inner_cand)[1]
    d_inner = gelu_pull(d_active)[0].astype(jnp.bfloat16)
    inner_weight_grad = left_product(first_cand, d_inner)
    inner_bias_grad = jnp.sum(d_inner.astype(jnp.float32), axis=0)
    d_first = d_second + right_product(d_inner, inner_weight)
    first_gain_grad = jnp.sum(d_first * normed_one, axis=0)
    first_shift_grad = jnp.sum(d_first, axis=0)
    d_attend = normalize_back(d_first, normed_one, inv_one, first_gain)
    d_attend_low = d_attend.astype(jnp.bfloat16)
    output_weight_grad = left_product(context_cand, d_attend_low)
    output_bias_grad = jnp.sum(d_attend_low.astype(jnp.float32), axis=0)
    cand_shape = (blocks, per_block, HEADS, HEAD_DIM)
    block_shape = (blocks, att_rows, HEADS, HEAD_DIM)
    d_context = right_product(d_attend_low, output_weight).astype(jnp.bfloat16).reshape(cand_shape)
    query_heads = query_cand.reshape(cand_shape)
    key_heads = key_rows.reshape(block_shape)
    value_heads = value_rows.reshape(block_shape)
    scores = (
        jnp.einsum("bihd,bjhd->bhij", query_heads, key_heads, preferred_element_type=jnp.float32)
        * head_scale
    )
    seg_blocks = seg_rows.reshape(blocks, att_rows)
    seg_cand = seg_blocks.reshape(blocks, per_block, QLEN)[..., 0]
    same_seg = (seg_cand[:, :, None] == seg_blocks[:, None, :])[:, None]
    attn_probs = jnp.where(same_seg, jnp.exp(scores - log_cand[..., None]), 0.0)
    d_probs = jnp.einsum(
        "bihd,bjhd->bhij", d_context, value_heads, preferred_element_type=jnp.float32
    )
    d_scores = (
        attn_probs * (d_probs - jnp.sum(attn_probs * d_probs, axis=-1, keepdims=True))
    ).astype(jnp.bfloat16)
    d_query = (
        (
            jnp.einsum("bhij,bjhd->bihd", d_scores, key_heads, preferred_element_type=jnp.float32)
            * head_scale
        )
        .reshape(cand_rows, D)
        .astype(jnp.bfloat16)
    )
    d_keys = (
        (
            jnp.einsum("bhij,bihd->bjhd", d_scores, query_heads, preferred_element_type=jnp.float32)
            * head_scale
        )
        .reshape(row_count, D)
        .astype(jnp.bfloat16)
    )
    d_values = (
        jnp.einsum(
            "bhij,bihd->bjhd",
            attn_probs.astype(jnp.bfloat16),
            d_context,
            preferred_element_type=jnp.float32,
        )
        .reshape(row_count, D)
        .astype(jnp.bfloat16)
    )
    query_weight_grad = left_product(hidden_cand, d_query)
    query_bias_grad = jnp.sum(d_query.astype(jnp.float32), axis=0)
    key_weight_grad = left_product(hidden_rows, d_keys)
    value_weight_grad = left_product(hidden_rows, d_values)
    value_bias_grad = jnp.sum(d_values.astype(jnp.float32), axis=0)
    d_hidden = right_product(d_keys, key_weight) + right_product(d_values, value_weight)
    d_cand = right_product(d_query, query_weight) + d_attend
    d_hidden = d_hidden.reshape(cand_rows, QLEN, D)
    d_hidden = jnp.concatenate(
        [d_hidden[:, :1] + d_cand[:, None], d_hidden[:, 1:]], axis=1
    ).reshape(row_count, D)
    gradients = (
        query_weight_grad,
        query_bias_grad,
        key_weight_grad,
        value_weight_grad,
        value_bias_grad,
        output_weight_grad,
        output_bias_grad,
        first_gain_grad,
        first_shift_grad,
        inner_weight_grad,
        inner_bias_grad,
        outer_weight_grad,
        outer_bias_grad,
        second_gain_grad,
        second_shift_grad,
    )
    return (d_hidden, gradients)


def general_body(
    hidden,
    query_weight,
    query_bias,
    key_weight,
    value_weight,
    value_bias,
    output_weight,
    output_bias,
    first_gain,
    first_shift,
    inner_weight,
    inner_bias,
    outer_weight,
    outer_bias,
    second_gain,
    second_shift,
    segment,
    positive,
    negative,
    bins,
    margins,
    clusters,
):
    weights = (
        query_weight,
        query_bias,
        key_weight,
        value_weight,
        value_bias,
        output_weight,
        output_bias,
        first_gain,
        first_shift,
        inner_weight,
        inner_bias,
        outer_weight,
        outer_bias,
        second_gain,
        second_shift,
    )
    micro_count = hidden.shape[0]
    row_count = hidden.shape[2]
    att_rows = min(512, row_count)
    cand_rows = row_count // QLEN
    slot_stride = PSLOT // QLEN
    emb_scale = D ** (-0.5)
    query_flag = jnp.where(lax.axis_index("role") == 0, 1.0, 0.0).astype(jnp.float32)
    first_query = lax.axis_index("batch") * cand_rows
    bin_ids = bins[..., 0]
    query_total = bin_ids.shape[0] * bin_ids.shape[1]
    bin_slots = jnp.arange(NBINS, dtype=jnp.int32)
    bin_counts = jnp.sum((bin_ids[..., None] == bin_slots).astype(jnp.float32), axis=(0, 1))
    bin_table = query_total / (NBINS * bin_counts)
    loss_accum = jnp.zeros((), jnp.float32)
    accum = None
    layer_list = []
    grad_list = []
    for micro_idx in range(micro_count):
        hidden_rows = hidden[micro_idx, 0]
        seg_rows = segment[micro_idx, 0]
        block_out, kept = encode(hidden_rows, seg_rows, weights, att_rows)
        layer_list.append(block_out.astype(jnp.bfloat16))
        cls_rows = select_rows(block_out, QLEN).astype(jnp.bfloat16)
        passage_cls = cls_rows.reshape(-1, slot_stride, D)[:, 0]
        gathered = lax.all_gather(passage_cls, ("role", "batch"), axis=0, tiled=True)
        offset = lax.axis_size("batch") * passage_cls.shape[0]
        passages = gathered[offset:]
        scores = right_product(cls_rows, passages) * emb_scale
        columns = jnp.arange(passages.shape[0], dtype=jnp.int32)
        pos_ids = lax.dynamic_slice_in_dim(positive[micro_idx], first_query, cand_rows)
        neg_ids = lax.dynamic_slice_in_dim(negative[micro_idx], first_query, cand_rows)
        bin_mine = lax.dynamic_slice_in_dim(bin_ids[micro_idx], first_query, cand_rows)
        margin_mine = lax.dynamic_slice_in_dim(margins[micro_idx], first_query, cand_rows)
        pos_hit = pos_ids[:, None] == columns
        neg_hit = neg_ids[:, None] == columns
        cluster_row = clusters[micro_idx]
        pos_cluster = jnp.sum(jnp.where(pos_hit, cluster_row[None, :], 0), axis=-1)
        allowed = cluster_row[None, :] == pos_cluster[:, None]
        masked = jnp.where(allowed, scores, very_low)
        row_max = jnp.max(masked, axis=-1, keepdims=True)
        raised = jnp.exp(masked - row_max)
        summed = jnp.sum(raised, axis=-1, keepdims=True)
        softened = raised / summed
        log_total = (row_max + jnp.log(summed))[:, 0]
        pos_score = jnp.sum(jnp.where(pos_hit, scores, 0.0), axis=-1)
        neg_score = jnp.sum(jnp.where(neg_hit, scores, 0.0), axis=-1)
        weight_query = jnp.sum(jnp.where(bin_mine[:, None] == bin_slots, bin_table, 0.0), axis=-1)
        margin_gap = pos_score - neg_score - margin_mine
        loss_accum = loss_accum + query_flag * jnp.sum(
            log_total - pos_score + weight_query * margin_gap * margin_gap
        )
        pos_float = pos_hit.astype(jnp.float32)
        neg_float = neg_hit.astype(jnp.float32)
        d_scores = query_flag * (
            softened
            - pos_float
            + (2.0 * weight_query * margin_gap)[:, None] * (pos_float - neg_float)
        )
        passages_wide = passages.astype(jnp.float32)
        cls_wide = cls_rows.astype(jnp.float32)
        d_cls = (
            jnp.dot(d_scores, passages_wide, precision=highest, preferred_element_type=jnp.float32)
            * emb_scale
        )
        padded = jnp.concatenate([jnp.zeros((cand_rows, offset), jnp.float32), d_scores], axis=1)
        received = lax.psum_scatter(
            jnp.einsum(
                "qp,qd->pd", padded, cls_wide, precision=highest, preferred_element_type=jnp.float32
            )
            * emb_scale,
            ("role", "batch"),
            scatter_dimension=0,
            tiled=True,
        )
        spread = jnp.concatenate(
            [received[:, None], jnp.zeros((received.shape[0], slot_stride - 1, D), jnp.float32)],
            axis=1,
        ).reshape(cand_rows, D)
        d_hidden, micro_grads = encode_back(
            d_cls + spread, hidden_rows, seg_rows, weights, kept, att_rows
        )
        grad_list.append(d_hidden)
        accum = micro_grads if accum is None else jax.tree.map(jnp.add, accum, micro_grads)
    shards = (
        lax.psum_scatter(accum[0], "batch", scatter_dimension=0, tiled=True),
        lax.psum_scatter(accum[1], "batch", scatter_dimension=0, tiled=True),
        lax.psum_scatter(accum[2], "batch", scatter_dimension=0, tiled=True),
        lax.psum_scatter(accum[3], "batch", scatter_dimension=0, tiled=True),
        lax.psum_scatter(accum[4], "batch", scatter_dimension=0, tiled=True),
        lax.psum_scatter(accum[5], "batch", scatter_dimension=0, tiled=True),
        lax.psum_scatter(accum[6], "batch", scatter_dimension=0, tiled=True),
        lax.psum_scatter(accum[7], "batch", scatter_dimension=0, tiled=True),
        lax.psum_scatter(accum[8], "batch", scatter_dimension=0, tiled=True),
        lax.psum_scatter(accum[9], "batch", scatter_dimension=0, tiled=True),
        lax.psum_scatter(accum[10], "batch", scatter_dimension=0, tiled=True),
        lax.psum_scatter(accum[11], "batch", scatter_dimension=0, tiled=True),
        lax.psum_scatter(accum[12], "batch", scatter_dimension=0, tiled=True),
        lax.psum_scatter(accum[13], "batch", scatter_dimension=0, tiled=True),
        lax.psum_scatter(accum[14], "batch", scatter_dimension=0, tiled=True),
    )
    summed_grads = lax.psum(
        (
            shards[0],
            shards[1],
            shards[2],
            shards[3],
            shards[4],
            shards[5],
            shards[6],
            shards[7],
            shards[8],
            shards[9],
            shards[10],
            shards[11],
            shards[12],
            shards[13],
            shards[14],
        ),
        "role",
    )
    loss_value = lax.psum(loss_accum, ("role", "batch")) / query_total
    layer_out = jnp.stack(layer_list)[:, None]
    in_grad = jnp.stack(grad_list)[:, None]
    return (
        layer_out,
        loss_value,
        in_grad,
        summed_grads[0],
        summed_grads[1],
        summed_grads[2],
        summed_grads[3],
        summed_grads[4],
        summed_grads[5],
        summed_grads[6],
        summed_grads[7],
        summed_grads[8],
        summed_grads[9],
        summed_grads[10],
        summed_grads[11],
        summed_grads[12],
        summed_grads[13],
        summed_grads[14],
    )


def solution(mesh):
    roles, batches = mesh.shape["role"], mesh.shape["batch"]
    small = batches <= 8
    step = functools.partial(body, roles, batches) if small else general_body
    placed = (
        P(None, "role", "batch", None),
        P(),
        P(),
        P(),
        P(),
        P(),
        P(),
        P(),
        P(),
        P(),
        P(),
        P(),
        P(),
        P(),
        P(),
        P(),
        P(None, "role", "batch"),
        P(),
        P(),
        P(),
        P(),
        P(),
    )
    return jax.shard_map(
        step,
        mesh=mesh,
        in_specs=placed,
        out_specs=(
            P(None, "role", "batch", None),
            P(),
            P(None, "role", "batch", None),
            P("batch", None),
            P("batch"),
            P("batch", None),
            P("batch", None),
            P("batch"),
            P("batch", None),
            P("batch"),
            P("batch"),
            P("batch"),
            P("batch", None),
            P("batch"),
            P("batch", None),
            P("batch"),
            P("batch"),
            P("batch"),
        ),
        check_vma=False,
    )
```

```python
import functools

import jax
import jax.numpy as jnp
from jax import lax
from jax.experimental import pallas as pl
from jax.experimental.pallas import tpu as pltpu
from jax.sharding import PartitionSpec as P

D = 768
HEADS = 12
HEAD_DIM = 64
QLEN = 32
PSLOT = 256
NBINS = 10

very_low = -1e30
epsilon = 1e-12
bf16 = jnp.bfloat16
f32 = jnp.float32
MESH = pl.DeviceIdType.MESH
VMEM_BYTES = 60 * 1024 * 1024


def dot(left, right):
    return jnp.dot(left, right, preferred_element_type=f32)


def dot_right(left, right):
    return lax.dot_general(left, right, (((1,), (1,)), ((), ())), preferred_element_type=f32)


def dot_left(left, right):
    return lax.dot_general(left, right, (((0,), (0,)), ((), ())), preferred_element_type=f32)


def three_parts(wide):
    high = wide.astype(bf16)
    rest = wide - high.astype(f32)
    middle = rest.astype(bf16)
    return high, middle, (rest - middle.astype(f32)).astype(bf16)


def norm_parts(incoming):
    center = incoming - jnp.mean(incoming, axis=-1, keepdims=True)
    inv_std = lax.rsqrt(jnp.mean(center * center, axis=-1, keepdims=True) + epsilon)
    return center * inv_std, inv_std


def norm_back(scaled, normed, inv_std):
    return inv_std * (
        scaled
        - jnp.mean(scaled, axis=-1, keepdims=True)
        - normed * jnp.mean(scaled * normed, axis=-1, keepdims=True)
    )


def gelu(u):
    return 0.5 * u * (1.0 + lax.erf(u * 0.7071067811865476))


def gelu_slope(u):
    return 0.5 * (1.0 + lax.erf(u * 0.7071067811865476)) + u * (
        0.3989422804014327 * jnp.exp(-0.5 * u * u)
    )


def head_mask(cands):
    rows = lax.broadcasted_iota(jnp.int32, (HEADS * cands, D), 0)
    cols = lax.broadcasted_iota(jnp.int32, (HEADS * cands, D), 1)
    return rows // cands == cols // HEAD_DIM


def per_head(rows, mask):
    return jnp.where(mask, jnp.concatenate([rows] * HEADS, axis=0), jnp.zeros((), rows.dtype))


def from_heads(wide, mask, cands):
    kept = jnp.where(mask, wide, 0.0)
    total = kept[:cands]
    for head in range(1, HEADS):
        total = total + kept[head * cands : (head + 1) * cands]
    return total


def picked_rows(cands, rows):
    return (
        lax.broadcasted_iota(jnp.int32, (cands, rows), 1)
        == lax.broadcasted_iota(jnp.int32, (cands, rows), 0) * QLEN
    )


class Moves:
    def __init__(self, pairs, sems):
        self.copies = [
            pltpu.make_async_copy(src, dst, sems.at[i]) for i, (src, dst) in enumerate(pairs)
        ]
        self.open = set()

    def start(self, *which):
        for i in which:
            self.copies[i].start()
            self.open.add(i)

    def need(self, *which):
        for i in which:
            if i in self.open:
                self.copies[i].wait()
                self.open.remove(i)

    def finish(self):
        self.need(*sorted(self.open))


def layer_steps(x_ref, seg_row, keys, values, wq, wo, wi, wu, vec, out, queries, context, need):
    need("wq")
    queries[...] = (
        (dot(x_ref[...], wq[...]) + vec[0:1, :]).astype(bf16).astype(f32) * HEAD_DIM**-0.5
    ).astype(bf16)
    rows = seg_row.shape[1]
    seg_row = seg_row.astype(f32)
    seg_col = jnp.broadcast_to(seg_row, (128, rows)).T
    lane = lax.broadcasted_iota(jnp.int32, (rows, 128), 1)
    hot = seg_col == (lane % HEAD_DIM - 1).astype(f32)
    apart = jnp.where(hot, 0.0, very_low).astype(bf16)
    member = jnp.where(hot, 1.0, 0.0).astype(bf16)
    ones = jnp.ones((rows, 128), bf16)
    low = lane < HEAD_DIM
    yield
    for pair in range(HEADS // 2):
        part = slice(pair * 128, (pair + 1) * 128)
        q, k, v = queries[:, part], keys[:, part], values[:, part]

        def one(q_ext, k_ext, v_ext):
            scores = dot_right(q_ext, k_ext)
            raised = jnp.exp(scores - jnp.max(scores, axis=-1, keepdims=True))
            return dot(raised.astype(bf16), v_ext)

        even = one(jnp.where(low, q, apart), jnp.where(low, k, member), jnp.where(low, v, ones))
        odd = one(jnp.where(low, apart, q), jnp.where(low, member, k), jnp.where(low, ones, v))
        summed = pltpu.roll(jnp.where(low, odd, even), HEAD_DIM, 1)
        context[:, part] = (jnp.where(low, even, odd) * (1.0 / summed)).astype(bf16)
        if pair % 2 == 1:
            yield
    need("wo", "wi", "wu")
    attended = dot(context[...], wo[...]) + vec[2:3, :]
    normed, _ = norm_parts(x_ref[...].astype(f32) + attended)
    first_norm = normed * vec[3:4, :] + vec[4:5, :]
    first_low = first_norm.astype(bf16)
    total = first_norm + vec[5:6, :]
    yield
    for j in range(wi.shape[1] // D):
        part = slice(j * D, (j + 1) * D)
        u = dot(first_low, wi[:, part]) + vec[8 + j : 9 + j, :]
        total = total + dot(gelu(u).astype(bf16), wu[part, :])
        if j % 2 == 1:
            yield
    normed, _ = norm_parts(total)
    out[...] = (normed * vec[6:7, :] + vec[7:8, :]).astype(bf16)


def run_beside(steps, actions):
    for at, _ in enumerate(steps):
        for action in actions.pop(at, ()):
            action()
    for at in sorted(actions):
        for action in actions[at]:
            action()


def peer_of(step, roles, batches):
    role, batch = lax.axis_index("role"), lax.axis_index("batch")
    other = lax.rem((role // 2) * batches + batch + step, (roles // 2) * batches)
    return (other // batches) * 2 + role % 2, other % batches


def greet(roles, batches):
    role, batch = lax.axis_index("role"), lax.axis_index("batch")
    count = (roles // 2) * batches
    barrier = pltpu.get_barrier_semaphore()
    for other in range(0, roles, 2):
        there = other + 1 - role % 2
        pl.semaphore_signal(barrier, inc=1, device_id=(there, batch), device_id_type=MESH)

    def signal(step, carry):
        role_to, batch_to = peer_of(step, roles, batches)
        pl.semaphore_signal(barrier, inc=1, device_id=(role_to, batch_to), device_id_type=MESH)
        return carry

    lax.fori_loop(1, count, signal, 0)
    return lambda: pl.semaphore_wait(barrier, count - 1 + roles // 2)


def remote(src, dst, out_sem, in_sem, role_to, batch_to):
    return pltpu.make_async_remote_copy(
        src_ref=src,
        dst_ref=dst,
        send_sem=out_sem,
        recv_sem=in_sem,
        device_id=(role_to, batch_to),
        device_id_type=MESH,
    )


def each(begin, end, do):
    def go(step, carry):
        do(step)
        return carry

    lax.fori_loop(begin, end, go, 0)


class Spread:
    def __init__(self, roles, batches, parts, query_ref, pass_ref, query_all, pass_all, sems):
        self.roles, self.batches, self.parts = roles, batches, parts
        self.wide = 2
        self.deep = batches // self.wide
        self.flat = (roles // 2) * self.wide
        self.query_ref, self.pass_ref = query_ref, pass_ref
        self.query_all, self.pass_all = query_all, pass_all
        (
            self.q_across, self.q_z, self.q_plane, self.q_on, self.q_in,
            self.p_z, self.p_plane, self.p_on, self.p_in, self.own,
        ) = sems
        self.role, self.batch = lax.axis_index("role"), lax.axis_index("batch")
        self.core = self.role % 2
        self.mate = self.role + 1 - 2 * self.core
        self.z, self.y = self.batch // self.wide, self.batch % self.wide

    @staticmethod
    def sems(roles, batches, parts):
        deep, flat = batches // 2, roles
        dma = pltpu.SemaphoreType.DMA
        return [
            dma((parts,)),
            dma((parts, deep)),
            dma((parts, deep, flat)),
            dma((batches, parts)),
            dma((batches, parts)),
            dma((deep,)),
            dma((deep, flat)),
            dma(((roles - 1) * batches,)),
            dma(((roles - 1) * batches,)),
            dma((parts,)),
        ]

    def along_z(self, step):
        return lax.rem(self.z + step, self.deep) * self.wide + self.y

    def in_plane(self, step):
        place = lax.rem((self.role // 2) * self.wide + self.y + step, self.flat)
        return (place // self.wide) * 2 + self.core, place % self.wide

    def query_to(self, slot, part, sem, role_to, batch_to, src=None):
        begin, size, _ = self.parts[part]
        there = self.query_all.at[slot, pl.ds(begin, size)]
        return remote(there if src is None else src, there, sem, self.q_in.at[slot, part], role_to, batch_to)

    def query_z(self, part, step):
        return self.query_to(self.batch, part, self.q_z.at[part, step], self.role, self.along_z(step))

    def query_plane(self, part, depth, step):
        role_to, y_to = self.in_plane(step)
        return self.query_to(
            self.along_z(depth), part, self.q_plane.at[part, depth, step], role_to, self.z * self.wide + y_to
        )

    def query_on(self, slot, part):
        return self.query_to(slot, part, self.q_on.at[slot, part], self.mate, self.batch)

    def across(self, part):
        return self.query_to(
            self.batch, part, self.q_across.at[part], lax.rem(self.role + 2, self.roles), self.batch
        )

    def pass_to(self, slot, sem, role_to, batch_to):
        there = self.pass_all.at[slot]
        return remote(there, there, sem, self.p_in.at[slot], role_to, batch_to)

    def pass_slot(self, role, batch):
        return (role - 1) * self.batches + batch

    def pass_z(self, step):
        mine = self.pass_slot(self.role, self.batch)
        return self.pass_to(mine, self.p_z.at[step], self.role, self.along_z(step))

    def pass_plane(self, depth, step):
        role_to, y_to = self.in_plane(step)
        slot = self.pass_slot(self.role, self.along_z(depth))
        return self.pass_to(slot, self.p_plane.at[depth, step], role_to, self.z * self.wide + y_to)

    def pass_on(self, slot):
        return self.pass_to(slot, self.p_on.at[slot], self.mate, self.batch)

    def planes(self, do):
        each(1, self.flat, do)

    def hand_query(self, part, depth):
        self.planes(lambda step: self.query_plane(part, depth, step).start())
        self.query_on(self.along_z(depth), part).start()

    def not_source(self, step, do):
        pl.when(step != self.wide)(do)

    def begin_query(self, part):
        @pl.when(self.role == 0)
        def _():
            begin, size, via = self.parts[part]
            keep = pltpu.make_async_copy(
                self.query_ref.at[pl.ds(begin, size)],
                self.query_all.at[self.batch, pl.ds(begin, size)],
                self.own.at[part],
            )
            keep.start()
            keep.wait()
            if via:
                self.across(part).start()
                self.query_on(self.batch, part).start()
            else:
                each(1, self.deep, lambda step: self.query_z(part, step).start())
                self.hand_query(part, 0)

    def second(self, part):
        @pl.when(self.role == 2)
        def _():
            self.query_on(self.batch, part).wait_recv()
            each(1, self.deep, lambda step: self.query_z(part, step).start())
            self.planes(
                lambda step: self.not_source(step, lambda: self.query_plane(part, 0, step).start())
            )
            self.query_on(self.batch, part).start()

    def begin_pass(self):
        @pl.when(self.role > 0)
        def _():
            mine = self.pass_slot(self.role, self.batch)
            keep = pltpu.make_async_copy(self.pass_ref, self.pass_all.at[mine], self.own.at[0])
            keep.start()
            keep.wait()
            each(1, self.deep, lambda step: self.pass_z(step).start())
            self.planes(lambda step: self.pass_plane(0, step).start())
            self.pass_on(mine).start()

    def carrier(self, part):
        return 2 if self.parts[part][2] else 0

    def relay_query(self, *parts):
        for part in parts:

            @pl.when(self.role == self.carrier(part))
            def _():
                def go(depth):
                    self.query_on(self.along_z(depth), part).wait_recv()
                    self.hand_query(part, depth)

                each(1, self.deep, go)

    def relay_pass(self):
        @pl.when(self.role > 0)
        def _():
            def go(depth):
                slot = self.pass_slot(self.role, self.along_z(depth))
                self.pass_on(slot).wait_recv()
                self.planes(lambda step: self.pass_plane(depth, step).start())
                self.pass_on(slot).start()

            each(1, self.deep, go)

    def from_plane(self, part, do):
        via = self.parts[part][2]

        @pl.when(self.core == 0)
        def _():
            def go(slot):
                mine = jnp.logical_and(self.role == self.carrier(part), slot % self.wide == self.y)
                if via:
                    mine = jnp.logical_or(
                        mine, jnp.logical_and(self.role == 0, slot == self.batch)
                    )
                pl.when(jnp.logical_not(mine))(lambda: do(slot))

            each(0, self.batches, go)

    def pass_from_plane(self, do):
        def plane(step):
            role_of, y_of = self.in_plane(step)

            def go(depth):
                do(self.pass_slot(role_of, depth * self.wide + y_of))

            pl.when(role_of > 0)(lambda: each(0, self.deep, go))

        self.planes(plane)

    def share_query(self, *parts):
        for part in parts:

            def go(slot):
                self.query_on(slot, part).wait_recv()
                self.query_on(slot, part).start()

            self.from_plane(part, go)

    def share_pass(self):
        def go(slot):
            self.pass_on(slot).wait_recv()
            self.pass_on(slot).start()

        self.pass_from_plane(go)

    def take(self):
        @pl.when(self.core == 1)
        def _():
            def go(slot):
                for part in range(len(self.parts)):
                    self.query_on(slot, part).wait_recv()

            each(0, self.batches, go)

        for other in range(0, self.roles, 2):
            role_of = other + 1 - self.core

            def go(batch):
                self.pass_on(self.pass_slot(role_of, batch)).wait_recv()

            pl.when(role_of > 0)(lambda: each(0, self.batches, go))

    def end(self):
        def query_sent(part):
            via = self.parts[part][2]

            @pl.when(self.role == self.carrier(part))
            def _():
                each(1, self.deep, lambda step: self.query_z(part, step).wait_send())

                def go(depth):
                    def plane(step):
                        done = self.query_plane(part, depth, step).wait_send
                        if via:
                            pl.when(jnp.logical_or(depth > 0, step != self.wide))(lambda: done())
                        else:
                            done()

                    self.planes(plane)

                each(0, self.deep, go)

            if via:
                pl.when(self.role == 0)(lambda: self.across(part).wait_send())

            @pl.when(self.core == 0)
            def _():
                each(0, self.batches, lambda slot: self.query_on(slot, part).wait_send())

        for part in range(len(self.parts)):
            query_sent(part)

        @pl.when(self.role > 0)
        def _():
            each(1, self.deep, lambda step: self.pass_z(step).wait_send())

            def go(depth):
                self.planes(lambda step: self.pass_plane(depth, step).wait_send())
                self.pass_on(self.pass_slot(self.role, self.along_z(depth))).wait_send()

            each(0, self.deep, go)

        self.pass_from_plane(lambda slot: self.pass_on(slot).wait_send())


def first_kernel(
    roles, batches, micros, rows, early,
    seg, hid_far, wq_far, wk_far, wv_far, wo_far, wi_far, wu_far, *refs,
):
    lines, refs = refs[:9], refs[9:]
    keys_far, values_far, probs_far, query_far, pass_far, layer_far, query_c, vec = refs[:8]
    hid, wq, wk, wv, wo, wi, wu, keys, values, probs, out, queries, context = refs[8:21]
    query_msg, pass_msg, query_all, pass_all, in_sems, out_sems = refs[21:27]
    sems = refs[27:]
    cands = rows // QLEN
    total = micros * cands
    names = ["hid", "wq", "wk", "wv", "wo", "wi", "wu"]
    far = (hid_far, wq_far, wk_far, wv_far, wo_far, wi_far, wu_far)
    moves = Moves(list(zip(far, (hid, wq, wk, wv, wo, wi, wu))), in_sems)
    moves.start(0, 2, 3, 1, 4, 5, 6)

    def need(*which):
        moves.need(*[names.index(name) for name in which])

    blocks = [pl.ds(m * rows, rows) for m in range(micros)]
    stores = Moves(
        [(keys, keys_far), (values, values_far), (probs, probs_far), (query_all, query_far), (pass_all, pass_far)]
        + [(out.at[blocks[m]], layer_far.at[blocks[m]]) for m in range(early)],
        out_sems,
    )
    greeted = greet(roles, batches)
    half = total // 2
    parts = [(at, half, at % total > 0) for at in range(0, 2 * total, half)]
    spread = Spread(roles, batches, parts, query_msg, pass_msg, query_all, pass_all, sems)

    at = 0
    for line in lines:
        wide = line[...].astype(f32).reshape(1, -1)
        for j in range(wide.shape[1] // D):
            vec[at : at + 1, :] = wide[:, j * D : (j + 1) * D]
            at += 1
    mask = head_mask(cands)
    pick = picked_rows(cands, rows)
    pick_low = pick.astype(f32).astype(bf16)
    need("hid")
    x_cand = jnp.concatenate(
        [dot(pick_low, hid[blocks[m], :]).astype(bf16) for m in range(micros)], axis=0
    )
    query_msg[0:total, :] = x_cand
    need("wk", "wv", "wq")
    q_cand = (
        (dot(x_cand, wq[...]) + vec[0:1, :]).astype(bf16).astype(f32) * HEAD_DIM**-0.5
    ).astype(bf16)
    query_c[...] = q_cand

    def project(m):
        x = hid[blocks[m], :]
        keys[blocks[m], :] = dot(x, wk[...]).astype(bf16)
        values[blocks[m], :] = (dot(x, wv[...]) + vec[1:2, :]).astype(bf16)

    project(0)
    for m in range(micros):
        seg_row = seg[m].astype(f32)
        seg_col = jnp.sum(jnp.where(pick, seg_row, 0.0), axis=-1, keepdims=True)
        bias = jnp.where(seg_col == seg_row, 0.0, very_low)
        q_wide = per_head(q_cand[m * cands : (m + 1) * cands], mask)
        scores = dot_right(q_wide, keys[blocks[m], :]) + jnp.concatenate([bias] * HEADS, axis=0)
        if m + 1 < micros:
            project(m + 1)
        raised = jnp.exp(scores - jnp.max(scores, axis=-1, keepdims=True))
        prob = raised * (1.0 / jnp.sum(raised, axis=-1, keepdims=True))
        probs[m * HEADS * cands : (m + 1) * HEADS * cands, :] = prob
        attended = from_heads(dot(prob.astype(bf16), values[blocks[m], :]), mask, cands)
        query_msg[total + m * cands : total + (m + 1) * cands, :] = attended.astype(bf16)
        if m == 0:
            greeted()
            spread.begin_query(1)
            spread.begin_query(0)
        if m == micros // 2 - 1:
            spread.begin_query(2)
        if m == micros - 1:
            spread.begin_query(3)
        if m == 1:
            spread.second(1)
    wide = query_msg[...].astype(f32)
    per_slot = PSLOT // QLEN
    chosen = []
    for part in range(2):
        for m in range(micros):
            for slot in range(cands // per_slot):
                at = (part * micros + m) * cands + slot * per_slot
                chosen.append(wide[at : at + 1])
    pass_msg[...] = jnp.concatenate(chosen, axis=0).astype(bf16)
    spread.begin_pass()
    stores.start(0, 1, 2)

    def steps():
        for m in range(early):
            yield from layer_steps(
                hid.at[blocks[m]], seg[m], keys.at[blocks[m]], values.at[blocks[m]],
                wq, wo, wi, wu, vec, out.at[blocks[m]], queries, context, need,
            )
            stores.start(5 + m)
            yield

    run_beside(steps(), first_plan(spread, len(parts)))
    spread.take()
    stores.start(3, 4)
    spread.end()
    stores.finish()


def first_plan(spread, parts):
    every = range(parts)
    return {
        1: [lambda: spread.second(parts - 1)],
        2: [lambda: spread.relay_query(*every[:-1]), spread.relay_pass],
        4: [lambda: spread.relay_query(parts - 1)],
        8: [lambda: spread.share_query(*every[:-1])],
        12: [lambda: spread.share_query(parts - 1), spread.share_pass],
    }


def first_stage(hid, seg, weights, lines, micros, early, roles, batches):
    rows = hid.shape[0] // micros
    cands = rows // QLEN
    total = micros * cands
    passes = micros * (rows // PSLOT)
    vmem = pl.BlockSpec(memory_space=pltpu.VMEM)
    far = pl.BlockSpec(memory_space=pl.ANY)
    query_all = (batches, 2 * total, D)
    pass_all = ((roles - 1) * batches, 2 * passes, D)
    probs = (micros * HEADS * cands, rows)
    held = pltpu.VMEM(hid.shape, bf16)
    return pl.pallas_call(
        functools.partial(first_kernel, roles, batches, micros, rows, early),
        in_specs=[vmem] + [far] * 7 + [vmem] * len(lines),
        out_specs=(far,) * 6 + (vmem,) * 2,
        out_shape=(
            jax.ShapeDtypeStruct(hid.shape, bf16),
            jax.ShapeDtypeStruct(hid.shape, bf16),
            jax.ShapeDtypeStruct(probs, f32),
            jax.ShapeDtypeStruct(query_all, bf16),
            jax.ShapeDtypeStruct(pass_all, bf16),
            jax.ShapeDtypeStruct((early * rows, D), bf16),
            jax.ShapeDtypeStruct((total, D), bf16),
            jax.ShapeDtypeStruct((sum(line.size for line in lines) // D, D), f32),
        ),
        scratch_shapes=[held]
        + [pltpu.VMEM(w.shape, bf16) for w in weights]
        + [held, held, pltpu.VMEM(probs, f32), pltpu.VMEM((early * rows, D), bf16)]
        + [pltpu.VMEM((rows, D), bf16)] * 2
        + [
            pltpu.VMEM((2 * total, D), bf16),
            pltpu.VMEM((2 * passes, D), bf16),
            pltpu.VMEM(query_all, bf16),
            pltpu.VMEM(pass_all, bf16),
            pltpu.SemaphoreType.DMA((7,)),
            pltpu.SemaphoreType.DMA((5 + early,)),
        ]
        + Spread.sems(roles, batches, 4),
        compiler_params=pltpu.CompilerParams(
            collective_id=1, has_side_effects=True, vmem_limit_bytes=VMEM_BYTES
        ),
        name="first",
    )(seg, hid, *weights, *lines)


def middle_kernel(
    micros,
    cands,
    columns,
    query_all,
    pass_all,
    wo_far,
    wi_far,
    wu_far,
    layer_early,
    vec,
    positive,
    negative,
    bins,
    margins,
    clusters,
    loss_out,
    inner_grad,
    outer_grad,
    output_grad,
    value_bias,
    output_bias,
    first_gain,
    first_shift,
    inner_bias,
    outer_bias,
    second_gain,
    second_shift,
    x_slice,
    d_own,
    layer_far,
    wo,
    wi,
    wu,
    early,
    sems,
    vectors,
    inner_row,
    x_all,
    c_all,
    u_all,
    g_all,
    n_one,
    d_rows,
):
    role, batch = lax.axis_index("role"), lax.axis_index("batch")
    batches = query_all.shape[0]
    own_rows = micros * cands
    n_query = batches * own_rows
    n_dev = pass_all.shape[0]
    per_dev = pass_all.shape[1] // 2
    per_micro = per_dev // micros
    n_pass = n_dev * per_dev
    n_rows = n_query + n_pass
    inner = wi.shape[1]
    chunks = [slice(j * D, (j + 1) * D) for j in range(inner // D)]

    moves = Moves(
        [
            (wo_far, wo),
            (wi_far, wi),
            (wu_far, wu),
            (layer_early, early),
            (early, layer_far.at[pl.ds(0, early.shape[0])]),
        ],
        sems,
    )
    moves.start(0, 1, 2, 3)
    for b in range(batches):
        x_all[b * own_rows : (b + 1) * own_rows, :] = query_all[b, 0:own_rows, :]
        c_all[b * own_rows : (b + 1) * own_rows, :] = query_all[b, own_rows : 2 * own_rows, :]
    wide = pass_all[...].astype(f32)
    x_all[n_query:n_rows, :] = wide[:, 0:per_dev, :].reshape(n_pass, D).astype(bf16)
    c_all[n_query:n_rows, :] = wide[:, per_dev:, :].reshape(n_pass, D).astype(bf16)

    moves.need(0)
    attended = dot(c_all[...], wo[...]) + vec[2:3, :]
    normed, inv_one = norm_parts(x_all[...].astype(f32) + attended)
    n_one[...] = normed
    first_norm = normed * vec[3:4, :] + vec[4:5, :]
    first_low = first_norm.astype(bf16)
    total = first_norm + vec[5:6, :]
    moves.need(1, 2, 3)
    moves.start(4)
    for j, part in enumerate(chunks):
        u = dot(first_low, wi[:, part]) + vec[8 + j : 9 + j, :]
        u_all[:, part] = u
        g = gelu(u).astype(bf16)
        g_all[:, part] = g
        total = total + dot(g, wu[part, :])
    n_two, inv_two = norm_parts(total)
    low = (n_two * vec[6:7, :] + vec[7:8, :]).astype(bf16)
    q_low, p_low = low[:n_query], low[n_query:]

    bin_ids = bins[...]
    queries_total = bin_ids.shape[0] * bin_ids.shape[1]
    weight = jnp.zeros(bin_ids.shape, f32)
    for k in range(NBINS):
        hit = (bin_ids == k).astype(f32)
        amount = jnp.sum(jnp.sum(hit, axis=1, keepdims=True), axis=0, keepdims=True)
        weight = weight + hit * (queries_total / (NBINS * jnp.maximum(amount, 1.0)))

    lane = lax.broadcasted_iota(jnp.int32, (n_query, bin_ids.shape[1]), 1)
    row = lax.broadcasted_iota(jnp.int32, (n_query, bin_ids.shape[1]), 0)
    here = lane == (row // own_rows) * cands + row % cands

    def by_micro(table):
        parts = [
            jnp.broadcast_to(table[m : m + 1, :], (cands, table.shape[1])) for m in range(micros)
        ]
        return jnp.concatenate(parts * batches, axis=0)

    def per_query(table):
        return jnp.sum(jnp.where(here, by_micro(table), 0.0), axis=-1, keepdims=True)

    pos = per_query(positive[...].astype(f32))
    neg = per_query(negative[...].astype(f32))
    margin = per_query(margins[...])
    weight = per_query(weight)

    col = lax.broadcasted_iota(jnp.int32, (n_query, n_pass), 1)
    row = lax.broadcasted_iota(jnp.int32, (n_query, n_pass), 0)
    same = (col % per_dev) // per_micro == (row % own_rows) // cands
    ident = ((col // per_dev) * per_micro + col % per_micro).astype(f32)
    n_ids = n_dev * per_micro
    tab_row = lax.broadcasted_iota(jnp.int32, (n_ids, n_pass), 0)
    tab_col = lax.broadcasted_iota(jnp.int32, (n_ids, n_pass), 1)
    table = tab_row == (tab_col // per_dev) * per_micro + tab_col % per_micro
    cluster = by_micro(dot(clusters[...].astype(f32).astype(bf16), table.astype(f32).astype(bf16)))
    pos_hit = jnp.logical_and(same, ident == pos)
    neg_hit = jnp.logical_and(same, ident == neg)
    pos_cluster = jnp.sum(jnp.where(pos_hit, cluster, 0.0), axis=-1, keepdims=True)
    allowed = jnp.logical_and(same, cluster == pos_cluster)
    scores = dot_right(q_low, p_low) * D**-0.5
    masked = jnp.where(allowed, scores, very_low)
    row_max = jnp.max(masked, axis=-1, keepdims=True)
    raised = jnp.exp(masked - row_max)
    summed = jnp.sum(raised, axis=-1, keepdims=True)
    pos_score = jnp.sum(jnp.where(pos_hit, scores, 0.0), axis=-1, keepdims=True)
    neg_score = jnp.sum(jnp.where(neg_hit, scores, 0.0), axis=-1, keepdims=True)
    gap = pos_score - neg_score - margin
    terms = row_max + jnp.log(summed) - pos_score + weight * gap * gap
    loss_out[...] = jnp.broadcast_to(
        jnp.sum(terms, axis=0, keepdims=True) / queries_total, loss_out.shape
    )
    pull = 2.0 * weight * gap
    pos_one, neg_one = pos_hit.astype(f32), neg_hit.astype(f32)
    d_scores = (raised * (1.0 / summed) - pos_one + pull * (pos_one - neg_one)) * D**-0.5
    parts = three_parts(d_scores)
    d_query = sum(dot(part, p_low) for part in parts)
    d_pass = sum(dot_left(part, q_low) for part in parts)
    grad = jnp.concatenate([d_query, d_pass], axis=0)

    def total_of(array):
        return jnp.sum(array, axis=0, keepdims=True)

    vectors[6:7, :] = total_of(grad * n_two)
    vectors[7:8, :] = total_of(grad)
    d_two = norm_back(grad * vec[6:7, :], n_two, inv_two)
    d_outer = d_two.astype(bf16)
    vectors[5:6, :] = total_of(d_outer.astype(f32))
    select = (
        lax.broadcasted_iota(jnp.int32, (D, 128), 0)
        == lax.broadcasted_iota(jnp.int32, (D, 128), 1) + batch * columns
    )
    select = jnp.logical_and(select, lax.broadcasted_iota(jnp.int32, (D, 128), 1) < columns)
    select = select.astype(f32).astype(bf16)
    first_low = (n_one[...] * vec[3:4, :] + vec[4:5, :]).astype(bf16)
    y_slice = dot(first_low, select).astype(bf16)
    d_first = d_two
    for j, part in enumerate(chunks):
        d_inner = (dot_right(d_outer, wu[part, :]) * gelu_slope(u_all[:, part])).astype(bf16)
        inner_row[:, part] = total_of(d_inner.astype(f32))
        inner_grad[:, part] = dot_left(y_slice, d_inner)[:columns]
        d_first = d_first + dot_right(d_inner, wi[:, part])
    span = inner // batches
    outer_grad[...] = dot_left(g_all[:, pl.ds(pl.multiple_of(batch * span, 128), span)], d_outer)
    vectors[3:4, :] = total_of(d_first * n_one[...])
    vectors[4:5, :] = total_of(d_first)
    d_one = norm_back(d_first * vec[3:4, :], n_one[...], inv_one)
    d_rows[...] = d_one
    d_low = d_one.astype(bf16)
    bias_row = total_of(d_low.astype(f32))
    vectors[2:3, :] = bias_row
    vectors[1:2, :] = sum(dot_right(part, wo[...]) for part in three_parts(bias_row))
    vectors[0:1, :] = jnp.zeros_like(bias_row)
    c_slice = dot(c_all[...], select).astype(bf16)
    output_grad[...] = dot_left(c_slice, d_low)[:columns]
    x_slice[...] = dot(x_all[...], select).astype(bf16)
    mine = sum(dot(part, select) for part in three_parts(vectors[...]))
    outs = [value_bias, output_bias, first_gain, first_shift, outer_bias, second_gain, second_shift]
    for row, out in enumerate(outs):
        out[...] = mine[row + 1, :columns]
    inner_bias[...] = inner_row[0, pl.ds(pl.multiple_of(batch * span, 128), span)]

    moves.finish()

    @pl.when(role == 0)
    def _():
        d_own[...] = d_rows[pl.ds(pl.multiple_of(batch * own_rows, 8), own_rows), :]

    @pl.when(role > 0)
    def _():
        d_own[...] = jnp.zeros_like(d_own)
        begin = pl.multiple_of(n_query + ((role - 1) * batches + batch) * per_dev, 8)
        mine = d_rows[pl.ds(begin, per_dev), :]
        for m in range(micros):
            for slot in range(per_micro):
                at = m * cands + slot * (PSLOT // QLEN)
                d_own[at : at + 1, :] = mine[m * per_micro + slot : m * per_micro + slot + 1, :]


def middle_stage(
    query_all, pass_all, wo, wi, wu, layer_early, layer_rows, vec, positive, negative, bins, margins, clusters
):
    batches = query_all.shape[0]
    micros = positive.shape[0]
    own_rows = query_all.shape[1] // 2
    n_pass = pass_all.shape[0] * pass_all.shape[1] // 2
    n_rows = batches * own_rows + n_pass
    columns = D // batches
    inner = wi.shape[1]
    vmem = pl.BlockSpec(memory_space=pltpu.VMEM)
    far = pl.BlockSpec(memory_space=pl.ANY)
    return pl.pallas_call(
        functools.partial(middle_kernel, micros, own_rows // micros, columns),
        in_specs=[vmem] * 2 + [far] * 4 + [vmem] * 6,
        out_specs=(vmem,) * 14 + (far,),
        out_shape=(
            jax.ShapeDtypeStruct((1, 128), f32),
            jax.ShapeDtypeStruct((columns, inner), f32),
            jax.ShapeDtypeStruct((inner // batches, D), f32),
            jax.ShapeDtypeStruct((columns, D), f32),
        )
        + tuple(jax.ShapeDtypeStruct((size,), f32) for size in [columns] * 4 + [inner // batches] + [columns] * 3)
        + (
            jax.ShapeDtypeStruct((n_rows, 128), bf16),
            jax.ShapeDtypeStruct((own_rows, D), f32),
            jax.ShapeDtypeStruct((layer_rows, D), bf16),
        ),
        scratch_shapes=[pltpu.VMEM(w.shape, bf16) for w in (wo, wi, wu, layer_early)]
        + [
            pltpu.SemaphoreType.DMA((5,)),
            pltpu.VMEM((8, D), f32),
            pltpu.VMEM((1, inner), f32),
            pltpu.VMEM((n_rows, D), bf16),
            pltpu.VMEM((n_rows, D), bf16),
            pltpu.VMEM((n_rows, inner), f32),
            pltpu.VMEM((n_rows, inner), bf16),
            pltpu.VMEM((n_rows, D), f32),
            pltpu.VMEM((n_rows, D), f32),
        ],
        compiler_params=pltpu.CompilerParams(vmem_limit_bytes=VMEM_BYTES),
        name="middle",
    )(query_all, pass_all, wo, wi, wu, layer_early, vec, positive, negative, bins, margins, clusters)


def last_kernel(
    roles, batches, micros, rows, early,
    seg, vec, query_c, d_own, x_slice, hid_far, keys_far, values_far, probs_far,
    wq_far, wk_far, wv_far, wo_far, wi_far, wu_far,
    grads, query_bias, extra, both_far, back_far, layer_far,
    hid, keys, values, probs, wq, wk, wv, wo, wi, wu, out, queries, context,
    both, q_keep, c_keep, z_key, z_value, back, dq_ref, dq_pass, key_part, value_part,
    query_all, pass_all, from_mate, summed, from_x, halves, received, finals,
    in_sems, out_sems, mate_out, mate_in, x_out, x_in, part_out, part_in, last_out, last_in, *sems,
):
    role, batch = lax.axis_index("role"), lax.axis_index("batch")
    core, side = role % 2, role // 2
    mate = role + 1 - 2 * core
    across = lax.rem(role + 2, roles)
    cands = rows // QLEN
    total = micros * cands
    wide_rows = HEADS * cands
    columns = grads.shape[1]
    pieces = summed.shape[2]
    blocks = [pl.ds(m * rows, rows) for m in range(micros)]
    wides = [pl.ds(m * wide_rows, wide_rows) for m in range(micros)]
    names = ["wo", "wk", "wv", "wq", "wi", "wu"]
    pairs = [(wo_far, wo), (wk_far, wk), (wv_far, wv), (wq_far, wq), (wi_far, wi), (wu_far, wu)]
    for m in range(micros):
        names += [(m, "values"), (m, "probs"), (m, "keys"), (m, "hid")]
        pairs += [
            (values_far.at[blocks[m]], values.at[blocks[m]]),
            (probs_far.at[wides[m]], probs.at[wides[m]]),
            (keys_far.at[blocks[m]], keys.at[blocks[m]]),
            (hid_far.at[blocks[m]], hid.at[blocks[m]]),
        ]
    moves = Moves(pairs, in_sems)
    moves.start(0, *range(6, len(pairs)), 1, 2, 3, 4, 5)

    def need(*which):
        moves.need(*[names.index(name) for name in which])

    late = micros - early
    stores = Moves(
        [(out.at[blocks[m]], layer_far.at[blocks[m]]) for m in range(late)]
        + [(both, both_far), (back, back_far)],
        out_sems,
    )
    greeted = greet(roles, batches)
    spread = Spread(
        roles, batches, [(0, total // 2, False), (total // 2, total // 2, True)], dq_ref, dq_pass, query_all, pass_all, sems
    )

    mask = head_mask(cands)
    need("wo")
    d_context = dot_right(d_own[...].astype(bf16), wo[...]).astype(bf16)
    d_query = []
    for m in range(micros):
        need((m, "values"), (m, "probs"), (m, "keys"), (m, "hid"))
        cand = slice(m * cands, (m + 1) * cands)
        q_wide = per_head(query_c[cand, :], mask)
        c_wide = per_head(d_context[cand, :], mask)
        prob = probs[wides[m], :]
        pulled = prob * dot_right(c_wide, values[blocks[m], :])
        d_scores = (pulled - prob * jnp.sum(pulled, axis=-1, keepdims=True)).astype(bf16)
        pair = jnp.concatenate([d_scores, prob.astype(bf16)], axis=0)
        d_query.append(from_heads(dot(d_scores, keys[blocks[m], :]), mask, cands) * HEAD_DIM**-0.5)
        sums = dot(pair, hid[blocks[m], :])
        both[m] = pair
        z_key[wides[m], :] = sums[:wide_rows].astype(bf16)
        z_value[wides[m], :] = sums[wide_rows:].astype(bf16)
        q_keep[wides[m], :] = q_wide
        c_keep[wides[m], :] = c_wide
    d_query = jnp.concatenate(d_query, axis=0).astype(bf16)
    dq_ref[...] = d_query
    wide = d_query.astype(f32)
    per_slot = PSLOT // QLEN
    dq_pass[...] = jnp.concatenate(
        [wide[at : at + 1] for at in range(0, total, per_slot)], axis=0
    )
    split = summed.shape
    key_part[...] = dot_left(z_key[...], q_keep[...]).astype(bf16).reshape(split)
    value_part[...] = dot_left(z_value[...], c_keep[...]).astype(bf16).reshape(split)

    greeted()

    @pl.when(core == 0)
    def _():
        remote(value_part, from_mate, mate_out, mate_in, mate, batch).start()

    @pl.when(core == 1)
    def _():
        remote(key_part, from_mate, mate_out, mate_in, mate, batch).start()

    spread.begin_query(1)

    def to_x(piece):
        return remote(
            summed.at[:, 1 - side, piece], from_x.at[:, piece], x_out.at[piece], x_in.at[piece], across, batch
        )

    def begin_x():
        remote(key_part, from_mate, mate_out, mate_in, mate, batch).wait()

        @pl.when(core == 0)
        def _():
            summed[...] = (key_part[...].astype(f32) + from_mate[...].astype(f32)).astype(bf16)

        @pl.when(core == 1)
        def _():
            summed[...] = (value_part[...].astype(f32) + from_mate[...].astype(f32)).astype(bf16)

        for piece in range(pieces):
            to_x(piece).start()

    def to_batch(piece, step):
        other = lax.rem(batch + step, batches)
        return remote(
            halves.at[other, piece], received.at[batch, piece], part_out.at[other, piece],
            part_in.at[batch, piece], role, other,
        )

    def from_batch(piece, step):
        other = lax.rem(batch + step, batches)
        return remote(
            halves.at[other, piece], received.at[other, piece], part_out.at[other, piece],
            part_in.at[other, piece], role, other,
        )

    def begin_part(piece):
        to_x(piece).wait()
        halves[:, piece] = (
            summed[:, side, piece].astype(f32) + from_x[:, piece].astype(f32)
        ).astype(bf16)
        each(1, batches, lambda step: to_batch(piece, step).start())

    def to_role(step):
        other = lax.rem(role + step, roles)
        return remote(
            finals.at[role], finals.at[role], last_out.at[step], last_in.at[role], other, batch
        )

    def from_role(step):
        other = lax.rem(role + step, roles)
        return remote(
            finals.at[other], finals.at[other], last_out.at[step], last_in.at[other], other, batch
        )

    def begin_last():
        for piece in range(pieces):
            each(1, batches, lambda step: from_batch(piece, step).wait_recv())
            sum_all = halves[batch, piece].astype(f32)

            def add(step, so_far):
                return so_far + received[lax.rem(batch + step, batches), piece].astype(f32)

            finals[role, piece] = lax.fori_loop(1, batches, add, sum_all).astype(bf16)
        for step in range(1, roles):
            to_role(step).start()

    def steps():
        need("wk", "wv", "wq")
        extra[...] = dot_right(dq_ref[...], wq[...]) + d_own[...]
        q_back = dot_right(q_keep[...], wk[...]).astype(bf16)
        c_back = dot_right(c_keep[...], wv[...]).astype(bf16)
        for m in range(micros):
            at = slice(m * wide_rows, (m + 1) * wide_rows)
            back[m, :wide_rows, :] = q_back[at]
            back[m, wide_rows:, :] = c_back[at]
        stores.start(late, late + 1)
        yield
        for m in range(late):
            block = blocks[early + m]
            yield from layer_steps(
                hid.at[block], seg[early + m], keys.at[block], values.at[block],
                wq, wo, wi, wu, vec, out.at[blocks[m]], queries, context, need,
            )
            stores.start(m)
            yield

    parts = [functools.partial(begin_part, piece) for piece in range(pieces)]
    run_beside(steps(), last_plan(begin_x, spread, parts, begin_last))
    spread.take()
    count = batches * total
    all_query = query_all[...].reshape(count, D)
    all_pass = pass_all[...].reshape(-1, D)
    grads[0] = (
        dot_left(x_slice[0:count, :], all_query) + dot_left(x_slice[count:, :], all_pass.astype(bf16))
    )[:columns]
    query_bias[...] = jnp.sum(all_query.astype(f32), axis=0, keepdims=True) + jnp.sum(
        all_pass, axis=0, keepdims=True
    )
    spread.end()
    for piece in range(pieces):
        each(1, batches, lambda step: to_batch(piece, step).wait_send())
    for step in range(1, roles):
        from_role(step).wait_recv()
        to_role(step).wait_send()
    half = pieces * finals.shape[2]
    for x in range(roles // 2):
        here = slice(x * half, (x + 1) * half)
        grads[1, here, :] = finals[2 * x].astype(f32).reshape(half, D)
        grads[2, here, :] = finals[2 * x + 1].astype(f32).reshape(half, D)
    stores.finish()
    moves.finish()


def last_plan(begin_x, spread, parts, begin_last):
    return {
        0: [begin_x, lambda: spread.second(1), lambda: spread.begin_query(0), spread.begin_pass],
        3: [lambda: spread.relay_query(0, 1), spread.relay_pass],
        7: [parts[0]],
        10: [parts[1]],
        13: [parts[2]],
        14: [lambda: spread.share_query(0, 1), spread.share_pass],
        99: [begin_last],
    }


def last_stage(
    seg, vec, query_c, d_own, x_slice, hid, keys, values, probs, weights, early, roles, batches
):
    columns = D // batches
    micros, _, rows = seg.shape
    total = query_c.shape[0]
    passes = micros * (rows // PSLOT)
    wide = micros * HEADS * (rows // QLEN)
    vmem = pl.BlockSpec(memory_space=pltpu.VMEM)
    far = pl.BlockSpec(memory_space=pl.ANY)
    block = (columns, D)
    sides, tile = roles // 2, 16
    pieces = columns // sides // tile
    split = (batches, sides, pieces, tile, D)
    half = (batches, pieces, tile, D)
    dma = pltpu.SemaphoreType.DMA
    late = micros - early
    held = pltpu.VMEM(hid.shape, bf16)
    wide_rows = pltpu.VMEM((wide, D), bf16)
    both = (micros, 2 * wide // micros, rows)
    back = (micros, 2 * wide // micros, D)
    return pl.pallas_call(
        functools.partial(last_kernel, roles, batches, micros, rows, early),
        in_specs=[vmem] * 5 + [far] * 10,
        out_specs=(vmem,) * 3 + (far,) * 3,
        out_shape=(
            jax.ShapeDtypeStruct((3,) + block, f32),
            jax.ShapeDtypeStruct((1, D), f32),
            jax.ShapeDtypeStruct((total, D), f32),
            jax.ShapeDtypeStruct(both, bf16),
            jax.ShapeDtypeStruct(back, bf16),
            jax.ShapeDtypeStruct((late * rows, D), bf16),
        ),
        scratch_shapes=[held, held, held, pltpu.VMEM(probs.shape, f32)]
        + [pltpu.VMEM(w.shape, bf16) for w in weights]
        + [pltpu.VMEM((late * rows, D), bf16)]
        + [pltpu.VMEM((rows, D), bf16)] * 2
        + [
            pltpu.VMEM(both, bf16),
            wide_rows,
            wide_rows,
            wide_rows,
            wide_rows,
            pltpu.VMEM(back, bf16),
            pltpu.VMEM((total, D), bf16),
            pltpu.VMEM((passes, D), f32),
            pltpu.VMEM(split, bf16),
            pltpu.VMEM(split, bf16),
            pltpu.VMEM((batches, total, D), bf16),
            pltpu.VMEM(((roles - 1) * batches, passes, D), f32),
            pltpu.VMEM(split, bf16),
            pltpu.VMEM(split, bf16),
            pltpu.VMEM(half, bf16),
            pltpu.VMEM(half, bf16),
            pltpu.VMEM(half, bf16),
            pltpu.VMEM((roles, pieces, tile, D), bf16),
            dma((6 + 4 * micros,)),
            dma((late + 2,)),
            dma,
            dma,
            dma((pieces,)),
            dma((pieces,)),
            dma((batches, pieces)),
            dma((batches, pieces)),
            dma((roles,)),
            dma((roles,)),
        ]
        + Spread.sems(roles, batches, 2),
        compiler_params=pltpu.CompilerParams(
            collective_id=2, has_side_effects=True, vmem_limit_bytes=VMEM_BYTES
        ),
        name="last",
    )(seg, vec, query_c, d_own, x_slice, hid, keys, values, probs, *weights)


def finish_kernel(
    columns, layer_in, late, both, back, extra, grads, query_bias,
    layer_out, in_grad, query_grad, key_grad, value_grad, bias_out,
):
    del layer_in
    m = pl.program_id(0)
    layer_out[...] = late[...]

    @pl.when(m == 0)
    def _():
        query_grad[...] = grads[0]
        key_grad[...] = grads[1]
        value_grad[...] = grads[2]
        select = (
            lax.broadcasted_iota(jnp.int32, (D, 128), 0)
            == lax.broadcasted_iota(jnp.int32, (D, 128), 1) + lax.axis_index("batch") * columns
        )
        select = select.astype(f32).astype(bf16)
        mine = sum(dot(part, select) for part in three_parts(jnp.broadcast_to(query_bias[...], (8, D))))
        bias_out[...] = mine[0, :columns]

    in_grad[...] = dot_left(both[0], back[0])
    for cand in range(extra.shape[0]):
        at = slice(cand * QLEN, cand * QLEN + 1)
        in_grad[at, :] = in_grad[at, :] + extra[cand : cand + 1, :]


def finish_stage(layer, layer_late, both, back, extra, grads, query_bias):
    micros, wide, rows = both.shape
    columns = grads.shape[1]
    far = pl.BlockSpec(memory_space=pl.ANY)
    cands = rows // QLEN

    def fixed(shape):
        return pl.BlockSpec(shape, lambda m: (0,) * len(shape))

    block = (columns, D)
    piece = layer_late.shape[0] // micros
    skip = (layer.shape[0] - layer_late.shape[0]) // piece
    return pl.pallas_call(
        functools.partial(finish_kernel, columns),
        grid=(micros,),
        in_specs=[
            far,
            pl.BlockSpec((piece, D), lambda m: (m, 0)),
            pl.BlockSpec((1, wide, rows), lambda m: (m, 0, 0)),
            pl.BlockSpec((1, wide, D), lambda m: (m, 0, 0)),
            pl.BlockSpec((cands, D), lambda m: (m, 0)),
            fixed((3,) + block),
            fixed((1, D)),
        ],
        out_specs=(
            pl.BlockSpec((piece, D), lambda m: (m + skip, 0)),
            pl.BlockSpec((rows, D), lambda m: (m, 0)),
            fixed(block),
            fixed(block),
            fixed(block),
            fixed((columns,)),
        ),
        out_shape=(
            jax.ShapeDtypeStruct(layer.shape, layer.dtype),
            jax.ShapeDtypeStruct((micros * rows, D), f32),
            jax.ShapeDtypeStruct(block, f32),
            jax.ShapeDtypeStruct(block, f32),
            jax.ShapeDtypeStruct(block, f32),
            jax.ShapeDtypeStruct((columns,), f32),
        ),
        input_output_aliases={0: 0},
        compiler_params=pltpu.CompilerParams(vmem_limit_bytes=VMEM_BYTES),
        name="finish",
    )(layer, layer_late, both, back, extra, grads, query_bias)


def body(
    roles,
    batches,
    hidden,
    query_weight,
    query_bias,
    key_weight,
    value_weight,
    value_bias,
    output_weight,
    output_bias,
    first_gain,
    first_shift,
    inner_weight,
    inner_bias,
    outer_weight,
    outer_bias,
    second_gain,
    second_shift,
    segment,
    positive,
    negative,
    bins,
    margins,
    clusters,
):
    micros, rows = hidden.shape[0], hidden.shape[2]
    hid = hidden.reshape(micros * rows, D)
    lines = [
        query_bias,
        value_bias,
        output_bias,
        first_gain,
        first_shift,
        outer_bias,
        second_gain,
        second_shift,
        inner_bias,
    ]
    early = micros // 2
    weights = (query_weight, key_weight, value_weight, output_weight, inner_weight, outer_weight)
    keys, values, probs, query_all, pass_all, layer_early, query_c, vec = first_stage(
        hid, segment, weights, lines, micros, early, roles, batches
    )
    loss, inner_grad, outer_grad, output_grad, *biases, x_slice, d_own, layer = middle_stage(
        query_all,
        pass_all,
        output_weight,
        inner_weight,
        outer_weight,
        layer_early,
        micros * rows,
        vec,
        positive,
        negative,
        bins[..., 0],
        margins,
        clusters,
    )
    grads, query_bias_row, extra, both, back, layer_late = last_stage(
        segment, vec, query_c, d_own, x_slice, hid, keys, values, probs, weights, early, roles, batches
    )
    layer_out, in_grad, query_grad, key_grad, value_grad, mine_query = finish_stage(
        layer, layer_late, both, back, extra, grads, query_bias_row
    )
    value_b, output_b, first_g, first_s, inner_b, outer_b, second_g, second_s = biases
    return (
        layer_out.reshape(hidden.shape),
        loss[0, 0],
        in_grad.reshape(hidden.shape),
        query_grad,
        mine_query,
        key_grad,
        value_grad,
        value_b,
        output_grad,
        output_b,
        first_g,
        first_s,
        inner_grad,
        inner_b,
        outer_grad,
        outer_b,
        second_g,
        second_s,
    )


highest = lax.Precision.HIGHEST


def multiply(left, right):
    return jnp.dot(left, right, preferred_element_type=jnp.float32)


def left_product(left, right):
    return jnp.einsum("rd,re->de", left, right, preferred_element_type=jnp.float32)


def right_product(left, right):
    return jnp.einsum("rd,ed->re", left, right, preferred_element_type=jnp.float32)


def select_rows(array, stride):
    return array.reshape((array.shape[0] // stride, stride) + array.shape[1:])[:, 0]


def normalize(incoming, gain_vec, shift_vec):
    center = incoming - jnp.mean(incoming, axis=-1, keepdims=True)
    inv_std = lax.rsqrt(jnp.mean(center * center, axis=-1, keepdims=True) + epsilon)
    normed = center * inv_std
    return (normed * gain_vec + shift_vec, normed, inv_std)


def normalize_back(grad_in, normed, inv_std, gain_vec):
    scaled = grad_in * gain_vec
    return inv_std * (
        scaled
        - jnp.mean(scaled, axis=-1, keepdims=True)
        - normed * jnp.mean(scaled * normed, axis=-1, keepdims=True)
    )


def encode(hidden_rows, seg_rows, weights, att_rows):
    (
        query_weight,
        query_bias,
        key_weight,
        value_weight,
        value_bias,
        output_weight,
        output_bias,
        first_gain,
        first_shift,
        inner_weight,
        inner_bias,
        outer_weight,
        outer_bias,
        second_gain,
        second_shift,
    ) = weights
    row_count = hidden_rows.shape[0]
    blocks = row_count // att_rows
    head_scale = HEAD_DIM ** (-0.5)
    block_shape = (blocks, att_rows, HEADS, HEAD_DIM)
    query_rows = (multiply(hidden_rows, query_weight) + query_bias).astype(jnp.bfloat16)
    key_rows = multiply(hidden_rows, key_weight).astype(jnp.bfloat16)
    value_rows = (multiply(hidden_rows, value_weight) + value_bias).astype(jnp.bfloat16)
    scores = (
        jnp.einsum(
            "bihd,bjhd->bhij",
            query_rows.reshape(block_shape),
            key_rows.reshape(block_shape),
            preferred_element_type=jnp.float32,
        )
        * head_scale
    )
    seg_blocks = seg_rows.reshape(blocks, att_rows)
    same_seg = (seg_blocks[:, :, None] == seg_blocks[:, None, :])[:, None]
    scores = jnp.where(same_seg, scores, very_low)
    row_max = jnp.max(scores, axis=-1, keepdims=True)
    raised = jnp.exp(scores - row_max)
    summed = jnp.sum(raised, axis=-1, keepdims=True)
    attn_probs = (raised / summed).astype(jnp.bfloat16)
    log_total = (row_max + jnp.log(summed))[..., 0]
    context = (
        jnp.einsum(
            "bhij,bjhd->bihd",
            attn_probs,
            value_rows.reshape(block_shape),
            preferred_element_type=jnp.float32,
        )
        .reshape(row_count, D)
        .astype(jnp.bfloat16)
    )
    attended = multiply(context, output_weight) + output_bias
    first_norm, normed_one, inv_one = normalize(
        hidden_rows.astype(jnp.float32) + attended, first_gain, first_shift
    )
    first_low = first_norm.astype(jnp.bfloat16)
    inner_pre = multiply(first_low, inner_weight) + inner_bias
    activated = jax.nn.gelu(inner_pre, approximate=False).astype(jnp.bfloat16)
    outer_out = multiply(activated, outer_weight) + outer_bias
    block_out, normed_two, inv_two = normalize(first_norm + outer_out, second_gain, second_shift)
    log_cand = log_total.reshape(blocks, HEADS, att_rows // QLEN, QLEN)[..., 0]
    kept = (
        key_rows,
        value_rows,
        select_rows(query_rows, QLEN),
        log_cand,
        select_rows(context, QLEN),
        select_rows(normed_one, QLEN),
        select_rows(inv_one, QLEN),
        select_rows(first_low, QLEN),
        select_rows(inner_pre, QLEN),
        select_rows(activated, QLEN),
        select_rows(normed_two, QLEN),
        select_rows(inv_two, QLEN),
    )
    return (block_out, kept)


def encode_back(grad_out, hidden_rows, seg_rows, weights, kept, att_rows):
    (
        query_weight,
        query_bias,
        key_weight,
        value_weight,
        value_bias,
        output_weight,
        output_bias,
        first_gain,
        first_shift,
        inner_weight,
        inner_bias,
        outer_weight,
        outer_bias,
        second_gain,
        second_shift,
    ) = weights
    (
        key_rows,
        value_rows,
        query_cand,
        log_cand,
        context_cand,
        normed_one,
        inv_one,
        first_cand,
        inner_cand,
        active_cand,
        normed_two,
        inv_two,
    ) = kept
    row_count = hidden_rows.shape[0]
    blocks = row_count // att_rows
    cand_rows = row_count // QLEN
    per_block = att_rows // QLEN
    head_scale = HEAD_DIM ** (-0.5)
    hidden_cand = select_rows(hidden_rows, QLEN)
    second_gain_grad = jnp.sum(grad_out * normed_two, axis=0)
    second_shift_grad = jnp.sum(grad_out, axis=0)
    d_second = normalize_back(grad_out, normed_two, inv_two, second_gain)
    d_outer = d_second.astype(jnp.bfloat16)
    outer_weight_grad = left_product(active_cand, d_outer)
    outer_bias_grad = jnp.sum(d_outer.astype(jnp.float32), axis=0)
    d_active = right_product(d_outer, outer_weight)
    gelu_pull = jax.vjp(functools.partial(jax.nn.gelu, approximate=False), inner_cand)[1]
    d_inner = gelu_pull(d_active)[0].astype(jnp.bfloat16)
    inner_weight_grad = left_product(first_cand, d_inner)
    inner_bias_grad = jnp.sum(d_inner.astype(jnp.float32), axis=0)
    d_first = d_second + right_product(d_inner, inner_weight)
    first_gain_grad = jnp.sum(d_first * normed_one, axis=0)
    first_shift_grad = jnp.sum(d_first, axis=0)
    d_attend = normalize_back(d_first, normed_one, inv_one, first_gain)
    d_attend_low = d_attend.astype(jnp.bfloat16)
    output_weight_grad = left_product(context_cand, d_attend_low)
    output_bias_grad = jnp.sum(d_attend_low.astype(jnp.float32), axis=0)
    cand_shape = (blocks, per_block, HEADS, HEAD_DIM)
    block_shape = (blocks, att_rows, HEADS, HEAD_DIM)
    d_context = right_product(d_attend_low, output_weight).astype(jnp.bfloat16).reshape(cand_shape)
    query_heads = query_cand.reshape(cand_shape)
    key_heads = key_rows.reshape(block_shape)
    value_heads = value_rows.reshape(block_shape)
    scores = (
        jnp.einsum("bihd,bjhd->bhij", query_heads, key_heads, preferred_element_type=jnp.float32)
        * head_scale
    )
    seg_blocks = seg_rows.reshape(blocks, att_rows)
    seg_cand = seg_blocks.reshape(blocks, per_block, QLEN)[..., 0]
    same_seg = (seg_cand[:, :, None] == seg_blocks[:, None, :])[:, None]
    attn_probs = jnp.where(same_seg, jnp.exp(scores - log_cand[..., None]), 0.0)
    d_probs = jnp.einsum(
        "bihd,bjhd->bhij", d_context, value_heads, preferred_element_type=jnp.float32
    )
    d_scores = (
        attn_probs * (d_probs - jnp.sum(attn_probs * d_probs, axis=-1, keepdims=True))
    ).astype(jnp.bfloat16)
    d_query = (
        (
            jnp.einsum("bhij,bjhd->bihd", d_scores, key_heads, preferred_element_type=jnp.float32)
            * head_scale
        )
        .reshape(cand_rows, D)
        .astype(jnp.bfloat16)
    )
    d_keys = (
        (
            jnp.einsum("bhij,bihd->bjhd", d_scores, query_heads, preferred_element_type=jnp.float32)
            * head_scale
        )
        .reshape(row_count, D)
        .astype(jnp.bfloat16)
    )
    d_values = (
        jnp.einsum(
            "bhij,bihd->bjhd",
            attn_probs.astype(jnp.bfloat16),
            d_context,
            preferred_element_type=jnp.float32,
        )
        .reshape(row_count, D)
        .astype(jnp.bfloat16)
    )
    query_weight_grad = left_product(hidden_cand, d_query)
    query_bias_grad = jnp.sum(d_query.astype(jnp.float32), axis=0)
    key_weight_grad = left_product(hidden_rows, d_keys)
    value_weight_grad = left_product(hidden_rows, d_values)
    value_bias_grad = jnp.sum(d_values.astype(jnp.float32), axis=0)
    d_hidden = right_product(d_keys, key_weight) + right_product(d_values, value_weight)
    d_cand = right_product(d_query, query_weight) + d_attend
    d_hidden = d_hidden.reshape(cand_rows, QLEN, D)
    d_hidden = jnp.concatenate(
        [d_hidden[:, :1] + d_cand[:, None], d_hidden[:, 1:]], axis=1
    ).reshape(row_count, D)
    gradients = (
        query_weight_grad,
        query_bias_grad,
        key_weight_grad,
        value_weight_grad,
        value_bias_grad,
        output_weight_grad,
        output_bias_grad,
        first_gain_grad,
        first_shift_grad,
        inner_weight_grad,
        inner_bias_grad,
        outer_weight_grad,
        outer_bias_grad,
        second_gain_grad,
        second_shift_grad,
    )
    return (d_hidden, gradients)


def general_body(
    hidden,
    query_weight,
    query_bias,
    key_weight,
    value_weight,
    value_bias,
    output_weight,
    output_bias,
    first_gain,
    first_shift,
    inner_weight,
    inner_bias,
    outer_weight,
    outer_bias,
    second_gain,
    second_shift,
    segment,
    positive,
    negative,
    bins,
    margins,
    clusters,
):
    weights = (
        query_weight,
        query_bias,
        key_weight,
        value_weight,
        value_bias,
        output_weight,
        output_bias,
        first_gain,
        first_shift,
        inner_weight,
        inner_bias,
        outer_weight,
        outer_bias,
        second_gain,
        second_shift,
    )
    micro_count = hidden.shape[0]
    row_count = hidden.shape[2]
    att_rows = min(512, row_count)
    cand_rows = row_count // QLEN
    slot_stride = PSLOT // QLEN
    emb_scale = D ** (-0.5)
    query_flag = jnp.where(lax.axis_index("role") == 0, 1.0, 0.0).astype(jnp.float32)
    first_query = lax.axis_index("batch") * cand_rows
    bin_ids = bins[..., 0]
    query_total = bin_ids.shape[0] * bin_ids.shape[1]
    bin_slots = jnp.arange(NBINS, dtype=jnp.int32)
    bin_counts = jnp.sum((bin_ids[..., None] == bin_slots).astype(jnp.float32), axis=(0, 1))
    bin_table = query_total / (NBINS * bin_counts)
    loss_accum = jnp.zeros((), jnp.float32)
    accum = None
    layer_list = []
    grad_list = []
    for micro_idx in range(micro_count):
        hidden_rows = hidden[micro_idx, 0]
        seg_rows = segment[micro_idx, 0]
        block_out, kept = encode(hidden_rows, seg_rows, weights, att_rows)
        layer_list.append(block_out.astype(jnp.bfloat16))
        cls_rows = select_rows(block_out, QLEN).astype(jnp.bfloat16)
        passage_cls = cls_rows.reshape(-1, slot_stride, D)[:, 0]
        gathered = lax.all_gather(passage_cls, ("role", "batch"), axis=0, tiled=True)
        offset = lax.axis_size("batch") * passage_cls.shape[0]
        passages = gathered[offset:]
        scores = right_product(cls_rows, passages) * emb_scale
        columns = jnp.arange(passages.shape[0], dtype=jnp.int32)
        pos_ids = lax.dynamic_slice_in_dim(positive[micro_idx], first_query, cand_rows)
        neg_ids = lax.dynamic_slice_in_dim(negative[micro_idx], first_query, cand_rows)
        bin_mine = lax.dynamic_slice_in_dim(bin_ids[micro_idx], first_query, cand_rows)
        margin_mine = lax.dynamic_slice_in_dim(margins[micro_idx], first_query, cand_rows)
        pos_hit = pos_ids[:, None] == columns
        neg_hit = neg_ids[:, None] == columns
        cluster_row = clusters[micro_idx]
        pos_cluster = jnp.sum(jnp.where(pos_hit, cluster_row[None, :], 0), axis=-1)
        allowed = cluster_row[None, :] == pos_cluster[:, None]
        masked = jnp.where(allowed, scores, very_low)
        row_max = jnp.max(masked, axis=-1, keepdims=True)
        raised = jnp.exp(masked - row_max)
        summed = jnp.sum(raised, axis=-1, keepdims=True)
        softened = raised / summed
        log_total = (row_max + jnp.log(summed))[:, 0]
        pos_score = jnp.sum(jnp.where(pos_hit, scores, 0.0), axis=-1)
        neg_score = jnp.sum(jnp.where(neg_hit, scores, 0.0), axis=-1)
        weight_query = jnp.sum(jnp.where(bin_mine[:, None] == bin_slots, bin_table, 0.0), axis=-1)
        margin_gap = pos_score - neg_score - margin_mine
        loss_accum = loss_accum + query_flag * jnp.sum(
            log_total - pos_score + weight_query * margin_gap * margin_gap
        )
        pos_float = pos_hit.astype(jnp.float32)
        neg_float = neg_hit.astype(jnp.float32)
        d_scores = query_flag * (
            softened
            - pos_float
            + (2.0 * weight_query * margin_gap)[:, None] * (pos_float - neg_float)
        )
        passages_wide = passages.astype(jnp.float32)
        cls_wide = cls_rows.astype(jnp.float32)
        d_cls = (
            jnp.dot(d_scores, passages_wide, precision=highest, preferred_element_type=jnp.float32)
            * emb_scale
        )
        padded = jnp.concatenate([jnp.zeros((cand_rows, offset), jnp.float32), d_scores], axis=1)
        received = lax.psum_scatter(
            jnp.einsum(
                "qp,qd->pd", padded, cls_wide, precision=highest, preferred_element_type=jnp.float32
            )
            * emb_scale,
            ("role", "batch"),
            scatter_dimension=0,
            tiled=True,
        )
        spread = jnp.concatenate(
            [received[:, None], jnp.zeros((received.shape[0], slot_stride - 1, D), jnp.float32)],
            axis=1,
        ).reshape(cand_rows, D)
        d_hidden, micro_grads = encode_back(
            d_cls + spread, hidden_rows, seg_rows, weights, kept, att_rows
        )
        grad_list.append(d_hidden)
        accum = micro_grads if accum is None else jax.tree.map(jnp.add, accum, micro_grads)
    shards = (
        lax.psum_scatter(accum[0], "batch", scatter_dimension=0, tiled=True),
        lax.psum_scatter(accum[1], "batch", scatter_dimension=0, tiled=True),
        lax.psum_scatter(accum[2], "batch", scatter_dimension=0, tiled=True),
        lax.psum_scatter(accum[3], "batch", scatter_dimension=0, tiled=True),
        lax.psum_scatter(accum[4], "batch", scatter_dimension=0, tiled=True),
        lax.psum_scatter(accum[5], "batch", scatter_dimension=0, tiled=True),
        lax.psum_scatter(accum[6], "batch", scatter_dimension=0, tiled=True),
        lax.psum_scatter(accum[7], "batch", scatter_dimension=0, tiled=True),
        lax.psum_scatter(accum[8], "batch", scatter_dimension=0, tiled=True),
        lax.psum_scatter(accum[9], "batch", scatter_dimension=0, tiled=True),
        lax.psum_scatter(accum[10], "batch", scatter_dimension=0, tiled=True),
        lax.psum_scatter(accum[11], "batch", scatter_dimension=0, tiled=True),
        lax.psum_scatter(accum[12], "batch", scatter_dimension=0, tiled=True),
        lax.psum_scatter(accum[13], "batch", scatter_dimension=0, tiled=True),
        lax.psum_scatter(accum[14], "batch", scatter_dimension=0, tiled=True),
    )
    summed_grads = lax.psum(
        (
            shards[0],
            shards[1],
            shards[2],
            shards[3],
            shards[4],
            shards[5],
            shards[6],
            shards[7],
            shards[8],
            shards[9],
            shards[10],
            shards[11],
            shards[12],
            shards[13],
            shards[14],
        ),
        "role",
    )
    loss_value = lax.psum(loss_accum, ("role", "batch")) / query_total
    layer_out = jnp.stack(layer_list)[:, None]
    in_grad = jnp.stack(grad_list)[:, None]
    return (
        layer_out,
        loss_value,
        in_grad,
        summed_grads[0],
        summed_grads[1],
        summed_grads[2],
        summed_grads[3],
        summed_grads[4],
        summed_grads[5],
        summed_grads[6],
        summed_grads[7],
        summed_grads[8],
        summed_grads[9],
        summed_grads[10],
        summed_grads[11],
        summed_grads[12],
        summed_grads[13],
        summed_grads[14],
    )


def solution(mesh):
    roles, batches = mesh.shape["role"], mesh.shape["batch"]
    small = batches <= 8
    step = functools.partial(body, roles, batches) if small else general_body
    placed = (
        P(None, "role", "batch", None),
        P(),
        P(),
        P(),
        P(),
        P(),
        P(),
        P(),
        P(),
        P(),
        P(),
        P(),
        P(),
        P(),
        P(),
        P(),
        P(None, "role", "batch"),
        P(),
        P(),
        P(),
        P(),
        P(),
    )
    return jax.shard_map(
        step,
        mesh=mesh,
        in_specs=placed,
        out_specs=(
            P(None, "role", "batch", None),
            P(),
            P(None, "role", "batch", None),
            P("batch", None),
            P("batch"),
            P("batch", None),
            P("batch", None),
            P("batch"),
            P("batch", None),
            P("batch"),
            P("batch"),
            P("batch"),
            P("batch", None),
            P("batch"),
            P("batch", None),
            P("batch"),
            P("batch"),
            P("batch"),
        ),
        check_vma=False,
    )
```
